32 devices in a mesh: dp: 8 (over z, core), seq: 4 (over y, x).
Axes of the slice: x: 2, y: 2, z: 4, core: 2. Of those that a mesh axis runs over, the one named last changes fastest.
Arguments:
- hidden_in: bfloat16 [8, 1024, 2048], P('dp', 'seq'), may hold values from -6 to 6
- out_grads: bfloat16 [4, 8, 1024, 2048], P(None, 'dp', 'seq'), may hold values from -6 to 6
- w_in: float32 [2048, 8512], P(('dp', 'seq')), may hold values from -0.125 to 0.125
- w_in_m: float32 [2048, 8512], P(('dp', 'seq')), may hold values from -0.0012207031 to 0.0012207031
- w_in_v: float32 [2048, 8512], P(('dp', 'seq')), may hold values from 3.872789e-08 to 1.5491156e-07
- w_out: float32 [4096, 2048], P(('dp', 'seq')), may hold values from -0.1875 to 0.1875
- w_out_m: float32 [4096, 2048], P(('dp', 'seq')), may hold values from -0.0012207031 to 0.0012207031
- w_out_v: float32 [4096, 2048], P(('dp', 'seq')), may hold values from 3.872789e-08 to 1.5491156e-07
- chan_params: float32 [27904], P(('dp', 'seq')), may hold values from -1 to 6.5
- chan_m: float32 [27904], P(('dp', 'seq')), may hold values from -0.0034179688 to 0.0034179688
- chan_v: float32 [27904], P(('dp', 'seq')), may hold values from 3.4855103e-07 to 1.3942041e-06
- head_params: float32 [3, 64], replicated, may hold values from -7 to 1.5
- head_m: float32 [3, 64], replicated, may hold values from -0.009765625 to 0.009765625
- head_v: float32 [3, 64], replicated, may hold values from 2.478585e-06 to 9.91434e-06
Outputs:
- block_out: bfloat16 [4, 8, 1024, 2048], P(None, 'dp', 'seq')
- hidden_grad: float32 [8, 1024, 2048], P('dp', 'seq')
- grad_norm: float32 [], replicated
- w_in_new: float32 [2048, 8512], P(('dp', 'seq'))
- w_in_m_new: float32 [2048, 8512], P(('dp', 'seq'))
- w_in_v_new: float32 [2048, 8512], P(('dp', 'seq'))
- w_in_copy: bfloat16 [2048, 8512], P(('dp', 'seq'))
- w_out_new: float32 [4096, 2048], P(('dp', 'seq'))
- w_out_m_new: float32 [4096, 2048], P(('dp', 'seq'))
- w_out_v_new: float32 [4096, 2048], P(('dp', 'seq'))
- w_out_copy: bfloat16 [4096, 2048], P(('dp', 'seq'))
- chan_new: float32 [27904], P(('dp', 'seq'))
- chan_m_new: float32 [27904], P(('dp', 'seq'))
- chan_v_new: float32 [27904], P(('dp', 'seq'))
- head_new: float32 [3, 64], replicated
- head_m_new: float32 [3, 64], replicated
- head_v_new: float32 [3, 64], replicated
The draws below stay inside these ranges and needn't reach their ends.
All inputs are finite; a program needn't handle non-finite values.
Results may differ from the reference program's by a relative error of at most 0.012.
The reference program's roundings to bfloat16 on the way count: a program that leaves them out, or rounds other values in their place, can miss the bound.
Values may be sent and summed in bfloat16 or wider, within the bound.
A program may use at most 320 MiB of HBM per device.

```python
import math
import jax
import jax.numpy as jnp
from jax import lax

D = 2048
INNER = 4096
H = 64
P_SIZE = 64
N = 128
TAPS = 4
STRETCH = 256
STEP = 10
E_IN = 8512
CONV_CH = 4352
CHAN_LEN = 27904
LENGTH = 1024
SEQS = 8


def draw_chan_params(key, part):
    key = jax.random.fold_in(key, 11)
    keys = jax.random.split(key, 4)
    conv_taps = jax.random.uniform(keys[0], (TAPS * CONV_CH,), jnp.float32, -1.0, 1.0)
    conv_bias = jax.random.uniform(keys[1], (CONV_CH,), jnp.float32, -0.5, 0.5)
    top_gain = 3.0
    rough_in = jax.random.uniform(keys[2], (D,), jnp.float32, 0.9, 1.1)
    rough_out = jax.random.uniform(keys[3], (INNER,), jnp.float32, 0.9, 1.1)
    ramp_in = 1.0 + (top_gain - 1.0) * jnp.arange(D, dtype=jnp.float32) / D
    ramp_out = 1.0 + (top_gain - 1.0) * jnp.arange(INNER, dtype=jnp.float32) / INNER
    return jnp.concatenate([conv_taps, conv_bias, ramp_in * rough_in, ramp_out * rough_out])


def draw_head_params(key, part):
    key = jax.random.fold_in(key, 23)
    keys = jax.random.split(key, 3)
    rate_bias = jax.random.uniform(keys[0], (H,), jnp.float32, -4.0, -2.0)
    rate_log = jax.random.uniform(keys[1], (H,), jnp.float32, -6.0, 0.5)
    skip_gain = jax.random.uniform(keys[2], (H,), jnp.float32, 0.5, 1.5)
    return jnp.stack([rate_bias, rate_log, skip_gain])


def shard_levels(stream_key, shape, cuts, low, largest):
    factor_of, own = 1.0, jax.random.fold_in(stream_key, 6)
    for axis_at, blocks in cuts:
        steps = jnp.exp(jax.random.uniform(jax.random.fold_in(own, axis_at), (blocks,), jnp.float32, low / len(cuts), largest / len(cuts)))
        factor_of = factor_of * jnp.repeat(steps, shape[axis_at] // blocks).reshape([-1 if axis == axis_at else 1 for axis in range(len(shape))])
    return factor_of


def noise(rng, dims, scale, reach, cuts=(), held_as=jnp.bfloat16):
    level = shard_levels(rng, dims, cuts, -0.22, 0.18) if cuts else 1.0
    drawn = jax.random.normal(rng, dims, jnp.float32) * scale * level
    return jnp.minimum(jnp.maximum(drawn, -reach), reach).astype(held_as)


def setup_inputs(seed: int = 0) -> dict:
    arg_keys = jax.random.split(jax.random.key(seed), 15)
    hidden_in = noise(arg_keys[0], (SEQS, LENGTH, D), 1.0, 6.0, ((0, 8), (1, 4)))
    out_grads = noise(arg_keys[1], (4, SEQS, LENGTH, D), 1.0, 6.0, ((1, 8), (2, 4)))
    w_in = noise(arg_keys[2], (D, E_IN), D ** -0.5, 0.125, ((0, 32),), jnp.float32)
    w_in_m = noise(arg_keys[3], (D, E_IN), ((D * E_IN + INNER * D) ** -0.5), 0.0012207031, ((0, 32),), jnp.float32)
    w_in_v = jnp.clip(jnp.exp(math.log(1.549115609122964e-07) - 1.3862944 * jax.random.uniform(arg_keys[4], (D, E_IN), jnp.float32) ** shard_levels(arg_keys[4], (D, E_IN), ((0, 32),), -0.2, 0.2)), 3.87278902280741e-08, 1.549115609122964e-07)
    w_out = noise(arg_keys[5], (INNER, D), (INNER // 4) ** -0.5, 0.1875, ((0, 32),), jnp.float32)
    w_out_m = noise(arg_keys[6], (INNER, D), ((D * E_IN + INNER * D) ** -0.5), 0.0012207031, ((0, 32),), jnp.float32)
    w_out_v = jnp.clip(jnp.exp(math.log(1.549115609122964e-07) - 1.3862944 * jax.random.uniform(arg_keys[7], (INNER, D), jnp.float32) ** shard_levels(arg_keys[7], (INNER, D), ((0, 32),), -0.2, 0.2)), 3.87278902280741e-08, 1.549115609122964e-07)
    chan_params = draw_chan_params(jax.random.fold_in(arg_keys[14], 71), 0)
    chan_m = noise(arg_keys[9], (CHAN_LEN,), (3 * (D * E_IN + INNER * D) ** -0.5), 0.0034179688, ((0, 32),), jnp.float32)
    chan_v = jnp.clip(jnp.exp(math.log(1.3942041050540865e-06) - 1.3862944 * jax.random.uniform(arg_keys[10], (CHAN_LEN,), jnp.float32) ** shard_levels(arg_keys[10], (CHAN_LEN,), ((0, 32),), -0.2, 0.2)), 3.4855102626352163e-07, 1.3942041050540865e-06)
    head_params = draw_head_params(jax.random.fold_in(arg_keys[14], 71), 0)
    head_m = noise(arg_keys[12], (3, H), (8 * (D * E_IN + INNER * D) ** -0.5), 0.009765625, (), jnp.float32)
    head_v = jnp.clip(jnp.exp(jax.random.uniform(arg_keys[13], (3, H), jnp.float32, math.log(2.4785849745967425e-06), math.log(9.91433989838697e-06))), 2.4785849745967425e-06, 9.91433989838697e-06)
    return {"hidden_in": hidden_in, "out_grads": out_grads, "w_in": w_in, "w_in_m": w_in_m, "w_in_v": w_in_v, "w_out": w_out, "w_out_m": w_out_m, "w_out_v": w_out_v, "chan_params": chan_params, "chan_m": chan_m, "chan_v": chan_v, "head_params": head_params, "head_m": head_m, "head_v": head_v}


EXACT = lax.Precision.HIGHEST
EPS_IN = 1e-06
EPS_OUT = 1e-05
ADAM_EPS = 1e-08
BETA = 0.5
CLIP = 1.0

@jax.custom_vjp
def low(v):
    return lax.optimization_barrier(v.astype(jnp.bfloat16)).astype(jnp.float32)

@jax.custom_vjp
def low_back(v):
    return v

def low_keep(v):
    return (low(v), None)

def low_pass(kept, grad):
    return (grad,)

def back_keep(v):
    return (v, None)

def back_low(kept, grad):
    return (low(grad),)
low.defvjp(low_keep, low_pass)
low_back.defvjp(back_keep, back_low)

def unpack(chan_vec):
    conv_taps = chan_vec[:TAPS * CONV_CH].reshape(TAPS, CONV_CH)
    offset = TAPS * CONV_CH
    conv_bias = chan_vec[offset:offset + CONV_CH]
    offset = offset + CONV_CH
    gain_in = chan_vec[offset:offset + D]
    gain_out = chan_vec[offset + D:offset + D + INNER]
    return (conv_taps, conv_bias, gain_in, gain_out)

def ssd_block(carry_state, pieces, skip_gain):
    head_in, state_in, state_out, step_size, log_rate = pieces
    log_decay = jnp.cumsum(log_rate, axis=0)
    places = jnp.arange(STRETCH)
    causal = (places[:, None] >= places[None, :])[None]
    spread = log_decay.T[:, :, None] - log_decay.T[:, None, :]
    decay_mat = jnp.where(causal, jnp.exp(jnp.where(causal, spread, 0.0)), 0.0)
    scores = jnp.dot(state_out, state_in.T, precision=EXACT)
    mixing = decay_mat * scores[None] * step_size.T[:, None, :]
    inner_part = jnp.einsum('hij,jhp->ihp', mixing, head_in, precision=EXACT)
    carried = jnp.exp(log_decay)[:, :, None] * jnp.einsum('hpn,in->ihp', carry_state, state_out, precision=EXACT)
    result = inner_part + carried + skip_gain[None, :, None] * head_in
    tail_weight = jnp.exp(log_decay[-1][None, :] - log_decay) * step_size
    fresh_state = jnp.einsum('jh,jhp,jn->hpn', tail_weight, head_in, state_in, precision=EXACT)
    new_state = jnp.exp(log_decay[-1])[:, None, None] * carry_state + fresh_state
    return (new_state, result)

def forward(tokens, w_in, w_out, chan_vec, head_vec):
    conv_taps, conv_bias, gain_in, gain_out = unpack(low(chan_vec))
    square = lax.optimization_barrier(jnp.mean(tokens * tokens, axis=-1, keepdims=True))
    normed = low(tokens * lax.rsqrt(square + EPS_IN) * gain_in)
    projected = low_back(jnp.dot(normed, low(w_in), precision=EXACT))
    gate_in = projected[:, :INNER]
    conv_in = projected[:, INNER:INNER + CONV_CH]
    rate_in = projected[:, INNER + CONV_CH:]
    padded = jnp.concatenate([jnp.zeros((TAPS - 1, CONV_CH), jnp.float32), conv_in], axis=0)
    conv_out = conv_bias[None, :]
    for tap_index in range(TAPS):
        conv_out = conv_out + conv_taps[tap_index] * padded[tap_index:tap_index + LENGTH]
    activated = jax.nn.silu(conv_out)
    head_in = activated[:, :INNER].reshape(LENGTH, H, P_SIZE)
    state_in = activated[:, INNER:INNER + N]
    state_out = activated[:, INNER + N:]
    step_size = jax.nn.softplus(rate_in + head_vec[0])
    log_rate = -step_size * jnp.exp(head_vec[1])
    blocks = LENGTH // STRETCH
    pieces = (head_in.reshape(blocks, STRETCH, H, P_SIZE), state_in.reshape(blocks, STRETCH, N), state_out.reshape(blocks, STRETCH, N), step_size.reshape(blocks, STRETCH, H), log_rate.reshape(blocks, STRETCH, H))

    def block_step(carry_state, block_pieces):
        return ssd_block(carry_state, block_pieces, head_vec[2])
    _, mixed_out = lax.scan(jax.checkpoint(block_step), jnp.zeros((H, P_SIZE, N), jnp.float32), pieces)
    mixed_out = mixed_out.reshape(LENGTH, INNER)
    gate_act = jax.nn.silu(gate_in)
    out_low = low(w_out)
    results = []
    for width_level in range(4):
        span_width = INNER * 2 ** width_level // 8
        gated_rows = mixed_out[:, :span_width] * gate_act[:, :span_width]
        scaled = gated_rows * lax.rsqrt(lax.optimization_barrier(jnp.mean(gated_rows * gated_rows, axis=-1, keepdims=True)) + EPS_OUT) * gain_out[:span_width]
        results.append(tokens + jnp.dot(low(scaled), out_low[:span_width], precision=EXACT))
    return jnp.stack(results)

def adam_step(weight, gradient, moment, second, step_rate, weight_decay):
    new_moment = BETA * moment + (1.0 - BETA) * gradient
    new_second = BETA * second + (1.0 - BETA) * gradient * gradient
    correction = 1.0 - BETA ** STEP
    update = new_moment / correction / (jnp.sqrt(new_second / correction) + ADAM_EPS)
    return (weight - step_rate * (update + weight_decay * weight), new_moment, new_second)

def reference(hidden_in, out_grads, w_in, w_in_m, w_in_v, w_out, w_out_m, w_out_v, chan_params, chan_m, chan_v, head_params, head_m, head_v):
    tokens_all = hidden_in.astype(jnp.float32)
    cotangent = jnp.moveaxis(out_grads.astype(jnp.float32), 0, 1)

    def per_sequence(totals, seq_item):
        tokens, grad_out = seq_item
        block_out, pullback = jax.vjp(forward, tokens, w_in, w_out, chan_params, head_params)
        grad_parts = pullback(grad_out)
        totals = tuple((running + new_part for running, new_part in zip(totals, grad_parts[1:])))
        return (totals, (block_out.astype(jnp.bfloat16), grad_parts[0]))
    start_grads = (jnp.zeros_like(w_in), jnp.zeros_like(w_out), jnp.zeros_like(chan_params), jnp.zeros_like(head_params))
    totals, (block_out, hidden_grad) = lax.scan(per_sequence, start_grads, (tokens_all, cotangent))
    block_out = jnp.moveaxis(block_out, 0, 1)
    squares = jnp.sum(totals[0] * totals[0]) + jnp.sum(totals[1] * totals[1])
    squares = squares + jnp.sum(totals[2] * totals[2]) + jnp.sum(totals[3] * totals[3])
    grad_norm = jnp.sqrt(squares)
    clip_factor = jnp.minimum(1.0, CLIP / grad_norm)
    w_in_new, w_in_m_new, w_in_v_new = adam_step(w_in, clip_factor * totals[0], w_in_m, w_in_v, 0.02, 0.1)
    w_out_new, w_out_m_new, w_out_v_new = adam_step(w_out, clip_factor * totals[1], w_out_m, w_out_v, 0.03, 0.1)
    chan_new, chan_m_new, chan_v_new = adam_step(chan_params, clip_factor * totals[2], chan_m, chan_v, 0.2, 0.0)
    head_new, head_m_new, head_v_new = adam_step(head_params, clip_factor * totals[3], head_m, head_v, 1.0, 0.0)
    return (block_out, hidden_grad, grad_norm, w_in_new, w_in_m_new, w_in_v_new, w_in_new.astype(jnp.bfloat16), w_out_new, w_out_m_new, w_out_v_new, w_out_new.astype(jnp.bfloat16), chan_new, chan_m_new, chan_v_new, head_new, head_m_new, head_v_new)
```

```python
import functools

import jax
import jax.numpy as jnp
from jax import lax
from jax.experimental import pallas as pl
from jax.experimental.pallas import tpu as pltpu
from jax.sharding import PartitionSpec as P

D = 2048
INNER = 4096
H = 64
P_SIZE = 64
N = 128
TAPS = 4
STEP = 10
E_IN = 8512
CONV_CH = 4352
LANES = 128
CHUNK = 128
LEVELS = 4

EXACT = lax.Precision.HIGHEST
EPS_IN = 1e-06
EPS_OUT = 1e-05
ADAM_EPS = 1e-08
BETA = 0.5
CLIP = 1.0
F32 = jnp.float32
BF16 = jnp.bfloat16
MASKED = -1e30


def level_width(level):
    return INNER * 2**level // 8


SEGMENTS = tuple(
    (0 if level == 0 else level_width(level - 1), level_width(level)) for level in range(LEVELS)
)


def dot(a, b, dims=((1,), (0,)), precision=None):
    return lax.dot_general(a, b, (dims, ((), ())), precision=precision, preferred_element_type=F32)


NT = ((1,), (1,))
TN = ((0,), (0,))


def softplus(v):
    return jnp.maximum(v, 0.0) + jnp.log1p(jnp.exp(-jnp.abs(v)))


def two_terms(v):
    high = v.astype(BF16)
    return high, (v - high.astype(F32)).astype(BF16)


def spread_heads(v, spread):
    high, rest = two_terms(v)
    return dot(high, spread) + dot(rest, spread)


def rates(dt_raw, heads):
    step = softplus(dt_raw + heads[0:1, :])
    return step, step * heads[1:2, :]


def triangle(size):
    row = lax.broadcasted_iota(jnp.int32, (size, size), 0)
    col = lax.broadcasted_iota(jnp.int32, (size, size), 1)
    return row, col


def conv_block(taps, xbuf, lanes):
    out = taps[TAPS : TAPS + 1, lanes]
    for tap in range(TAPS):
        out = out + taps[tap : tap + 1, lanes] * xbuf[5 + tap : 5 + tap + CHUNK, lanes]
    return out


def pair_decay(cum, cum_t, causal, head):
    gap = cum[:, head : head + 1] - cum_t[head : head + 1, :]
    return jnp.exp(jnp.where(causal, gap, MASKED))


def scan_forward_kernel(cw, px, taps, heads, skip, spread, y, states, xbuf, state, xdt, carried):
    cc = cw + 2 * N

    @pl.when(pl.program_id(0) == 0)
    def _():
        state[...] = jnp.zeros_like(state)
        xbuf[0:8, :] = jnp.zeros((8, cc), F32)

    xbuf[8 : 8 + CHUNK, :] = px[:, :cc]
    step, rate = rates(px[:, cc:], heads)
    row, col = triangle(CHUNK)
    causal = row >= col
    cum = dot(causal.astype(F32), rate, precision=EXACT)
    cum_t = cum.T
    spread_m = spread[...]
    last = cum[CHUNK - 1 : CHUNK, :]
    step_x = spread_heads(step, spread_m)
    grow_x = spread_heads(jnp.exp(cum), spread_m)
    tail_x = spread_heads(jnp.exp(last - cum), spread_m)

    def activated(lanes):
        conv = conv_block(taps, xbuf, lanes)
        return conv * jax.nn.sigmoid(conv)

    state_in = activated(slice(cw, cw + N))
    state_out = activated(slice(cw + N, cw + 2 * N))
    scores = dot(state_out, state_in, NT, EXACT)
    states[0] = state[...].astype(BF16)
    carried[...] = dot(state_out.astype(BF16), state[...].astype(BF16))
    first = lax.broadcasted_iota(jnp.int32, (1, LANES), 1) < P_SIZE
    for pair in range(cw // LANES):
        lanes = slice(pair * LANES, (pair + 1) * LANES)
        x = activated(lanes)
        xd = (x * step_x[:, lanes]).astype(BF16).astype(F32)
        xdt[:, lanes] = (xd * tail_x[:, lanes]).astype(BF16)
        stacked = jnp.concatenate([jnp.where(first, xd, 0.0), jnp.where(first, 0.0, xd)], axis=0)
        mixing = jnp.concatenate(
            [
                (pair_decay(cum, cum_t, causal, 2 * pair + k) * scores).astype(BF16)
                for k in range(2)
            ],
            axis=1,
        )
        y[:, lanes] = (
            dot(mixing, stacked.astype(BF16))
            + grow_x[:, lanes] * carried[:, lanes]
            + skip[:, lanes] * x
        )
    state[...] = grow_x[CHUNK - 1 : CHUNK, :] * state[...] + dot(
        state_in.astype(BF16), xdt[...], TN
    )
    xbuf[0:8, :] = xbuf[CHUNK : CHUNK + 8, :]


def scan_backward_kernel(
    cw, px, halo, taps, heads, skip, spread, gather, dy, y, states,
    dpx, dtaps, dheads, dskip,
    xbuf, dstate, dcbuf, slope, xact, xd_s, dxd_s, acc_s,
):
    cc = cw + 2 * N
    at = pl.program_id(0)

    @pl.when(at == 0)
    def _():
        dstate[...] = jnp.zeros_like(dstate)
        dcbuf[CHUNK : CHUNK + 8, :] = jnp.zeros((8, cc), F32)
        dtaps[...] = jnp.zeros_like(dtaps)
        dheads[...] = jnp.zeros_like(dheads)
        dskip[...] = jnp.zeros_like(dskip)

    xbuf[0:8, :] = jnp.where(at == pl.num_programs(0) - 1, 0.0, halo[:, :cc])
    xbuf[8 : 8 + CHUNK, :] = px[:, :cc]
    dt_raw = px[:, cc:]
    step, rate = rates(dt_raw, heads)
    row, col = triangle(CHUNK)
    causal = row >= col
    cum = dot(causal.astype(F32), rate, precision=EXACT)
    cum_t = cum.T
    spread_m = spread[...]
    last = cum[CHUNK - 1 : CHUNK, :]
    step_x = spread_heads(step, spread_m)
    grow_x = spread_heads(jnp.exp(cum), spread_m)
    tail_x = spread_heads(jnp.exp(last - cum), spread_m)

    for block in range(cc // LANES):
        lanes = slice(block * LANES, (block + 1) * LANES)
        conv = conv_block(taps, xbuf, lanes)
        sig = jax.nn.sigmoid(conv)
        act = conv * sig
        xact[:, lanes] = act
        slope[:, lanes] = sig + act * (1.0 - sig)
    state_in = xact[:, cw : cw + N]
    state_out = xact[:, cw + N : cc]
    scores = dot(state_out, state_in, NT, EXACT)
    in_low = state_in.astype(BF16)
    out_low = state_out.astype(BF16)
    dstate_low = dstate[...].astype(BF16)
    acc_s[...] = jnp.zeros_like(acc_s)
    dxd_s[...] = tail_x * dot(in_low, dstate_low)
    dskip[0:1, :] += jnp.sum(xact[:, :cw] * dy[...], axis=0, keepdims=True)
    first = lax.broadcasted_iota(jnp.int32, (1, LANES), 1) < P_SIZE
    xd_s[...] = (xact[:, :cw] * step_x).astype(BF16)
    total = jnp.sum(xd_s[...].astype(F32) * dxd_s[...], axis=0, keepdims=True) + grow_x[
        CHUNK - 1 : CHUNK, :
    ] * jnp.sum(dstate[...] * states[0].astype(F32), axis=0, keepdims=True)
    dscores = jnp.zeros((CHUNK, CHUNK), F32)
    for pair in range(cw // LANES):
        lanes = slice(pair * LANES, (pair + 1) * LANES)
        dyp = dy[:, lanes]
        stacked = jnp.concatenate(
            [jnp.where(first, dyp, 0.0), jnp.where(first, 0.0, dyp)], axis=0
        ).astype(BF16)
        decays = [pair_decay(cum, cum_t, causal, 2 * pair + k) for k in range(2)]
        mixing = jnp.concatenate([(decay * scores).astype(BF16) for decay in decays], axis=0)
        dxd_s[:, lanes] += dot(mixing, stacked, TN)
        dmix = dot(stacked, xd_s[:, lanes], NT)
        dscores = dscores + decays[0] * dmix[:CHUNK] + decays[1] * dmix[CHUNK:]
    dy_low = dy[...].astype(BF16)
    dy_f = dy_low.astype(F32)
    xd_f = xd_s[...].astype(F32)
    dxd = dxd_s[...]
    y_scan = y[...] - skip[...] * xact[:, :cw]
    final = lax.broadcasted_iota(jnp.int32, (CHUNK, 1), 0) == CHUNK - 1
    gather_m = gather[...]
    dcum = spread_heads(dy_f * y_scan - xd_f * dxd + jnp.where(final, total, 0.0), gather_m)
    dstep = spread_heads(xact[:, :cw] * dxd, gather_m)
    drate = dot((row <= col).astype(F32), dcum, precision=EXACT)
    dstep = dstep + drate * heads[1:2, :]
    ddt = dstep * jax.nn.sigmoid(dt_raw + heads[0:1, :])
    dheads[0:1, :] += jnp.sum(ddt, axis=0, keepdims=True)
    dheads[1:2, :] += jnp.sum(drate * rate, axis=0, keepdims=True)
    grown = (grow_x * dy_f).astype(BF16)
    dscores_low = dscores.astype(BF16)
    dout = dot(dscores_low, in_low) + dot(grown, states[0], NT)
    din = dot(dscores_low, out_low, TN) + dot((tail_x * xd_f).astype(BF16), dstate_low, NT)
    dstate[...] = grow_x[CHUNK - 1 : CHUNK, :] * dstate[...] + dot(out_low, grown, TN)
    dcbuf[:CHUNK, :cw] = (step_x * dxd + skip[...] * dy[...]) * slope[:, :cw]
    dcbuf[:CHUNK, cw : cw + N] = din * slope[:, cw : cw + N]
    dcbuf[:CHUNK, cw + N :] = dout * slope[:, cw + N :]
    for block in range(cc // LANES):
        lanes = slice(block * LANES, (block + 1) * LANES)
        dconv = dcbuf[:CHUNK, lanes]
        dtaps[TAPS : TAPS + 1, lanes] += jnp.sum(dconv, axis=0, keepdims=True)
        back = taps[TAPS - 1 : TAPS, lanes] * dconv
        for tap in range(TAPS):
            dtaps[tap : tap + 1, lanes] += jnp.sum(
                dconv * xbuf[5 + tap : 5 + tap + CHUNK, lanes], axis=0, keepdims=True
            )
            if tap < TAPS - 1:
                reach = TAPS - 1 - tap
                back = back + taps[tap : tap + 1, lanes] * dcbuf[reach : reach + CHUNK, lanes]
        dpx[:, lanes] = back.astype(BF16)
    dpx[:, cc:] = ddt.astype(BF16)
    dcbuf[CHUNK : CHUNK + 8, :] = dcbuf[0:8, :]


def whole(shape):
    return pl.BlockSpec(shape, lambda i: (0,) * len(shape))


def scan_forward(px, taps, heads, skip, spread):
    length, width = px.shape
    cw = skip.shape[1]
    cc = cw + 2 * N
    chunks = length // CHUNK
    return pl.pallas_call(
        functools.partial(scan_forward_kernel, cw),
        grid=(chunks,),
        in_specs=[
            pl.BlockSpec((CHUNK, width), lambda i: (i, 0)),
            whole(taps.shape),
            whole(heads.shape),
            whole(skip.shape),
            whole(spread.shape),
        ],
        out_specs=[
            pl.BlockSpec((CHUNK, cw), lambda i: (i, 0)),
            pl.BlockSpec((1, N, cw), lambda i: (i, 0, 0)),
        ],
        out_shape=[
            jax.ShapeDtypeStruct((length, cw), F32),
            jax.ShapeDtypeStruct((chunks, N, cw), BF16),
        ],
        scratch_shapes=[
            pltpu.VMEM((CHUNK + 8, cc), F32),
            pltpu.VMEM((N, cw), F32),
            pltpu.VMEM((CHUNK, cw), BF16),
            pltpu.VMEM((CHUNK, cw), F32),
        ],
        compiler_params=pltpu.CompilerParams(vmem_limit_bytes=48 * 2**20),
        name="scan_forward",
    )(px, taps, heads, skip, spread)


def scan_backward(px, taps, heads, skip, spread, gather, dy, y, states):
    length, width = px.shape
    cw = skip.shape[1]
    cc = cw + 2 * N
    chunks = length // CHUNK
    eighths = CHUNK // 8
    return pl.pallas_call(
        functools.partial(scan_backward_kernel, cw),
        grid=(chunks,),
        in_specs=[
            pl.BlockSpec((CHUNK, width), lambda i: (chunks - 1 - i, 0)),
            pl.BlockSpec(
                (8, width), lambda i: (jnp.maximum((chunks - 1 - i) * eighths - 1, 0), 0)
            ),
            whole(taps.shape),
            whole(heads.shape),
            whole(skip.shape),
            whole(spread.shape),
            whole(gather.shape),
            pl.BlockSpec((CHUNK, cw), lambda i: (chunks - 1 - i, 0)),
            pl.BlockSpec((CHUNK, cw), lambda i: (chunks - 1 - i, 0)),
            pl.BlockSpec((1, N, cw), lambda i: (chunks - 1 - i, 0, 0)),
        ],
        out_specs=[
            pl.BlockSpec((CHUNK, width), lambda i: (chunks - 1 - i, 0)),
            whole((8, cc)),
            whole((8, LANES)),
            whole((8, cw)),
        ],
        out_shape=[
            jax.ShapeDtypeStruct((length, width), BF16),
            jax.ShapeDtypeStruct((8, cc), F32),
            jax.ShapeDtypeStruct((8, LANES), F32),
            jax.ShapeDtypeStruct((8, cw), F32),
        ],
        scratch_shapes=[
            pltpu.VMEM((CHUNK + 8, cc), F32),
            pltpu.VMEM((N, cw), F32),
            pltpu.VMEM((CHUNK + 8, cc), F32),
            pltpu.VMEM((CHUNK, cc), F32),
            pltpu.VMEM((CHUNK, cc), F32),
            pltpu.VMEM((CHUNK, cw), BF16),
            pltpu.VMEM((CHUNK, cw), F32),
            pltpu.VMEM((CHUNK, CHUNK), F32),
        ],
        compiler_params=pltpu.CompilerParams(vmem_limit_bytes=48 * 2**20),
        name="scan_backward",
    )(px, px, taps, heads, skip, spread, gather, dy, y, states)


def adam_step(weight, gradient, moment, second, step_rate, weight_decay):
    new_moment = BETA * moment + (1.0 - BETA) * gradient
    new_second = BETA * second + (1.0 - BETA) * gradient * gradient
    correction = 1.0 - BETA**STEP
    update = new_moment / correction / (jnp.sqrt(new_second / correction) + ADAM_EPS)
    return (weight - step_rate * (update + weight_decay * weight), new_moment, new_second)


def all_sum(value, axis):
    size = lax.axis_size(axis)
    by = 1
    while by < size:
        value = value + lax.ppermute(value, axis, [(i, i ^ by) for i in range(size)])
        by *= 2
    return value


def swap_blocks(blocks):
    return lax.all_to_all(blocks, "seq", split_axis=0, concat_axis=0, tiled=True)


def pack_terms(values):
    high = lax.reduce_precision(values, 8, 7)
    packed = jnp.concatenate([high, values - high], axis=-1).astype(BF16)
    return jnp.pad(packed, ((0, 0), (0, LANES - packed.shape[-1])))


def unpack_terms(packed, count):
    packed = packed.astype(F32)
    return packed[..., :count] + packed[..., count : 2 * count]


def on_device(
    hidden_in, out_grads, w_in, w_in_m, w_in_v, w_out, w_out_m, w_out_v,
    chan_params, chan_m, chan_v, head_params, head_m, head_v,
):
    parts = lax.axis_size("seq")
    groups = lax.axis_size("dp")
    q = lax.axis_index("seq")
    rows = hidden_in.shape[1]
    length = rows * parts
    cw = INNER // parts
    hq = H // parts
    cc = cw + 2 * N
    in_rows = w_in.shape[0]
    out_rows = w_out.shape[0]

    in_low = w_in.astype(BF16)
    out_low = w_out.astype(BF16)
    z_blocks = in_low[:, :INNER].reshape(in_rows, parts, cw).transpose(1, 0, 2)
    x_blocks = in_low[:, INNER : 2 * INNER].reshape(in_rows, parts, cw).transpose(1, 0, 2)
    bc_block = jnp.broadcast_to(
        in_low[None, :, 2 * INNER : 2 * INNER + 2 * N], (parts, in_rows, 2 * N)
    )
    dt_blocks = in_low[:, 2 * INNER + 2 * N :].reshape(in_rows, parts, hq).transpose(1, 0, 2)
    dt_blocks = jnp.pad(dt_blocks, ((0, 0), (0, 0), (0, LANES - hq)))
    x_blocks = jnp.concatenate([x_blocks, bc_block, dt_blocks], axis=2)
    wx = lax.all_gather(swap_blocks(x_blocks), "dp", axis=0).reshape(D, cc + LANES)
    hidden = lax.all_gather(hidden_in[0], "seq", axis=0, tiled=True)
    chan_full = lax.all_gather(chan_params.astype(BF16), ("dp", "seq"), axis=0, tiled=True).astype(
        F32
    )
    wz = lax.all_gather(swap_blocks(z_blocks), "dp", axis=0).reshape(D, cw)
    wo = lax.all_gather(out_low, ("dp", "seq"), axis=0, tiled=True)

    conv_taps = chan_full[: TAPS * CONV_CH].reshape(TAPS, CONV_CH)
    conv_bias = chan_full[TAPS * CONV_CH : (TAPS + 1) * CONV_CH].reshape(1, CONV_CH)
    offset = (TAPS + 1) * CONV_CH
    gain_in = chan_full[offset : offset + D]
    gain_out = chan_full[offset + D : offset + D + INNER]
    taps_all = jnp.concatenate(
        [conv_taps, conv_bias, jnp.zeros((8 - TAPS - 1, CONV_CH), F32)], axis=0
    )
    taps = jnp.concatenate(
        [lax.dynamic_slice(taps_all, (0, q * cw), (8, cw)), taps_all[:, INNER:]], axis=1
    )
    own_gain = lax.dynamic_slice(gain_out, (q * cw,), (cw,))
    own_heads = lax.dynamic_slice(head_params, (0, q * hq), (3, hq))
    heads = jnp.pad(
        jnp.stack([own_heads[0], -jnp.exp(own_heads[1])]), ((0, 6), (0, LANES - hq))
    )
    skip = jnp.repeat(own_heads[2], P_SIZE).reshape(1, cw)
    spread = (
        jnp.arange(LANES)[:, None] == (jnp.arange(cw) // P_SIZE)[None, :]
    ).astype(BF16)

    tokens = hidden.astype(F32)
    scale = lax.rsqrt(jnp.mean(tokens * tokens, axis=-1, keepdims=True) + EPS_IN)
    normed = (tokens * scale * gain_in).astype(BF16)
    px = dot(normed, wx)
    y, states = scan_forward(px, taps, heads, skip, spread)
    z = dot(normed, wz)
    sig = jax.nn.sigmoid(z)
    gate = z * sig
    gated = y * gate
    channel = q * cw + jnp.arange(cw)
    squares = jnp.stack(
        [
            jnp.sum(jnp.where((channel >= low) & (channel < high), gated * gated, 0.0), axis=-1)
            for low, high in SEGMENTS
        ],
        axis=-1,
    )
    u_blocks = jnp.concatenate([(gated * own_gain).astype(BF16), pack_terms(squares)], axis=-1)
    u_blocks = swap_blocks(u_blocks.reshape(parts, rows, cw + LANES))
    u = u_blocks[:, :, :cw].transpose(1, 0, 2).reshape(rows, INNER)
    squares = jnp.cumsum(
        jnp.sum(unpack_terms(u_blocks[:, :, cw:], LEVELS), axis=0), axis=-1
    )

    own_tokens = hidden_in[0].astype(F32)
    cotangent = out_grads[:, 0]
    norms = [
        lax.rsqrt(squares[:, k : k + 1] / level_width(k) + EPS_OUT) for k in range(LEVELS)
    ]
    branch = jnp.zeros((rows, D), F32)
    block_out = []
    pulls = []
    for k, (low, high) in enumerate(SEGMENTS):
        branch = branch + dot(u[:, low:high], wo[low:high])
        block_out.append((own_tokens + norms[k] * branch).astype(BF16))
        inner = jnp.sum(cotangent[k].astype(F32) * branch, axis=-1, keepdims=True)
        pulls.append(norms[k] ** 3 * (inner / level_width(k)))
    block_out = jnp.stack(block_out)[:, None]
    mixed = [None] * LEVELS
    coefs = [None] * LEVELS
    running = jnp.zeros((rows, D), F32)
    coef = jnp.zeros((rows, 1), F32)
    for k in reversed(range(LEVELS)):
        running = running + norms[k] * cotangent[k].astype(F32)
        coef = coef + pulls[k]
        mixed[k] = running.astype(BF16)
        coefs[k] = coef
    back = jnp.concatenate(
        [dot(mixed[k], wo[low:high], NT).astype(BF16) for k, (low, high) in enumerate(SEGMENTS)],
        axis=-1,
    )
    coefs = jnp.concatenate(coefs, axis=-1)
    back_blocks = jnp.concatenate(
        [
            back.reshape(rows, parts, cw).transpose(1, 0, 2),
            jnp.broadcast_to(pack_terms(coefs)[None], (parts, rows, LANES)),
        ],
        axis=-1,
    )
    back_own = swap_blocks(back_blocks).reshape(length, cw + LANES)
    dwo = jnp.concatenate(
        [dot(u[:, low:high], mixed[k], TN).astype(BF16) for k, (low, high) in enumerate(SEGMENTS)],
        axis=0,
    )
    dwo = lax.psum_scatter(
        dwo.reshape(groups, parts, out_rows, D).transpose(1, 0, 2, 3), "seq", scatter_dimension=0
    )
    out_part = lax.psum_scatter(dwo, "dp", scatter_dimension=0).astype(F32)

    coefs = unpack_terms(back_own[:, cw:], LEVELS)
    pull = coefs[:, LEVELS - 1 :]
    for k in reversed(range(LEVELS - 1)):
        pull = jnp.where(channel[None, :] < level_width(k), coefs[:, k : k + 1], pull)
    back = back_own[:, :cw].astype(F32)
    dgated = own_gain * back - gated * pull
    dgain_out = jnp.sum(back * gated, axis=0)
    dz = (dgated * y * (sig + gate * (1.0 - sig))).astype(BF16)
    dy = dgated * gate
    dwz = dot(normed, dz, TN).astype(BF16)
    dwz = lax.psum_scatter(dwz, "dp", scatter_dimension=0, tiled=True)
    dpx, dtaps, dheads, dskip = scan_backward(
        px, taps, heads, skip, spread, spread.T, dy, y, states
    )
    dwx = dot(normed, dpx, TN).astype(BF16)
    dwx = lax.psum_scatter(dwx, "dp", scatter_dimension=0, tiled=True)
    dnormed = (dot(dz, wz, NT) + dot(dpx, wx, NT)).astype(BF16)
    dnormed = jnp.sum(swap_blocks(dnormed.reshape(parts, rows, D)).astype(F32), axis=0)
    own_scale = lax.rsqrt(jnp.mean(own_tokens * own_tokens, axis=-1, keepdims=True) + EPS_IN)
    dgain_in = jnp.sum(dnormed * own_tokens * own_scale, axis=0)
    scaled = dnormed * gain_in
    hidden_grad = (
        own_scale * scaled
        - own_tokens
        * (own_scale**3 * (jnp.sum(scaled * own_tokens, axis=-1, keepdims=True) / D))
        + jnp.sum(cotangent.astype(F32), axis=0)
    )[None]

    z_part = swap_blocks(dwz.reshape(parts, in_rows, cw)).astype(F32)
    x_part = swap_blocks(dwx.reshape(parts, in_rows, cc + LANES)).astype(F32)
    in_part = jnp.concatenate(
        [
            z_part.transpose(1, 0, 2).reshape(in_rows, INNER),
            x_part[:, :, :cw].transpose(1, 0, 2).reshape(in_rows, INNER),
            jnp.sum(x_part[:, :, cw:cc], axis=0),
            x_part[:, :, cc : cc + hq].transpose(1, 0, 2).reshape(in_rows, H),
        ],
        axis=1,
    )
    taps_grad = jnp.zeros((TAPS + 1, CONV_CH), F32)
    taps_grad = lax.dynamic_update_slice(taps_grad, dtaps[: TAPS + 1, :cw], (0, q * cw))
    taps_grad = taps_grad.at[:, INNER:].set(dtaps[: TAPS + 1, cw:])
    gain_grad = lax.dynamic_update_slice(jnp.zeros((INNER,), F32), dgain_out, (q * cw,))
    skip_grad = jnp.sum(dskip[0].reshape(hq, P_SIZE), axis=-1)
    head_grad = lax.dynamic_update_slice(
        jnp.zeros((3, H), F32),
        jnp.stack([dheads[0, :hq], dheads[1, :hq], skip_grad]),
        (0, q * hq),
    )
    small = jnp.concatenate(
        [taps_grad.reshape(-1), dgain_in, gain_grad, head_grad.reshape(-1)]
    )
    small = all_sum(all_sum(small, "seq"), "dp")
    chan_len = chan_params.shape[0]
    chan_total = small[: small.shape[0] - 3 * H]
    head_total = small[small.shape[0] - 3 * H :].reshape(3, H)
    owner = lax.axis_index("dp") * parts + q
    chan_part = lax.dynamic_slice(chan_total, (owner * chan_len,), (chan_len,))
    local_squares = jnp.sum(in_part * in_part) + jnp.sum(out_part * out_part)
    total_squares = all_sum(all_sum(local_squares.reshape(1, 1), "seq"), "dp")[0, 0]
    grad_norm = jnp.sqrt(
        total_squares + jnp.sum(chan_total * chan_total) + jnp.sum(head_total * head_total)
    )
    clip_factor = jnp.minimum(1.0, CLIP / grad_norm)
    w_in_new, w_in_m_new, w_in_v_new = adam_step(
        w_in, clip_factor * in_part, w_in_m, w_in_v, 0.02, 0.1
    )
    w_out_new, w_out_m_new, w_out_v_new = adam_step(
        w_out, clip_factor * out_part, w_out_m, w_out_v, 0.03, 0.1
    )
    chan_new, chan_m_new, chan_v_new = adam_step(
        chan_params, clip_factor * chan_part, chan_m, chan_v, 0.2, 0.0
    )
    head_new, head_m_new, head_v_new = adam_step(
        head_params, clip_factor * head_total, head_m, head_v, 1.0, 0.0
    )
    return (
        block_out, hidden_grad, grad_norm,
        w_in_new, w_in_m_new, w_in_v_new, w_in_new.astype(BF16),
        w_out_new, w_out_m_new, w_out_v_new, w_out_new.astype(BF16),
        chan_new, chan_m_new, chan_v_new, head_new, head_m_new, head_v_new,
    )


def solution(mesh):
    rows = P(("dp", "seq"), None)
    flat = P(("dp", "seq"))
    in_specs = (
        P("dp", "seq", None),
        P(None, "dp", "seq", None),
        *([rows] * 6),
        *([flat] * 3),
        *([P()] * 3),
    )
    out_specs = (
        P(None, "dp", "seq", None),
        P("dp", "seq", None),
        P(),
        *([rows] * 8),
        *([flat] * 3),
        *([P()] * 3),
    )
    return jax.shard_map(
        on_device, mesh=mesh, in_specs=in_specs, out_specs=out_specs, check_vma=False
    )
```

```python
import functools

import jax
import jax.numpy as jnp
from jax import lax
from jax.experimental import pallas as pl
from jax.experimental.pallas import tpu as pltpu
from jax.sharding import PartitionSpec as P

D = 2048
INNER = 4096
H = 64
P_SIZE = 64
N = 128
TAPS = 4
STEP = 10
E_IN = 8512
CONV_CH = 4352
LANES = 128
CHUNK = 128
LEVELS = 4

EXACT = lax.Precision.HIGHEST
EPS_IN = 1e-06
EPS_OUT = 1e-05
ADAM_EPS = 1e-08
BETA = 0.5
CLIP = 1.0
F32 = jnp.float32
BF16 = jnp.bfloat16
MASKED = -1e30


def level_width(level):
    return INNER * 2**level // 8


SEGMENTS = tuple(
    (0 if level == 0 else level_width(level - 1), level_width(level)) for level in range(LEVELS)
)


def dot(a, b, dims=((1,), (0,)), precision=None):
    return lax.dot_general(a, b, (dims, ((), ())), precision=precision, preferred_element_type=F32)


NT = ((1,), (1,))
TN = ((0,), (0,))


def softplus(v):
    return jnp.maximum(v, 0.0) + jnp.log1p(jnp.exp(-jnp.abs(v)))


def two_terms(v):
    high = v.astype(BF16)
    return high, (v - high.astype(F32)).astype(BF16)


def spread_heads(v, spread):
    high, rest = two_terms(v)
    return dot(high, spread) + dot(rest, spread)


def rates(dt_raw, heads):
    step = softplus(dt_raw + heads[0:1, :])
    return step, step * heads[1:2, :]


def triangle(size):
    row = lax.broadcasted_iota(jnp.int32, (size, size), 0)
    col = lax.broadcasted_iota(jnp.int32, (size, size), 1)
    return row, col


def conv_block(taps, xbuf, lanes):
    out = taps[TAPS : TAPS + 1, lanes]
    for tap in range(TAPS):
        out = out + taps[tap : tap + 1, lanes] * xbuf[5 + tap : 5 + tap + CHUNK, lanes]
    return out


def pair_decay(cum, cum_t, causal, head):
    gap = cum[:, head : head + 1] - cum_t[head : head + 1, :]
    return jnp.exp(jnp.where(causal, gap, MASKED))


def scan_forward_kernel(cw, px, taps, heads, skip, spread, y, states, xbuf, state, xdt, carried):
    cc = cw + 2 * N

    @pl.when(pl.program_id(0) == 0)
    def _():
        state[...] = jnp.zeros_like(state)
        xbuf[0:8, :] = jnp.zeros((8, cc), F32)

    xbuf[8 : 8 + CHUNK, :] = px[:, :cc]
    step, rate = rates(px[:, cc:], heads)
    row, col = triangle(CHUNK)
    causal = row >= col
    cum = dot(causal.astype(F32), rate, precision=EXACT)
    cum_t = cum.T
    spread_m = spread[...]
    last = cum[CHUNK - 1 : CHUNK, :]
    step_x = spread_heads(step, spread_m)
    grow_x = spread_heads(jnp.exp(cum), spread_m)
    tail_x = spread_heads(jnp.exp(last - cum), spread_m)

    def activated(lanes):
        conv = conv_block(taps, xbuf, lanes)
        return conv * jax.nn.sigmoid(conv)

    state_in = activated(slice(cw, cw + N))
    state_out = activated(slice(cw + N, cw + 2 * N))
    scores = dot(state_out, state_in, NT, EXACT)
    states[0] = state[...].astype(BF16)
    carried[...] = dot(state_out.astype(BF16), state[...].astype(BF16))
    first = lax.broadcasted_iota(jnp.int32, (1, LANES), 1) < P_SIZE
    for pair in range(cw // LANES):
        lanes = slice(pair * LANES, (pair + 1) * LANES)
        x = activated(lanes)
        xd = (x * step_x[:, lanes]).astype(BF16).astype(F32)
        xdt[:, lanes] = (xd * tail_x[:, lanes]).astype(BF16)
        stacked = jnp.concatenate([jnp.where(first, xd, 0.0), jnp.where(first, 0.0, xd)], axis=0)
        mixing = jnp.concatenate(
            [
                (pair_decay(cum, cum_t, causal, 2 * pair + k) * scores).astype(BF16)
                for k in range(2)
            ],
            axis=1,
        )
        y[:, lanes] = (
            dot(mixing, stacked.astype(BF16))
            + grow_x[:, lanes] * carried[:, lanes]
            + skip[:, lanes] * x
        )
    state[...] = grow_x[CHUNK - 1 : CHUNK, :] * state[...] + dot(
        state_in.astype(BF16), xdt[...], TN
    )
    xbuf[0:8, :] = xbuf[CHUNK : CHUNK + 8, :]


def scan_backward_kernel(
    cw, px, halo, taps, heads, skip, spread, gather, dy, y, states,
    dpx, dtaps, dheads, dskip,
    xbuf, dstate, dcbuf, slope, xact, xd_s, dxd_s, acc_s,
):
    cc = cw + 2 * N
    at = pl.program_id(0)

    @pl.when(at == 0)
    def _():
        dstate[...] = jnp.zeros_like(dstate)
        dcbuf[CHUNK : CHUNK + 8, :] = jnp.zeros((8, cc), F32)
        dtaps[...] = jnp.zeros_like(dtaps)
        dheads[...] = jnp.zeros_like(dheads)
        dskip[...] = jnp.zeros_like(dskip)

    xbuf[0:8, :] = jnp.where(at == pl.num_programs(0) - 1, 0.0, halo[:, :cc])
    xbuf[8 : 8 + CHUNK, :] = px[:, :cc]
    dt_raw = px[:, cc:]
    step, rate = rates(dt_raw, heads)
    row, col = triangle(CHUNK)
    causal = row >= col
    cum = dot(causal.astype(F32), rate, precision=EXACT)
    cum_t = cum.T
    spread_m = spread[...]
    last = cum[CHUNK - 1 : CHUNK, :]
    step_x = spread_heads(step, spread_m)
    grow_x = spread_heads(jnp.exp(cum), spread_m)
    tail_x = spread_heads(jnp.exp(last - cum), spread_m)

    for block in range(cc // LANES):
        lanes = slice(block * LANES, (block + 1) * LANES)
        conv = conv_block(taps, xbuf, lanes)
        sig = jax.nn.sigmoid(conv)
        act = conv * sig
        xact[:, lanes] = act
        slope[:, lanes] = sig + act * (1.0 - sig)
    state_in = xact[:, cw : cw + N]
    state_out = xact[:, cw + N : cc]
    scores = dot(state_out, state_in, NT, EXACT)
    in_low = state_in.astype(BF16)
    out_low = state_out.astype(BF16)
    dstate_low = dstate[...].astype(BF16)
    acc_s[...] = jnp.zeros_like(acc_s)
    dxd_s[...] = tail_x * dot(in_low, dstate_low)
    dskip[0:1, :] += jnp.sum(xact[:, :cw] * dy[...], axis=0, keepdims=True)
    first = lax.broadcasted_iota(jnp.int32, (1, LANES), 1) < P_SIZE
    xd_s[...] = (xact[:, :cw] * step_x).astype(BF16)
    total = jnp.sum(xd_s[...].astype(F32) * dxd_s[...], axis=0, keepdims=True) + grow_x[
        CHUNK - 1 : CHUNK, :
    ] * jnp.sum(dstate[...] * states[0].astype(F32), axis=0, keepdims=True)
    dscores = jnp.zeros((CHUNK, CHUNK), F32)
    for pair in range(cw // LANES):
        lanes = slice(pair * LANES, (pair + 1) * LANES)
        dyp = dy[:, lanes]
        stacked = jnp.concatenate(
            [jnp.where(first, dyp, 0.0), jnp.where(first, 0.0, dyp)], axis=0
        ).astype(BF16)
        decays = [pair_decay(cum, cum_t, causal, 2 * pair + k) for k in range(2)]
        mixing = jnp.concatenate([(decay * scores).astype(BF16) for decay in decays], axis=0)
        dxd_s[:, lanes] += dot(mixing, stacked, TN)
        dmix = dot(stacked, xd_s[:, lanes], NT)
        dscores = dscores + decays[0] * dmix[:CHUNK] + decays[1] * dmix[CHUNK:]
    dy_low = dy[...].astype(BF16)
    dy_f = dy_low.astype(F32)
    xd_f = xd_s[...].astype(F32)
    dxd = dxd_s[...]
    y_scan = y[...] - skip[...] * xact[:, :cw]
    final = lax.broadcasted_iota(jnp.int32, (CHUNK, 1), 0) == CHUNK - 1
    gather_m = gather[...]
    dcum = spread_heads(dy_f * y_scan - xd_f * dxd + jnp.where(final, total, 0.0), gather_m)
    dstep = spread_heads(xact[:, :cw] * dxd, gather_m)
    drate = dot((row <= col).astype(F32), dcum, precision=EXACT)
    dstep = dstep + drate * heads[1:2, :]
    ddt = dstep * jax.nn.sigmoid(dt_raw + heads[0:1, :])
    dheads[0:1, :] += jnp.sum(ddt, axis=0, keepdims=True)
    dheads[1:2, :] += jnp.sum(drate * rate, axis=0, keepdims=True)
    grown = (grow_x * dy_f).astype(BF16)
    dscores_low = dscores.astype(BF16)
    dout = dot(dscores_low, in_low) + dot(grown, states[0], NT)
    din = dot(dscores_low, out_low, TN) + dot((tail_x * xd_f).astype(BF16), dstate_low, NT)
    dstate[...] = grow_x[CHUNK - 1 : CHUNK, :] * dstate[...] + dot(out_low, grown, TN)
    dcbuf[:CHUNK, :cw] = (step_x * dxd + skip[...] * dy[...]) * slope[:, :cw]
    dcbuf[:CHUNK, cw : cw + N] = din * slope[:, cw : cw + N]
    dcbuf[:CHUNK, cw + N :] = dout * slope[:, cw + N :]
    for block in range(cc // LANES):
        lanes = slice(block * LANES, (block + 1) * LANES)
        dconv = dcbuf[:CHUNK, lanes]
        dtaps[TAPS : TAPS + 1, lanes] += jnp.sum(dconv, axis=0, keepdims=True)
        back = taps[TAPS - 1 : TAPS, lanes] * dconv
        for tap in range(TAPS):
            dtaps[tap : tap + 1, lanes] += jnp.sum(
                dconv * xbuf[5 + tap : 5 + tap + CHUNK, lanes], axis=0, keepdims=True
            )
            if tap < TAPS - 1:
                reach = TAPS - 1 - tap
                back = back + taps[tap : tap + 1, lanes] * dcbuf[reach : reach + CHUNK, lanes]
        dpx[:, lanes] = back.astype(BF16)
    dpx[:, cc:] = ddt.astype(BF16)
    dcbuf[CHUNK : CHUNK + 8, :] = dcbuf[0:8, :]


def whole(shape):
    return pl.BlockSpec(shape, lambda i: (0,) * len(shape))


def scan_forward(px, taps, heads, skip, spread):
    length, width = px.shape
    cw = skip.shape[1]
    cc = cw + 2 * N
    chunks = length // CHUNK
    return pl.pallas_call(
        functools.partial(scan_forward_kernel, cw),
        grid=(chunks,),
        in_specs=[
            pl.BlockSpec((CHUNK, width), lambda i: (i, 0)),
            whole(taps.shape),
            whole(heads.shape),
            whole(skip.shape),
            whole(spread.shape),
        ],
        out_specs=[
            pl.BlockSpec((CHUNK, cw), lambda i: (i, 0)),
            pl.BlockSpec((1, N, cw), lambda i: (i, 0, 0)),
        ],
        out_shape=[
            jax.ShapeDtypeStruct((length, cw), F32),
            jax.ShapeDtypeStruct((chunks, N, cw), BF16),
        ],
        scratch_shapes=[
            pltpu.VMEM((CHUNK + 8, cc), F32),
            pltpu.VMEM((N, cw), F32),
            pltpu.VMEM((CHUNK, cw), BF16),
            pltpu.VMEM((CHUNK, cw), F32),
        ],
        compiler_params=pltpu.CompilerParams(vmem_limit_bytes=48 * 2**20),
        name="scan_forward",
    )(px, taps, heads, skip, spread)


def scan_backward(px, taps, heads, skip, spread, gather, dy, y, states):
    length, width = px.shape
    cw = skip.shape[1]
    cc = cw + 2 * N
    chunks = length // CHUNK
    eighths = CHUNK // 8
    return pl.pallas_call(
        functools.partial(scan_backward_kernel, cw),
        grid=(chunks,),
        in_specs=[
            pl.BlockSpec((CHUNK, width), lambda i: (chunks - 1 - i, 0)),
            pl.BlockSpec(
                (8, width), lambda i: (jnp.maximum((chunks - 1 - i) * eighths - 1, 0), 0)
            ),
            whole(taps.shape),
            whole(heads.shape),
            whole(skip.shape),
            whole(spread.shape),
            whole(gather.shape),
            pl.BlockSpec((CHUNK, cw), lambda i: (chunks - 1 - i, 0)),
            pl.BlockSpec((CHUNK, cw), lambda i: (chunks - 1 - i, 0)),
            pl.BlockSpec((1, N, cw), lambda i: (chunks - 1 - i, 0, 0)),
        ],
        out_specs=[
            pl.BlockSpec((CHUNK, width), lambda i: (chunks - 1 - i, 0)),
            whole((8, cc)),
            whole((8, LANES)),
            whole((8, cw)),
        ],
        out_shape=[
            jax.ShapeDtypeStruct((length, width), BF16),
            jax.ShapeDtypeStruct((8, cc), F32),
            jax.ShapeDtypeStruct((8, LANES), F32),
            jax.ShapeDtypeStruct((8, cw), F32),
        ],
        scratch_shapes=[
            pltpu.VMEM((CHUNK + 8, cc), F32),
            pltpu.VMEM((N, cw), F32),
            pltpu.VMEM((CHUNK + 8, cc), F32),
            pltpu.VMEM((CHUNK, cc), F32),
            pltpu.VMEM((CHUNK, cc), F32),
            pltpu.VMEM((CHUNK, cw), BF16),
            pltpu.VMEM((CHUNK, cw), F32),
            pltpu.VMEM((CHUNK, CHUNK), F32),
        ],
        compiler_params=pltpu.CompilerParams(vmem_limit_bytes=48 * 2**20),
        name="scan_backward",
    )(px, px, taps, heads, skip, spread, gather, dy, y, states)


WIDE = 512


def widths_kernel(cw, u, wo, cotangent, tokens, block_out, back, mixed, branch, norms, pulls):
    at = pl.program_id(0)
    ends = [level_width(k) // WIDE - 1 for k in range(LEVELS)]

    @pl.when(at == 0)
    def _():
        terms = u[0, :, cw:].astype(F32)
        for part in range(1, u.shape[0]):
            terms = terms + u[part, :, cw:].astype(F32)
        squares = jnp.zeros((terms.shape[0], 1), F32)
        for k in range(LEVELS):
            squares = squares + terms[:, k : k + 1] + terms[:, LEVELS + k : LEVELS + k + 1]
            norms[:, k : k + 1] = lax.rsqrt(squares / level_width(k) + EPS_OUT)
        running = jnp.zeros(branch.shape, F32)
        for k in reversed(range(LEVELS)):
            running = running + norms[:, k : k + 1] * cotangent[k].astype(F32)
            mixed[k] = running.astype(BF16)
        branch[...] = jnp.zeros_like(branch)

    part = at * WIDE // cw
    lanes = pl.ds(pl.multiple_of(lax.rem(at * WIDE, cw), WIDE), WIDE)
    level = sum((at > end).astype(jnp.int32) for end in ends[:-1])
    branch[...] += dot(u[part, :, lanes], wo[...])
    back[part, :, lanes] = dot(mixed[level], wo[...], NT).astype(BF16)
    for k in range(LEVELS):

        @pl.when(at == ends[k])
        def _():
            norm = norms[:, k : k + 1]
            block_out[k] = (tokens[...].astype(F32) + norm * branch[...]).astype(BF16)
            inner = jnp.sum(cotangent[k].astype(F32) * branch[...], axis=-1, keepdims=True)
            pulls[:, k : k + 1] = norm * norm * norm * (inner / level_width(k))

    @pl.when(at == ends[-1])
    def _():
        coef = jnp.zeros((branch.shape[0], 1), F32)
        lane = lax.broadcasted_iota(jnp.int32, (1, LANES), 1)
        packed = jnp.zeros((branch.shape[0], LANES), F32)
        for k in reversed(range(LEVELS)):
            coef = coef + pulls[:, k : k + 1]
            high, rest = two_terms(coef)
            packed = jnp.where(lane == k, high.astype(F32), packed)
            packed = jnp.where(lane == LEVELS + k, rest.astype(F32), packed)
        for p in range(back.shape[0]):
            back[p, :, cw:] = packed.astype(BF16)


def widths(u, wo, cotangent, tokens):
    parts, rows, wide = u.shape
    cw = wide - LANES

    def full(shape):
        return pl.BlockSpec(shape, lambda i: (0,) * len(shape), pipeline_mode=pl.Buffered(1))

    return pl.pallas_call(
        functools.partial(widths_kernel, cw),
        grid=(INNER // WIDE,),
        in_specs=[
            full(u.shape),
            pl.BlockSpec((WIDE, D), lambda i: (i, 0)),
            full(cotangent.shape),
            full(tokens.shape),
        ],
        out_specs=[full(cotangent.shape), full(u.shape), full(cotangent.shape)],
        out_shape=[
            jax.ShapeDtypeStruct(cotangent.shape, BF16),
            jax.ShapeDtypeStruct(u.shape, BF16),
            jax.ShapeDtypeStruct(cotangent.shape, BF16),
        ],
        scratch_shapes=[
            pltpu.VMEM((rows, D), F32),
            pltpu.VMEM((rows, LANES), F32),
            pltpu.VMEM((rows, LANES), F32),
        ],
        compiler_params=pltpu.CompilerParams(vmem_limit_bytes=48 * 2**20),
        name="widths",
    )(u, wo, cotangent, tokens)


MESH = pl.DeviceIdType.MESH


def remote(src, dst, sends, recvs, index, device):
    return pltpu.make_async_remote_copy(
        src_ref=src,
        dst_ref=dst,
        send_sem=sends.at[index],
        recv_sem=recvs.at[index],
        device_id=device,
        device_id_type=MESH,
    )


def greet(devices):
    barrier = pltpu.get_barrier_semaphore()
    for device in devices:
        pl.semaphore_signal(barrier, inc=1, device_id=device, device_id_type=MESH)
    pl.semaphore_wait(barrier, len(devices))


def seq_peers(parts):
    group, q = lax.axis_index("dp"), lax.axis_index("seq")
    return [(group, lax.rem(q + k, parts)) for k in range(1, parts)]


def dp_peers(groups):
    group, q = lax.axis_index("dp"), lax.axis_index("seq")
    return [(lax.rem(group + k, groups), q) for k in range(1, groups)]


def swap_kernel(parts, count, *refs):
    sources, results = refs[:count], refs[count : 2 * count]
    sends, recvs, local = refs[2 * count :]
    q = lax.axis_index("seq")
    peers = seq_peers(parts)
    greet(peers)
    copies = []
    for k, peer in enumerate(peers):
        for a in range(count):
            copy = remote(
                sources[a].at[peer[1]], results[a].at[q], sends, recvs, k * count + a, peer
            )
            copy.start()
            copies.append(copy)
    own = [
        pltpu.make_async_copy(sources[a].at[q], results[a].at[q], local.at[a])
        for a in range(count)
    ]
    for copy in own:
        copy.start()
    for copy in own + copies:
        copy.wait()


def swap(collective_id, *arrays):
    parts = arrays[0].shape[0]
    count = len(arrays)
    return pl.pallas_call(
        functools.partial(swap_kernel, parts, count),
        in_specs=[pl.BlockSpec(memory_space=pl.ANY)] * count,
        out_specs=[pl.BlockSpec(memory_space=pl.ANY)] * count,
        out_shape=[jax.ShapeDtypeStruct(a.shape, a.dtype) for a in arrays],
        scratch_shapes=[
            pltpu.SemaphoreType.DMA(((parts - 1) * count,)),
            pltpu.SemaphoreType.DMA(((parts - 1) * count,)),
            pltpu.SemaphoreType.DMA((count,)),
        ],
        compiler_params=pltpu.CompilerParams(collective_id=collective_id, has_side_effects=True),
        name="swap",
    )(*arrays)


def all_peers(groups, parts):
    devices = groups * parts
    me = lax.axis_index("dp") * parts + lax.axis_index("seq")
    peers = []
    for k in range(1, devices):
        other = lax.rem(me + k, devices)
        peers.append((other // parts, lax.rem(other, parts)))
    return peers


def broadcast_kernel(
    groups, parts, block, near, total, near_out, out, sends, recvs, near_s, near_r, local
):
    group, q = lax.axis_index("dp"), lax.axis_index("seq")
    me = group * parts + q
    everyone = all_peers(groups, parts)
    greet(everyone)
    copies = [
        remote(block, out.at[me], sends, recvs, k, peer) for k, peer in enumerate(everyone)
    ]
    copies += [
        remote(near, near_out.at[q], near_s, near_r, k, peer)
        for k, peer in enumerate(seq_peers(parts))
    ]
    copies += [
        pltpu.make_async_copy(block, out.at[me], local.at[0]),
        pltpu.make_async_copy(near, near_out.at[q], local.at[1]),
    ]
    for copy in copies:
        copy.start()
    for copy in copies:
        copy.wait()
    total[...] = jnp.sum(out[...], axis=0)


def broadcast(collective_id, block, near, groups, parts):
    devices = groups * parts
    sem = pltpu.SemaphoreType.DMA
    return pl.pallas_call(
        functools.partial(broadcast_kernel, groups, parts),
        in_specs=[pl.BlockSpec(memory_space=pltpu.VMEM)] * 2,
        out_specs=[pl.BlockSpec(memory_space=pltpu.VMEM)] * 2,
        out_shape=[
            jax.ShapeDtypeStruct(block.shape, block.dtype),
            jax.ShapeDtypeStruct((parts,) + near.shape, near.dtype),
        ],
        scratch_shapes=[
            pltpu.VMEM((devices,) + block.shape, block.dtype),
            sem((devices - 1,)), sem((devices - 1,)), sem((parts - 1,)), sem((parts - 1,)),
            sem((2,)),
        ],
        compiler_params=pltpu.CompilerParams(collective_id=collective_id, has_side_effects=True),
        name="broadcast",
    )(block, near)


def collect_kernel(
    groups, parts, hidden, blocks, chan, hid_out, w_out, chan_out,
    chan_s, chan_r, hid_s, hid_r, swap_s, swap_r, line_s, line_r, core_s, core_r, local,
):
    line = groups // 2
    group, q = lax.axis_index("dp"), lax.axis_index("seq")
    z, core = group // 2, lax.rem(group, 2)
    sibling = (2 * z + 1 - core, q)
    peers = seq_peers(parts)
    everyone = all_peers(groups, parts)
    greet(everyone)
    swaps = []
    for k, peer in enumerate(peers):
        copy = remote(blocks.at[peer[1]], w_out.at[group, q], swap_s, swap_r, k, peer)
        copy.start()
        swaps.append(copy)
    mine = pltpu.make_async_copy(blocks.at[q], w_out.at[group, q], local.at[0])
    mine.start()
    keep = pltpu.make_async_copy(hidden, hid_out.at[q], local.at[1])
    keep.start()
    chans = []
    for k, peer in enumerate(everyone):
        copy = remote(chan, chan_out.at[group * parts + q], chan_s, chan_r, k, peer)
        copy.start()
        chans.append(copy)
    chan_keep = pltpu.make_async_copy(chan, chan_out.at[group * parts + q], local.at[2])
    chan_keep.start()
    mine.wait()
    for copy in swaps:
        copy.wait()
    hids = []
    for k, peer in enumerate(peers):
        copy = remote(hidden, hid_out.at[q], hid_s, hid_r, k, peer)
        copy.start()
        hids.append(copy)

    def along(from_z, up):
        block = w_out.at[2 * from_z + core]
        to = z + 1 if up else z - 1
        return remote(
            block, block, line_s.at[0 if up else 1], line_r.at[0 if up else 1], from_z,
            (2 * to + core, q),
        )

    def across(from_z):
        block = w_out.at[2 * from_z + core]
        return remote(block, block, core_s, core_r, from_z, sibling)

    for t in range(line):
        low, high = z - t, z + t
        if t == 0:
            across(z).start()

            @pl.when(z < line - 1)
            def _():
                along(z, True).start()

            @pl.when(z > 0)
            def _():
                along(z, False).start()

            continue

        @pl.when(low >= 0)
        def _():
            along(low, True).wait_recv()

            @pl.when(z < line - 1)
            def _():
                along(low, True).start()

            across(low).start()

        @pl.when(high <= line - 1)
        def _():
            along(high, False).wait_recv()

            @pl.when(z > 0)
            def _():
                along(high, False).start()

            across(high).start()

    for from_z in range(line):
        across(from_z).wait_send()
        block = w_out.at[2 * from_z + 1 - core]
        remote(block, block, core_s, core_r, from_z, sibling).wait_recv()

        @pl.when((from_z <= z) & (z < line - 1))
        def _():
            along(from_z, True).wait_send()

        @pl.when((from_z >= z) & (z > 0))
        def _():
            along(from_z, False).wait_send()

    keep.wait()
    chan_keep.wait()
    for copy in hids + chans:
        copy.wait()


def collect(collective_id, hidden, blocks, chan, groups):
    parts, rows, width = blocks.shape
    line = groups // 2
    sem = pltpu.SemaphoreType.DMA
    return pl.pallas_call(
        functools.partial(collect_kernel, groups, parts),
        in_specs=[pl.BlockSpec(memory_space=pl.ANY)] * 3,
        out_specs=[pl.BlockSpec(memory_space=pl.ANY)] * 3,
        out_shape=[
            jax.ShapeDtypeStruct((parts,) + hidden.shape, hidden.dtype),
            jax.ShapeDtypeStruct((groups, parts, rows, width), blocks.dtype),
            jax.ShapeDtypeStruct((groups * parts,) + chan.shape, chan.dtype),
        ],
        scratch_shapes=[
            sem((groups * parts - 1,)), sem((groups * parts - 1,)), sem((parts - 1,)), sem((parts - 1,)), sem((parts - 1,)), sem((parts - 1,)),
            sem((2, line)), sem((2, line)), sem((line,)), sem((line,)), sem((3,)),
        ],
        compiler_params=pltpu.CompilerParams(collective_id=collective_id, has_side_effects=True),
        name="collect",
    )(hidden, blocks, chan)


def add_blocks(out, a, b, rows, steps):
    def step(i, carry):
        at = pl.ds(pl.multiple_of(i * rows, rows), rows)
        out[at] = (a[at].astype(F32) + b[at].astype(F32)).astype(out.dtype)
        return carry

    lax.fori_loop(0, steps, step, 0)


def reduce_kernel(
    groups, parts, rows, grad, back, small, part, back_out, small_all,
    held, acc, down, up,
    core_s, core_r, up_s, up_r, down_s, down_r, part_s, part_r, back_s, back_r,
    small_s, small_r, local,
):
    line = groups // 2
    span = parts * rows
    group, q = lax.axis_index("dp"), lax.axis_index("seq")
    z, core = group // 2, lax.rem(group, 2)
    sibling = (2 * z + 1 - core, q)
    peers, others = seq_peers(parts), dp_peers(groups)
    greet(peers + others)

    def share(of):
        return grad.at[pl.ds(pl.multiple_of(of * span, span), span)]

    cores = []
    for d in range(line):
        copy = remote(share(2 * d + 1 - core), held.at[d], core_s, core_r, d, sibling)
        copy.start()
        cores.append(copy)
    waiting = []
    for k, peer in enumerate(peers):
        copy = remote(back.at[peer[1]], back_out.at[q], back_s, back_r, k, peer)
        copy.start()
        waiting.append(copy)
    for k, peer in enumerate(others):
        copy = remote(small, small_all.at[group], small_s, small_r, k, peer)
        copy.start()
        waiting.append(copy)
    own_back = pltpu.make_async_copy(back.at[q], back_out.at[q], local.at[0])
    own_back.start()
    own_small = pltpu.make_async_copy(small, small_all.at[group], local.at[1])
    own_small.start()
    for d in range(line):
        cores[d].wait()
        add_blocks(acc.at[d], share(2 * d + core), held.at[d], rows, parts)

    def ahead(d, first):
        block = acc.at[d] if first else up.at[d]
        return remote(block, up.at[d], up_s, up_r, d, (2 * (z + 1) + core, q))

    def behind(d, first):
        block = acc.at[d] if first else down.at[d]
        return remote(block, down.at[d], down_s, down_r, d, (2 * (z - 1) + core, q))

    for t in range(line - 1):
        far = line - 1 - t + z

        @pl.when((z == 0) & (z < line - 1))
        def _():
            ahead(line - 1 - t, True).start()

        @pl.when((z > 0) & (z <= t) & (z < line - 1))
        def _():
            ahead(far, False).wait_recv()
            add_blocks(up.at[far], up.at[far], acc.at[far], rows, parts)
            ahead(far, False).start()

        near = t - (line - 1 - z)

        @pl.when((z == line - 1) & (z > 0))
        def _():
            behind(t, True).start()

        @pl.when((z < line - 1) & (line - 1 - z <= t) & (z > 0))
        def _():
            behind(near, False).wait_recv()
            add_blocks(down.at[near], down.at[near], acc.at[near], rows, parts)
            behind(near, False).start()

    @pl.when(z > 0)
    def _():
        ahead(z, False).wait_recv()
        add_blocks(acc.at[z], acc.at[z], up.at[z], rows, parts)

    @pl.when(z < line - 1)
    def _():
        behind(z, False).wait_recv()
        add_blocks(acc.at[z], acc.at[z], down.at[z], rows, parts)

    parts_copies = []
    for k, peer in enumerate(peers):
        block = acc.at[z, pl.ds(pl.multiple_of(peer[1] * rows, rows), rows)]
        copy = remote(block, part.at[q], part_s, part_r, k, peer)
        copy.start()
        parts_copies.append(copy)
    own = pltpu.make_async_copy(
        acc.at[z, pl.ds(pl.multiple_of(q * rows, rows), rows)], part.at[q], local.at[2]
    )
    own.start()
    for t in range(line - 1):
        far = line - 1 - t + z
        near = t - (line - 1 - z)

        @pl.when((z == 0) & (z < line - 1))
        def _():
            ahead(line - 1 - t, True).wait_send()

        @pl.when((z > 0) & (z <= t) & (z < line - 1))
        def _():
            ahead(far, False).wait_send()

        @pl.when((z == line - 1) & (z > 0))
        def _():
            behind(t, True).wait_send()

        @pl.when((z < line - 1) & (line - 1 - z <= t) & (z > 0))
        def _():
            behind(near, False).wait_send()

    own.wait()
    own_back.wait()
    own_small.wait()
    for copy in parts_copies + waiting:
        copy.wait()


def reduce_to_owners(collective_id, grad, back, small, groups):
    parts = back.shape[0]
    line = groups // 2
    rows = grad.shape[0] // (groups * parts)
    span, width = rows * parts, grad.shape[1]
    sem = pltpu.SemaphoreType.DMA
    vmem = pl.BlockSpec(memory_space=pltpu.VMEM)
    hbm = pl.BlockSpec(memory_space=pl.ANY)
    return pl.pallas_call(
        functools.partial(reduce_kernel, groups, parts, rows),
        in_specs=[vmem, hbm, vmem],
        out_specs=[hbm, hbm, vmem],
        out_shape=[
            jax.ShapeDtypeStruct((parts, rows, width), grad.dtype),
            jax.ShapeDtypeStruct(back.shape, back.dtype),
            jax.ShapeDtypeStruct((groups,) + small.shape, small.dtype),
        ],
        scratch_shapes=[
            pltpu.VMEM((line, span, width), grad.dtype),
            pltpu.VMEM((line, span, width), grad.dtype),
            pltpu.VMEM((line, span, width), grad.dtype),
            pltpu.VMEM((line, span, width), grad.dtype),
            sem((line,)), sem((line,)), sem((line,)), sem((line,)), sem((line,)), sem((line,)),
            sem((parts - 1,)), sem((parts - 1,)), sem((parts - 1,)), sem((parts - 1,)),
            sem((groups - 1,)), sem((groups - 1,)), sem((3,)),
        ],
        compiler_params=pltpu.CompilerParams(
            collective_id=collective_id, has_side_effects=True, vmem_limit_bytes=48 * 2**20
        ),
        name="reduce_to_owners",
    )(grad, back, small)
def adam_step(weight, gradient, moment, second, step_rate, weight_decay):
    new_moment = BETA * moment + (1.0 - BETA) * gradient
    new_second = BETA * second + (1.0 - BETA) * gradient * gradient
    correction = 1.0 - BETA**STEP
    update = new_moment / correction / (jnp.sqrt(new_second / correction) + ADAM_EPS)
    return (weight - step_rate * (update + weight_decay * weight), new_moment, new_second)


def pack_terms(values):
    high = lax.reduce_precision(values, 8, 7)
    packed = jnp.concatenate([high, values - high], axis=-1).astype(BF16)
    return jnp.pad(packed, ((0, 0), (0, LANES - packed.shape[-1])))


def unpack_terms(packed, count):
    packed = packed.astype(F32)
    return packed[..., :count] + packed[..., count : 2 * count]


def on_device(
    hidden_in, out_grads, w_in, w_in_m, w_in_v, w_out, w_out_m, w_out_v,
    chan_params, chan_m, chan_v, head_params, head_m, head_v,
):
    parts = lax.axis_size("seq")
    groups = lax.axis_size("dp")
    q = lax.axis_index("seq")
    rows = hidden_in.shape[1]
    length = rows * parts
    cw = INNER // parts
    hq = H // parts
    cc = cw + 2 * N
    in_rows = w_in.shape[0]
    out_rows = w_out.shape[0]

    in_low = w_in.astype(BF16)
    out_low = w_out.astype(BF16)
    z_blocks = in_low[:, :INNER].reshape(in_rows, parts, cw).transpose(1, 0, 2)
    x_blocks = in_low[:, INNER : 2 * INNER].reshape(in_rows, parts, cw).transpose(1, 0, 2)
    bc_block = jnp.broadcast_to(
        in_low[None, :, 2 * INNER : 2 * INNER + 2 * N], (parts, in_rows, 2 * N)
    )
    dt_blocks = in_low[:, 2 * INNER + 2 * N :].reshape(in_rows, parts, hq).transpose(1, 0, 2)
    dt_blocks = jnp.pad(dt_blocks, ((0, 0), (0, 0), (0, LANES - hq)))
    x_blocks = jnp.concatenate([x_blocks, bc_block, dt_blocks], axis=2)
    chan_len = chan_params.shape[0]
    chan_rows = -(-chan_len // (8 * LANES)) * 8
    chan_block = jnp.pad(
        lax.reduce_precision(chan_params, 8, 7), (0, chan_rows * LANES - chan_len)
    ).reshape(chan_rows, LANES)
    hidden, wx, chan_full = collect(0, hidden_in[0], x_blocks, chan_block, groups)
    hidden = hidden.reshape(length, D)
    wx = wx.reshape(D, cc + LANES)
    chan_full = chan_full.reshape(groups * parts, chan_rows * LANES)[:, :chan_len].reshape(-1)
    wz = lax.all_gather(swap(1, z_blocks)[0], "dp", axis=0).reshape(D, cw)
    wo = lax.all_gather(out_low, ("dp", "seq"), axis=0, tiled=True)

    conv_taps = chan_full[: TAPS * CONV_CH].reshape(TAPS, CONV_CH)
    conv_bias = chan_full[TAPS * CONV_CH : (TAPS + 1) * CONV_CH].reshape(1, CONV_CH)
    offset = (TAPS + 1) * CONV_CH
    gain_in = chan_full[offset : offset + D]
    gain_out = chan_full[offset + D : offset + D + INNER]
    taps_all = jnp.concatenate(
        [conv_taps, conv_bias, jnp.zeros((8 - TAPS - 1, CONV_CH), F32)], axis=0
    )
    taps = jnp.concatenate(
        [lax.dynamic_slice(taps_all, (0, q * cw), (8, cw)), taps_all[:, INNER:]], axis=1
    )
    own_gain = lax.dynamic_slice(gain_out, (q * cw,), (cw,))
    own_heads = lax.dynamic_slice(head_params, (0, q * hq), (3, hq))
    heads = jnp.pad(
        jnp.stack([own_heads[0], -jnp.exp(own_heads[1])]), ((0, 6), (0, LANES - hq))
    )
    skip = jnp.repeat(own_heads[2], P_SIZE).reshape(1, cw)
    spread = (
        jnp.arange(LANES)[:, None] == (jnp.arange(cw) // P_SIZE)[None, :]
    ).astype(BF16)

    tokens = hidden.astype(F32)
    scale = lax.rsqrt(jnp.mean(tokens * tokens, axis=-1, keepdims=True) + EPS_IN)
    normed = (tokens * scale * gain_in).astype(BF16)
    px = dot(normed, wx)
    y, states = scan_forward(px, taps, heads, skip, spread)
    z = dot(normed, wz)
    sig = jax.nn.sigmoid(z)
    gate = z * sig
    gated = y * gate
    channel = q * cw + jnp.arange(cw)
    squares = jnp.stack(
        [
            jnp.sum(jnp.where((channel >= low) & (channel < high), gated * gated, 0.0), axis=-1)
            for low, high in SEGMENTS
        ],
        axis=-1,
    )
    u_blocks = jnp.concatenate([(gated * own_gain).astype(BF16), pack_terms(squares)], axis=-1)
    u = swap(2, u_blocks.reshape(parts, rows, cw + LANES))[0]

    own_tokens = hidden_in[0].astype(F32)
    cotangent = out_grads[:, 0]
    block_out, back_blocks, mixed = widths(u, wo, cotangent, hidden_in[0])
    block_out = block_out[:, None]
    back_own = swap(3, back_blocks)[0].reshape(length, cw + LANES)
    u = u[:, :, :cw].transpose(1, 0, 2).reshape(rows, INNER)
    dwo = jnp.concatenate(
        [dot(u[:, low:high], mixed[k], TN).astype(BF16) for k, (low, high) in enumerate(SEGMENTS)],
        axis=0,
    )
    dwo = lax.psum_scatter(
        dwo.reshape(groups, parts, out_rows, D).transpose(1, 0, 2, 3), "seq", scatter_dimension=0
    )
    out_part = lax.psum_scatter(dwo, "dp", scatter_dimension=0).astype(F32)

    coefs = unpack_terms(back_own[:, cw:], LEVELS)
    pull = coefs[:, LEVELS - 1 :]
    for k in reversed(range(LEVELS - 1)):
        pull = jnp.where(channel[None, :] < level_width(k), coefs[:, k : k + 1], pull)
    back = back_own[:, :cw].astype(F32)
    dgated = own_gain * back - gated * pull
    dgain_out = jnp.sum(back * gated, axis=0)
    dz = (dgated * y * (sig + gate * (1.0 - sig))).astype(BF16)
    dy = dgated * gate
    dwz = dot(normed, dz, TN).astype(BF16)
    dwz = lax.psum_scatter(dwz, "dp", scatter_dimension=0, tiled=True)
    dpx, dtaps, dheads, dskip = scan_backward(
        px, taps, heads, skip, spread, spread.T, dy, y, states
    )
    dwx = dot(normed, dpx, TN).astype(BF16)
    dnormed = (dot(dz, wz, NT) + dot(dpx, wx, NT)).astype(BF16)
    skip_grad = jnp.sum(dskip[0].reshape(hq, P_SIZE), axis=-1)
    small = jnp.concatenate(
        [dtaps[: TAPS + 1].reshape(-1), dgain_out, dheads[0, :hq], dheads[1, :hq], skip_grad]
    )
    small_rows = -(-small.shape[0] // (8 * LANES)) * 8
    small = jnp.pad(small, (0, small_rows * LANES - small.shape[0])).reshape(small_rows, LANES)
    x_part, dnormed, small = reduce_to_owners(4, dwx, dnormed.reshape(parts, rows, D), small, groups)
    dnormed = jnp.sum(dnormed.astype(F32), axis=0)
    small = jnp.sum(small, axis=0)
    own_scale = lax.rsqrt(jnp.mean(own_tokens * own_tokens, axis=-1, keepdims=True) + EPS_IN)
    dgain_in = jnp.sum(dnormed * own_tokens * own_scale, axis=0)
    scaled = dnormed * gain_in
    hidden_grad = (
        own_scale * scaled
        - own_tokens
        * (own_scale**3 * (jnp.sum(scaled * own_tokens, axis=-1, keepdims=True) / D))
        + jnp.sum(cotangent.astype(F32), axis=0)
    )[None]

    z_part = swap(5, dwz.reshape(parts, in_rows, cw))[0].astype(F32)
    x_part = x_part.astype(F32)
    in_part = jnp.concatenate(
        [
            z_part.transpose(1, 0, 2).reshape(in_rows, INNER),
            x_part[:, :, :cw].transpose(1, 0, 2).reshape(in_rows, INNER),
            jnp.sum(x_part[:, :, cw:cc], axis=0),
            x_part[:, :, cc : cc + hq].transpose(1, 0, 2).reshape(in_rows, H),
        ],
        axis=1,
    )
    local_squares = jnp.sum(in_part * in_part) + jnp.sum(out_part * out_part)
    block = jnp.concatenate(
        [dgain_in.reshape(D // LANES, LANES), jnp.full((8, LANES), local_squares)], axis=0
    )
    block, small = broadcast(6, block, small, groups, parts)
    small = small.reshape(parts, small_rows * LANES)
    taps_size = (TAPS + 1) * cc
    taps_grad = small[:, :taps_size].reshape(parts, TAPS + 1, cc)
    taps_grad = jnp.concatenate(
        [
            taps_grad[:, :, :cw].transpose(1, 0, 2).reshape(TAPS + 1, INNER),
            jnp.sum(taps_grad[:, :, cw:], axis=0),
        ],
        axis=1,
    )
    head_total = small[:, taps_size + cw : taps_size + cw + 3 * hq]
    head_total = head_total.reshape(parts, 3, hq).transpose(1, 0, 2).reshape(3, H)
    chan_total = jnp.concatenate(
        [
            taps_grad.reshape(-1),
            block[: D // LANES].reshape(-1),
            small[:, taps_size : taps_size + cw].reshape(-1),
        ]
    )
    owner = lax.axis_index("dp") * parts + q
    chan_part = lax.dynamic_slice(chan_total, (owner * chan_len,), (chan_len,))
    grad_norm = jnp.sqrt(
        block[D // LANES, 0]
        + jnp.sum(chan_total * chan_total)
        + jnp.sum(head_total * head_total)
    )
    clip_factor = jnp.minimum(1.0, CLIP / grad_norm)
    w_in_new, w_in_m_new, w_in_v_new = adam_step(
        w_in, clip_factor * in_part, w_in_m, w_in_v, 0.02, 0.1
    )
    w_out_new, w_out_m_new, w_out_v_new = adam_step(
        w_out, clip_factor * out_part, w_out_m, w_out_v, 0.03, 0.1
    )
    chan_new, chan_m_new, chan_v_new = adam_step(
        chan_params, clip_factor * chan_part, chan_m, chan_v, 0.2, 0.0
    )
    head_new, head_m_new, head_v_new = adam_step(
        head_params, clip_factor * head_total, head_m, head_v, 1.0, 0.0
    )
    return (
        block_out, hidden_grad, grad_norm,
        w_in_new, w_in_m_new, w_in_v_new, w_in_new.astype(BF16),
        w_out_new, w_out_m_new, w_out_v_new, w_out_new.astype(BF16),
        chan_new, chan_m_new, chan_v_new, head_new, head_m_new, head_v_new,
    )


def solution(mesh):
    rows = P(("dp", "seq"), None)
    flat = P(("dp", "seq"))
    in_specs = (
        P("dp", "seq", None),
        P(None, "dp", "seq", None),
        *([rows] * 6),
        *([flat] * 3),
        *([P()] * 3),
    )
    out_specs = (
        P(None, "dp", "seq", None),
        P("dp", "seq", None),
        P(),
        *([rows] * 8),
        *([flat] * 3),
        *([P()] * 3),
    )
    return jax.shard_map(
        on_device, mesh=mesh, in_specs=in_specs, out_specs=out_specs, check_vma=False
    )
```

```python
import functools

import jax
import jax.numpy as jnp
from jax import lax
from jax.experimental import pallas as pl
from jax.experimental.pallas import tpu as pltpu
from jax.sharding import PartitionSpec as P

D = 2048
INNER = 4096
H = 64
P_SIZE = 64
N = 128
TAPS = 4
STEP = 10
E_IN = 8512
CONV_CH = 4352
LANES = 128
CHUNK = 128
LEVELS = 4

EXACT = lax.Precision.HIGHEST
EPS_IN = 1e-06
EPS_OUT = 1e-05
ADAM_EPS = 1e-08
BETA = 0.5
CLIP = 1.0
F32 = jnp.float32
BF16 = jnp.bfloat16
MASKED = -1e30


def level_width(level):
    return INNER * 2**level // 8


SEGMENTS = tuple(
    (0 if level == 0 else level_width(level - 1), level_width(level)) for level in range(LEVELS)
)


def dot(a, b, dims=((1,), (0,)), precision=None):
    return lax.dot_general(a, b, (dims, ((), ())), precision=precision, preferred_element_type=F32)


NT = ((1,), (1,))
TN = ((0,), (0,))


def softplus(v):
    return jnp.maximum(v, 0.0) + jnp.log1p(jnp.exp(-jnp.abs(v)))


def two_terms(v):
    high = v.astype(BF16)
    return high, (v - high.astype(F32)).astype(BF16)


def spread_heads(v, spread):
    high, rest = two_terms(v)
    return dot(high, spread) + dot(rest, spread)


def own_heads_first(dt_raw, hq, back=False):
    by = lax.axis_index("seq") * hq
    return pltpu.roll(dt_raw, by if back else lax.rem(LANES - by, LANES), 1)


def rates(dt_raw, heads):
    step = softplus(dt_raw + heads[0:1, :])
    return step, step * heads[1:2, :]


def triangle(size):
    row = lax.broadcasted_iota(jnp.int32, (size, size), 0)
    col = lax.broadcasted_iota(jnp.int32, (size, size), 1)
    return row, col


def conv_block(taps, xbuf, lanes):
    out = taps[TAPS : TAPS + 1, lanes]
    for tap in range(TAPS):
        out = out + taps[tap : tap + 1, lanes] * xbuf[5 + tap : 5 + tap + CHUNK, lanes]
    return out


def pair_decay(cum, cum_t, causal, head):
    gap = cum[:, head : head + 1] - cum_t[head : head + 1, :]
    return jnp.exp(jnp.where(causal, gap, MASKED))


def scan_forward_kernel(cw, px, taps, heads, skip, spread, y, states, xbuf, state, xdt, carried):
    cc = cw + 2 * N

    @pl.when(pl.program_id(0) == 0)
    def _():
        state[...] = jnp.zeros_like(state)
        xbuf[0:8, :] = jnp.zeros((8, cc), F32)

    xbuf[8 : 8 + CHUNK, :] = px[:, :cc]
    step, rate = rates(own_heads_first(px[:, cc:], cw // P_SIZE), heads)
    row, col = triangle(CHUNK)
    causal = row >= col
    cum = dot(causal.astype(F32), rate, precision=EXACT)
    cum_t = cum.T
    spread_m = spread[...]
    last = cum[CHUNK - 1 : CHUNK, :]
    step_x = spread_heads(step, spread_m)
    grow_x = spread_heads(jnp.exp(cum), spread_m)
    tail_x = spread_heads(jnp.exp(last - cum), spread_m)

    def activated(lanes):
        conv = conv_block(taps, xbuf, lanes)
        return conv * jax.nn.sigmoid(conv)

    state_in = activated(slice(cw, cw + N))
    state_out = activated(slice(cw + N, cw + 2 * N))
    scores = dot(state_out, state_in, NT, EXACT)
    states[0] = state[...].astype(BF16)
    carried[...] = dot(state_out.astype(BF16), state[...].astype(BF16))
    first = lax.broadcasted_iota(jnp.int32, (1, LANES), 1) < P_SIZE
    for pair in range(cw // LANES):
        lanes = slice(pair * LANES, (pair + 1) * LANES)
        x = activated(lanes)
        xd = (x * step_x[:, lanes]).astype(BF16).astype(F32)
        xdt[:, lanes] = (xd * tail_x[:, lanes]).astype(BF16)
        stacked = jnp.concatenate([jnp.where(first, xd, 0.0), jnp.where(first, 0.0, xd)], axis=0)
        mixing = jnp.concatenate(
            [
                (pair_decay(cum, cum_t, causal, 2 * pair + k) * scores).astype(BF16)
                for k in range(2)
            ],
            axis=1,
        )
        y[:, lanes] = (
            dot(mixing, stacked.astype(BF16))
            + grow_x[:, lanes] * carried[:, lanes]
            + skip[:, lanes] * x
        )
    state[...] = grow_x[CHUNK - 1 : CHUNK, :] * state[...] + dot(
        state_in.astype(BF16), xdt[...], TN
    )
    xbuf[0:8, :] = xbuf[CHUNK : CHUNK + 8, :]


def scan_backward_kernel(
    groups, parts, cw,
    px, halo, taps, heads, skip, spread, gather, dy, y, states, wide, gate,
    dpx, dtaps, dheads, dskip, wide_sum, gate_sum,
    xbuf, dstate, dcbuf, slope, xact, xd_s, dxd_s, acc_s,
    wide_in, gate_held, gate_acc, gate_in,
    wide_s, wide_r, core_s, core_r, gate_s, gate_r,
):
    line = groups // 2
    group, q = lax.axis_index("dp"), lax.axis_index("seq")
    z, core = group // 2, lax.rem(group, 2)
    sibling = (2 * z + 1 - core, q)
    peers = seq_peers(parts)
    places = [lax.rem(z + k, line) for k in range(1, line)]

    def wide_copy(k):
        return remote(wide.at[peers[k][1]], wide_in.at[k], wide_s, wide_r, k, peers[k])

    def core_copy(d):
        return remote(gate.at[d, 1 - core], gate_held.at[d], core_s, core_r, d, sibling)

    def gate_copy(k):
        to = (2 * places[k] + core, q)
        return remote(gate_acc.at[places[k]], gate_in.at[k], gate_s, gate_r, k, to)

    @pl.when(pl.program_id(0) == 0)
    def _():
        greet(peers + dp_peers(groups))
        for d in range(line):
            core_copy(d).start()
        for k in range(parts - 1):
            wide_copy(k).start()

    @pl.when(pl.program_id(0) == 1)
    def _():
        for d in range(line):
            core_copy(d).wait()
            add_blocks(gate_acc.at[d], gate.at[d, core], gate_held.at[d], 32, gate.shape[2] // 32)
        for k in range(line - 1):
            gate_copy(k).start()

    scan_backward_step(
        cw, px, halo, taps, heads, skip, spread, gather, dy, y, states,
        dpx, dtaps, dheads, dskip, xbuf, dstate, dcbuf, slope, xact, xd_s, dxd_s, acc_s,
    )

    @pl.when(pl.program_id(0) == pl.num_programs(0) - 1)
    def _():
        for k in range(line - 1):
            gate_copy(k).wait()
        sum_blocks(gate_sum, [gate_acc.at[z]] + [gate_in.at[k] for k in range(line - 1)], 32)
        for k in range(parts - 1):
            wide_copy(k).wait()
        for d in range(line):
            sum_blocks(
                wide_sum.at[d],
                [wide.at[q, d]] + [wide_in.at[k, d] for k in range(parts - 1)],
                16,
            )


def scan_backward_step(
    cw, px, halo, taps, heads, skip, spread, gather, dy, y, states,
    dpx, dtaps, dheads, dskip,
    xbuf, dstate, dcbuf, slope, xact, xd_s, dxd_s, acc_s,
):
    cc = cw + 2 * N
    at = pl.program_id(0)

    @pl.when(at == 0)
    def _():
        dstate[...] = jnp.zeros_like(dstate)
        dcbuf[CHUNK : CHUNK + 8, :] = jnp.zeros((8, cc), F32)
        dtaps[...] = jnp.zeros_like(dtaps)
        dheads[...] = jnp.zeros_like(dheads)
        dskip[...] = jnp.zeros_like(dskip)

    xbuf[0:8, :] = jnp.where(at == pl.num_programs(0) - 1, 0.0, halo[:, :cc])
    xbuf[8 : 8 + CHUNK, :] = px[:, :cc]
    dt_raw = own_heads_first(px[:, cc:], cw // P_SIZE)
    step, rate = rates(dt_raw, heads)
    row, col = triangle(CHUNK)
    causal = row >= col
    cum = dot(causal.astype(F32), rate, precision=EXACT)
    cum_t = cum.T
    spread_m = spread[...]
    last = cum[CHUNK - 1 : CHUNK, :]
    step_x = spread_heads(step, spread_m)
    grow_x = spread_heads(jnp.exp(cum), spread_m)
    tail_x = spread_heads(jnp.exp(last - cum), spread_m)

    for block in range(cc // LANES):
        lanes = slice(block * LANES, (block + 1) * LANES)
        conv = conv_block(taps, xbuf, lanes)
        sig = jax.nn.sigmoid(conv)
        act = conv * sig
        xact[:, lanes] = act
        slope[:, lanes] = sig + act * (1.0 - sig)
    state_in = xact[:, cw : cw + N]
    state_out = xact[:, cw + N : cc]
    scores = dot(state_out, state_in, NT, EXACT)
    in_low = state_in.astype(BF16)
    out_low = state_out.astype(BF16)
    dstate_low = dstate[...].astype(BF16)
    acc_s[...] = jnp.zeros_like(acc_s)
    dxd_s[...] = tail_x * dot(in_low, dstate_low)
    dskip[0:1, :] += jnp.sum(xact[:, :cw] * dy[...], axis=0, keepdims=True)
    first = lax.broadcasted_iota(jnp.int32, (1, LANES), 1) < P_SIZE
    xd_s[...] = (xact[:, :cw] * step_x).astype(BF16)
    total = jnp.sum(xd_s[...].astype(F32) * dxd_s[...], axis=0, keepdims=True) + grow_x[
        CHUNK - 1 : CHUNK, :
    ] * jnp.sum(dstate[...] * states[0].astype(F32), axis=0, keepdims=True)
    dscores = jnp.zeros((CHUNK, CHUNK), F32)
    for pair in range(cw // LANES):
        lanes = slice(pair * LANES, (pair + 1) * LANES)
        dyp = dy[:, lanes]
        stacked = jnp.concatenate(
            [jnp.where(first, dyp, 0.0), jnp.where(first, 0.0, dyp)], axis=0
        ).astype(BF16)
        decays = [pair_decay(cum, cum_t, causal, 2 * pair + k) for k in range(2)]
        mixing = jnp.concatenate([(decay * scores).astype(BF16) for decay in decays], axis=0)
        dxd_s[:, lanes] += dot(mixing, stacked, TN)
        dmix = dot(stacked, xd_s[:, lanes], NT)
        dscores = dscores + decays[0] * dmix[:CHUNK] + decays[1] * dmix[CHUNK:]
    dy_low = dy[...].astype(BF16)
    dy_f = dy_low.astype(F32)
    xd_f = xd_s[...].astype(F32)
    dxd = dxd_s[...]
    y_scan = y[...] - skip[...] * xact[:, :cw]
    final = lax.broadcasted_iota(jnp.int32, (CHUNK, 1), 0) == CHUNK - 1
    gather_m = gather[...]
    dcum = spread_heads(dy_f * y_scan - xd_f * dxd + jnp.where(final, total, 0.0), gather_m)
    dstep = spread_heads(xact[:, :cw] * dxd, gather_m)
    drate = dot((row <= col).astype(F32), dcum, precision=EXACT)
    dstep = dstep + drate * heads[1:2, :]
    ddt = dstep * jax.nn.sigmoid(dt_raw + heads[0:1, :])
    dheads[0:1, :] += jnp.sum(ddt, axis=0, keepdims=True)
    dheads[1:2, :] += jnp.sum(drate * rate, axis=0, keepdims=True)
    grown = (grow_x * dy_f).astype(BF16)
    dscores_low = dscores.astype(BF16)
    dout = dot(dscores_low, in_low) + dot(grown, states[0], NT)
    din = dot(dscores_low, out_low, TN) + dot((tail_x * xd_f).astype(BF16), dstate_low, NT)
    dstate[...] = grow_x[CHUNK - 1 : CHUNK, :] * dstate[...] + dot(out_low, grown, TN)
    dcbuf[:CHUNK, :cw] = (step_x * dxd + skip[...] * dy[...]) * slope[:, :cw]
    dcbuf[:CHUNK, cw : cw + N] = din * slope[:, cw : cw + N]
    dcbuf[:CHUNK, cw + N :] = dout * slope[:, cw + N :]
    for block in range(cc // LANES):
        lanes = slice(block * LANES, (block + 1) * LANES)
        dconv = dcbuf[:CHUNK, lanes]
        dtaps[TAPS : TAPS + 1, lanes] += jnp.sum(dconv, axis=0, keepdims=True)
        back = taps[TAPS - 1 : TAPS, lanes] * dconv
        for tap in range(TAPS):
            dtaps[tap : tap + 1, lanes] += jnp.sum(
                dconv * xbuf[5 + tap : 5 + tap + CHUNK, lanes], axis=0, keepdims=True
            )
            if tap < TAPS - 1:
                reach = TAPS - 1 - tap
                back = back + taps[tap : tap + 1, lanes] * dcbuf[reach : reach + CHUNK, lanes]
        dpx[:, lanes] = back.astype(BF16)
    ours = lax.broadcasted_iota(jnp.int32, (1, LANES), 1) < cw // P_SIZE
    ddt = own_heads_first(jnp.where(ours, ddt, 0.0), cw // P_SIZE, back=True)
    dpx[:, cc:] = ddt.astype(BF16)
    dcbuf[CHUNK : CHUNK + 8, :] = dcbuf[0:8, :]


def whole(shape):
    return pl.BlockSpec(shape, lambda i: (0,) * len(shape))


def scan_forward(px, taps, heads, skip, spread):
    length, width = px.shape
    cw = skip.shape[1]
    cc = cw + 2 * N
    chunks = length // CHUNK
    return pl.pallas_call(
        functools.partial(scan_forward_kernel, cw),
        grid=(chunks,),
        in_specs=[
            pl.BlockSpec((CHUNK, width), lambda i: (i, 0)),
            whole(taps.shape),
            whole(heads.shape),
            whole(skip.shape),
            whole(spread.shape),
        ],
        out_specs=[
            pl.BlockSpec((CHUNK, cw), lambda i: (i, 0)),
            pl.BlockSpec((1, N, cw), lambda i: (i, 0, 0)),
        ],
        out_shape=[
            jax.ShapeDtypeStruct((length, cw), F32),
            jax.ShapeDtypeStruct((chunks, N, cw), BF16),
        ],
        scratch_shapes=[
            pltpu.VMEM((CHUNK + 8, cc), F32),
            pltpu.VMEM((N, cw), F32),
            pltpu.VMEM((CHUNK, cw), BF16),
            pltpu.VMEM((CHUNK, cw), F32),
        ],
        compiler_params=pltpu.CompilerParams(vmem_limit_bytes=48 * 2**20),
        cost_estimate=pl.CostEstimate(
            flops=3 * 10**9, bytes_accessed=40 * 10**6, transcendentals=10**7
        ),
        name="scan_forward",
    )(px, taps, heads, skip, spread)


def scan_backward(collective_id, px, taps, heads, skip, spread, gather, dy, y, states, wide, gate):
    length, width = px.shape
    cw = skip.shape[1]
    cc = cw + 2 * N
    chunks = length // CHUNK
    eighths = CHUNK // 8
    parts, line, out_rows, half = wide.shape
    span = gate.shape[2]
    sem = pltpu.SemaphoreType.DMA
    vmem = pl.BlockSpec(memory_space=pltpu.VMEM)
    return pl.pallas_call(
        functools.partial(scan_backward_kernel, 2 * line, parts, cw),
        grid=(chunks,),
        in_specs=[
            pl.BlockSpec((CHUNK, width), lambda i: (chunks - 1 - i, 0)),
            pl.BlockSpec(
                (8, width), lambda i: (jnp.maximum((chunks - 1 - i) * eighths - 1, 0), 0)
            ),
            whole(taps.shape),
            whole(heads.shape),
            whole(skip.shape),
            whole(spread.shape),
            whole(gather.shape),
            pl.BlockSpec((CHUNK, cw), lambda i: (chunks - 1 - i, 0)),
            pl.BlockSpec((CHUNK, cw), lambda i: (chunks - 1 - i, 0)),
            pl.BlockSpec((1, N, cw), lambda i: (chunks - 1 - i, 0, 0)),
            vmem,
            vmem,
        ],
        out_specs=[
            pl.BlockSpec((CHUNK, width), lambda i: (chunks - 1 - i, 0)),
            whole((8, cc)),
            whole((8, LANES)),
            whole((8, cw)),
            vmem,
            vmem,
        ],
        out_shape=[
            jax.ShapeDtypeStruct((length, width), BF16),
            jax.ShapeDtypeStruct((8, cc), F32),
            jax.ShapeDtypeStruct((8, LANES), F32),
            jax.ShapeDtypeStruct((8, cw), F32),
            jax.ShapeDtypeStruct(wide.shape[1:], BF16),
            jax.ShapeDtypeStruct((span, cw), BF16),
        ],
        scratch_shapes=[
            pltpu.VMEM((CHUNK + 8, cc), F32),
            pltpu.VMEM((N, cw), F32),
            pltpu.VMEM((CHUNK + 8, cc), F32),
            pltpu.VMEM((CHUNK, cc), F32),
            pltpu.VMEM((CHUNK, cc), F32),
            pltpu.VMEM((CHUNK, cw), BF16),
            pltpu.VMEM((CHUNK, cw), F32),
            pltpu.VMEM((CHUNK, CHUNK), F32),
            pltpu.VMEM((parts - 1,) + wide.shape[1:], BF16),
            pltpu.VMEM((line, span, cw), BF16),
            pltpu.VMEM((line, span, cw), BF16),
            pltpu.VMEM((line - 1, span, cw), BF16),
            sem((parts - 1,)), sem((parts - 1,)), sem((line,)), sem((line,)),
            sem((line - 1,)), sem((line - 1,)),
        ],
        compiler_params=pltpu.CompilerParams(
            collective_id=collective_id, has_side_effects=True, vmem_limit_bytes=56 * 2**20
        ),
        cost_estimate=pl.CostEstimate(
            flops=10**10, bytes_accessed=100 * 10**6, transcendentals=10**7
        ),
        name="scan_backward",
    )(px, px, taps, heads, skip, spread, gather, dy, y, states, wide, gate)


WIDE = 512


def widths_kernel(cw, u, wo, cotangent, tokens, block_out, back, mixed, branch, norms, pulls):
    at = pl.program_id(0)
    ends = [level_width(k) // WIDE - 1 for k in range(LEVELS)]

    @pl.when(at == 0)
    def _():
        terms = u[0, :, cw:].astype(F32)
        for part in range(1, u.shape[0]):
            terms = terms + u[part, :, cw:].astype(F32)
        squares = jnp.zeros((terms.shape[0], 1), F32)
        for k in range(LEVELS):
            squares = squares + terms[:, k : k + 1] + terms[:, LEVELS + k : LEVELS + k + 1]
            norms[:, k : k + 1] = lax.rsqrt(squares / level_width(k) + EPS_OUT)
        running = jnp.zeros(branch.shape, F32)
        for k in reversed(range(LEVELS)):
            running = running + norms[:, k : k + 1] * cotangent[k].astype(F32)
            mixed[k] = running.astype(BF16)
        branch[...] = jnp.zeros_like(branch)

    part = at * WIDE // cw
    lanes = pl.ds(pl.multiple_of(lax.rem(at * WIDE, cw), WIDE), WIDE)
    level = sum((at > end).astype(jnp.int32) for end in ends[:-1])
    branch[...] += dot(u[part, :, lanes], wo[...])
    back[part, :, lanes] = dot(mixed[level], wo[...], NT).astype(BF16)
    for k in range(LEVELS):

        @pl.when(at == ends[k])
        def _():
            norm = norms[:, k : k + 1]
            block_out[k] = (tokens[...].astype(F32) + norm * branch[...]).astype(BF16)
            inner = jnp.sum(cotangent[k].astype(F32) * branch[...], axis=-1, keepdims=True)
            pulls[:, k : k + 1] = norm * norm * norm * (inner / level_width(k))

    @pl.when(at == ends[-1])
    def _():
        coef = jnp.zeros((branch.shape[0], 1), F32)
        lane = lax.broadcasted_iota(jnp.int32, (1, LANES), 1)
        packed = jnp.zeros((branch.shape[0], LANES), F32)
        for k in reversed(range(LEVELS)):
            coef = coef + pulls[:, k : k + 1]
            high, rest = two_terms(coef)
            packed = jnp.where(lane == k, high.astype(F32), packed)
            packed = jnp.where(lane == LEVELS + k, rest.astype(F32), packed)
        for p in range(back.shape[0]):
            back[p, :, cw:] = packed.astype(BF16)


def widths(u, wo, cotangent, tokens):
    parts, rows, wide = u.shape
    cw = wide - LANES

    def full(shape):
        return pl.BlockSpec(shape, lambda i: (0,) * len(shape), pipeline_mode=pl.Buffered(1))

    return pl.pallas_call(
        functools.partial(widths_kernel, cw),
        grid=(INNER // WIDE,),
        in_specs=[
            full(u.shape),
            pl.BlockSpec((WIDE, D), lambda i: (i, 0)),
            full(cotangent.shape),
            full(tokens.shape),
        ],
        out_specs=[full(cotangent.shape), full(u.shape), full(cotangent.shape)],
        out_shape=[
            jax.ShapeDtypeStruct(cotangent.shape, BF16),
            jax.ShapeDtypeStruct(u.shape, BF16),
            jax.ShapeDtypeStruct(cotangent.shape, BF16),
        ],
        scratch_shapes=[
            pltpu.VMEM((rows, D), F32),
            pltpu.VMEM((rows, LANES), F32),
            pltpu.VMEM((rows, LANES), F32),
        ],
        compiler_params=pltpu.CompilerParams(vmem_limit_bytes=48 * 2**20),
        name="widths",
    )(u, wo, cotangent, tokens)


MESH = pl.DeviceIdType.MESH


def remote(src, dst, sends, recvs, index, device):
    return pltpu.make_async_remote_copy(
        src_ref=src,
        dst_ref=dst,
        send_sem=sends.at[index],
        recv_sem=recvs.at[index],
        device_id=device,
        device_id_type=MESH,
    )


def greet(devices):
    barrier = pltpu.get_barrier_semaphore()
    for device in devices:
        pl.semaphore_signal(barrier, inc=1, device_id=device, device_id_type=MESH)
    pl.semaphore_wait(barrier, len(devices))


def seq_peers(parts):
    group, q = lax.axis_index("dp"), lax.axis_index("seq")
    return [(group, lax.rem(q + k, parts)) for k in range(1, parts)]


def dp_peers(groups):
    group, q = lax.axis_index("dp"), lax.axis_index("seq")
    return [(lax.rem(group + k, groups), q) for k in range(1, groups)]


def swap_kernel(parts, count, *refs):
    sources, results = refs[:count], refs[count : 2 * count]
    sends, recvs, local = refs[2 * count :]
    q = lax.axis_index("seq")
    peers = seq_peers(parts)
    greet(peers)
    copies = []
    for k, peer in enumerate(peers):
        for a in range(count):
            copy = remote(
                sources[a].at[peer[1]], results[a].at[q], sends, recvs, k * count + a, peer
            )
            copy.start()
            copies.append(copy)
    own = [
        pltpu.make_async_copy(sources[a].at[q], results[a].at[q], local.at[a])
        for a in range(count)
    ]
    for copy in own:
        copy.start()
    for copy in own + copies:
        copy.wait()


def swap(collective_id, *arrays):
    parts = arrays[0].shape[0]
    count = len(arrays)
    return pl.pallas_call(
        functools.partial(swap_kernel, parts, count),
        in_specs=[pl.BlockSpec(memory_space=pl.ANY)] * count,
        out_specs=[pl.BlockSpec(memory_space=pl.ANY)] * count,
        out_shape=[jax.ShapeDtypeStruct(a.shape, a.dtype) for a in arrays],
        scratch_shapes=[
            pltpu.SemaphoreType.DMA(((parts - 1) * count,)),
            pltpu.SemaphoreType.DMA(((parts - 1) * count,)),
            pltpu.SemaphoreType.DMA((count,)),
        ],
        compiler_params=pltpu.CompilerParams(collective_id=collective_id, has_side_effects=True),
        name="swap",
    )(*arrays)


def all_peers(groups, parts):
    devices = groups * parts
    me = lax.axis_index("dp") * parts + lax.axis_index("seq")
    peers = []
    for k in range(1, devices):
        other = lax.rem(me + k, devices)
        peers.append((other // parts, lax.rem(other, parts)))
    return peers


def broadcast_kernel(
    groups, parts, block, near, total, near_out, out, sends, recvs, near_s, near_r, local
):
    group, q = lax.axis_index("dp"), lax.axis_index("seq")
    me = group * parts + q
    everyone = all_peers(groups, parts)
    greet(everyone)
    copies = [
        remote(block, out.at[me], sends, recvs, k, peer) for k, peer in enumerate(everyone)
    ]
    copies += [
        remote(near, near_out.at[q], near_s, near_r, k, peer)
        for k, peer in enumerate(seq_peers(parts))
    ]
    copies += [
        pltpu.make_async_copy(block, out.at[me], local.at[0]),
        pltpu.make_async_copy(near, near_out.at[q], local.at[1]),
    ]
    for copy in copies:
        copy.start()
    for copy in copies:
        copy.wait()
    total[...] = jnp.sum(out[...], axis=0)


def broadcast(collective_id, block, near, groups, parts):
    devices = groups * parts
    sem = pltpu.SemaphoreType.DMA
    return pl.pallas_call(
        functools.partial(broadcast_kernel, groups, parts),
        in_specs=[pl.BlockSpec(memory_space=pltpu.VMEM)] * 2,
        out_specs=[pl.BlockSpec(memory_space=pltpu.VMEM)] * 2,
        out_shape=[
            jax.ShapeDtypeStruct(block.shape, block.dtype),
            jax.ShapeDtypeStruct((parts,) + near.shape, near.dtype),
        ],
        scratch_shapes=[
            pltpu.VMEM((devices,) + block.shape, block.dtype),
            sem((devices - 1,)), sem((devices - 1,)), sem((parts - 1,)), sem((parts - 1,)),
            sem((2,)),
        ],
        compiler_params=pltpu.CompilerParams(collective_id=collective_id, has_side_effects=True),
        name="broadcast",
    )(block, near)


def collect_kernel(
    groups, parts, hidden, w_in, chan, hid_out, w_out, gate_out, chan_out,
    blocks, gates, chan_s, chan_r, hid_s, hid_r, swap_s, swap_r, gate_s, gate_r,
    line_s, line_r, core_s, core_r, local,
):
    line = groups // 2
    cw = INNER // parts
    cc = cw + 2 * N
    group, q = lax.axis_index("dp"), lax.axis_index("seq")
    z, core = group // 2, lax.rem(group, 2)
    sibling = (2 * z + 1 - core, q)
    peers = seq_peers(parts)
    everyone = all_peers(groups, parts)
    shared = w_in[:, 2 * INNER :].astype(BF16)
    for part in range(parts):
        at = INNER + part * cw
        blocks[part, :, :cw] = w_in[:, at : at + cw].astype(BF16)
        blocks[part, :, cw : cc + H] = shared
        blocks[part, :, cc + H :] = jnp.zeros((w_in.shape[0], LANES - H), BF16)
    greet(everyone)
    swaps = []
    for k, peer in enumerate(peers):
        copy = remote(blocks.at[peer[1]], w_out.at[group, q], swap_s, swap_r, k, peer)
        copy.start()
        swaps.append(copy)
    mine = pltpu.make_async_copy(blocks.at[q], w_out.at[group, q], local.at[0])
    mine.start()
    keep = pltpu.make_async_copy(hidden, hid_out.at[q], local.at[1])
    keep.start()
    chans = []
    for k, peer in enumerate(everyone):
        copy = remote(chan, chan_out.at[group * parts + q], chan_s, chan_r, k, peer)
        copy.start()
        chans.append(copy)
    chan_keep = pltpu.make_async_copy(chan, chan_out.at[group * parts + q], local.at[2])
    chan_keep.start()
    for part in range(parts):
        gates[part] = w_in[:, part * cw : (part + 1) * cw].astype(BF16)
    mine.wait()
    for copy in swaps:
        copy.wait()
    hids = []
    for k, peer in enumerate(peers):
        copy = remote(hidden, hid_out.at[q], hid_s, hid_r, k, peer)
        copy.start()
        hids.append(copy)
    for k, peer in enumerate(peers):
        copy = remote(gates.at[peer[1]], gate_out.at[q], gate_s, gate_r, k, peer)
        copy.start()
        hids.append(copy)
    gate_keep = pltpu.make_async_copy(gates.at[q], gate_out.at[q], local.at[3])
    gate_keep.start()

    def along(from_z, up):
        block = w_out.at[2 * from_z + core]
        to = z + 1 if up else z - 1
        return remote(
            block, block, line_s.at[0 if up else 1], line_r.at[0 if up else 1], from_z,
            (2 * to + core, q),
        )

    def across(from_z):
        block = w_out.at[2 * from_z + core]
        return remote(block, block, core_s, core_r, from_z, sibling)

    for t in range(line):
        low, high = z - t, z + t
        if t == 0:
            across(z).start()

            @pl.when(z < line - 1)
            def _():
                along(z, True).start()

            @pl.when(z > 0)
            def _():
                along(z, False).start()

            continue

        @pl.when(low >= 0)
        def _():
            along(low, True).wait_recv()

            @pl.when(z < line - 1)
            def _():
                along(low, True).start()

            across(low).start()

        @pl.when(high <= line - 1)
        def _():
            along(high, False).wait_recv()

            @pl.when(z > 0)
            def _():
                along(high, False).start()

            across(high).start()

    for from_z in range(line):
        across(from_z).wait_send()
        block = w_out.at[2 * from_z + 1 - core]
        remote(block, block, core_s, core_r, from_z, sibling).wait_recv()

        @pl.when((from_z <= z) & (z < line - 1))
        def _():
            along(from_z, True).wait_send()

        @pl.when((from_z >= z) & (z > 0))
        def _():
            along(from_z, False).wait_send()

    keep.wait()
    chan_keep.wait()
    gate_keep.wait()
    for copy in hids + chans:
        copy.wait()


def collect(collective_id, hidden, w_in, chan, groups, parts):
    rows = w_in.shape[0]
    line = groups // 2
    cw = INNER // parts
    width = cw + 2 * N + LANES
    sem = pltpu.SemaphoreType.DMA
    hbm = pl.BlockSpec(memory_space=pl.ANY)
    return pl.pallas_call(
        functools.partial(collect_kernel, groups, parts),
        in_specs=[hbm, pl.BlockSpec(memory_space=pltpu.VMEM), hbm],
        out_specs=[hbm] * 4,
        out_shape=[
            jax.ShapeDtypeStruct((parts,) + hidden.shape, hidden.dtype),
            jax.ShapeDtypeStruct((groups, parts, rows, width), BF16),
            jax.ShapeDtypeStruct((parts, rows, cw), BF16),
            jax.ShapeDtypeStruct((groups * parts,) + chan.shape, chan.dtype),
        ],
        scratch_shapes=[
            pltpu.VMEM((parts, rows, width), BF16),
            pltpu.VMEM((parts, rows, cw), BF16),
            *([sem((groups * parts - 1,))] * 2),
            *([sem((parts - 1,))] * 6),
            sem((2, line)), sem((2, line)), sem((line,)), sem((line,)), sem((4,)),
        ],
        compiler_params=pltpu.CompilerParams(
            collective_id=collective_id, has_side_effects=True, vmem_limit_bytes=48 * 2**20
        ),
        name="collect",
    )(hidden, w_in, chan)


def add_blocks(out, a, b, rows, steps):
    def step(i, carry):
        at = pl.ds(pl.multiple_of(i * rows, rows), rows)
        out[at] = (a[at].astype(F32) + b[at].astype(F32)).astype(out.dtype)
        return carry

    lax.fori_loop(0, steps, step, 0)


def level_of(channel, width):
    return sum((channel >= level_width(k)).astype(jnp.int32) for k in range(LEVELS - 1))


def swap_back_kernel(
    groups, parts, cw, back, u, mixed, back_out, left, right,
    sent, held, sends, recvs, core_s, core_r, local,
):
    line = groups // 2
    group, q = lax.axis_index("dp"), lax.axis_index("seq")
    z, core = group // 2, lax.rem(group, 2)
    sibling = (2 * z + 1 - core, q)
    peers = seq_peers(parts)
    greet(peers + [sibling])
    copies = [
        remote(back.at[peer[1]], back_out.at[q], sends, recvs, k, peer)
        for k, peer in enumerate(peers)
    ]
    copies.append(pltpu.make_async_copy(back.at[q], back_out.at[q], local))
    for copy in copies:
        copy.start()
    width = INNER // groups
    rows = width // parts
    tile = 512
    halves = D // 2 // tile

    def product(of, j):
        channel = of * width
        lanes = pl.ds(pl.multiple_of(lax.rem(channel, cw), width), width)
        cols = pl.ds(pl.multiple_of(j * tile, tile), tile)
        return dot(u[channel // cw, :, lanes], mixed[level_of(channel, width), :, cols], TN)

    cores = []
    for d in range(line):

        def send_step(j, carry, d=d):
            cols = pl.ds(pl.multiple_of(j * tile, tile), tile)
            sent[d, :, cols] = product(2 * d + 1 - core, j).astype(BF16)
            return carry

        lax.fori_loop(0, 2 * halves, send_step, 0)
        copy = remote(sent.at[d], held.at[d], core_s, core_r, d, sibling)
        copy.start()
        cores.append(copy)
    for d in range(line):
        cores[d].wait_recv()
        for out, first in ((left, 0), (right, halves)):

            def keep_step(j, carry, d=d, out=out, first=first):
                at = pl.ds(pl.multiple_of((j + first) * tile, tile), tile)
                cols = pl.ds(pl.multiple_of(j * tile, tile), tile)
                total = product(2 * d + core, j + first) + held[d, :, at].astype(F32)
                total = total.astype(BF16)
                for part in range(parts):
                    out[part, d, :, cols] = total[part * rows : (part + 1) * rows]
                return carry

            lax.fori_loop(0, halves, keep_step, 0)
    for copy in cores:
        copy.wait_send()
    for copy in copies:
        copy.wait()


def swap_back(collective_id, back, u, mixed, groups):
    parts, rows, wide = back.shape
    line, width = groups // 2, INNER // groups
    sem = pltpu.SemaphoreType.DMA
    vmem = pl.BlockSpec(memory_space=pltpu.VMEM)
    hbm = pl.BlockSpec(memory_space=pl.ANY)
    return pl.pallas_call(
        functools.partial(swap_back_kernel, groups, parts, wide - LANES),
        in_specs=[hbm, vmem, vmem],
        out_specs=[hbm, vmem, vmem],
        out_shape=[
            jax.ShapeDtypeStruct(back.shape, back.dtype),
            *([jax.ShapeDtypeStruct((parts, line, width // parts, D // 2), BF16)] * 2),
        ],
        scratch_shapes=[
            pltpu.VMEM((line, width, D), BF16),
            pltpu.VMEM((line, width, D), BF16),
            sem((parts - 1,)), sem((parts - 1,)), sem((line,)), sem((line,)), sem,
        ],
        compiler_params=pltpu.CompilerParams(
            collective_id=collective_id, has_side_effects=True, vmem_limit_bytes=56 * 2**20
        ),
        name="swap_back",
    )(back, u, mixed)


def sum_blocks(out, blocks, rows):
    def step(i, carry):
        at = pl.ds(pl.multiple_of(i * rows, rows), rows)
        total = blocks[0][at].astype(F32)
        for block in blocks[1:]:
            total = total + block[at].astype(F32)
        out[at] = total.astype(out.dtype)
        return carry

    lax.fori_loop(0, out.shape[0] // rows, step, 0)


class LineSum:
    def __init__(self, line, z, core, q, acc, up, down, up_s, up_r, down_s, down_r, rows, steps):
        self.line, self.z, self.core, self.q = line, z, core, q
        self.acc, self.up, self.down = acc, up, down
        self.up_s, self.up_r, self.down_s, self.down_r = up_s, up_r, down_s, down_r
        self.rows, self.steps = rows, steps

    def ahead(self, d, first):
        block = self.acc.at[d] if first else self.up.at[d]
        to = (2 * (self.z + 1) + self.core, self.q)
        return remote(block, self.up.at[d], self.up_s, self.up_r, d, to)

    def behind(self, d, first):
        block = self.acc.at[d] if first else self.down.at[d]
        to = (2 * (self.z - 1) + self.core, self.q)
        return remote(block, self.down.at[d], self.down_s, self.down_r, d, to)

    def add(self, into, d):
        add_blocks(into.at[d], into.at[d], self.acc.at[d], self.rows, self.steps)

    def step(self, t):
        line, z = self.line, self.z
        far, near = line - 1 - t + z, t - (line - 1 - z)

        @pl.when(z == 0)
        def _():
            self.ahead(line - 1 - t, True).start()

        @pl.when((z > 0) & (z <= t))
        def _():
            self.ahead(far, False).wait_recv()
            self.add(self.up, far)
            self.ahead(far, False).start()

        @pl.when(z == line - 1)
        def _():
            self.behind(t, True).start()

        @pl.when((z < line - 1) & (line - 1 - z <= t))
        def _():
            self.behind(near, False).wait_recv()
            self.add(self.down, near)
            self.behind(near, False).start()

    def sent(self, t):
        line, z = self.line, self.z
        far, near = line - 1 - t + z, t - (line - 1 - z)

        @pl.when(z == 0)
        def _():
            self.ahead(line - 1 - t, True).wait_send()

        @pl.when((z > 0) & (z <= t))
        def _():
            self.ahead(far, False).wait_send()

        @pl.when(z == line - 1)
        def _():
            self.behind(t, True).wait_send()

        @pl.when((z < line - 1) & (line - 1 - z <= t))
        def _():
            self.behind(near, False).wait_send()

    def finish(self, out):
        line, z = self.line, self.z

        @pl.when(z == 0)
        def _():
            self.behind(z, False).wait_recv()
            add_blocks(out, self.acc.at[z], self.down.at[z], self.rows, self.steps)

        @pl.when(z == line - 1)
        def _():
            self.ahead(z, False).wait_recv()
            add_blocks(out, self.acc.at[z], self.up.at[z], self.rows, self.steps)

        @pl.when((z > 0) & (z < line - 1))
        def _():
            self.ahead(z, False).wait_recv()
            self.add(self.up, z)
            self.behind(z, False).wait_recv()
            add_blocks(out, self.up.at[z], self.down.at[z], self.rows, self.steps)


def owners_kernel(
    groups, parts, rows,
    normed, left, right, gate, small, dz, dpx, wz, wx,
    part, left_out, right_out, gate_out, back_out, small_all,
    made, held, acc, up, down, final, left_up, left_down, right_in, right_acc, right_up, right_down,
    normed_v, dz_v, dpx_v, wz_v, wx_v, back,
    core_s, core_r, up_s, up_r, down_s, down_r, lup_s, lup_r, ldown_s, ldown_r,
    rup_s, rup_r, rdown_s, rdown_r,
    part_s, part_r, back_s, back_r, gate_s, gate_r, right_s, right_r, small_s, small_r,
    load, local,
):
    line = groups // 2
    span = parts * rows
    group, q = lax.axis_index("dp"), lax.axis_index("seq")
    z, core = group // 2, lax.rem(group, 2)
    sibling = (2 * z + 1 - core, q)
    peers, others = seq_peers(parts), dp_peers(groups)
    tokens = back.shape[1]
    loads = [
        pltpu.make_async_copy(source, target, load.at[k])
        for k, (source, target) in enumerate(
            [(normed, normed_v), (dpx, dpx_v), (dz, dz_v), (wz, wz_v), (wx, wx_v)]
        )
    ]
    for copy in loads:
        copy.start()
    greet(peers + others)
    half_rows = left.shape[1] // 2
    lefts = LineSum(
        line, z, core, q, left, left_up, left_down, lup_s, lup_r, ldown_s, ldown_r, half_rows, 2
    )
    rights = LineSum(
        line, z, core, q, right_acc, right_up, right_down, rup_s, rup_r, rdown_s, rdown_r,
        half_rows, 2,
    )
    wholes = LineSum(
        line, z, core, q, acc, up, down, up_s, up_r, down_s, down_r, rows, parts
    )
    lefts.step(0)
    rights_in = []
    for k, peer in enumerate(peers):
        copy = remote(right.at[peer[1]], right_in.at[k], right_s, right_r, k, peer)
        copy.start()
        rights_in.append(copy)
    waiting = []
    for k, peer in enumerate(peers):
        copy = remote(gate.at[peer[1]], gate_out.at[q], gate_s, gate_r, k, peer)
        copy.start()
        waiting.append(copy)
    for k, peer in enumerate(others):
        copy = remote(small, small_all.at[group], small_s, small_r, k, peer)
        copy.start()
        waiting.append(copy)
    own = [
        pltpu.make_async_copy(gate.at[q], gate_out.at[q], local.at[0]),
        pltpu.make_async_copy(small, small_all.at[group], local.at[1]),
    ]
    for copy in own:
        copy.start()
    loads[0].wait()
    loads[1].wait()
    tile = 512

    def dweight(of, out):
        at = pl.ds(pl.multiple_of(of * span, span), span)
        out[...] = dot(normed_v[:, at], dpx_v[...], TN).astype(BF16)

    cores = []
    for d in range(line):
        dweight(2 * d + 1 - core, made.at[d])
        copy = remote(made.at[d], held.at[d], core_s, core_r, d, sibling)
        copy.start()
        cores.append(copy)
    for d in range(line):
        dweight(2 * d + core, acc.at[d])
    for d in range(line):
        cores[d].wait()
        add_blocks(acc.at[d], acc.at[d], held.at[d], rows, parts)
    lefts.sent(0)
    wholes.step(0)
    for copy in loads[2:]:
        copy.wait()

    def dnormed(of):
        at = pl.ds(pl.multiple_of(of * tokens, tokens), tokens)

        def step(j, carry):
            cols = pl.ds(pl.multiple_of(j * tile, tile), tile)
            back[of, :, cols] = (
                dot(dz_v[at, :], wz_v[cols, :], NT) + dot(dpx_v[at, :], wx_v[cols, :], NT)
            ).astype(BF16)
            return carry

        lax.fori_loop(0, D // tile, step, 0)

    for k, peer in enumerate(peers):
        dnormed(peer[1])
        copy = remote(back.at[peer[1]], back_out.at[q], back_s, back_r, k, peer)
        copy.start()
        waiting.append(copy)
    dnormed(q)
    copy = pltpu.make_async_copy(back.at[q], back_out.at[q], local.at[2])
    copy.start()
    own.append(copy)
    for t in range(1, line - 1):
        wholes.sent(t - 1)
        lefts.step(t)
        lefts.sent(t)
        wholes.step(t)
    lefts.finish(left_out)
    for copy in rights_in:
        copy.wait()
    for d in range(line):
        sum_blocks(
            right_acc.at[d],
            [right.at[q, d]] + [right_in.at[k, d] for k in range(parts - 1)],
            16,
        )
    wholes.sent(line - 2)
    rights.step(0)
    wholes.finish(final)
    for k, peer in enumerate(peers):
        block = final.at[pl.ds(pl.multiple_of(peer[1] * rows, rows), rows)]
        copy = remote(block, part.at[q], part_s, part_r, k, peer)
        copy.start()
        waiting.append(copy)
    copy = pltpu.make_async_copy(
        final.at[pl.ds(pl.multiple_of(q * rows, rows), rows)], part.at[q], local.at[3]
    )
    copy.start()
    own.append(copy)
    for t in range(1, line - 1):
        rights.sent(t - 1)
        rights.step(t)
    rights.finish(right_out)
    rights.sent(line - 2)
    for copy in own + waiting:
        copy.wait()


def sum_to_owners(collective_id, normed, left, right, gate, small, dz, dpx, wz, wx):
    parts, line, out_rows, half = right.shape
    groups = 2 * line
    rows = gate.shape[1]
    span, width = rows * parts, dpx.shape[1]
    tokens = dz.shape[0] // parts
    sem = pltpu.SemaphoreType.DMA
    vmem = pl.BlockSpec(memory_space=pltpu.VMEM)
    hbm = pl.BlockSpec(memory_space=pl.ANY)
    return pl.pallas_call(
        functools.partial(owners_kernel, groups, parts, rows),
        in_specs=[hbm, vmem, vmem, hbm, vmem, hbm, hbm, hbm, hbm],
        out_specs=[hbm, vmem, vmem, hbm, hbm, vmem],
        out_shape=[
            jax.ShapeDtypeStruct((parts, rows, width), BF16),
            *([jax.ShapeDtypeStruct((out_rows, half), F32)] * 2),
            jax.ShapeDtypeStruct(gate.shape, BF16),
            jax.ShapeDtypeStruct((parts, tokens, D), BF16),
            jax.ShapeDtypeStruct((groups,) + small.shape, F32),
        ],
        scratch_shapes=[
            *([pltpu.VMEM((line, span, width), BF16)] * 5),
            pltpu.VMEM((span, width), BF16),
            *([pltpu.VMEM(left.shape, BF16)] * 2),
            pltpu.VMEM((parts - 1,) + left.shape, BF16),
            *([pltpu.VMEM(left.shape, BF16)] * 3),
            *[pltpu.VMEM(a.shape, BF16) for a in (normed, dz, dpx, wz, wx)],
            pltpu.VMEM((parts, tokens, D), BF16),
            *([sem((line,))] * 14),
            *([sem((parts - 1,))] * 8),
            *([sem((groups - 1,))] * 2),
            sem((5,)),
            sem((4,)),
        ],
        compiler_params=pltpu.CompilerParams(
            collective_id=collective_id, has_side_effects=True, vmem_limit_bytes=63 * 2**20
        ),
        name="sum_to_owners",
    )(normed, left, right, gate, small, dz, dpx, wz, wx)


def adam_step(weight, gradient, moment, second, step_rate, weight_decay):
    new_moment = BETA * moment + (1.0 - BETA) * gradient
    new_second = BETA * second + (1.0 - BETA) * gradient * gradient
    correction = 1.0 - BETA**STEP
    update = new_moment / correction / (jnp.sqrt(new_second / correction) + ADAM_EPS)
    return (weight - step_rate * (update + weight_decay * weight), new_moment, new_second)


def pack_terms(values):
    high = lax.reduce_precision(values, 8, 7)
    packed = jnp.concatenate([high, values - high], axis=-1).astype(BF16)
    return jnp.pad(packed, ((0, 0), (0, LANES - packed.shape[-1])))


def unpack_terms(packed, count):
    packed = packed.astype(F32)
    return packed[..., :count] + packed[..., count : 2 * count]


def on_device(
    hidden_in, out_grads, w_in, w_in_m, w_in_v, w_out, w_out_m, w_out_v,
    chan_params, chan_m, chan_v, head_params, head_m, head_v,
):
    parts = lax.axis_size("seq")
    groups = lax.axis_size("dp")
    q = lax.axis_index("seq")
    rows = hidden_in.shape[1]
    length = rows * parts
    cw = INNER // parts
    hq = H // parts
    cc = cw + 2 * N
    in_rows = w_in.shape[0]
    out_rows = w_out.shape[0]

    chan_len = chan_params.shape[0]
    chan_rows = -(-chan_len // (8 * LANES)) * 8
    chan_block = jnp.pad(
        lax.reduce_precision(chan_params, 8, 7), (0, chan_rows * LANES - chan_len)
    ).reshape(chan_rows, LANES)
    hidden, wx, wz, chan_full = collect(0, hidden_in[0], w_in, chan_block, groups, parts)
    out_low, chan_full = lax.optimization_barrier((w_out.astype(BF16), chan_full))
    wo = lax.all_gather(out_low, ("dp", "seq"), axis=0, tiled=True)
    hidden = hidden.reshape(length, D)
    wx = wx.reshape(D, cc + LANES)
    chan_full = chan_full.reshape(groups * parts, chan_rows * LANES)[:, :chan_len].reshape(-1)
    line = groups // 2
    group = lax.axis_index("dp")
    core, place = group % 2, group // 2
    wz_line = jnp.zeros((line,) + wz.shape, BF16)
    wz_line = lax.dynamic_update_index_in_dim(wz_line, wz, place, 0)
    for k in range(1, line):
        block = lax.ppermute(wz, "dp", [(i, i ^ (2 * k)) for i in range(groups)])
        wz_line = lax.dynamic_update_index_in_dim(wz_line, block, place ^ k, 0)
    other = lax.ppermute(wz_line, "dp", [(i, i ^ 1) for i in range(groups)])
    wz = jnp.where(core == 0, jnp.stack([wz_line, other], 1), jnp.stack([other, wz_line], 1))
    wz = wz.reshape(D, cw)

    conv_taps = chan_full[: TAPS * CONV_CH].reshape(TAPS, CONV_CH)
    conv_bias = chan_full[TAPS * CONV_CH : (TAPS + 1) * CONV_CH].reshape(1, CONV_CH)
    offset = (TAPS + 1) * CONV_CH
    gain_in = chan_full[offset : offset + D]
    gain_out = chan_full[offset + D : offset + D + INNER]
    taps_all = jnp.concatenate(
        [conv_taps, conv_bias, jnp.zeros((8 - TAPS - 1, CONV_CH), F32)], axis=0
    )
    taps = jnp.concatenate(
        [lax.dynamic_slice(taps_all, (0, q * cw), (8, cw)), taps_all[:, INNER:]], axis=1
    )
    own_gain = lax.dynamic_slice(gain_out, (q * cw,), (cw,))
    own_heads = lax.dynamic_slice(head_params, (0, q * hq), (3, hq))
    heads = jnp.pad(
        jnp.stack([own_heads[0], -jnp.exp(own_heads[1])]), ((0, 6), (0, LANES - hq))
    )
    skip = jnp.repeat(own_heads[2], P_SIZE).reshape(1, cw)
    spread = (
        jnp.arange(LANES)[:, None] == (jnp.arange(cw) // P_SIZE)[None, :]
    ).astype(BF16)

    tokens = hidden.astype(F32)
    scale = lax.rsqrt(jnp.mean(tokens * tokens, axis=-1, keepdims=True) + EPS_IN)
    normed = (tokens * scale * gain_in).astype(BF16)
    px = dot(normed, wx)
    y, states = scan_forward(px, taps, heads, skip, spread)
    z = dot(normed, wz)
    sig = jax.nn.sigmoid(z)
    gate = z * sig
    gated = y * gate
    channel = q * cw + jnp.arange(cw)
    squares = jnp.stack(
        [
            jnp.sum(jnp.where((channel >= low) & (channel < high), gated * gated, 0.0), axis=-1)
            for low, high in SEGMENTS
        ],
        axis=-1,
    )
    u_blocks = jnp.concatenate([(gated * own_gain).astype(BF16), pack_terms(squares)], axis=-1)
    u = swap(2, u_blocks.reshape(parts, rows, cw + LANES))[0]

    own_tokens = hidden_in[0].astype(F32)
    cotangent = out_grads[:, 0]
    block_out, back_blocks, mixed = widths(u, wo, cotangent, hidden_in[0])
    block_out = block_out[:, None]
    back_own, dwo_left, dwo_right = swap_back(3, back_blocks, u, mixed, groups)
    back_own = back_own.reshape(length, cw + LANES)

    coefs = unpack_terms(back_own[:, cw:], LEVELS)
    pull = coefs[:, LEVELS - 1 :]
    for k in reversed(range(LEVELS - 1)):
        pull = jnp.where(channel[None, :] < level_width(k), coefs[:, k : k + 1], pull)
    back = back_own[:, :cw].astype(F32)
    dgated = own_gain * back - gated * pull
    dgain_out = jnp.sum(back * gated, axis=0)
    dz = (dgated * y * (sig + gate * (1.0 - sig))).astype(BF16)
    dy = dgated * gate
    dwz = dot(normed, dz, TN).astype(BF16)
    dwz = dwz.reshape(line, 2, parts * in_rows, cw)
    dpx, dtaps, dheads, dskip, dwo_left, dwz = scan_backward(
        5, px, taps, heads, skip, spread, spread.T, dy, y, states, dwo_left, dwz
    )
    skip_grad = jnp.sum(dskip[0].reshape(hq, P_SIZE), axis=-1)
    small = jnp.concatenate(
        [dtaps[: TAPS + 1].reshape(-1), dgain_out, dheads[0, :hq], dheads[1, :hq], skip_grad]
    )
    small_rows = -(-small.shape[0] // (8 * LANES)) * 8
    small = jnp.pad(small, (0, small_rows * LANES - small.shape[0])).reshape(small_rows, LANES)
    x_part, left_part, right_part, z_part, dnormed, small = sum_to_owners(
        4, normed, dwo_left, dwo_right, dwz.reshape(parts, in_rows, cw), small, dz, dpx, wz, wx
    )
    out_part = jnp.concatenate([left_part, right_part], axis=1)
    dnormed = jnp.sum(dnormed.astype(F32), axis=0)
    small = jnp.sum(small, axis=0)
    own_scale = lax.rsqrt(jnp.mean(own_tokens * own_tokens, axis=-1, keepdims=True) + EPS_IN)
    dgain_in = jnp.sum(dnormed * own_tokens * own_scale, axis=0)
    scaled = dnormed * gain_in
    hidden_grad = (
        own_scale * scaled
        - own_tokens
        * (own_scale**3 * (jnp.sum(scaled * own_tokens, axis=-1, keepdims=True) / D))
        + jnp.sum(cotangent.astype(F32), axis=0)
    )[None]

    z_part = z_part.astype(F32)
    x_part = x_part.astype(F32)
    in_part = jnp.concatenate(
        [
            z_part.transpose(1, 0, 2).reshape(in_rows, INNER),
            x_part[:, :, :cw].transpose(1, 0, 2).reshape(in_rows, INNER),
            jnp.sum(x_part[:, :, cw : cc + H], axis=0),
        ],
        axis=1,
    )
    local_squares = jnp.sum(in_part * in_part) + jnp.sum(out_part * out_part)
    block = jnp.concatenate(
        [dgain_in.reshape(D // LANES, LANES), jnp.full((8, LANES), local_squares)], axis=0
    )
    block, small = broadcast(6, block, small, groups, parts)
    small = small.reshape(parts, small_rows * LANES)
    taps_size = (TAPS + 1) * cc
    taps_grad = small[:, :taps_size].reshape(parts, TAPS + 1, cc)
    taps_grad = jnp.concatenate(
        [
            taps_grad[:, :, :cw].transpose(1, 0, 2).reshape(TAPS + 1, INNER),
            jnp.sum(taps_grad[:, :, cw:], axis=0),
        ],
        axis=1,
    )
    head_total = small[:, taps_size + cw : taps_size + cw + 3 * hq]
    head_total = head_total.reshape(parts, 3, hq).transpose(1, 0, 2).reshape(3, H)
    chan_total = jnp.concatenate(
        [
            taps_grad.reshape(-1),
            block[: D // LANES].reshape(-1),
            small[:, taps_size : taps_size + cw].reshape(-1),
        ]
    )
    owner = lax.axis_index("dp") * parts + q
    chan_part = lax.dynamic_slice(chan_total, (owner * chan_len,), (chan_len,))
    grad_norm = jnp.sqrt(
        block[D // LANES, 0]
        + jnp.sum(chan_total * chan_total)
        + jnp.sum(head_total * head_total)
    )
    clip_factor = jnp.minimum(1.0, CLIP / grad_norm)
    w_in_new, w_in_m_new, w_in_v_new = adam_step(
        w_in, clip_factor * in_part, w_in_m, w_in_v, 0.02, 0.1
    )
    w_out_new, w_out_m_new, w_out_v_new = adam_step(
        w_out, clip_factor * out_part, w_out_m, w_out_v, 0.03, 0.1
    )
    chan_new, chan_m_new, chan_v_new = adam_step(
        chan_params, clip_factor * chan_part, chan_m, chan_v, 0.2, 0.0
    )
    head_new, head_m_new, head_v_new = adam_step(
        head_params, clip_factor * head_total, head_m, head_v, 1.0, 0.0
    )
    return (
        block_out, hidden_grad, grad_norm,
        w_in_new, w_in_m_new, w_in_v_new, w_in_new.astype(BF16),
        w_out_new, w_out_m_new, w_out_v_new, w_out_new.astype(BF16),
        chan_new, chan_m_new, chan_v_new, head_new, head_m_new, head_v_new,
    )


def solution(mesh):
    rows = P(("dp", "seq"), None)
    flat = P(("dp", "seq"))
    in_specs = (
        P("dp", "seq", None),
        P(None, "dp", "seq", None),
        *([rows] * 6),
        *([flat] * 3),
        *([P()] * 3),
    )
    out_specs = (
        P(None, "dp", "seq", None),
        P("dp", "seq", None),
        P(),
        *([rows] * 8),
        *([flat] * 3),
        *([P()] * 3),
    )
    return jax.shard_map(
        on_device, mesh=mesh, in_specs=in_specs, out_specs=out_specs, check_vma=False
    )
```

```python
import functools

import jax
import jax.numpy as jnp
from jax import lax
from jax.experimental import pallas as pl
from jax.experimental.pallas import tpu as pltpu
from jax.sharding import PartitionSpec as P

D = 2048
INNER = 4096
H = 64
P_SIZE = 64
N = 128
TAPS = 4
STEP = 10
E_IN = 8512
CONV_CH = 4352
LANES = 128
CHUNK = 128
LEVELS = 4

EXACT = lax.Precision.HIGHEST
EPS_IN = 1e-06
EPS_OUT = 1e-05
ADAM_EPS = 1e-08
BETA = 0.5
CLIP = 1.0
F32 = jnp.float32
BF16 = jnp.bfloat16
MASKED = -1e30


def level_width(level):
    return INNER * 2**level // 8


SEGMENTS = tuple(
    (0 if level == 0 else level_width(level - 1), level_width(level)) for level in range(LEVELS)
)


def dot(a, b, dims=((1,), (0,)), precision=None):
    return lax.dot_general(a, b, (dims, ((), ())), precision=precision, preferred_element_type=F32)


NT = ((1,), (1,))
TN = ((0,), (0,))


def softplus(v):
    return jnp.maximum(v, 0.0) + jnp.log1p(jnp.exp(-jnp.abs(v)))


def two_terms(v):
    high = v.astype(BF16)
    return high, (v - high.astype(F32)).astype(BF16)


def spread_heads(v, spread):
    high, rest = two_terms(v)
    return dot(high, spread) + dot(rest, spread)


def own_heads_first(dt_raw, hq, back=False):
    by = lax.axis_index("seq") * hq
    return pltpu.roll(dt_raw, by if back else lax.rem(LANES - by, LANES), 1)


def rates(dt_raw, heads):
    step = softplus(dt_raw + heads[0:1, :])
    return step, step * heads[1:2, :]


def triangle(size):
    row = lax.broadcasted_iota(jnp.int32, (size, size), 0)
    col = lax.broadcasted_iota(jnp.int32, (size, size), 1)
    return row, col


def conv_block(taps, xbuf, lanes):
    out = taps[TAPS : TAPS + 1, lanes]
    for tap in range(TAPS):
        out = out + taps[tap : tap + 1, lanes] * xbuf[5 + tap : 5 + tap + CHUNK, lanes]
    return out


def pair_decay(cum, cum_t, causal, head):
    gap = cum[:, head : head + 1] - cum_t[head : head + 1, :]
    return jnp.exp(jnp.where(causal, gap, MASKED))


def scan_forward_kernel(cw, px, taps, heads, skip, spread, y, states, xbuf, state, xdt, carried):
    cc = cw + 2 * N

    @pl.when(pl.program_id(0) == 0)
    def _():
        state[...] = jnp.zeros_like(state)
        xbuf[0:8, :] = jnp.zeros((8, cc), F32)

    xbuf[8 : 8 + CHUNK, :] = px[:, :cc]
    step, rate = rates(own_heads_first(px[:, cc:], cw // P_SIZE), heads)
    row, col = triangle(CHUNK)
    causal = row >= col
    cum = dot(causal.astype(F32), rate, precision=EXACT)
    cum_t = cum.T
    spread_m = spread[...]
    last = cum[CHUNK - 1 : CHUNK, :]
    step_x = spread_heads(step, spread_m)
    grow_x = spread_heads(jnp.exp(cum), spread_m)
    tail_x = spread_heads(jnp.exp(last - cum), spread_m)

    def activated(lanes):
        conv = conv_block(taps, xbuf, lanes)
        return conv * jax.nn.sigmoid(conv)

    state_in = activated(slice(cw, cw + N))
    state_out = activated(slice(cw + N, cw + 2 * N))
    scores = dot(state_out, state_in, NT, EXACT)
    states[0] = state[...].astype(BF16)
    carried[...] = dot(state_out.astype(BF16), state[...].astype(BF16))
    first = lax.broadcasted_iota(jnp.int32, (1, LANES), 1) < P_SIZE
    for pair in range(cw // LANES):
        lanes = slice(pair * LANES, (pair + 1) * LANES)
        x = activated(lanes)
        xd = (x * step_x[:, lanes]).astype(BF16).astype(F32)
        xdt[:, lanes] = (xd * tail_x[:, lanes]).astype(BF16)
        stacked = jnp.concatenate([jnp.where(first, xd, 0.0), jnp.where(first, 0.0, xd)], axis=0)
        mixing = jnp.concatenate(
            [
                (pair_decay(cum, cum_t, causal, 2 * pair + k) * scores).astype(BF16)
                for k in range(2)
            ],
            axis=1,
        )
        y[:, lanes] = (
            dot(mixing, stacked.astype(BF16))
            + grow_x[:, lanes] * carried[:, lanes]
            + skip[:, lanes] * x
        )
    state[...] = grow_x[CHUNK - 1 : CHUNK, :] * state[...] + dot(
        state_in.astype(BF16), xdt[...], TN
    )
    xbuf[0:8, :] = xbuf[CHUNK : CHUNK + 8, :]


def scan_backward_kernel(
    groups, parts, cw, chunks,
    px, halo, taps, heads, skip, spread, gather, dy, y, states, wide, gate,
    dpx, dtaps, dheads, dskip, wide_sum, gate_sum,
    xbuf, dstate, dcbuf, slope, xact, xd_s, dxd_s, acc_s,
    first, second, wide_s, wide_r, gate_held, gate_acc, gate_up, gate_down,
    core_s, core_r, up_s, up_r, down_s, down_r,
):
    line = groups // 2
    group, q = lax.axis_index("dp"), lax.axis_index("seq")
    z, core = group // 2, lax.rem(group, 2)
    sibling = (2 * z + 1 - core, q)
    last = chunks - 1
    plane = PlaneSum(parts, group, q, wide, first, second, wide_s, wide_r)
    rows = gate.shape[2] // 4
    gates = LineSum(
        line, z, core, q, gate_acc, gate_up, gate_down, up_s, up_r, down_s, down_r, rows, 4
    )

    def core_copy(d):
        return remote(gate.at[d, 1 - core], gate_held.at[d], core_s, core_r, d, sibling)

    @pl.when(pl.program_id(0) == 0)
    def _():
        greet(seq_peers(parts) + dp_peers(groups))
        for d in range(line):
            core_copy(d).start()
        plane.start(0)
        plane.start(1)

    @pl.when(pl.program_id(0) == 1)
    def _():
        for d in range(line):
            core_copy(d).wait()
            add_blocks(gate_acc.at[d], gate.at[d, core], gate_held.at[d], rows, 4)
        gates.step(0)

    for t in range(1, line - 1):

        @pl.when(pl.program_id(0) == min(1 + 3 * t, last))
        def _(t=t):
            gates.sent(t - 1)
            gates.step(t)

    @pl.when(pl.program_id(0) == min(6, last))
    def _():
        plane.turn(32)

    scan_backward_step(
        cw, px, halo, taps, heads, skip, spread, gather, dy, y, states,
        dpx, dtaps, dheads, dskip, xbuf, dstate, dcbuf, slope, xact, xd_s, dxd_s, acc_s,
    )

    @pl.when(pl.program_id(0) == last)
    def _():
        plane.finish(wide_sum, 32)
        gates.finish(gate_sum)
        gates.sent(line - 2)


def scan_backward_step(
    cw, px, halo, taps, heads, skip, spread, gather, dy, y, states,
    dpx, dtaps, dheads, dskip,
    xbuf, dstate, dcbuf, slope, xact, xd_s, dxd_s, acc_s,
):
    cc = cw + 2 * N
    at = pl.program_id(0)

    @pl.when(at == 0)
    def _():
        dstate[...] = jnp.zeros_like(dstate)
        dcbuf[CHUNK : CHUNK + 8, :] = jnp.zeros((8, cc), F32)
        dtaps[...] = jnp.zeros_like(dtaps)
        dheads[...] = jnp.zeros_like(dheads)
        dskip[...] = jnp.zeros_like(dskip)

    xbuf[0:8, :] = jnp.where(at == pl.num_programs(0) - 1, 0.0, halo[:, :cc])
    xbuf[8 : 8 + CHUNK, :] = px[:, :cc]
    dt_raw = own_heads_first(px[:, cc:], cw // P_SIZE)
    step, rate = rates(dt_raw, heads)
    row, col = triangle(CHUNK)
    causal = row >= col
    cum = dot(causal.astype(F32), rate, precision=EXACT)
    cum_t = cum.T
    spread_m = spread[...]
    last = cum[CHUNK - 1 : CHUNK, :]
    step_x = spread_heads(step, spread_m)
    grow_x = spread_heads(jnp.exp(cum), spread_m)
    tail_x = spread_heads(jnp.exp(last - cum), spread_m)

    for block in range(cc // LANES):
        lanes = slice(block * LANES, (block + 1) * LANES)
        conv = conv_block(taps, xbuf, lanes)
        sig = jax.nn.sigmoid(conv)
        act = conv * sig
        xact[:, lanes] = act
        slope[:, lanes] = sig + act * (1.0 - sig)
    state_in = xact[:, cw : cw + N]
    state_out = xact[:, cw + N : cc]
    scores = dot(state_out, state_in, NT, EXACT)
    in_low = state_in.astype(BF16)
    out_low = state_out.astype(BF16)
    dstate_low = dstate[...].astype(BF16)
    acc_s[...] = jnp.zeros_like(acc_s)
    dxd_s[...] = tail_x * dot(in_low, dstate_low)
    dskip[0:1, :] += jnp.sum(xact[:, :cw] * dy[...], axis=0, keepdims=True)
    first = lax.broadcasted_iota(jnp.int32, (1, LANES), 1) < P_SIZE
    xd_s[...] = (xact[:, :cw] * step_x).astype(BF16)
    total = jnp.sum(xd_s[...].astype(F32) * dxd_s[...], axis=0, keepdims=True) + grow_x[
        CHUNK - 1 : CHUNK, :
    ] * jnp.sum(dstate[...] * states[0].astype(F32), axis=0, keepdims=True)
    dscores = jnp.zeros((CHUNK, CHUNK), F32)
    for pair in range(cw // LANES):
        lanes = slice(pair * LANES, (pair + 1) * LANES)
        dyp = dy[:, lanes]
        stacked = jnp.concatenate(
            [jnp.where(first, dyp, 0.0), jnp.where(first, 0.0, dyp)], axis=0
        ).astype(BF16)
        decays = [pair_decay(cum, cum_t, causal, 2 * pair + k) for k in range(2)]
        mixing = jnp.concatenate([(decay * scores).astype(BF16) for decay in decays], axis=0)
        dxd_s[:, lanes] += dot(mixing, stacked, TN)
        dmix = dot(stacked, xd_s[:, lanes], NT)
        dscores = dscores + decays[0] * dmix[:CHUNK] + decays[1] * dmix[CHUNK:]
    dy_low = dy[...].astype(BF16)
    dy_f = dy_low.astype(F32)
    xd_f = xd_s[...].astype(F32)
    dxd = dxd_s[...]
    y_scan = y[...] - skip[...] * xact[:, :cw]
    final = lax.broadcasted_iota(jnp.int32, (CHUNK, 1), 0) == CHUNK - 1
    gather_m = gather[...]
    dcum = spread_heads(dy_f * y_scan - xd_f * dxd + jnp.where(final, total, 0.0), gather_m)
    dstep = spread_heads(xact[:, :cw] * dxd, gather_m)
    drate = dot((row <= col).astype(F32), dcum, precision=EXACT)
    dstep = dstep + drate * heads[1:2, :]
    ddt = dstep * jax.nn.sigmoid(dt_raw + heads[0:1, :])
    dheads[0:1, :] += jnp.sum(ddt, axis=0, keepdims=True)
    dheads[1:2, :] += jnp.sum(drate * rate, axis=0, keepdims=True)
    grown = (grow_x * dy_f).astype(BF16)
    dscores_low = dscores.astype(BF16)
    dout = dot(dscores_low, in_low) + dot(grown, states[0], NT)
    din = dot(dscores_low, out_low, TN) + dot((tail_x * xd_f).astype(BF16), dstate_low, NT)
    dstate[...] = grow_x[CHUNK - 1 : CHUNK, :] * dstate[...] + dot(out_low, grown, TN)
    dcbuf[:CHUNK, :cw] = (step_x * dxd + skip[...] * dy[...]) * slope[:, :cw]
    dcbuf[:CHUNK, cw : cw + N] = din * slope[:, cw : cw + N]
    dcbuf[:CHUNK, cw + N :] = dout * slope[:, cw + N :]
    for block in range(cc // LANES):
        lanes = slice(block * LANES, (block + 1) * LANES)
        dconv = dcbuf[:CHUNK, lanes]
        dtaps[TAPS : TAPS + 1, lanes] += jnp.sum(dconv, axis=0, keepdims=True)
        back = taps[TAPS - 1 : TAPS, lanes] * dconv
        for tap in range(TAPS):
            dtaps[tap : tap + 1, lanes] += jnp.sum(
                dconv * xbuf[5 + tap : 5 + tap + CHUNK, lanes], axis=0, keepdims=True
            )
            if tap < TAPS - 1:
                reach = TAPS - 1 - tap
                back = back + taps[tap : tap + 1, lanes] * dcbuf[reach : reach + CHUNK, lanes]
        dpx[:, lanes] = back.astype(BF16)
    ours = lax.broadcasted_iota(jnp.int32, (1, LANES), 1) < cw // P_SIZE
    ddt = own_heads_first(jnp.where(ours, ddt, 0.0), cw // P_SIZE, back=True)
    dpx[:, cc:] = ddt.astype(BF16)
    dcbuf[CHUNK : CHUNK + 8, :] = dcbuf[0:8, :]


def whole(shape):
    return pl.BlockSpec(shape, lambda i: (0,) * len(shape))


def scan_forward(px, taps, heads, skip, spread):
    length, width = px.shape
    cw = skip.shape[1]
    cc = cw + 2 * N
    chunks = length // CHUNK
    return pl.pallas_call(
        functools.partial(scan_forward_kernel, cw),
        grid=(chunks,),
        in_specs=[
            pl.BlockSpec((CHUNK, width), lambda i: (i, 0)),
            whole(taps.shape),
            whole(heads.shape),
            whole(skip.shape),
            whole(spread.shape),
        ],
        out_specs=[
            pl.BlockSpec((CHUNK, cw), lambda i: (i, 0)),
            pl.BlockSpec((1, N, cw), lambda i: (i, 0, 0)),
        ],
        out_shape=[
            jax.ShapeDtypeStruct((length, cw), F32),
            jax.ShapeDtypeStruct((chunks, N, cw), BF16),
        ],
        scratch_shapes=[
            pltpu.VMEM((CHUNK + 8, cc), F32),
            pltpu.VMEM((N, cw), F32),
            pltpu.VMEM((CHUNK, cw), BF16),
            pltpu.VMEM((CHUNK, cw), F32),
        ],
        compiler_params=pltpu.CompilerParams(vmem_limit_bytes=48 * 2**20),
        cost_estimate=pl.CostEstimate(
            flops=3 * 10**9, bytes_accessed=40 * 10**6, transcendentals=10**7
        ),
        name="scan_forward",
    )(px, taps, heads, skip, spread)


def scan_backward(collective_id, px, taps, heads, skip, spread, gather, dy, y, states, wide, gate):
    length, width = px.shape
    cw = skip.shape[1]
    cc = cw + 2 * N
    chunks = length // CHUNK
    eighths = CHUNK // 8
    parts, line, out_rows, half = wide.shape
    span = gate.shape[2]
    sem = pltpu.SemaphoreType.DMA
    vmem = pl.BlockSpec(memory_space=pltpu.VMEM)
    return pl.pallas_call(
        functools.partial(scan_backward_kernel, 2 * line, parts, cw, chunks),
        grid=(chunks,),
        in_specs=[
            pl.BlockSpec((CHUNK, width), lambda i: (chunks - 1 - i, 0)),
            pl.BlockSpec(
                (8, width), lambda i: (jnp.maximum((chunks - 1 - i) * eighths - 1, 0), 0)
            ),
            whole(taps.shape),
            whole(heads.shape),
            whole(skip.shape),
            whole(spread.shape),
            whole(gather.shape),
            pl.BlockSpec((CHUNK, cw), lambda i: (chunks - 1 - i, 0)),
            pl.BlockSpec((CHUNK, cw), lambda i: (chunks - 1 - i, 0)),
            pl.BlockSpec((1, N, cw), lambda i: (chunks - 1 - i, 0, 0)),
            vmem,
            vmem,
        ],
        out_specs=[
            pl.BlockSpec((CHUNK, width), lambda i: (chunks - 1 - i, 0)),
            whole((8, cc)),
            whole((8, LANES)),
            whole((8, cw)),
            vmem,
            vmem,
        ],
        out_shape=[
            jax.ShapeDtypeStruct((length, width), BF16),
            jax.ShapeDtypeStruct((8, cc), F32),
            jax.ShapeDtypeStruct((8, LANES), F32),
            jax.ShapeDtypeStruct((8, cw), F32),
            jax.ShapeDtypeStruct(wide.shape[1:], BF16),
            jax.ShapeDtypeStruct((span, cw), BF16),
        ],
        scratch_shapes=[
            pltpu.VMEM((CHUNK + 8, cc), F32),
            pltpu.VMEM((N, cw), F32),
            pltpu.VMEM((CHUNK + 8, cc), F32),
            pltpu.VMEM((CHUNK, cc), F32),
            pltpu.VMEM((CHUNK, cc), F32),
            pltpu.VMEM((CHUNK, cw), BF16),
            pltpu.VMEM((CHUNK, cw), F32),
            pltpu.VMEM((CHUNK, CHUNK), F32),
            *PlaneSum.scratch(parts, wide.shape[1:], BF16),
            *([pltpu.VMEM((line, span, cw), BF16)] * 4),
            *([sem((line,))] * 6),
        ],
        compiler_params=pltpu.CompilerParams(
            collective_id=collective_id, has_side_effects=True, vmem_limit_bytes=63 * 2**20
        ),
        cost_estimate=pl.CostEstimate(
            flops=10**10, bytes_accessed=100 * 10**6, transcendentals=10**7
        ),
        name="scan_backward",
    )(px, px, taps, heads, skip, spread, gather, dy, y, states, wide, gate)


WIDE = 512


def widths_kernel(cw, u, wo, cotangent, tokens, block_out, back, mixed, branch, norms, pulls):
    at = pl.program_id(0)
    ends = [level_width(k) // WIDE - 1 for k in range(LEVELS)]

    @pl.when(at == 0)
    def _():
        terms = u[0, :, cw:].astype(F32)
        for part in range(1, u.shape[0]):
            terms = terms + u[part, :, cw:].astype(F32)
        squares = jnp.zeros((terms.shape[0], 1), F32)
        for k in range(LEVELS):
            squares = squares + terms[:, k : k + 1] + terms[:, LEVELS + k : LEVELS + k + 1]
            norms[:, k : k + 1] = lax.rsqrt(squares / level_width(k) + EPS_OUT)
        running = jnp.zeros(branch.shape, F32)
        for k in reversed(range(LEVELS)):
            running = running + norms[:, k : k + 1] * cotangent[k].astype(F32)
            mixed[k] = running.astype(BF16)
        branch[...] = jnp.zeros_like(branch)

    part = at * WIDE // cw
    lanes = pl.ds(pl.multiple_of(lax.rem(at * WIDE, cw), WIDE), WIDE)
    level = sum((at > end).astype(jnp.int32) for end in ends[:-1])
    branch[...] += dot(u[part, :, lanes], wo[...])
    back[part, :, lanes] = dot(mixed[level], wo[...], NT).astype(BF16)
    for k in range(LEVELS):

        @pl.when(at == ends[k])
        def _():
            norm = norms[:, k : k + 1]
            block_out[k] = (tokens[...].astype(F32) + norm * branch[...]).astype(BF16)
            inner = jnp.sum(cotangent[k].astype(F32) * branch[...], axis=-1, keepdims=True)
            pulls[:, k : k + 1] = norm * norm * norm * (inner / level_width(k))

    @pl.when(at == ends[-1])
    def _():
        coef = jnp.zeros((branch.shape[0], 1), F32)
        lane = lax.broadcasted_iota(jnp.int32, (1, LANES), 1)
        packed = jnp.zeros((branch.shape[0], LANES), F32)
        for k in reversed(range(LEVELS)):
            coef = coef + pulls[:, k : k + 1]
            high, rest = two_terms(coef)
            packed = jnp.where(lane == k, high.astype(F32), packed)
            packed = jnp.where(lane == LEVELS + k, rest.astype(F32), packed)
        for p in range(back.shape[0]):
            back[p, :, cw:] = packed.astype(BF16)


def widths(u, wo, cotangent, tokens):
    parts, rows, wide = u.shape
    cw = wide - LANES

    def full(shape):
        return pl.BlockSpec(shape, lambda i: (0,) * len(shape), pipeline_mode=pl.Buffered(1))

    return pl.pallas_call(
        functools.partial(widths_kernel, cw),
        grid=(INNER // WIDE,),
        in_specs=[
            full(u.shape),
            pl.BlockSpec((WIDE, D), lambda i: (i, 0)),
            full(cotangent.shape),
            full(tokens.shape),
        ],
        out_specs=[full(cotangent.shape), full(u.shape), full(cotangent.shape)],
        out_shape=[
            jax.ShapeDtypeStruct(cotangent.shape, BF16),
            jax.ShapeDtypeStruct(u.shape, BF16),
            jax.ShapeDtypeStruct(cotangent.shape, BF16),
        ],
        scratch_shapes=[
            pltpu.VMEM((rows, D), F32),
            pltpu.VMEM((rows, LANES), F32),
            pltpu.VMEM((rows, LANES), F32),
        ],
        compiler_params=pltpu.CompilerParams(vmem_limit_bytes=63 * 2**20),
        name="widths",
    )(u, wo, cotangent, tokens)


MESH = pl.DeviceIdType.MESH


def remote(src, dst, sends, recvs, index, device):
    return pltpu.make_async_remote_copy(
        src_ref=src,
        dst_ref=dst,
        send_sem=sends.at[index],
        recv_sem=recvs.at[index],
        device_id=device,
        device_id_type=MESH,
    )


def greet(devices):
    barrier = pltpu.get_barrier_semaphore()
    for device in devices:
        pl.semaphore_signal(barrier, inc=1, device_id=device, device_id_type=MESH)
    pl.semaphore_wait(barrier, len(devices))


def seq_peers(parts):
    group, q = lax.axis_index("dp"), lax.axis_index("seq")
    return [(group, lax.rem(q + k, parts)) for k in range(1, parts)]


def dp_peers(groups):
    group, q = lax.axis_index("dp"), lax.axis_index("seq")
    return [(lax.rem(group + k, groups), q) for k in range(1, groups)]


def swap_kernel(parts, count, *refs):
    sources, results = refs[:count], refs[count : 2 * count]
    sends, recvs, local = refs[2 * count :]
    q = lax.axis_index("seq")
    peers = seq_peers(parts)
    greet(peers)
    copies = []
    for k, peer in enumerate(peers):
        for a in range(count):
            copy = remote(
                sources[a].at[peer[1]], results[a].at[q], sends, recvs, k * count + a, peer
            )
            copy.start()
            copies.append(copy)
    own = [
        pltpu.make_async_copy(sources[a].at[q], results[a].at[q], local.at[a])
        for a in range(count)
    ]
    for copy in own:
        copy.start()
    for copy in own + copies:
        copy.wait()


def swap(collective_id, *arrays):
    parts = arrays[0].shape[0]
    count = len(arrays)
    return pl.pallas_call(
        functools.partial(swap_kernel, parts, count),
        in_specs=[pl.BlockSpec(memory_space=pltpu.HBM)] * count,
        out_specs=[pl.BlockSpec(memory_space=pltpu.HBM)] * count,
        out_shape=[jax.ShapeDtypeStruct(a.shape, a.dtype) for a in arrays],
        scratch_shapes=[
            pltpu.SemaphoreType.DMA(((parts - 1) * count,)),
            pltpu.SemaphoreType.DMA(((parts - 1) * count,)),
            pltpu.SemaphoreType.DMA((count,)),
        ],
        compiler_params=pltpu.CompilerParams(collective_id=collective_id, has_side_effects=True),
        name="swap",
    )(*arrays)


def all_peers(groups, parts):
    devices = groups * parts
    me = lax.axis_index("dp") * parts + lax.axis_index("seq")
    peers = []
    for k in range(1, devices):
        other = lax.rem(me + k, devices)
        peers.append((other // parts, lax.rem(other, parts)))
    return peers


CHAN_ROWS = ((TAPS + 1) * CONV_CH + D + INNER) // LANES


def adam_tile(weight, gradient, moment, second, step_rate, weight_decay):
    new_moment = BETA * moment + (1.0 - BETA) * gradient
    new_second = BETA * second + (1.0 - BETA) * gradient * gradient
    correction = 1.0 - BETA**STEP
    update = new_moment / correction / (jnp.sqrt(new_second / correction) + ADAM_EPS)
    return weight - step_rate * (update + weight_decay * weight), new_moment, new_second


def total_of(value):
    return jnp.sum(jnp.sum(value, axis=1, keepdims=True), axis=0, keepdims=True)


def norm_kernel(
    groups, parts,
    part_h, gate_h, left_h, right_h, back_h, small_h, hidden_h, gain, cotangent,
    hidden_grad, chan, head, norm,
    part, gate, left, right, back, small, hidden,
    cot_v, block, near, all_block, all_near, sends, recvs, near_s, near_r, load, local,
):
    group, q = lax.axis_index("dp"), lax.axis_index("seq")
    me = group * parts + q
    cw = INNER // parts
    cc = cw + 2 * N
    everyone = all_peers(groups, parts)
    fetches = [
        pltpu.make_async_copy(source, target, load.at[k])
        for k, (source, target) in enumerate(
            [(back_h, back), (hidden_h, hidden), (part_h, part), (gate_h, gate),
             (left_h, left), (right_h, right), (small_h, small), (cotangent, cot_v)]
        )
    ]
    for copy in fetches:
        copy.start()
    barrier = pltpu.get_barrier_semaphore()
    for device in everyone:
        pl.semaphore_signal(barrier, inc=1, device_id=device, device_id_type=MESH)
    for copy in fetches[:7]:
        copy.wait()
    total = small[0]
    for k in range(1, groups):
        total = total + small[k]
    near[...] = total
    rows = 32

    def summed(at):
        down = back[at, :]
        tokens = hidden[at, :].astype(F32)
        mean = jnp.sum(tokens * tokens, axis=-1, keepdims=True) / D
        return down, tokens, lax.rsqrt(mean + EPS_IN)

    def gain_rows(i, dgain):
        at = pl.ds(pl.multiple_of(i * rows, rows), rows)
        down, tokens, scale = summed(at)
        return dgain + jnp.sum(down * tokens * scale, axis=0, keepdims=True)

    dgain = lax.fori_loop(0, hidden.shape[0] // rows, gain_rows, jnp.zeros((1, D), F32))
    tail = part[0, :, cw : cc + H].astype(F32)
    for k in range(1, parts):
        tail = tail + part[k, :, cw : cc + H].astype(F32)
    squares = total_of(tail * tail)
    for k in range(parts):
        x = part[k, :, :cw].astype(F32)
        g = gate[k].astype(F32)
        squares = squares + total_of(x * x + g * g)
    squares = squares + total_of(left[...] * left[...] + right[...] * right[...])
    for k in range(D // LANES):
        block[k : k + 1, :] = dgain[:, k * LANES : (k + 1) * LANES]
    block[D // LANES :, :] = jnp.broadcast_to(squares, (8, LANES))
    pl.semaphore_wait(barrier, len(everyone))
    copies = [
        remote(block, all_block.at[me], sends, recvs, k, peer) for k, peer in enumerate(everyone)
    ]
    copies += [
        remote(near, all_near.at[q], near_s, near_r, k, peer)
        for k, peer in enumerate(seq_peers(parts))
    ]
    copies += [
        pltpu.make_async_copy(block, all_block.at[me], local.at[0]),
        pltpu.make_async_copy(near, all_near.at[q], local.at[1]),
    ]
    for copy in copies:
        copy.start()
    fetches[7].wait()

    def grad_rows(i, carry):
        at = pl.ds(pl.multiple_of(i * rows, rows), rows)
        down, tokens, scale = summed(at)
        scaled = down * gain[...]
        inner = jnp.sum(scaled * tokens, axis=-1, keepdims=True) / D
        direct = cot_v[0, at, :].astype(F32)
        for k in range(1, LEVELS):
            direct = direct + cot_v[k, at, :].astype(F32)
        hidden_grad[at, :] = (
            scale * scaled - tokens * (scale * scale * scale * inner) + direct
        )
        return carry

    lax.fori_loop(0, hidden.shape[0] // rows, grad_rows, 0)
    for copy in copies:
        copy.wait()
    total = jnp.sum(all_block[...], axis=0)
    own, wide = cw // LANES, cc // LANES
    span = CONV_CH // LANES
    for tap in range(TAPS + 1):
        for k in range(parts):
            at = tap * span + k * own
            chan[at : at + own, :] = all_near[k, tap * wide : tap * wide + own, :]
        shared = all_near[0, tap * wide + own : (tap + 1) * wide, :]
        for k in range(1, parts):
            shared = shared + all_near[k, tap * wide + own : (tap + 1) * wide, :]
        chan[tap * span + INNER // LANES : (tap + 1) * span, :] = shared
    at = (TAPS + 1) * span
    chan[at : at + D // LANES, :] = total[: D // LANES]
    at = at + D // LANES
    for k in range(parts):
        first = (TAPS + 1) * wide
        chan[at + k * own : at + (k + 1) * own, :] = all_near[k, first : first + own, :]
        head[k : k + 1, :] = all_near[k, first + own : first + own + 1, :]
    squares = (
        total[D // LANES : D // LANES + 1, :1]
        + total_of(chan[:CHAN_ROWS, :] * chan[:CHAN_ROWS, :])
        + total_of(head[:parts, :] * head[:parts, :])
    )
    grad_norm = jnp.sqrt(squares)
    norm[0:1, :] = jnp.broadcast_to(grad_norm, (1, LANES))
    norm[1:2, :] = jnp.broadcast_to(jnp.minimum(1.0, CLIP / grad_norm), (1, LANES))


def gradient_norm(
    collective_id, part, gate, left, right, back, small, hidden, gain, cotangent, groups
):
    parts = part.shape[0]
    devices = groups * parts
    sem = pltpu.SemaphoreType.DMA
    vmem = pl.BlockSpec(memory_space=pltpu.VMEM)
    hbm = pl.BlockSpec(memory_space=pltpu.HBM)
    block = (D // LANES + 8, LANES)
    chan_rows = -(-CHAN_ROWS // 8) * 8
    return pl.pallas_call(
        functools.partial(norm_kernel, groups, parts),
        in_specs=[*([hbm] * 7), vmem, hbm],
        out_specs=[vmem] * 4,
        out_shape=[
            jax.ShapeDtypeStruct(hidden.shape, F32),
            jax.ShapeDtypeStruct((chan_rows, LANES), F32),
            jax.ShapeDtypeStruct((8, LANES), F32),
            jax.ShapeDtypeStruct((8, LANES), F32),
        ],
        scratch_shapes=[
            *[pltpu.VMEM(a.shape, a.dtype) for a in (part, gate, left, right, back, small, hidden)],
            pltpu.VMEM(cotangent.shape, BF16),
            pltpu.VMEM(block, F32),
            pltpu.VMEM(small.shape[1:], F32),
            pltpu.VMEM((devices,) + block, F32),
            pltpu.VMEM((parts,) + small.shape[1:], F32),
            sem((devices - 1,)), sem((devices - 1,)), sem((parts - 1,)), sem((parts - 1,)),
            sem((8,)), sem((2,)),
        ],
        compiler_params=pltpu.CompilerParams(
            collective_id=collective_id, has_side_effects=True, vmem_limit_bytes=63 * 2**20
        ),
        name="gradient_norm",
    )(part, gate, left, right, back, small, hidden, gain, cotangent)


BLOCKS = 4


def update_kernel(
    parts, norm, part_h, gate_h, left_h, right_h, hidden_grad, *refs
):
    ins, refs = refs[:6], refs[6:]
    hidden_out, outs, refs = refs[0], refs[1:9], refs[9:]
    held, made = refs[:6], refs[6:14]
    part, gate, left, right, hidden_v, load, store, grads = refs[14:]
    clip = norm[1:2, :1]
    cw = INNER // parts
    cc = cw + 2 * N
    fetches = [
        pltpu.make_async_copy(source, target, grads.at[k])
        for k, (source, target) in enumerate(
            [(part_h, part), (gate_h, gate), (left_h, left), (right_h, right),
             (hidden_grad, hidden_v)]
        )
    ]
    for copy in fetches:
        copy.start()

    def at(a, i):
        rows = ins[a].shape[0] // BLOCKS
        return pl.ds(i * rows, rows)

    loads = [
        [
            pltpu.make_async_copy(ins[a].at[at(a, i)], held[a].at[at(a, i)], load.at[a * BLOCKS + i])
            for a in range(6)
        ]
        for i in range(BLOCKS)
    ]
    for weight in (0, 3):
        for i in range(BLOCKS):
            for a in range(weight, weight + 3):
                loads[i][a].start()
    stores = []

    def update(weight, rows, lanes, gradient, rate, decay):
        first = 0 if weight == 0 else 4
        new, moment, second = adam_tile(
            held[weight][rows, lanes], clip * gradient, held[weight + 1][rows, lanes],
            held[weight + 2][rows, lanes], rate, decay,
        )
        made[first][rows, lanes] = new
        made[first + 1][rows, lanes] = moment
        made[first + 2][rows, lanes] = second
        made[first + 3][rows, lanes] = new.astype(BF16)

    def send(first, rows, i):
        for a in range(first, first + 4):
            copy = pltpu.make_async_copy(
                made[a].at[rows], outs[a].at[rows], store.at[a * BLOCKS + i]
            )
            copy.start()
            stores.append(copy)

    for copy in fetches[:4]:
        copy.wait()
    for i in range(BLOCKS):
        rows = at(0, i)
        for a in range(3):
            loads[i][a].wait()
        for source, first in ((gate, 0), (part, INNER)):

            def step(k, carry, source=source, first=first, rows=rows):
                to = pl.ds(pl.multiple_of(first + k * cw, cw), cw)
                update(0, rows, to, source[k, rows, :cw].astype(F32), 0.02, 0.1)
                return carry

            lax.fori_loop(0, parts, step, 0)
        tail = part[0, rows, cw : cc + H].astype(F32)
        for k in range(1, parts):
            tail = tail + part[k, rows, cw : cc + H].astype(F32)
        update(0, rows, slice(2 * INNER, E_IN), tail, 0.02, 0.1)
        send(0, rows, i)
    fetches[4].wait()
    pass_on = pltpu.make_async_copy(hidden_v, hidden_out, grads.at[5])
    pass_on.start()
    half = D // 2
    for i in range(BLOCKS):
        rows = at(3, i)
        for a in range(3, 6):
            loads[i][a].wait()
        update(3, rows, slice(0, half), left[rows, :], 0.03, 0.1)
        update(3, rows, slice(half, D), right[rows, :], 0.03, 0.1)
        send(4, rows, i)
    pass_on.wait()
    for copy in stores:
        copy.wait()


def update_weights(norm, part, gate, left, right, hidden_grad, weights):
    parts = part.shape[0]
    w_in, w_out = weights[0], weights[3]
    sem = pltpu.SemaphoreType.DMA
    vmem = pl.BlockSpec(memory_space=pltpu.VMEM)
    hbm = pl.BlockSpec(memory_space=pltpu.HBM)
    made = [
        jax.ShapeDtypeStruct(w.shape, dtype) for w in (w_in, w_out) for dtype in (F32, F32, F32, BF16)
    ]
    return pl.pallas_call(
        functools.partial(update_kernel, parts),
        in_specs=[vmem, *([hbm] * 11)],
        out_specs=[hbm] * 9,
        out_shape=[jax.ShapeDtypeStruct(hidden_grad.shape, F32), *made],
        scratch_shapes=[
            *[pltpu.VMEM(w.shape, F32) for w in weights],
            *[pltpu.VMEM(m.shape, m.dtype) for m in made],
            *[pltpu.VMEM(a.shape, a.dtype) for a in (part, gate, left, right, hidden_grad)],
            sem((6 * BLOCKS,)), sem((8 * BLOCKS,)), sem((6,)),
        ],
        compiler_params=pltpu.CompilerParams(vmem_limit_bytes=63 * 2**20),
        name="update_weights",
    )(norm, part, gate, left, right, hidden_grad, *weights)


def collect_kernel(
    groups, parts, hidden, w_in, chan, hid_out, w_out, gate_out, chan_out,
    blocks, gates, chan_s, chan_r, hid_s, hid_r, swap_s, swap_r, gate_s, gate_r,
    line_s, line_r, core_s, core_r, local,
):
    line = groups // 2
    cw = INNER // parts
    cc = cw + 2 * N
    group, q = lax.axis_index("dp"), lax.axis_index("seq")
    z, core = group // 2, lax.rem(group, 2)
    sibling = (2 * z + 1 - core, q)
    peers = seq_peers(parts)
    everyone = all_peers(groups, parts)
    shared = w_in[:, 2 * INNER :].astype(BF16)
    for part in range(parts):
        at = INNER + part * cw
        blocks[part, :, :cw] = w_in[:, at : at + cw].astype(BF16)
        blocks[part, :, cw : cc + H] = shared
        blocks[part, :, cc + H :] = jnp.zeros((w_in.shape[0], LANES - H), BF16)
    greet(everyone)
    swaps = []
    for k, peer in enumerate(peers):
        copy = remote(blocks.at[peer[1]], w_out.at[group, q], swap_s, swap_r, k, peer)
        copy.start()
        swaps.append(copy)
    mine = pltpu.make_async_copy(blocks.at[q], w_out.at[group, q], local.at[0])
    mine.start()
    keep = pltpu.make_async_copy(hidden, hid_out.at[q], local.at[1])
    keep.start()
    chans = []
    for k, peer in enumerate(everyone):
        copy = remote(chan, chan_out.at[group * parts + q], chan_s, chan_r, k, peer)
        copy.start()
        chans.append(copy)
    chan_keep = pltpu.make_async_copy(chan, chan_out.at[group * parts + q], local.at[2])
    chan_keep.start()
    for part in range(parts):
        gates[part] = w_in[:, part * cw : (part + 1) * cw].astype(BF16)
    mine.wait()
    for copy in swaps:
        copy.wait()
    hids = []
    for k, peer in enumerate(peers):
        copy = remote(hidden, hid_out.at[q], hid_s, hid_r, k, peer)
        copy.start()
        hids.append(copy)
    for k, peer in enumerate(peers):
        copy = remote(gates.at[peer[1]], gate_out.at[q], gate_s, gate_r, k, peer)
        copy.start()
        hids.append(copy)
    gate_keep = pltpu.make_async_copy(gates.at[q], gate_out.at[q], local.at[3])
    gate_keep.start()

    def along(from_z, up):
        block = w_out.at[2 * from_z + core]
        to = z + 1 if up else z - 1
        return remote(
            block, block, line_s.at[0 if up else 1], line_r.at[0 if up else 1], from_z,
            (2 * to + core, q),
        )

    def across(from_z):
        block = w_out.at[2 * from_z + core]
        return remote(block, block, core_s, core_r, from_z, sibling)

    for t in range(line):
        low, high = z - t, z + t
        if t == 0:
            across(z).start()

            @pl.when(z < line - 1)
            def _():
                along(z, True).start()

            @pl.when(z > 0)
            def _():
                along(z, False).start()

            continue

        @pl.when(low >= 0)
        def _():
            along(low, True).wait_recv()

            @pl.when(z < line - 1)
            def _():
                along(low, True).start()

            across(low).start()

        @pl.when(high <= line - 1)
        def _():
            along(high, False).wait_recv()

            @pl.when(z > 0)
            def _():
                along(high, False).start()

            across(high).start()

    for from_z in range(line):
        across(from_z).wait_send()
        block = w_out.at[2 * from_z + 1 - core]
        remote(block, block, core_s, core_r, from_z, sibling).wait_recv()

        @pl.when((from_z <= z) & (z < line - 1))
        def _():
            along(from_z, True).wait_send()

        @pl.when((from_z >= z) & (z > 0))
        def _():
            along(from_z, False).wait_send()

    keep.wait()
    chan_keep.wait()
    gate_keep.wait()
    for copy in hids + chans:
        copy.wait()


def collect(collective_id, hidden, w_in, chan, groups, parts):
    rows = w_in.shape[0]
    line = groups // 2
    cw = INNER // parts
    width = cw + 2 * N + LANES
    sem = pltpu.SemaphoreType.DMA
    hbm = pl.BlockSpec(memory_space=pltpu.HBM)
    return pl.pallas_call(
        functools.partial(collect_kernel, groups, parts),
        in_specs=[hbm, pl.BlockSpec(memory_space=pltpu.VMEM), hbm],
        out_specs=[hbm] * 4,
        out_shape=[
            jax.ShapeDtypeStruct((parts,) + hidden.shape, hidden.dtype),
            jax.ShapeDtypeStruct((groups, parts, rows, width), BF16),
            jax.ShapeDtypeStruct((parts, rows, cw), BF16),
            jax.ShapeDtypeStruct((groups * parts,) + chan.shape, chan.dtype),
        ],
        scratch_shapes=[
            pltpu.VMEM((parts, rows, width), BF16),
            pltpu.VMEM((parts, rows, cw), BF16),
            *([sem((groups * parts - 1,))] * 2),
            *([sem((parts - 1,))] * 6),
            sem((2, line)), sem((2, line)), sem((line,)), sem((line,)), sem((4,)),
        ],
        compiler_params=pltpu.CompilerParams(
            collective_id=collective_id, has_side_effects=True, vmem_limit_bytes=48 * 2**20
        ),
        name="collect",
    )(hidden, w_in, chan)


def add_blocks(out, a, b, rows, steps):
    def step(i, carry):
        at = pl.ds(pl.multiple_of(i * rows, rows), rows)
        out[at] = (a[at].astype(F32) + b[at].astype(F32)).astype(out.dtype)
        return carry

    lax.fori_loop(0, steps, step, 0)


def level_of(channel, width):
    return sum((channel >= level_width(k)).astype(jnp.int32) for k in range(LEVELS - 1))


def swap_back_kernel(
    groups, parts, cw, back, u, mixed, back_out, left, right,
    sent, held, sends, recvs, core_s, core_r, local,
):
    line = groups // 2
    group, q = lax.axis_index("dp"), lax.axis_index("seq")
    z, core = group // 2, lax.rem(group, 2)
    sibling = (2 * z + 1 - core, q)
    peers = seq_peers(parts)
    greet(peers + [sibling])
    copies = [
        remote(back.at[peer[1]], back_out.at[q], sends, recvs, k, peer)
        for k, peer in enumerate(peers)
    ]
    copies.append(pltpu.make_async_copy(back.at[q], back_out.at[q], local))
    for copy in copies:
        copy.start()
    width = INNER // groups
    rows = width // parts
    tile = 512
    halves = D // 2 // tile

    def product(of, j):
        channel = of * width
        lanes = pl.ds(pl.multiple_of(lax.rem(channel, cw), width), width)
        cols = pl.ds(pl.multiple_of(j * tile, tile), tile)
        return dot(u[channel // cw, :, lanes], mixed[level_of(channel, width), :, cols], TN)

    cores = []
    for d in range(line):

        def send_step(j, carry, d=d):
            cols = pl.ds(pl.multiple_of(j * tile, tile), tile)
            sent[d, :, cols] = product(2 * d + 1 - core, j).astype(BF16)
            return carry

        lax.fori_loop(0, 2 * halves, send_step, 0)
        copy = remote(sent.at[d], held.at[d], core_s, core_r, d, sibling)
        copy.start()
        cores.append(copy)
    for d in range(line):
        cores[d].wait_recv()
        for out, first in ((left, 0), (right, halves)):

            def keep_step(j, carry, d=d, out=out, first=first):
                at = pl.ds(pl.multiple_of((j + first) * tile, tile), tile)
                cols = pl.ds(pl.multiple_of(j * tile, tile), tile)
                total = product(2 * d + core, j + first) + held[d, :, at].astype(F32)
                total = total.astype(BF16)
                for part in range(parts):
                    out[part, d, :, cols] = total[part * rows : (part + 1) * rows]
                return carry

            lax.fori_loop(0, halves, keep_step, 0)
    for copy in cores:
        copy.wait_send()
    for copy in copies:
        copy.wait()


def swap_back(collective_id, back, u, mixed, groups):
    parts, rows, wide = back.shape
    line, width = groups // 2, INNER // groups
    sem = pltpu.SemaphoreType.DMA
    vmem = pl.BlockSpec(memory_space=pltpu.VMEM)
    hbm = pl.BlockSpec(memory_space=pltpu.HBM)
    return pl.pallas_call(
        functools.partial(swap_back_kernel, groups, parts, wide - LANES),
        in_specs=[hbm, vmem, vmem],
        out_specs=[hbm, vmem, vmem],
        out_shape=[
            jax.ShapeDtypeStruct(back.shape, back.dtype),
            *([jax.ShapeDtypeStruct((parts, line, width // parts, D // 2), BF16)] * 2),
        ],
        scratch_shapes=[
            pltpu.VMEM((line, width, D), BF16),
            pltpu.VMEM((line, width, D), BF16),
            sem((parts - 1,)), sem((parts - 1,)), sem((line,)), sem((line,)), sem,
        ],
        compiler_params=pltpu.CompilerParams(
            collective_id=collective_id, has_side_effects=True, vmem_limit_bytes=63 * 2**20
        ),
        name="swap_back",
    )(back, u, mixed)


def sum_blocks(out, blocks, rows):
    def step(i, carry):
        at = pl.ds(pl.multiple_of(i * rows, rows), rows)
        total = blocks[0][at].astype(F32)
        for block in blocks[1:]:
            total = total + block[at].astype(F32)
        out[at] = total.astype(out.dtype)
        return carry

    lax.fori_loop(0, out.shape[0] // rows, step, 0)


class PlaneSum:
    def __init__(self, parts, group, q, blocks, first, second, sends, recvs):
        self.parts, self.group, self.q = parts, group, q
        self.blocks, self.first, self.second = blocks, first, second
        self.sends, self.recvs = sends, recvs
        self.half = blocks.shape[1] // 2
        if parts == 4:
            self.near = [q + 1 - 2 * lax.rem(q, 2), lax.rem(q + 2, 4)]
            self.far = 3 - q

    @staticmethod
    def scratch(parts, shape, dtype):
        if parts == 4:
            half = (shape[0] // 2,) + shape[1:]
            first, second, count = (2, 2) + half, (2, 2) + half, 6
        else:
            first, second, count = (parts - 1,) + shape, (1, 16, LANES), parts - 1
        sem = pltpu.SemaphoreType.DMA
        return [pltpu.VMEM(first, dtype), pltpu.VMEM(second, dtype), sem((count,)), sem((count,))]

    def piece(self, of, h):
        return self.blocks.at[of, pl.ds(h * self.half, self.half)]

    def early(self, h):
        if self.parts != 4:
            return []
        near = self.near[h]
        to = (self.group, near)
        return [
            remote(self.piece(of, h), self.first.at[h, k], self.sends, self.recvs, 2 * h + k, to)
            for k, of in enumerate((near, self.far))
        ]

    def late(self, h):
        to = (self.group, self.near[1 - h])
        return remote(
            self.second.at[h, 0], self.second.at[h, 1], self.sends, self.recvs, 4 + h, to
        )

    def direct(self):
        peers = seq_peers(self.parts)
        return [
            remote(self.blocks.at[peer[1]], self.first.at[k], self.sends, self.recvs, k, peer)
            for k, peer in enumerate(peers)
        ]

    def start(self, h):
        for copy in self.early(h):
            copy.start()
        if self.parts != 4 and h == 1:
            for copy in self.direct():
                copy.start()

    def turn(self, rows):
        if self.parts != 4:
            return
        for h in range(2):
            for copy in self.early(h):
                copy.wait()
            beyond = self.piece(self.near[1 - h], h)
            each(self.second.at[h, 0], [beyond, self.first.at[h, 1]], rows)
            self.late(h).start()

    def finish(self, out, rows):
        if self.parts != 4:
            for copy in self.direct():
                copy.wait()
            each(
                out,
                [self.blocks.at[self.q]] + [self.first.at[k] for k in range(self.parts - 1)],
                rows,
            )
            return
        for h in range(2):
            self.late(h).wait()
            each(
                out.at[pl.ds(h * self.half, self.half)],
                [self.piece(self.q, h), self.first.at[h, 0], self.second.at[h, 1]],
                rows,
            )


def each(out, blocks, rows):
    if len(out.shape) == 2:
        sum_blocks(out, blocks, rows)
        return
    for d in range(out.shape[0]):
        sum_blocks(out.at[d], [block.at[d] for block in blocks], rows)


class LineSum:
    def __init__(self, line, z, core, q, acc, up, down, up_s, up_r, down_s, down_r, rows, steps):
        self.line, self.z, self.core, self.q = line, z, core, q
        self.acc, self.up, self.down = acc, up, down
        self.up_s, self.up_r, self.down_s, self.down_r = up_s, up_r, down_s, down_r
        self.rows, self.steps = rows, steps

    def ahead(self, d, first):
        block = self.acc.at[d] if first else self.up.at[d]
        to = (2 * (self.z + 1) + self.core, self.q)
        return remote(block, self.up.at[d], self.up_s, self.up_r, d, to)

    def behind(self, d, first):
        block = self.acc.at[d] if first else self.down.at[d]
        to = (2 * (self.z - 1) + self.core, self.q)
        return remote(block, self.down.at[d], self.down_s, self.down_r, d, to)

    def add(self, into, d):
        add_blocks(into.at[d], into.at[d], self.acc.at[d], self.rows, self.steps)

    def step(self, t):
        line, z = self.line, self.z
        far, near = line - 1 - t + z, t - (line - 1 - z)

        @pl.when(z == 0)
        def _():
            self.ahead(line - 1 - t, True).start()

        @pl.when((z > 0) & (z <= t))
        def _():
            self.ahead(far, False).wait_recv()
            self.add(self.up, far)
            self.ahead(far, False).start()

        @pl.when(z == line - 1)
        def _():
            self.behind(t, True).start()

        @pl.when((z < line - 1) & (line - 1 - z <= t))
        def _():
            self.behind(near, False).wait_recv()
            self.add(self.down, near)
            self.behind(near, False).start()

    def sent(self, t):
        line, z = self.line, self.z
        far, near = line - 1 - t + z, t - (line - 1 - z)

        @pl.when(z == 0)
        def _():
            self.ahead(line - 1 - t, True).wait_send()

        @pl.when((z > 0) & (z <= t))
        def _():
            self.ahead(far, False).wait_send()

        @pl.when(z == line - 1)
        def _():
            self.behind(t, True).wait_send()

        @pl.when((z < line - 1) & (line - 1 - z <= t))
        def _():
            self.behind(near, False).wait_send()

    def finish(self, out):
        line, z = self.line, self.z

        @pl.when(z == 0)
        def _():
            self.behind(z, False).wait_recv()
            add_blocks(out, self.acc.at[z], self.down.at[z], self.rows, self.steps)

        @pl.when(z == line - 1)
        def _():
            self.ahead(z, False).wait_recv()
            add_blocks(out, self.acc.at[z], self.up.at[z], self.rows, self.steps)

        @pl.when((z > 0) & (z < line - 1))
        def _():
            self.ahead(z, False).wait_recv()
            self.add(self.up, z)
            self.behind(z, False).wait_recv()
            add_blocks(out, self.up.at[z], self.down.at[z], self.rows, self.steps)


def owners_kernel(
    groups, parts, rows,
    normed, left, right, gate, small, dz, dpx, wz, wx,
    part, left_out, right_out, gate_out, back_out, small_all,
    made, held, acc, up, down, final, left_up, left_down, right_acc, right_up, right_down,
    normed_v, dz_v, dpx_v, wz_v, wx_v, back, back_sum,
    right_1, right_2, right_s, right_r, back_1, back_2, back_s, back_r,
    core_s, core_r, up_s, up_r, down_s, down_r, lup_s, lup_r, ldown_s, ldown_r,
    rup_s, rup_r, rdown_s, rdown_r, part_s, part_r, gate_s, gate_r, small_s, small_r,
    load, local,
):
    line = groups // 2
    span = parts * rows
    group, q = lax.axis_index("dp"), lax.axis_index("seq")
    z, core = group // 2, lax.rem(group, 2)
    sibling = (2 * z + 1 - core, q)
    peers, others = seq_peers(parts), dp_peers(groups)
    tokens = back.shape[1]
    loads = [
        pltpu.make_async_copy(source, target, load.at[k])
        for k, (source, target) in enumerate(
            [(normed, normed_v), (dpx, dpx_v), (dz, dz_v), (wz, wz_v), (wx, wx_v)]
        )
    ]
    for copy in loads:
        copy.start()
    greet(peers + others)
    half_rows = left.shape[1] // 2
    lefts = LineSum(
        line, z, core, q, left, left_up, left_down, lup_s, lup_r, ldown_s, ldown_r, half_rows, 2
    )
    rights = LineSum(
        line, z, core, q, right_acc, right_up, right_down, rup_s, rup_r, rdown_s, rdown_r,
        half_rows, 2,
    )
    wholes = LineSum(
        line, z, core, q, acc, up, down, up_s, up_r, down_s, down_r, rows, parts
    )
    lefts.step(0)
    right_plane = PlaneSum(parts, group, q, right, right_1, right_2, right_s, right_r)
    back_plane = PlaneSum(parts, group, q, back, back_1, back_2, back_s, back_r)
    right_plane.start(0)
    right_plane.start(1)
    waiting = []
    for k, peer in enumerate(peers):
        copy = remote(gate.at[peer[1]], gate_out.at[q], gate_s, gate_r, k, peer)
        copy.start()
        waiting.append(copy)
    for k, peer in enumerate(others):
        copy = remote(small, small_all.at[group], small_s, small_r, k, peer)
        copy.start()
        waiting.append(copy)
    own = [
        pltpu.make_async_copy(gate.at[q], gate_out.at[q], local.at[0]),
        pltpu.make_async_copy(small, small_all.at[group], local.at[1]),
    ]
    for copy in own:
        copy.start()
    loads[0].wait()
    loads[1].wait()
    tile = 512

    def dweight(of, out):
        at = pl.ds(pl.multiple_of(of * span, span), span)
        out[...] = dot(normed_v[:, at], dpx_v[...], TN).astype(BF16)

    cores = {}
    order = [d for k in range(line // 2) for d in (line - 1 - k, k)]

    def share_core(d):
        dweight(2 * d + 1 - core, made.at[d])
        copy = remote(made.at[d], held.at[d], core_s, core_r, d, sibling)
        copy.start()
        cores[d] = copy

    def sum_core(d):
        dweight(2 * d + core, acc.at[d])
        cores[d].wait()
        add_blocks(acc.at[d], acc.at[d], held.at[d], rows, parts)

    share_core(order[0])
    lefts.sent(0)
    lefts.step(1)
    share_core(order[1])
    sum_core(order[0])
    for t in range(2, line - 1):
        lefts.sent(t - 1)
        lefts.step(t)
    sum_core(order[1])
    wholes.step(0)
    for d in order[2:]:
        share_core(d)
    for d in order[2:]:
        sum_core(d)
    for copy in loads[2:]:
        copy.wait()

    def dnormed(of):
        at = pl.ds(pl.multiple_of(of * tokens, tokens), tokens)

        def step(j, carry):
            cols = pl.ds(pl.multiple_of(j * tile, tile), tile)
            back[of, :, cols] = (
                dot(dz_v[at, :], wz_v[cols, :], NT) + dot(dpx_v[at, :], wx_v[cols, :], NT)
            ).astype(BF16)
            return carry

        lax.fori_loop(0, D // tile, step, 0)

    right_plane.turn(32)
    if parts == 4:
        dnormed(back_plane.far)
        dnormed(back_plane.near[0])
        back_plane.start(0)
    wholes.sent(0)
    wholes.step(1)
    if parts == 4:
        dnormed(back_plane.near[1])
    else:
        for peer in peers:
            dnormed(peer[1])
    back_plane.start(1)
    dnormed(q)
    right_plane.finish(right_acc, 32)
    for t in range(2, line - 1):
        wholes.sent(t - 1)
        wholes.step(t)
    back_plane.turn(32)
    lefts.finish(left_out)
    lefts.sent(line - 2)
    wholes.sent(line - 2)
    rights.step(0)
    wholes.finish(final)
    for k, peer in enumerate(peers):
        block = final.at[pl.ds(pl.multiple_of(peer[1] * rows, rows), rows)]
        copy = remote(block, part.at[q], part_s, part_r, k, peer)
        copy.start()
        waiting.append(copy)
    copy = pltpu.make_async_copy(
        final.at[pl.ds(pl.multiple_of(q * rows, rows), rows)], part.at[q], local.at[2]
    )
    copy.start()
    own.append(copy)
    rights.sent(0)
    rights.step(1)
    back_plane.finish(back_sum, 32)
    copy = pltpu.make_async_copy(back_sum, back_out, local.at[3])
    copy.start()
    own.append(copy)
    for t in range(2, line - 1):
        rights.sent(t - 1)
        rights.step(t)
    rights.finish(right_out)
    rights.sent(line - 2)
    for copy in own + waiting:
        copy.wait()


def sum_to_owners(collective_id, normed, left, right, gate, small, dz, dpx, wz, wx):
    parts, line, out_rows, half = right.shape
    groups = 2 * line
    rows = gate.shape[1]
    span, width = rows * parts, dpx.shape[1]
    tokens = dz.shape[0] // parts
    sem = pltpu.SemaphoreType.DMA
    vmem = pl.BlockSpec(memory_space=pltpu.VMEM)
    hbm = pl.BlockSpec(memory_space=pltpu.HBM)
    return pl.pallas_call(
        functools.partial(owners_kernel, groups, parts, rows),
        in_specs=[hbm, vmem, vmem, hbm, vmem, hbm, hbm, hbm, hbm],
        out_specs=[hbm, vmem, vmem, hbm, hbm, vmem],
        out_shape=[
            jax.ShapeDtypeStruct((parts, rows, width), BF16),
            *([jax.ShapeDtypeStruct((out_rows, half), F32)] * 2),
            jax.ShapeDtypeStruct(gate.shape, BF16),
            jax.ShapeDtypeStruct((tokens, D), F32),
            jax.ShapeDtypeStruct((groups,) + small.shape, F32),
        ],
        scratch_shapes=[
            *([pltpu.VMEM((line, span, width), BF16)] * 5),
            pltpu.VMEM((span, width), BF16),
            *([pltpu.VMEM(left.shape, BF16)] * 5),
            *[pltpu.VMEM(a.shape, BF16) for a in (normed, dz, dpx, wz, wx)],
            pltpu.VMEM((parts, tokens, D), BF16),
            pltpu.VMEM((tokens, D), F32),
            *PlaneSum.scratch(parts, right.shape[1:], BF16),
            *PlaneSum.scratch(parts, (tokens, D), BF16),
            *([sem((line,))] * 14),
            *([sem((parts - 1,))] * 4),
            *([sem((groups - 1,))] * 2),
            sem((5,)),
            sem((4,)),
        ],
        compiler_params=pltpu.CompilerParams(
            collective_id=collective_id, has_side_effects=True, vmem_limit_bytes=63 * 2**20
        ),
        name="sum_to_owners",
    )(normed, left, right, gate, small, dz, dpx, wz, wx)


def pack_terms(values):
    high = lax.reduce_precision(values, 8, 7)
    packed = jnp.concatenate([high, values - high], axis=-1).astype(BF16)
    return jnp.pad(packed, ((0, 0), (0, LANES - packed.shape[-1])))


def unpack_terms(packed, count):
    packed = packed.astype(F32)
    return packed[..., :count] + packed[..., count : 2 * count]


def on_device(
    hidden_in, out_grads, w_in, w_in_m, w_in_v, w_out, w_out_m, w_out_v,
    chan_params, chan_m, chan_v, head_params, head_m, head_v,
):
    parts = lax.axis_size("seq")
    groups = lax.axis_size("dp")
    q = lax.axis_index("seq")
    rows = hidden_in.shape[1]
    length = rows * parts
    cw = INNER // parts
    hq = H // parts
    cc = cw + 2 * N
    in_rows = w_in.shape[0]
    out_rows = w_out.shape[0]

    chan_len = chan_params.shape[0]
    chan_rows = -(-chan_len // (8 * LANES)) * 8
    chan_block = jnp.pad(
        lax.reduce_precision(chan_params, 8, 7), (0, chan_rows * LANES - chan_len)
    ).reshape(chan_rows, LANES)
    hidden, wx, wz, chan_full = collect(0, hidden_in[0], w_in, chan_block, groups, parts)
    out_low, chan_full = lax.optimization_barrier((w_out.astype(BF16), chan_full))
    wo = lax.all_gather(out_low, ("dp", "seq"), axis=0, tiled=True)
    hidden = hidden.reshape(length, D)
    wx = wx.reshape(D, cc + LANES)
    chan_full = chan_full.reshape(groups * parts, chan_rows * LANES)[:, :chan_len].reshape(-1)
    line = groups // 2
    group = lax.axis_index("dp")
    core, place = group % 2, group // 2
    wz_blocks = [
        lax.ppermute(wz, "dp", [(i, i ^ (2 * k)) for i in range(groups)]) for k in range(1, line)
    ]

    conv_taps = chan_full[: TAPS * CONV_CH].reshape(TAPS, CONV_CH)
    conv_bias = chan_full[TAPS * CONV_CH : (TAPS + 1) * CONV_CH].reshape(1, CONV_CH)
    offset = (TAPS + 1) * CONV_CH
    gain_in = chan_full[offset : offset + D]
    gain_out = chan_full[offset + D : offset + D + INNER]
    taps_all = jnp.concatenate(
        [conv_taps, conv_bias, jnp.zeros((8 - TAPS - 1, CONV_CH), F32)], axis=0
    )
    taps = jnp.concatenate(
        [lax.dynamic_slice(taps_all, (0, q * cw), (8, cw)), taps_all[:, INNER:]], axis=1
    )
    own_gain = lax.dynamic_slice(gain_out, (q * cw,), (cw,))
    own_heads = lax.dynamic_slice(head_params, (0, q * hq), (3, hq))
    heads = jnp.pad(
        jnp.stack([own_heads[0], -jnp.exp(own_heads[1])]), ((0, 6), (0, LANES - hq))
    )
    skip = jnp.repeat(own_heads[2], P_SIZE).reshape(1, cw)
    spread = (
        jnp.arange(LANES)[:, None] == (jnp.arange(cw) // P_SIZE)[None, :]
    ).astype(BF16)

    tokens = hidden.astype(F32)
    scale = lax.rsqrt(jnp.mean(tokens * tokens, axis=-1, keepdims=True) + EPS_IN)
    normed = (tokens * scale * gain_in).astype(BF16)
    px = dot(normed, wx)
    y, states = scan_forward(px, taps, heads, skip, spread)
    wz_blocks, y = lax.optimization_barrier((wz_blocks, y))
    wz_line = lax.dynamic_update_index_in_dim(
        jnp.zeros((line,) + wz.shape, BF16), wz, place, 0
    )
    for k in range(1, line):
        wz_line = lax.dynamic_update_index_in_dim(wz_line, wz_blocks[k - 1], place ^ k, 0)
    other = lax.ppermute(wz_line, "dp", [(i, i ^ 1) for i in range(groups)])
    wz = jnp.where(core == 0, jnp.stack([wz_line, other], 1), jnp.stack([other, wz_line], 1))
    wz = wz.reshape(D, cw)
    z = dot(normed, wz)
    sig = jax.nn.sigmoid(z)
    gate = z * sig
    gated = y * gate
    channel = q * cw + jnp.arange(cw)
    squares = jnp.stack(
        [
            jnp.sum(jnp.where((channel >= low) & (channel < high), gated * gated, 0.0), axis=-1)
            for low, high in SEGMENTS
        ],
        axis=-1,
    )
    u_blocks = jnp.concatenate([(gated * own_gain).astype(BF16), pack_terms(squares)], axis=-1)
    u = swap(2, u_blocks.reshape(parts, rows, cw + LANES))[0]

    own_tokens = hidden_in[0].astype(F32)
    cotangent = out_grads[:, 0]
    block_out, back_blocks, mixed = widths(u, wo, cotangent, hidden_in[0])
    block_out = block_out[:, None]
    back_own, dwo_left, dwo_right = swap_back(3, back_blocks, u, mixed, groups)
    back_own = back_own.reshape(length, cw + LANES)

    coefs = unpack_terms(back_own[:, cw:], LEVELS)
    pull = coefs[:, LEVELS - 1 :]
    for k in reversed(range(LEVELS - 1)):
        pull = jnp.where(channel[None, :] < level_width(k), coefs[:, k : k + 1], pull)
    back = back_own[:, :cw].astype(F32)
    dgated = own_gain * back - gated * pull
    dgain_out = jnp.sum(back * gated, axis=0)
    dz = (dgated * y * (sig + gate * (1.0 - sig))).astype(BF16)
    dy = dgated * gate
    dwz = dot(normed, dz, TN).astype(BF16)
    dwz = dwz.reshape(line, 2, parts * in_rows, cw)
    dpx, dtaps, dheads, dskip, dwo_left, dwz = scan_backward(
        5, px, taps, heads, skip, spread, spread.T, dy, y, states, dwo_left, dwz
    )
    skip_grad = jnp.sum(dskip[0].reshape(hq, P_SIZE), axis=-1)
    small = jnp.concatenate(
        [dtaps[: TAPS + 1].reshape(-1), dgain_out, dheads[0, :hq], dheads[1, :hq], skip_grad]
    )
    small_rows = -(-small.shape[0] // (8 * LANES)) * 8
    small = jnp.pad(small, (0, small_rows * LANES - small.shape[0])).reshape(small_rows, LANES)
    x_part, left_part, right_part, z_part, dnormed, small = sum_to_owners(
        4, normed, dwo_left, dwo_right, dwz.reshape(parts, in_rows, cw), small, dz, dpx, wz, wx
    )
    hidden_grad, chan_total, head_total, norm = gradient_norm(
        6, x_part, z_part, left_part, right_part, dnormed, small, hidden_in[0],
        gain_in.reshape(1, D), cotangent, groups,
    )
    (
        hidden_grad, w_in_new, w_in_m_new, w_in_v_new, w_in_copy,
        w_out_new, w_out_m_new, w_out_v_new, w_out_copy,
    ) = update_weights(
        norm, x_part, z_part, left_part, right_part, hidden_grad,
        (w_in, w_in_m, w_in_v, w_out, w_out_m, w_out_v),
    )
    hidden_grad = hidden_grad[None]
    grad_norm, clip_factor = norm[0, 0], norm[1, 0]
    owner = group * parts + q
    chan_part = lax.dynamic_slice(chan_total.reshape(-1), (owner * chan_len,), (chan_len,))
    head_total = head_total[:parts, : 3 * hq].reshape(parts, 3, hq)
    head_total = head_total.transpose(1, 0, 2).reshape(3, H)
    chan_new, chan_m_new, chan_v_new = adam_tile(
        chan_params, clip_factor * chan_part, chan_m, chan_v, 0.2, 0.0
    )
    head_new, head_m_new, head_v_new = adam_tile(
        head_params, clip_factor * head_total, head_m, head_v, 1.0, 0.0
    )
    return (
        block_out, hidden_grad, grad_norm,
        w_in_new, w_in_m_new, w_in_v_new, w_in_copy,
        w_out_new, w_out_m_new, w_out_v_new, w_out_copy,
        chan_new, chan_m_new, chan_v_new, head_new, head_m_new, head_v_new,
    )


def solution(mesh):
    rows = P(("dp", "seq"), None)
    flat = P(("dp", "seq"))
    in_specs = (
        P("dp", "seq", None),
        P(None, "dp", "seq", None),
        *([rows] * 6),
        *([flat] * 3),
        *([P()] * 3),
    )
    out_specs = (
        P(None, "dp", "seq", None),
        P("dp", "seq", None),
        P(),
        *([rows] * 8),
        *([flat] * 3),
        *([P()] * 3),
    )
    return jax.shard_map(
        on_device, mesh=mesh, in_specs=in_specs, out_specs=out_specs, check_vma=False
    )
```

```python
import functools

import jax
import jax.numpy as jnp
from jax import lax
from jax.experimental import pallas as pl
from jax.experimental.pallas import tpu as pltpu
from jax.sharding import PartitionSpec as P

D = 2048
INNER = 4096
H = 64
P_SIZE = 64
N = 128
TAPS = 4
STEP = 10
E_IN = 8512
CONV_CH = 4352
LANES = 128
CHUNK = 128
LEVELS = 4

EXACT = lax.Precision.HIGHEST
EPS_IN = 1e-06
EPS_OUT = 1e-05
ADAM_EPS = 1e-08
BETA = 0.5
CLIP = 1.0
F32 = jnp.float32
BF16 = jnp.bfloat16
MASKED = -1e30


def level_width(level):
    return INNER * 2**level // 8


SEGMENTS = tuple(
    (0 if level == 0 else level_width(level - 1), level_width(level)) for level in range(LEVELS)
)


def dot(a, b, dims=((1,), (0,)), precision=None):
    return lax.dot_general(a, b, (dims, ((), ())), precision=precision, preferred_element_type=F32)


NT = ((1,), (1,))
TN = ((0,), (0,))


def softplus(v):
    return jnp.maximum(v, 0.0) + jnp.log1p(jnp.exp(-jnp.abs(v)))


def two_terms(v):
    high = v.astype(BF16)
    return high, (v - high.astype(F32)).astype(BF16)


def spread_heads(v, spread):
    high, rest = two_terms(v)
    return dot(high, spread) + dot(rest, spread)


def own_heads_first(dt_raw, hq, back=False):
    by = lax.axis_index("seq") * hq
    return pltpu.roll(dt_raw, by if back else lax.rem(LANES - by, LANES), 1)


def rates(dt_raw, heads):
    step = softplus(dt_raw + heads[0:1, :])
    return step, step * heads[1:2, :]


def triangle(size):
    row = lax.broadcasted_iota(jnp.int32, (size, size), 0)
    col = lax.broadcasted_iota(jnp.int32, (size, size), 1)
    return row, col


def conv_block(taps, xbuf, lanes):
    out = taps[TAPS : TAPS + 1, lanes]
    for tap in range(TAPS):
        out = out + taps[tap : tap + 1, lanes] * xbuf[5 + tap : 5 + tap + CHUNK, lanes]
    return out


def pair_decay(cum, cum_t, causal, head):
    gap = cum[:, head : head + 1] - cum_t[head : head + 1, :]
    return jnp.exp(jnp.where(causal, gap, MASKED))


def scan_forward_step(cw, px, taps, heads, skip, spread, y, states, xbuf, state, xdt, carried):
    cc = cw + 2 * N
    xbuf[8 : 8 + CHUNK, :] = px[:, :cc]
    step, rate = rates(own_heads_first(px[:, cc:], cw // P_SIZE), heads)
    row, col = triangle(CHUNK)
    causal = row >= col
    cum = dot(causal.astype(F32), rate, precision=EXACT)
    cum_t = cum.T
    spread_m = spread[...]
    last = cum[CHUNK - 1 : CHUNK, :]
    step_x = spread_heads(step, spread_m)
    grow_x = spread_heads(jnp.exp(cum), spread_m)
    tail_x = spread_heads(jnp.exp(last - cum), spread_m)

    def activated(lanes):
        conv = conv_block(taps, xbuf, lanes)
        return conv * jax.nn.sigmoid(conv)

    state_in = activated(slice(cw, cw + N))
    state_out = activated(slice(cw + N, cw + 2 * N))
    scores = dot(state_out, state_in, NT, EXACT)
    states[...] = state[...].astype(BF16)
    carried[...] = dot(state_out.astype(BF16), state[...].astype(BF16))
    first = lax.broadcasted_iota(jnp.int32, (1, LANES), 1) < P_SIZE
    for pair in range(cw // LANES):
        lanes = slice(pair * LANES, (pair + 1) * LANES)
        x = activated(lanes)
        xd = (x * step_x[:, lanes]).astype(BF16).astype(F32)
        xdt[:, lanes] = (xd * tail_x[:, lanes]).astype(BF16)
        stacked = jnp.concatenate([jnp.where(first, xd, 0.0), jnp.where(first, 0.0, xd)], axis=0)
        mixing = jnp.concatenate(
            [
                (pair_decay(cum, cum_t, causal, 2 * pair + k) * scores).astype(BF16)
                for k in range(2)
            ],
            axis=1,
        )
        y[:, lanes] = (
            dot(mixing, stacked.astype(BF16))
            + grow_x[:, lanes] * carried[:, lanes]
            + skip[:, lanes] * x
        )
    state[...] = grow_x[CHUNK - 1 : CHUNK, :] * state[...] + dot(
        state_in.astype(BF16), xdt[...], TN
    )
    xbuf[0:8, :] = xbuf[CHUNK : CHUNK + 8, :]


def scan_backward_kernel(
    groups, parts, cw, chunks,
    px, halo, taps, heads, skip, spread, gather, dy, y, states, wide, gate,
    dpx, dtaps, dheads, dskip, wide_sum, gate_sum,
    xbuf, dstate, dcbuf, slope, xact, xd_s, dxd_s, acc_s,
    first, second, wide_s, wide_r, gate_held, gate_acc, gate_up, gate_down,
    core_s, core_r, up_s, up_r, down_s, down_r,
):
    line = groups // 2
    group, q = lax.axis_index("dp"), lax.axis_index("seq")
    z, core = group // 2, lax.rem(group, 2)
    sibling = (2 * z + 1 - core, q)
    last = chunks - 1
    plane = PlaneSum(parts, group, q, wide, first, second, wide_s, wide_r)
    rows = gate.shape[2] // 4
    gates = LineSum(
        line, z, core, q, gate_acc, gate_up, gate_down, up_s, up_r, down_s, down_r, rows, 4
    )

    def core_copy(d):
        return remote(gate.at[d, 1 - core], gate_held.at[d], core_s, core_r, d, sibling)

    @pl.when(pl.program_id(0) == 0)
    def _():
        greet(seq_peers(parts) + dp_peers(groups))
        for d in range(line):
            core_copy(d).start()
        plane.start(0)
        plane.start(1)

    @pl.when(pl.program_id(0) == 1)
    def _():
        for d in range(line):
            core_copy(d).wait()
            add_blocks(gate_acc.at[d], gate.at[d, core], gate_held.at[d], rows, 4)
        gates.step(0)

    for t in range(1, line - 1):

        @pl.when(pl.program_id(0) == min(1 + 3 * t, last))
        def _(t=t):
            gates.sent(t - 1)
            gates.step(t)

    @pl.when(pl.program_id(0) == min(6, last))
    def _():
        plane.turn(32)

    scan_backward_step(
        cw, px, halo, taps, heads, skip, spread, gather, dy, y, states,
        dpx, dtaps, dheads, dskip, xbuf, dstate, dcbuf, slope, xact, xd_s, dxd_s, acc_s,
    )

    @pl.when(pl.program_id(0) == last)
    def _():
        plane.finish(wide_sum, 32)
        gates.finish(gate_sum)
        gates.sent(line - 2)


def scan_backward_step(
    cw, px, halo, taps, heads, skip, spread, gather, dy, y, states,
    dpx, dtaps, dheads, dskip,
    xbuf, dstate, dcbuf, slope, xact, xd_s, dxd_s, acc_s,
):
    cc = cw + 2 * N
    at = pl.program_id(0)

    @pl.when(at == 0)
    def _():
        dstate[...] = jnp.zeros_like(dstate)
        dcbuf[CHUNK : CHUNK + 8, :] = jnp.zeros((8, cc), F32)
        dtaps[...] = jnp.zeros_like(dtaps)
        dheads[...] = jnp.zeros_like(dheads)
        dskip[...] = jnp.zeros_like(dskip)

    xbuf[0:8, :] = jnp.where(at == pl.num_programs(0) - 1, 0.0, halo[:, :cc])
    xbuf[8 : 8 + CHUNK, :] = px[:, :cc]
    dt_raw = own_heads_first(px[:, cc:], cw // P_SIZE)
    step, rate = rates(dt_raw, heads)
    row, col = triangle(CHUNK)
    causal = row >= col
    cum = dot(causal.astype(F32), rate, precision=EXACT)
    cum_t = cum.T
    spread_m = spread[...]
    last = cum[CHUNK - 1 : CHUNK, :]
    step_x = spread_heads(step, spread_m)
    grow_x = spread_heads(jnp.exp(cum), spread_m)
    tail_x = spread_heads(jnp.exp(last - cum), spread_m)

    for block in range(cc // LANES):
        lanes = slice(block * LANES, (block + 1) * LANES)
        conv = conv_block(taps, xbuf, lanes)
        sig = jax.nn.sigmoid(conv)
        act = conv * sig
        xact[:, lanes] = act
        slope[:, lanes] = sig + act * (1.0 - sig)
    state_in = xact[:, cw : cw + N]
    state_out = xact[:, cw + N : cc]
    scores = dot(state_out, state_in, NT, EXACT)
    in_low = state_in.astype(BF16)
    out_low = state_out.astype(BF16)
    dstate_low = dstate[...].astype(BF16)
    acc_s[...] = jnp.zeros_like(acc_s)
    dxd_s[...] = tail_x * dot(in_low, dstate_low)
    dskip[0:1, :] += jnp.sum(xact[:, :cw] * dy[...], axis=0, keepdims=True)
    first = lax.broadcasted_iota(jnp.int32, (1, LANES), 1) < P_SIZE
    xd_s[...] = (xact[:, :cw] * step_x).astype(BF16)
    total = jnp.sum(xd_s[...].astype(F32) * dxd_s[...], axis=0, keepdims=True) + grow_x[
        CHUNK - 1 : CHUNK, :
    ] * jnp.sum(dstate[...] * states[0].astype(F32), axis=0, keepdims=True)
    dscores = jnp.zeros((CHUNK, CHUNK), F32)
    for pair in range(cw // LANES):
        lanes = slice(pair * LANES, (pair + 1) * LANES)
        dyp = dy[:, lanes]
        stacked = jnp.concatenate(
            [jnp.where(first, dyp, 0.0), jnp.where(first, 0.0, dyp)], axis=0
        ).astype(BF16)
        decays = [pair_decay(cum, cum_t, causal, 2 * pair + k) for k in range(2)]
        mixing = jnp.concatenate([(decay * scores).astype(BF16) for decay in decays], axis=0)
        dxd_s[:, lanes] += dot(mixing, stacked, TN)
        dmix = dot(stacked, xd_s[:, lanes], NT)
        dscores = dscores + decays[0] * dmix[:CHUNK] + decays[1] * dmix[CHUNK:]
    dy_low = dy[...].astype(BF16)
    dy_f = dy_low.astype(F32)
    xd_f = xd_s[...].astype(F32)
    dxd = dxd_s[...]
    y_scan = y[...] - skip[...] * xact[:, :cw]
    final = lax.broadcasted_iota(jnp.int32, (CHUNK, 1), 0) == CHUNK - 1
    gather_m = gather[...]
    dcum = spread_heads(dy_f * y_scan - xd_f * dxd + jnp.where(final, total, 0.0), gather_m)
    dstep = spread_heads(xact[:, :cw] * dxd, gather_m)
    drate = dot((row <= col).astype(F32), dcum, precision=EXACT)
    dstep = dstep + drate * heads[1:2, :]
    ddt = dstep * jax.nn.sigmoid(dt_raw + heads[0:1, :])
    dheads[0:1, :] += jnp.sum(ddt, axis=0, keepdims=True)
    dheads[1:2, :] += jnp.sum(drate * rate, axis=0, keepdims=True)
    grown = (grow_x * dy_f).astype(BF16)
    dscores_low = dscores.astype(BF16)
    dout = dot(dscores_low, in_low) + dot(grown, states[0], NT)
    din = dot(dscores_low, out_low, TN) + dot((tail_x * xd_f).astype(BF16), dstate_low, NT)
    dstate[...] = grow_x[CHUNK - 1 : CHUNK, :] * dstate[...] + dot(out_low, grown, TN)
    dcbuf[:CHUNK, :cw] = (step_x * dxd + skip[...] * dy[...]) * slope[:, :cw]
    dcbuf[:CHUNK, cw : cw + N] = din * slope[:, cw : cw + N]
    dcbuf[:CHUNK, cw + N :] = dout * slope[:, cw + N :]
    for block in range(cc // LANES):
        lanes = slice(block * LANES, (block + 1) * LANES)
        dconv = dcbuf[:CHUNK, lanes]
        dtaps[TAPS : TAPS + 1, lanes] += jnp.sum(dconv, axis=0, keepdims=True)
        back = taps[TAPS - 1 : TAPS, lanes] * dconv
        for tap in range(TAPS):
            dtaps[tap : tap + 1, lanes] += jnp.sum(
                dconv * xbuf[5 + tap : 5 + tap + CHUNK, lanes], axis=0, keepdims=True
            )
            if tap < TAPS - 1:
                reach = TAPS - 1 - tap
                back = back + taps[tap : tap + 1, lanes] * dcbuf[reach : reach + CHUNK, lanes]
        dpx[:, lanes] = back.astype(BF16)
    ours = lax.broadcasted_iota(jnp.int32, (1, LANES), 1) < cw // P_SIZE
    ddt = own_heads_first(jnp.where(ours, ddt, 0.0), cw // P_SIZE, back=True)
    dpx[:, cc:] = ddt.astype(BF16)
    dcbuf[CHUNK : CHUNK + 8, :] = dcbuf[0:8, :]


def whole(shape):
    return pl.BlockSpec(shape, lambda i: (0,) * len(shape))


def scan_backward(collective_id, px, taps, heads, skip, spread, gather, dy, y, states, wide, gate):
    length, width = px.shape
    cw = skip.shape[1]
    cc = cw + 2 * N
    chunks = length // CHUNK
    eighths = CHUNK // 8
    parts, line, out_rows, half = wide.shape
    span = gate.shape[2]
    sem = pltpu.SemaphoreType.DMA
    vmem = pl.BlockSpec(memory_space=pltpu.VMEM)
    return pl.pallas_call(
        functools.partial(scan_backward_kernel, 2 * line, parts, cw, chunks),
        grid=(chunks,),
        in_specs=[
            pl.BlockSpec((CHUNK, width), lambda i: (chunks - 1 - i, 0)),
            pl.BlockSpec(
                (8, width), lambda i: (jnp.maximum((chunks - 1 - i) * eighths - 1, 0), 0)
            ),
            whole(taps.shape),
            whole(heads.shape),
            whole(skip.shape),
            whole(spread.shape),
            whole(gather.shape),
            pl.BlockSpec((CHUNK, cw), lambda i: (chunks - 1 - i, 0)),
            pl.BlockSpec((CHUNK, cw), lambda i: (chunks - 1 - i, 0)),
            pl.BlockSpec((1, N, cw), lambda i: (chunks - 1 - i, 0, 0)),
            vmem,
            vmem,
        ],
        out_specs=[
            pl.BlockSpec((CHUNK, width), lambda i: (chunks - 1 - i, 0)),
            whole((8, cc)),
            whole((8, LANES)),
            whole((8, cw)),
            vmem,
            vmem,
        ],
        out_shape=[
            jax.ShapeDtypeStruct((length, width), BF16),
            jax.ShapeDtypeStruct((8, cc), F32),
            jax.ShapeDtypeStruct((8, LANES), F32),
            jax.ShapeDtypeStruct((8, cw), F32),
            jax.ShapeDtypeStruct(wide.shape[1:], BF16),
            jax.ShapeDtypeStruct((span, cw), BF16),
        ],
        scratch_shapes=[
            pltpu.VMEM((CHUNK + 8, cc), F32),
            pltpu.VMEM((N, cw), F32),
            pltpu.VMEM((CHUNK + 8, cc), F32),
            pltpu.VMEM((CHUNK, cc), F32),
            pltpu.VMEM((CHUNK, cc), F32),
            pltpu.VMEM((CHUNK, cw), BF16),
            pltpu.VMEM((CHUNK, cw), F32),
            pltpu.VMEM((CHUNK, CHUNK), F32),
            *PlaneSum.scratch(parts, wide.shape[1:], BF16),
            *([pltpu.VMEM((line, span, cw), BF16)] * 4),
            *([sem((line,))] * 6),
        ],
        compiler_params=pltpu.CompilerParams(
            collective_id=collective_id, has_side_effects=True, vmem_limit_bytes=63 * 2**20
        ),
        cost_estimate=pl.CostEstimate(
            flops=10**10, bytes_accessed=100 * 10**6, transcendentals=10**7
        ),
        name="scan_backward",
    )(px, px, taps, heads, skip, spread, gather, dy, y, states, wide, gate)


WIDE = 512


def widths_kernel(cw, u, wo, cotangent, tokens, block_out, back, mixed, branch, norms, pulls):
    at = pl.program_id(0)
    ends = [level_width(k) // WIDE - 1 for k in range(LEVELS)]

    @pl.when(at == 0)
    def _():
        terms = u[0, :, cw:].astype(F32)
        for part in range(1, u.shape[0]):
            terms = terms + u[part, :, cw:].astype(F32)
        squares = jnp.zeros((terms.shape[0], 1), F32)
        for k in range(LEVELS):
            squares = squares + terms[:, k : k + 1] + terms[:, LEVELS + k : LEVELS + k + 1]
            norms[:, k : k + 1] = lax.rsqrt(squares / level_width(k) + EPS_OUT)
        running = jnp.zeros(branch.shape, F32)
        for k in reversed(range(LEVELS)):
            running = running + norms[:, k : k + 1] * cotangent[k].astype(F32)
            mixed[k] = running.astype(BF16)
        branch[...] = jnp.zeros_like(branch)

    part = at * WIDE // cw
    lanes = pl.ds(pl.multiple_of(lax.rem(at * WIDE, cw), WIDE), WIDE)
    level = sum((at > end).astype(jnp.int32) for end in ends[:-1])
    branch[...] += dot(u[part, :, lanes], wo[...])
    back[part, :, lanes] = dot(mixed[level], wo[...], NT).astype(BF16)
    for k in range(LEVELS):

        @pl.when(at == ends[k])
        def _():
            norm = norms[:, k : k + 1]
            block_out[k] = (tokens[...].astype(F32) + norm * branch[...]).astype(BF16)
            inner = jnp.sum(cotangent[k].astype(F32) * branch[...], axis=-1, keepdims=True)
            pulls[:, k : k + 1] = norm * norm * norm * (inner / level_width(k))

    @pl.when(at == ends[-1])
    def _():
        coef = jnp.zeros((branch.shape[0], 1), F32)
        lane = lax.broadcasted_iota(jnp.int32, (1, LANES), 1)
        packed = jnp.zeros((branch.shape[0], LANES), F32)
        for k in reversed(range(LEVELS)):
            coef = coef + pulls[:, k : k + 1]
            high, rest = two_terms(coef)
            packed = jnp.where(lane == k, high.astype(F32), packed)
            packed = jnp.where(lane == LEVELS + k, rest.astype(F32), packed)
        for p in range(back.shape[0]):
            back[p, :, cw:] = packed.astype(BF16)


def widths(u, wo, cotangent, tokens):
    parts, rows, wide = u.shape
    cw = wide - LANES

    def full(shape):
        return pl.BlockSpec(shape, lambda i: (0,) * len(shape), pipeline_mode=pl.Buffered(1))

    return pl.pallas_call(
        functools.partial(widths_kernel, cw),
        grid=(INNER // WIDE,),
        in_specs=[
            full(u.shape),
            pl.BlockSpec((WIDE, D), lambda i: (i, 0)),
            full(cotangent.shape),
            full(tokens.shape),
        ],
        out_specs=[full(cotangent.shape), full(u.shape), full(cotangent.shape)],
        out_shape=[
            jax.ShapeDtypeStruct(cotangent.shape, BF16),
            jax.ShapeDtypeStruct(u.shape, BF16),
            jax.ShapeDtypeStruct(cotangent.shape, BF16),
        ],
        scratch_shapes=[
            pltpu.VMEM((rows, D), F32),
            pltpu.VMEM((rows, LANES), F32),
            pltpu.VMEM((rows, LANES), F32),
        ],
        compiler_params=pltpu.CompilerParams(vmem_limit_bytes=63 * 2**20),
        name="widths",
    )(u, wo, cotangent, tokens)


MESH = pl.DeviceIdType.MESH


def remote(src, dst, sends, recvs, index, device):
    return pltpu.make_async_remote_copy(
        src_ref=src,
        dst_ref=dst,
        send_sem=sends.at[index],
        recv_sem=recvs.at[index],
        device_id=device,
        device_id_type=MESH,
    )


def greet(devices):
    barrier = pltpu.get_barrier_semaphore()
    for device in devices:
        pl.semaphore_signal(barrier, inc=1, device_id=device, device_id_type=MESH)
    pl.semaphore_wait(barrier, len(devices))


def seq_peers(parts):
    group, q = lax.axis_index("dp"), lax.axis_index("seq")
    return [(group, lax.rem(q + k, parts)) for k in range(1, parts)]


def dp_peers(groups):
    group, q = lax.axis_index("dp"), lax.axis_index("seq")
    return [(lax.rem(group + k, groups), q) for k in range(1, groups)]


def all_peers(groups, parts):
    devices = groups * parts
    me = lax.axis_index("dp") * parts + lax.axis_index("seq")
    peers = []
    for k in range(1, devices):
        other = lax.rem(me + k, devices)
        peers.append((other // parts, lax.rem(other, parts)))
    return peers


CHAN_ROWS = ((TAPS + 1) * CONV_CH + D + INNER) // LANES


def adam_tile(weight, gradient, moment, second, step_rate, weight_decay):
    new_moment = BETA * moment + (1.0 - BETA) * gradient
    new_second = BETA * second + (1.0 - BETA) * gradient * gradient
    correction = 1.0 - BETA**STEP
    update = new_moment / correction / (jnp.sqrt(new_second / correction) + ADAM_EPS)
    return weight - step_rate * (update + weight_decay * weight), new_moment, new_second


def total_of(value):
    return jnp.sum(jnp.sum(value, axis=1, keepdims=True), axis=0, keepdims=True)


def norm_kernel(
    groups, parts,
    part_h, gate_h, left_h, right_h, back_h, small_h, hidden_h, gain, cotangent,
    hidden_grad, chan, head, norm,
    part, gate, left, right, back, small, hidden,
    cot_v, block, near, all_block, all_near, sends, recvs, near_s, near_r, load, local,
):
    group, q = lax.axis_index("dp"), lax.axis_index("seq")
    me = group * parts + q
    cw = INNER // parts
    cc = cw + 2 * N
    everyone = all_peers(groups, parts)
    fetches = [
        pltpu.make_async_copy(source, target, load.at[k])
        for k, (source, target) in enumerate(
            [(back_h, back), (hidden_h, hidden), (part_h, part), (gate_h, gate),
             (left_h, left), (right_h, right), (small_h, small), (cotangent, cot_v)]
        )
    ]
    for copy in fetches:
        copy.start()
    barrier = pltpu.get_barrier_semaphore()
    for device in everyone:
        pl.semaphore_signal(barrier, inc=1, device_id=device, device_id_type=MESH)
    for copy in fetches[:7]:
        copy.wait()
    total = small[0]
    for k in range(1, groups):
        total = total + small[k]
    near[...] = total
    rows = 32

    def summed(at):
        down = back[at, :]
        tokens = hidden[at, :].astype(F32)
        mean = jnp.sum(tokens * tokens, axis=-1, keepdims=True) / D
        return down, tokens, lax.rsqrt(mean + EPS_IN)

    def gain_rows(i, dgain):
        at = pl.ds(pl.multiple_of(i * rows, rows), rows)
        down, tokens, scale = summed(at)
        return dgain + jnp.sum(down * tokens * scale, axis=0, keepdims=True)

    dgain = lax.fori_loop(0, hidden.shape[0] // rows, gain_rows, jnp.zeros((1, D), F32))
    tail = part[0, :, cw : cc + H].astype(F32)
    for k in range(1, parts):
        tail = tail + part[k, :, cw : cc + H].astype(F32)
    squares = total_of(tail * tail)
    for k in range(parts):
        x = part[k, :, :cw].astype(F32)
        g = gate[k].astype(F32)
        squares = squares + total_of(x * x + g * g)
    squares = squares + total_of(left[...] * left[...] + right[...] * right[...])
    for k in range(D // LANES):
        block[k : k + 1, :] = dgain[:, k * LANES : (k + 1) * LANES]
    block[D // LANES :, :] = jnp.broadcast_to(squares, (8, LANES))
    pl.semaphore_wait(barrier, len(everyone))
    copies = [
        remote(block, all_block.at[me], sends, recvs, k, peer) for k, peer in enumerate(everyone)
    ]
    copies += [
        remote(near, all_near.at[q], near_s, near_r, k, peer)
        for k, peer in enumerate(seq_peers(parts))
    ]
    copies += [
        pltpu.make_async_copy(block, all_block.at[me], local.at[0]),
        pltpu.make_async_copy(near, all_near.at[q], local.at[1]),
    ]
    for copy in copies:
        copy.start()
    fetches[7].wait()

    def grad_rows(i, carry):
        at = pl.ds(pl.multiple_of(i * rows, rows), rows)
        down, tokens, scale = summed(at)
        scaled = down * gain[...]
        inner = jnp.sum(scaled * tokens, axis=-1, keepdims=True) / D
        direct = cot_v[0, at, :].astype(F32)
        for k in range(1, LEVELS):
            direct = direct + cot_v[k, at, :].astype(F32)
        hidden_grad[at, :] = (
            scale * scaled - tokens * (scale * scale * scale * inner) + direct
        )
        return carry

    lax.fori_loop(0, hidden.shape[0] // rows, grad_rows, 0)
    for copy in copies:
        copy.wait()
    total = jnp.sum(all_block[...], axis=0)
    own, wide = cw // LANES, cc // LANES
    span = CONV_CH // LANES
    for tap in range(TAPS + 1):
        for k in range(parts):
            at = tap * span + k * own
            chan[at : at + own, :] = all_near[k, tap * wide : tap * wide + own, :]
        shared = all_near[0, tap * wide + own : (tap + 1) * wide, :]
        for k in range(1, parts):
            shared = shared + all_near[k, tap * wide + own : (tap + 1) * wide, :]
        chan[tap * span + INNER // LANES : (tap + 1) * span, :] = shared
    at = (TAPS + 1) * span
    chan[at : at + D // LANES, :] = total[: D // LANES]
    at = at + D // LANES
    for k in range(parts):
        first = (TAPS + 1) * wide
        chan[at + k * own : at + (k + 1) * own, :] = all_near[k, first : first + own, :]
        head[k : k + 1, :] = all_near[k, first + own : first + own + 1, :]
    squares = (
        total[D // LANES : D // LANES + 1, :1]
        + total_of(chan[:CHAN_ROWS, :] * chan[:CHAN_ROWS, :])
        + total_of(head[:parts, :] * head[:parts, :])
    )
    grad_norm = jnp.sqrt(squares)
    norm[0:1, :] = jnp.broadcast_to(grad_norm, (1, LANES))
    norm[1:2, :] = jnp.broadcast_to(jnp.minimum(1.0, CLIP / grad_norm), (1, LANES))


def gradient_norm(
    collective_id, part, gate, left, right, back, small, hidden, gain, cotangent, groups
):
    parts = part.shape[0]
    devices = groups * parts
    sem = pltpu.SemaphoreType.DMA
    vmem = pl.BlockSpec(memory_space=pltpu.VMEM)
    hbm = pl.BlockSpec(memory_space=pltpu.HBM)
    block = (D // LANES + 8, LANES)
    chan_rows = -(-CHAN_ROWS // 8) * 8
    return pl.pallas_call(
        functools.partial(norm_kernel, groups, parts),
        in_specs=[*([hbm] * 7), vmem, hbm],
        out_specs=[vmem] * 4,
        out_shape=[
            jax.ShapeDtypeStruct(hidden.shape, F32),
            jax.ShapeDtypeStruct((chan_rows, LANES), F32),
            jax.ShapeDtypeStruct((8, LANES), F32),
            jax.ShapeDtypeStruct((8, LANES), F32),
        ],
        scratch_shapes=[
            *[pltpu.VMEM(a.shape, a.dtype) for a in (part, gate, left, right, back, small, hidden)],
            pltpu.VMEM(cotangent.shape, BF16),
            pltpu.VMEM(block, F32),
            pltpu.VMEM(small.shape[1:], F32),
            pltpu.VMEM((devices,) + block, F32),
            pltpu.VMEM((parts,) + small.shape[1:], F32),
            sem((devices - 1,)), sem((devices - 1,)), sem((parts - 1,)), sem((parts - 1,)),
            sem((8,)), sem((2,)),
        ],
        compiler_params=pltpu.CompilerParams(
            collective_id=collective_id, has_side_effects=True, vmem_limit_bytes=63 * 2**20
        ),
        name="gradient_norm",
    )(part, gate, left, right, back, small, hidden, gain, cotangent)


BLOCKS = 4


def update_kernel(
    parts, norm, part_h, gate_h, left_h, right_h, hidden_grad, *refs
):
    ins, refs = refs[:6], refs[6:]
    hidden_out, outs, refs = refs[0], refs[1:9], refs[9:]
    held, made = refs[:6], refs[6:14]
    part, gate, left, right, hidden_v, load, store, grads = refs[14:]
    clip = norm[1:2, :1]
    cw = INNER // parts
    cc = cw + 2 * N
    fetches = [
        pltpu.make_async_copy(source, target, grads.at[k])
        for k, (source, target) in enumerate(
            [(part_h, part), (gate_h, gate), (left_h, left), (right_h, right),
             (hidden_grad, hidden_v)]
        )
    ]
    for copy in fetches:
        copy.start()

    def at(a, i):
        rows = ins[a].shape[0] // BLOCKS
        return pl.ds(i * rows, rows)

    loads = [
        [
            pltpu.make_async_copy(ins[a].at[at(a, i)], held[a].at[at(a, i)], load.at[a * BLOCKS + i])
            for a in range(6)
        ]
        for i in range(BLOCKS)
    ]
    for weight in (0, 3):
        for i in range(BLOCKS):
            for a in range(weight, weight + 3):
                loads[i][a].start()
    stores = []

    def update(weight, rows, lanes, gradient, rate, decay):
        first = 0 if weight == 0 else 4
        new, moment, second = adam_tile(
            held[weight][rows, lanes], clip * gradient, held[weight + 1][rows, lanes],
            held[weight + 2][rows, lanes], rate, decay,
        )
        made[first][rows, lanes] = new
        made[first + 1][rows, lanes] = moment
        made[first + 2][rows, lanes] = second
        made[first + 3][rows, lanes] = new.astype(BF16)

    def send(first, rows, i):
        for a in range(first, first + 4):
            copy = pltpu.make_async_copy(
                made[a].at[rows], outs[a].at[rows], store.at[a * BLOCKS + i]
            )
            copy.start()
            stores.append(copy)

    for copy in fetches[:4]:
        copy.wait()
    for i in range(BLOCKS):
        rows = at(0, i)
        for a in range(3):
            loads[i][a].wait()
        for source, first in ((gate, 0), (part, INNER)):

            def step(k, carry, source=source, first=first, rows=rows):
                to = pl.ds(pl.multiple_of(first + k * cw, cw), cw)
                update(0, rows, to, source[k, rows, :cw].astype(F32), 0.02, 0.1)
                return carry

            lax.fori_loop(0, parts, step, 0)
        tail = part[0, rows, cw : cc + H].astype(F32)
        for k in range(1, parts):
            tail = tail + part[k, rows, cw : cc + H].astype(F32)
        update(0, rows, slice(2 * INNER, E_IN), tail, 0.02, 0.1)
        send(0, rows, i)
    fetches[4].wait()
    pass_on = pltpu.make_async_copy(hidden_v, hidden_out, grads.at[5])
    pass_on.start()
    half = D // 2
    for i in range(BLOCKS):
        rows = at(3, i)
        for a in range(3, 6):
            loads[i][a].wait()
        update(3, rows, slice(0, half), left[rows, :], 0.03, 0.1)
        update(3, rows, slice(half, D), right[rows, :], 0.03, 0.1)
        send(4, rows, i)
    pass_on.wait()
    for copy in stores:
        copy.wait()


def update_weights(norm, part, gate, left, right, hidden_grad, weights):
    parts = part.shape[0]
    w_in, w_out = weights[0], weights[3]
    sem = pltpu.SemaphoreType.DMA
    vmem = pl.BlockSpec(memory_space=pltpu.VMEM)
    hbm = pl.BlockSpec(memory_space=pltpu.HBM)
    made = [
        jax.ShapeDtypeStruct(w.shape, dtype) for w in (w_in, w_out) for dtype in (F32, F32, F32, BF16)
    ]
    return pl.pallas_call(
        functools.partial(update_kernel, parts),
        in_specs=[vmem, *([hbm] * 11)],
        out_specs=[hbm] * 9,
        out_shape=[jax.ShapeDtypeStruct(hidden_grad.shape, F32), *made],
        scratch_shapes=[
            *[pltpu.VMEM(w.shape, F32) for w in weights],
            *[pltpu.VMEM(m.shape, m.dtype) for m in made],
            *[pltpu.VMEM(a.shape, a.dtype) for a in (part, gate, left, right, hidden_grad)],
            sem((6 * BLOCKS,)), sem((8 * BLOCKS,)), sem((6,)),
        ],
        compiler_params=pltpu.CompilerParams(vmem_limit_bytes=63 * 2**20),
        name="update_weights",
    )(norm, part, gate, left, right, hidden_grad, *weights)


class LineGather:
    def __init__(self, line, z, core, q, slot, own, sends, recvs):
        self.line, self.z, self.core, self.q = line, z, core, q
        self.slot, self.own, self.sends, self.recvs = slot, own, sends, recvs

    def along(self, from_z, up, first=False):
        to = self.z + 1 if up else self.z - 1
        return remote(
            self.own if first else self.slot(from_z),
            self.slot(from_z),
            self.sends.at[0 if up else 1],
            self.recvs.at[0 if up else 1],
            from_z,
            (2 * to + self.core, self.q),
        )

    def step(self, t, got=None):
        line, z = self.line, self.z
        low, high = z - t, z + t
        if t == 0:

            @pl.when(z < line - 1)
            def _():
                self.along(z, True, True).start()

            @pl.when(z > 0)
            def _():
                self.along(z, False, True).start()

            return

        @pl.when(low >= 0)
        def _():
            self.along(low, True).wait_recv()

            @pl.when(z < line - 1)
            def _():
                self.along(low, True).start()

            if got is not None:
                got(low)

        @pl.when(high <= line - 1)
        def _():
            self.along(high, False).wait_recv()

            @pl.when(z > 0)
            def _():
                self.along(high, False).start()

            if got is not None:
                got(high)

    def sent(self):
        for from_z in range(self.line):

            @pl.when((from_z <= self.z) & (self.z < self.line - 1))
            def _():
                self.along(from_z, True).wait_send()

            @pl.when((from_z >= self.z) & (self.z > 0))
            def _():
                self.along(from_z, False).wait_send()


def collect_kernel(
    groups, parts, hidden, w_in, w_own, chan, hid_out, w_out, gate_out, chan_out, wo_out,
    blocks, gates, low, chan_s, chan_r, hid_s, hid_r, swap_s, swap_r, gate_s, gate_r,
    wo_s, wo_r, line_s, line_r, lwo_s, lwo_r, core_s, core_r, local,
):
    line = groups // 2
    cw = INNER // parts
    cc = cw + 2 * N
    group, q = lax.axis_index("dp"), lax.axis_index("seq")
    z, core = group // 2, lax.rem(group, 2)
    sibling = (2 * z + 1 - core, q)
    peers = seq_peers(parts)
    everyone = all_peers(groups, parts)
    shared = w_in[:, 2 * INNER :].astype(BF16)
    for part in range(parts):
        at = INNER + part * cw
        blocks[part, :, :cw] = w_in[:, at : at + cw].astype(BF16)
        blocks[part, :, cw : cc + H] = shared
        blocks[part, :, cc + H :] = jnp.zeros((w_in.shape[0], LANES - H), BF16)
    low[...] = w_own[...].astype(BF16)
    greet(everyone)
    swaps = []
    for k, peer in enumerate(peers):
        copy = remote(blocks.at[peer[1]], w_out.at[group, q], swap_s, swap_r, k, peer)
        copy.start()
        swaps.append(copy)
    outs = LineGather(
        line, z, core, q, lambda from_z: wo_out.at[2 * from_z + core, q], low, lwo_s, lwo_r
    )
    outs.step(0)
    own = [
        pltpu.make_async_copy(blocks.at[q], w_out.at[group, q], local.at[0]),
        pltpu.make_async_copy(hidden, hid_out.at[q], local.at[1]),
        pltpu.make_async_copy(chan, chan_out.at[group * parts + q], local.at[2]),
        pltpu.make_async_copy(low, wo_out.at[group, q], local.at[3]),
    ]
    for copy in own:
        copy.start()
    waiting = []
    for k, peer in enumerate(everyone):
        copy = remote(chan, chan_out.at[group * parts + q], chan_s, chan_r, k, peer)
        copy.start()
        waiting.append(copy)
    for part in range(parts):
        gates[part] = w_in[:, part * cw : (part + 1) * cw].astype(BF16)
    copy = pltpu.make_async_copy(gates.at[q], gate_out.at[q], local.at[4])
    copy.start()
    own.append(copy)
    own[0].wait()
    for copy in swaps:
        copy.wait()
    for k, peer in enumerate(peers):
        for source, target, sends, recvs in (
            (hidden, hid_out.at[q], hid_s, hid_r),
            (gates.at[peer[1]], gate_out.at[q], gate_s, gate_r),
            (low, wo_out.at[group, q], wo_s, wo_r),
        ):
            copy = remote(source, target, sends, recvs, k, peer)
            copy.start()
            waiting.append(copy)

    def across(from_z):
        block = w_out.at[2 * from_z + core]
        return remote(block, block, core_s, core_r, from_z, sibling)

    ins = LineGather(
        line, z, core, q, lambda from_z: w_out.at[2 * from_z + core], w_out.at[group],
        line_s, line_r,
    )
    across(z).start()
    ins.step(0)
    for t in range(1, line):
        ins.step(t, lambda from_z: across(from_z).start())
        if t == line - 2 or line == 2:
            for s in range(1, line):
                outs.step(s)
    ins.sent()
    outs.sent()
    for from_z in range(line):
        across(from_z).wait_send()
        block = w_out.at[2 * from_z + 1 - core]
        remote(block, block, core_s, core_r, from_z, sibling).wait_recv()
    for copy in own[1:] + waiting:
        copy.wait()


def collect(collective_id, hidden, w_in, w_own, chan, groups, parts):
    rows = w_in.shape[0]
    line = groups // 2
    cw = INNER // parts
    width = cw + 2 * N + LANES
    sem = pltpu.SemaphoreType.DMA
    hbm = pl.BlockSpec(memory_space=pltpu.HBM)
    vmem = pl.BlockSpec(memory_space=pltpu.VMEM)
    return pl.pallas_call(
        functools.partial(collect_kernel, groups, parts),
        in_specs=[hbm, vmem, vmem, hbm],
        out_specs=[hbm] * 5,
        out_shape=[
            jax.ShapeDtypeStruct((parts,) + hidden.shape, hidden.dtype),
            jax.ShapeDtypeStruct((groups, parts, rows, width), BF16),
            jax.ShapeDtypeStruct((parts, rows, cw), BF16),
            jax.ShapeDtypeStruct((groups * parts,) + chan.shape, chan.dtype),
            jax.ShapeDtypeStruct((groups, parts) + w_own.shape, BF16),
        ],
        scratch_shapes=[
            pltpu.VMEM((parts, rows, width), BF16),
            pltpu.VMEM((parts, rows, cw), BF16),
            pltpu.VMEM(w_own.shape, BF16),
            *([sem((groups * parts - 1,))] * 2),
            *([sem((parts - 1,))] * 8),
            *([sem((2, line))] * 4),
            sem((line,)), sem((line,)), sem((5,)),
        ],
        compiler_params=pltpu.CompilerParams(
            collective_id=collective_id, has_side_effects=True, vmem_limit_bytes=48 * 2**20
        ),
        name="collect",
    )(hidden, w_in, w_own, chan)


def forward_kernel(
    groups, parts, cw,
    hidden_h, wx_h, gate_h, wo_in, gain_in, gain_out, taps, heads, skip, spread,
    normed_h, px_h, y_h, states_h, z_h, u_h, wz_h, wo,
    hidden, wx, wz, normed, px, y, states, zs, us, xbuf, state, xdt, carried,
    line_s, line_r, core_s, core_r, out_s, out_r, load, store,
):
    line = groups // 2
    cc = cw + 2 * N
    length = px.shape[0]
    chunks = length // CHUNK
    group, q = lax.axis_index("dp"), lax.axis_index("seq")
    z, core = group // 2, lax.rem(group, 2)
    sibling = (2 * z + 1 - core, q)
    peers = seq_peers(parts)
    loads = [
        pltpu.make_async_copy(source, target, load.at[k])
        for k, (source, target) in enumerate(
            [(hidden_h, hidden), (wx_h, wx), (gate_h, wz.at[group])]
        )
    ]
    for copy in loads:
        copy.start()
    greet(peers + dp_peers(groups))

    places = [lax.rem(z + k, line) for k in range(1, line)]

    def plane(k, k_to, device, block):
        return remote(block, block, out_s, out_r, k * (parts + 1) + k_to, device)

    if parts == 4:
        near = [q + 1 - 2 * lax.rem(q, 2), lax.rem(q + 2, 4)]
        half = wo.shape[2] // 2

    def early(k):
        block = wo.at[2 * places[k] + core, q]
        if parts == 4:
            return [plane(k, h, (group, near[h]), block) for h in range(2)]
        return [plane(k, j, peer, block) for j, peer in enumerate(peers)]

    def late(k, h):
        rows = pl.ds(h * half, half)
        block = wo.at[2 * places[k] + core, near[h], rows]
        return plane(k, 2 + h, (group, near[1 - h]), block)

    for k in range(line - 1):
        for copy in early(k):
            copy.start()

    def across(from_z):
        block = wz.at[2 * from_z + core]
        return remote(block, block, core_s, core_r, from_z, sibling)

    gates = LineGather(
        line, z, core, q, lambda from_z: wz.at[2 * from_z + core], wz.at[group], line_s, line_r
    )
    loads[2].wait()
    across(z).start()
    gates.step(0)
    loads[0].wait()

    def norm_rows(i, carry):
        rows = pl.ds(pl.multiple_of(i * 32, 32), 32)
        tokens = hidden[rows, :].astype(F32)
        mean = jnp.sum(tokens * tokens, axis=-1, keepdims=True) / D
        normed[rows, :] = (tokens * lax.rsqrt(mean + EPS_IN) * gain_in[...]).astype(BF16)
        return carry

    lax.fori_loop(0, length // 32, norm_rows, 0)
    loads[1].wait()
    tall = 256

    def project_rows(i, carry):
        rows = pl.ds(pl.multiple_of(i * tall, tall), tall)
        px[rows, :] = dot(normed[rows, :], wx[...])
        return carry

    lax.fori_loop(0, length // tall, project_rows, 0)
    stores = [
        pltpu.make_async_copy(normed, normed_h, store.at[0]),
        pltpu.make_async_copy(px, px_h, store.at[1]),
    ]
    for copy in stores:
        copy.start()
    state[...] = jnp.zeros_like(state)
    xbuf[0:8, :] = jnp.zeros((8, cc), F32)

    def scan_rows(i, carry):
        for t in range(1, line):

            @pl.when(i == min(3 * (t - 1), chunks - 1))
            def _(t=t):
                gates.step(t, lambda from_z: across(from_z).start())

        rows = pl.ds(pl.multiple_of(i * CHUNK, CHUNK), CHUNK)
        scan_forward_step(
            cw, px.at[rows], taps, heads, skip, spread, y.at[rows], states.at[i],
            xbuf, state, xdt, carried,
        )
        return carry

    lax.fori_loop(0, chunks, scan_rows, 0)
    for source, target, at in ((y, y_h, 2), (states, states_h, 3)):
        copy = pltpu.make_async_copy(source, target, store.at[at])
        copy.start()
        stores.append(copy)
    if parts == 4:
        for k in range(line - 1):
            for copy in early(k):
                copy.wait()
            for h in range(2):
                late(k, h).start()
    for from_z in range(line):
        across(from_z).wait_send()
        block = wz.at[2 * from_z + 1 - core]
        remote(block, block, core_s, core_r, from_z, sibling).wait_recv()
    gates.sent()
    copy = pltpu.make_async_copy(wz, wz_h, store.at[4])
    copy.start()
    stores.append(copy)
    lane = lax.broadcasted_iota(jnp.int32, (1, LANES), 1)
    wide = 512

    def gate_rows(i, carry):
        rows = pl.ds(pl.multiple_of(i * tall, tall), tall)
        weights = wz[...].reshape(D, cw)
        gate_in = dot(normed[rows, :], weights)
        zs[rows, :] = gate_in
        gated = y[rows, :] * (gate_in * jax.nn.sigmoid(gate_in))
        us[rows, :cw] = (gated * gain_out[...]).astype(BF16)
        highs = jnp.zeros((tall, LANES), F32)
        rests = jnp.zeros((tall, LANES), F32)
        for b in range(cw // wide):
            block = gated[:, b * wide : (b + 1) * wide]
            total = jnp.sum(block * block, axis=-1, keepdims=True)
            level = level_of(q * cw + b * wide, wide)
            highs = highs + jnp.where(lane == level, total, 0.0)
            rests = rests + jnp.where(lane == level + LEVELS, total, 0.0)
        rests = rests - rests.astype(BF16).astype(F32)
        us[rows, cw:] = jnp.where(lane < LEVELS, highs, rests).astype(BF16)
        return carry

    lax.fori_loop(0, length // tall, gate_rows, 0)
    for source, target, at in ((zs, z_h, 5), (us, u_h, 6)):
        copy = pltpu.make_async_copy(source, target, store.at[at])
        copy.start()
        stores.append(copy)
    for k in range(line - 1):
        if parts == 4:
            for h in range(2):
                late(k, h).wait()
        else:
            for copy in early(k):
                copy.wait()
    for copy in stores:
        copy.wait()


def forward(collective_id, hidden, wx, gate, wo, gain_in, gain_out, taps, heads, skip, spread):
    groups, parts = wo.shape[:2]
    line = groups // 2
    length = hidden.shape[0]
    rows, cw = gate.shape[1:]
    cc = cw + 2 * N
    width = cc + LANES
    chunks = length // CHUNK
    sem = pltpu.SemaphoreType.DMA
    hbm = pl.BlockSpec(memory_space=pltpu.HBM)
    vmem = pl.BlockSpec(memory_space=pltpu.VMEM)
    made = [
        jax.ShapeDtypeStruct((length, D), BF16),
        jax.ShapeDtypeStruct((length, width), F32),
        jax.ShapeDtypeStruct((length, cw), F32),
        jax.ShapeDtypeStruct((chunks, N, cw), BF16),
        jax.ShapeDtypeStruct((length, cw), F32),
        jax.ShapeDtypeStruct((length, cw + LANES), BF16),
    ]
    wz = jax.ShapeDtypeStruct((groups, parts, rows, cw), BF16)
    return pl.pallas_call(
        functools.partial(forward_kernel, groups, parts, cw),
        in_specs=[*([hbm] * 4), *([vmem] * 6)],
        out_specs=[hbm] * 8,
        out_shape=[*made, wz, jax.ShapeDtypeStruct(wo.shape, BF16)],
        input_output_aliases={3: 7},
        scratch_shapes=[
            pltpu.VMEM(hidden.shape, BF16),
            pltpu.VMEM(wx.shape, BF16),
            pltpu.VMEM(wz.shape, BF16),
            *[pltpu.VMEM(m.shape, m.dtype) for m in made],
            pltpu.VMEM((CHUNK + 8, cc), F32),
            pltpu.VMEM((N, cw), F32),
            pltpu.VMEM((CHUNK, cw), BF16),
            pltpu.VMEM((CHUNK, cw), F32),
            sem((2, line)), sem((2, line)), sem((line,)), sem((line,)),
            sem(((line - 1) * (parts + 1),)), sem(((line - 1) * (parts + 1),)),
            sem((3,)), sem((7,)),
        ],
        compiler_params=pltpu.CompilerParams(
            collective_id=collective_id, has_side_effects=True, vmem_limit_bytes=63 * 2**20
        ),
        name="forward",
    )(hidden, wx, gate, wo, gain_in, gain_out, taps, heads, skip, spread)


def swap_out_kernel(groups, parts, u, wo_in, u_out, wo, sends, recvs, core_s, core_r, local):
    group, q = lax.axis_index("dp"), lax.axis_index("seq")
    z, core = group // 2, lax.rem(group, 2)
    sibling = (2 * z + 1 - core, q)
    peers = seq_peers(parts)
    greet(peers + [sibling])
    copies = [
        remote(u.at[peer[1]], u_out.at[q], sends, recvs, k, peer) for k, peer in enumerate(peers)
    ]
    for d in range(groups // 2):
        block = wo.at[2 * d + core]
        copies.append(remote(block, block, core_s, core_r, d, sibling))
    copies.append(pltpu.make_async_copy(u.at[q], u_out.at[q], local))
    for copy in copies:
        copy.start()
    for copy in copies[: parts - 1]:
        copy.wait()
    for d in range(groups // 2):
        copies[parts - 1 + d].wait_send()
        block = wo.at[2 * d + 1 - core]
        remote(block, block, core_s, core_r, d, sibling).wait_recv()
    copies[-1].wait()


def swap_out(collective_id, u, wo):
    groups, parts = wo.shape[:2]
    sem = pltpu.SemaphoreType.DMA
    hbm = pl.BlockSpec(memory_space=pltpu.HBM)
    return pl.pallas_call(
        functools.partial(swap_out_kernel, groups, parts),
        in_specs=[hbm] * 2,
        out_specs=[hbm] * 2,
        out_shape=[jax.ShapeDtypeStruct(u.shape, BF16), jax.ShapeDtypeStruct(wo.shape, BF16)],
        input_output_aliases={1: 1},
        scratch_shapes=[
            sem((parts - 1,)), sem((parts - 1,)), sem((groups // 2,)), sem((groups // 2,)), sem,
        ],
        compiler_params=pltpu.CompilerParams(collective_id=collective_id, has_side_effects=True),
        name="swap_out",
    )(u, wo)


def add_blocks(out, a, b, rows, steps):
    def step(i, carry):
        at = pl.ds(pl.multiple_of(i * rows, rows), rows)
        out[at] = (a[at].astype(F32) + b[at].astype(F32)).astype(out.dtype)
        return carry

    lax.fori_loop(0, steps, step, 0)


def level_of(channel, width):
    return sum((channel >= level_width(k)).astype(jnp.int32) for k in range(LEVELS - 1))


def swap_back_kernel(
    groups, parts, cw, back, u, mixed, back_out, left, right,
    sent, held, sends, recvs, core_s, core_r, local,
):
    line = groups // 2
    group, q = lax.axis_index("dp"), lax.axis_index("seq")
    z, core = group // 2, lax.rem(group, 2)
    sibling = (2 * z + 1 - core, q)
    peers = seq_peers(parts)
    greet(peers + [sibling])
    copies = [
        remote(back.at[peer[1]], back_out.at[q], sends, recvs, k, peer)
        for k, peer in enumerate(peers)
    ]
    copies.append(pltpu.make_async_copy(back.at[q], back_out.at[q], local))
    for copy in copies:
        copy.start()
    width = INNER // groups
    rows = width // parts
    tile = 512
    halves = D // 2 // tile

    def product(of, j):
        channel = of * width
        lanes = pl.ds(pl.multiple_of(lax.rem(channel, cw), width), width)
        cols = pl.ds(pl.multiple_of(j * tile, tile), tile)
        return dot(u[channel // cw, :, lanes], mixed[level_of(channel, width), :, cols], TN)

    cores = []
    for d in range(line):

        def send_step(j, carry, d=d):
            cols = pl.ds(pl.multiple_of(j * tile, tile), tile)
            sent[d, :, cols] = product(2 * d + 1 - core, j).astype(BF16)
            return carry

        lax.fori_loop(0, 2 * halves, send_step, 0)
        copy = remote(sent.at[d], held.at[d], core_s, core_r, d, sibling)
        copy.start()
        cores.append(copy)
    for d in range(line):
        cores[d].wait_recv()
        for out, first in ((left, 0), (right, halves)):

            def keep_step(j, carry, d=d, out=out, first=first):
                at = pl.ds(pl.multiple_of((j + first) * tile, tile), tile)
                cols = pl.ds(pl.multiple_of(j * tile, tile), tile)
                total = product(2 * d + core, j + first) + held[d, :, at].astype(F32)
                total = total.astype(BF16)
                for part in range(parts):
                    out[part, d, :, cols] = total[part * rows : (part + 1) * rows]
                return carry

            lax.fori_loop(0, halves, keep_step, 0)
    for copy in cores:
        copy.wait_send()
    for copy in copies:
        copy.wait()


def swap_back(collective_id, back, u, mixed, groups):
    parts, rows, wide = back.shape
    line, width = groups // 2, INNER // groups
    sem = pltpu.SemaphoreType.DMA
    vmem = pl.BlockSpec(memory_space=pltpu.VMEM)
    hbm = pl.BlockSpec(memory_space=pltpu.HBM)
    return pl.pallas_call(
        functools.partial(swap_back_kernel, groups, parts, wide - LANES),
        in_specs=[hbm, vmem, vmem],
        out_specs=[hbm, vmem, vmem],
        out_shape=[
            jax.ShapeDtypeStruct(back.shape, back.dtype),
            *([jax.ShapeDtypeStruct((parts, line, width // parts, D // 2), BF16)] * 2),
        ],
        scratch_shapes=[
            pltpu.VMEM((line, width, D), BF16),
            pltpu.VMEM((line, width, D), BF16),
            sem((parts - 1,)), sem((parts - 1,)), sem((line,)), sem((line,)), sem,
        ],
        compiler_params=pltpu.CompilerParams(
            collective_id=collective_id, has_side_effects=True, vmem_limit_bytes=63 * 2**20
        ),
        name="swap_back",
    )(back, u, mixed)


def sum_blocks(out, blocks, rows):
    def step(i, carry):
        at = pl.ds(pl.multiple_of(i * rows, rows), rows)
        total = blocks[0][at].astype(F32)
        for block in blocks[1:]:
            total = total + block[at].astype(F32)
        out[at] = total.astype(out.dtype)
        return carry

    lax.fori_loop(0, out.shape[0] // rows, step, 0)


class PlaneSum:
    def __init__(self, parts, group, q, blocks, first, second, sends, recvs):
        self.parts, self.group, self.q = parts, group, q
        self.blocks, self.first, self.second = blocks, first, second
        self.sends, self.recvs = sends, recvs
        self.half = blocks.shape[1] // 2
        if parts == 4:
            self.near = [q + 1 - 2 * lax.rem(q, 2), lax.rem(q + 2, 4)]
            self.far = 3 - q

    @staticmethod
    def scratch(parts, shape, dtype):
        if parts == 4:
            half = (shape[0] // 2,) + shape[1:]
            first, second, count = (2, 2) + half, (2, 2) + half, 6
        else:
            first, second, count = (parts - 1,) + shape, (1, 16, LANES), parts - 1
        sem = pltpu.SemaphoreType.DMA
        return [pltpu.VMEM(first, dtype), pltpu.VMEM(second, dtype), sem((count,)), sem((count,))]

    def piece(self, of, h):
        return self.blocks.at[of, pl.ds(h * self.half, self.half)]

    def early(self, h):
        if self.parts != 4:
            return []
        near = self.near[h]
        to = (self.group, near)
        return [
            remote(self.piece(of, h), self.first.at[h, k], self.sends, self.recvs, 2 * h + k, to)
            for k, of in enumerate((near, self.far))
        ]

    def late(self, h):
        to = (self.group, self.near[1 - h])
        return remote(
            self.second.at[h, 0], self.second.at[h, 1], self.sends, self.recvs, 4 + h, to
        )

    def direct(self):
        peers = seq_peers(self.parts)
        return [
            remote(self.blocks.at[peer[1]], self.first.at[k], self.sends, self.recvs, k, peer)
            for k, peer in enumerate(peers)
        ]

    def start(self, h):
        for copy in self.early(h):
            copy.start()
        if self.parts != 4 and h == 1:
            for copy in self.direct():
                copy.start()

    def turn(self, rows):
        if self.parts != 4:
            return
        for h in range(2):
            for copy in self.early(h):
                copy.wait()
            beyond = self.piece(self.near[1 - h], h)
            each(self.second.at[h, 0], [beyond, self.first.at[h, 1]], rows)
            self.late(h).start()

    def finish(self, out, rows):
        if self.parts != 4:
            for copy in self.direct():
                copy.wait()
            each(
                out,
                [self.blocks.at[self.q]] + [self.first.at[k] for k in range(self.parts - 1)],
                rows,
            )
            return
        for h in range(2):
            self.late(h).wait()
            each(
                out.at[pl.ds(h * self.half, self.half)],
                [self.piece(self.q, h), self.first.at[h, 0], self.second.at[h, 1]],
                rows,
            )


def each(out, blocks, rows):
    if len(out.shape) == 2:
        sum_blocks(out, blocks, rows)
        return
    for d in range(out.shape[0]):
        sum_blocks(out.at[d], [block.at[d] for block in blocks], rows)


class LineSum:
    def __init__(self, line, z, core, q, acc, up, down, up_s, up_r, down_s, down_r, rows, steps):
        self.line, self.z, self.core, self.q = line, z, core, q
        self.acc, self.up, self.down = acc, up, down
        self.up_s, self.up_r, self.down_s, self.down_r = up_s, up_r, down_s, down_r
        self.rows, self.steps = rows, steps

    def ahead(self, d, first):
        block = self.acc.at[d] if first else self.up.at[d]
        to = (2 * (self.z + 1) + self.core, self.q)
        return remote(block, self.up.at[d], self.up_s, self.up_r, d, to)

    def behind(self, d, first):
        block = self.acc.at[d] if first else self.down.at[d]
        to = (2 * (self.z - 1) + self.core, self.q)
        return remote(block, self.down.at[d], self.down_s, self.down_r, d, to)

    def add(self, into, d):
        add_blocks(into.at[d], into.at[d], self.acc.at[d], self.rows, self.steps)

    def step(self, t):
        line, z = self.line, self.z
        far, near = line - 1 - t + z, t - (line - 1 - z)

        @pl.when(z == 0)
        def _():
            self.ahead(line - 1 - t, True).start()

        @pl.when((z > 0) & (z <= t))
        def _():
            self.ahead(far, False).wait_recv()
            self.add(self.up, far)
            self.ahead(far, False).start()

        @pl.when(z == line - 1)
        def _():
            self.behind(t, True).start()

        @pl.when((z < line - 1) & (line - 1 - z <= t))
        def _():
            self.behind(near, False).wait_recv()
            self.add(self.down, near)
            self.behind(near, False).start()

    def sent(self, t):
        line, z = self.line, self.z
        far, near = line - 1 - t + z, t - (line - 1 - z)

        @pl.when(z == 0)
        def _():
            self.ahead(line - 1 - t, True).wait_send()

        @pl.when((z > 0) & (z <= t))
        def _():
            self.ahead(far, False).wait_send()

        @pl.when(z == line - 1)
        def _():
            self.behind(t, True).wait_send()

        @pl.when((z < line - 1) & (line - 1 - z <= t))
        def _():
            self.behind(near, False).wait_send()

    def finish(self, out):
        line, z = self.line, self.z

        @pl.when(z == 0)
        def _():
            self.behind(z, False).wait_recv()
            add_blocks(out, self.acc.at[z], self.down.at[z], self.rows, self.steps)

        @pl.when(z == line - 1)
        def _():
            self.ahead(z, False).wait_recv()
            add_blocks(out, self.acc.at[z], self.up.at[z], self.rows, self.steps)

        @pl.when((z > 0) & (z < line - 1))
        def _():
            self.ahead(z, False).wait_recv()
            self.add(self.up, z)
            self.behind(z, False).wait_recv()
            add_blocks(out, self.up.at[z], self.down.at[z], self.rows, self.steps)


def owners_kernel(
    groups, parts, rows,
    normed, left, right, gate, small, dz, dpx, wz, wx,
    part, left_out, right_out, gate_out, back_out, small_all,
    made, held, acc, up, down, final, left_up, left_down, right_acc, right_up, right_down,
    normed_v, dz_v, dpx_v, wz_v, wx_v, back, back_sum,
    right_1, right_2, right_s, right_r, back_1, back_2, back_s, back_r,
    core_s, core_r, up_s, up_r, down_s, down_r, lup_s, lup_r, ldown_s, ldown_r,
    rup_s, rup_r, rdown_s, rdown_r, part_s, part_r, gate_s, gate_r, small_s, small_r,
    load, local,
):
    line = groups // 2
    span = parts * rows
    group, q = lax.axis_index("dp"), lax.axis_index("seq")
    z, core = group // 2, lax.rem(group, 2)
    sibling = (2 * z + 1 - core, q)
    peers, others = seq_peers(parts), dp_peers(groups)
    tokens = back.shape[1]
    loads = [
        pltpu.make_async_copy(source, target, load.at[k])
        for k, (source, target) in enumerate(
            [(normed, normed_v), (dpx, dpx_v), (dz, dz_v), (wz, wz_v), (wx, wx_v)]
        )
    ]
    for copy in loads:
        copy.start()
    greet(peers + others)
    half_rows = left.shape[1] // 2
    lefts = LineSum(
        line, z, core, q, left, left_up, left_down, lup_s, lup_r, ldown_s, ldown_r, half_rows, 2
    )
    rights = LineSum(
        line, z, core, q, right_acc, right_up, right_down, rup_s, rup_r, rdown_s, rdown_r,
        half_rows, 2,
    )
    wholes = LineSum(
        line, z, core, q, acc, up, down, up_s, up_r, down_s, down_r, rows, parts
    )
    lefts.step(0)
    right_plane = PlaneSum(parts, group, q, right, right_1, right_2, right_s, right_r)
    back_plane = PlaneSum(parts, group, q, back, back_1, back_2, back_s, back_r)
    right_plane.start(0)
    right_plane.start(1)
    waiting = []
    for k, peer in enumerate(peers):
        copy = remote(gate.at[peer[1]], gate_out.at[q], gate_s, gate_r, k, peer)
        copy.start()
        waiting.append(copy)
    for k, peer in enumerate(others):
        copy = remote(small, small_all.at[group], small_s, small_r, k, peer)
        copy.start()
        waiting.append(copy)
    own = [
        pltpu.make_async_copy(gate.at[q], gate_out.at[q], local.at[0]),
        pltpu.make_async_copy(small, small_all.at[group], local.at[1]),
    ]
    for copy in own:
        copy.start()
    loads[0].wait()
    loads[1].wait()
    tile = 512

    def dweight(of, out):
        at = pl.ds(pl.multiple_of(of * span, span), span)
        out[...] = dot(normed_v[:, at], dpx_v[...], TN).astype(BF16)

    cores = {}
    order = [d for k in range(line // 2) for d in (line - 1 - k, k)]

    def share_core(d):
        dweight(2 * d + 1 - core, made.at[d])
        copy = remote(made.at[d], held.at[d], core_s, core_r, d, sibling)
        copy.start()
        cores[d] = copy

    def sum_core(d):
        dweight(2 * d + core, acc.at[d])
        cores[d].wait()
        add_blocks(acc.at[d], acc.at[d], held.at[d], rows, parts)

    share_core(order[0])
    lefts.sent(0)
    lefts.step(1)
    share_core(order[1])
    sum_core(order[0])
    for t in range(2, line - 1):
        lefts.sent(t - 1)
        lefts.step(t)
    sum_core(order[1])
    wholes.step(0)
    for d in order[2:]:
        share_core(d)
    for d in order[2:]:
        sum_core(d)
    for copy in loads[2:]:
        copy.wait()

    def dnormed(of):
        at = pl.ds(pl.multiple_of(of * tokens, tokens), tokens)

        def step(j, carry):
            cols = pl.ds(pl.multiple_of(j * tile, tile), tile)
            back[of, :, cols] = (
                dot(dz_v[at, :], wz_v[cols, :], NT) + dot(dpx_v[at, :], wx_v[cols, :], NT)
            ).astype(BF16)
            return carry

        lax.fori_loop(0, D // tile, step, 0)

    right_plane.turn(32)
    if parts == 4:
        dnormed(back_plane.far)
        dnormed(back_plane.near[0])
        back_plane.start(0)
    wholes.sent(0)
    wholes.step(1)
    if parts == 4:
        dnormed(back_plane.near[1])
    else:
        for peer in peers:
            dnormed(peer[1])
    back_plane.start(1)
    dnormed(q)
    right_plane.finish(right_acc, 32)
    for t in range(2, line - 1):
        wholes.sent(t - 1)
        wholes.step(t)
    back_plane.turn(32)
    lefts.finish(left_out)
    lefts.sent(line - 2)
    wholes.sent(line - 2)
    rights.step(0)
    wholes.finish(final)
    for k, peer in enumerate(peers):
        block = final.at[pl.ds(pl.multiple_of(peer[1] * rows, rows), rows)]
        copy = remote(block, part.at[q], part_s, part_r, k, peer)
        copy.start()
        waiting.append(copy)
    copy = pltpu.make_async_copy(
        final.at[pl.ds(pl.multiple_of(q * rows, rows), rows)], part.at[q], local.at[2]
    )
    copy.start()
    own.append(copy)
    rights.sent(0)
    rights.step(1)
    back_plane.finish(back_sum, 32)
    copy = pltpu.make_async_copy(back_sum, back_out, local.at[3])
    copy.start()
    own.append(copy)
    for t in range(2, line - 1):
        rights.sent(t - 1)
        rights.step(t)
    rights.finish(right_out)
    rights.sent(line - 2)
    for copy in own + waiting:
        copy.wait()


def sum_to_owners(collective_id, normed, left, right, gate, small, dz, dpx, wz, wx):
    parts, line, out_rows, half = right.shape
    groups = 2 * line
    rows = gate.shape[1]
    span, width = rows * parts, dpx.shape[1]
    tokens = dz.shape[0] // parts
    sem = pltpu.SemaphoreType.DMA
    vmem = pl.BlockSpec(memory_space=pltpu.VMEM)
    hbm = pl.BlockSpec(memory_space=pltpu.HBM)
    return pl.pallas_call(
        functools.partial(owners_kernel, groups, parts, rows),
        in_specs=[hbm, vmem, vmem, hbm, vmem, hbm, hbm, hbm, hbm],
        out_specs=[hbm, vmem, vmem, hbm, hbm, vmem],
        out_shape=[
            jax.ShapeDtypeStruct((parts, rows, width), BF16),
            *([jax.ShapeDtypeStruct((out_rows, half), F32)] * 2),
            jax.ShapeDtypeStruct(gate.shape, BF16),
            jax.ShapeDtypeStruct((tokens, D), F32),
            jax.ShapeDtypeStruct((groups,) + small.shape, F32),
        ],
        scratch_shapes=[
            *([pltpu.VMEM((line, span, width), BF16)] * 5),
            pltpu.VMEM((span, width), BF16),
            *([pltpu.VMEM(left.shape, BF16)] * 5),
            *[pltpu.VMEM(a.shape, BF16) for a in (normed, dz, dpx, wz, wx)],
            pltpu.VMEM((parts, tokens, D), BF16),
            pltpu.VMEM((tokens, D), F32),
            *PlaneSum.scratch(parts, right.shape[1:], BF16),
            *PlaneSum.scratch(parts, (tokens, D), BF16),
            *([sem((line,))] * 14),
            *([sem((parts - 1,))] * 4),
            *([sem((groups - 1,))] * 2),
            sem((5,)),
            sem((4,)),
        ],
        compiler_params=pltpu.CompilerParams(
            collective_id=collective_id, has_side_effects=True, vmem_limit_bytes=63 * 2**20
        ),
        name="sum_to_owners",
    )(normed, left, right, gate, small, dz, dpx, wz, wx)


def unpack_terms(packed, count):
    packed = packed.astype(F32)
    return packed[..., :count] + packed[..., count : 2 * count]


def on_device(
    hidden_in, out_grads, w_in, w_in_m, w_in_v, w_out, w_out_m, w_out_v,
    chan_params, chan_m, chan_v, head_params, head_m, head_v,
):
    parts = lax.axis_size("seq")
    groups = lax.axis_size("dp")
    q = lax.axis_index("seq")
    rows = hidden_in.shape[1]
    length = rows * parts
    cw = INNER // parts
    hq = H // parts
    cc = cw + 2 * N
    in_rows = w_in.shape[0]
    out_rows = w_out.shape[0]

    chan_len = chan_params.shape[0]
    chan_rows = -(-chan_len // (8 * LANES)) * 8
    chan_block = jnp.pad(
        lax.reduce_precision(chan_params, 8, 7), (0, chan_rows * LANES - chan_len)
    ).reshape(chan_rows, LANES)
    hidden, wx, gate, chan_full, wo = collect(
        0, hidden_in[0], w_in, w_out, chan_block, groups, parts
    )
    chan_full = chan_full.reshape(groups * parts, chan_rows * LANES)[:, :chan_len].reshape(-1)
    line = groups // 2
    group = lax.axis_index("dp")

    conv_taps = chan_full[: TAPS * CONV_CH].reshape(TAPS, CONV_CH)
    conv_bias = chan_full[TAPS * CONV_CH : (TAPS + 1) * CONV_CH].reshape(1, CONV_CH)
    offset = (TAPS + 1) * CONV_CH
    gain_in = chan_full[offset : offset + D]
    gain_out = chan_full[offset + D : offset + D + INNER]
    taps_all = jnp.concatenate(
        [conv_taps, conv_bias, jnp.zeros((8 - TAPS - 1, CONV_CH), F32)], axis=0
    )
    taps = jnp.concatenate(
        [lax.dynamic_slice(taps_all, (0, q * cw), (8, cw)), taps_all[:, INNER:]], axis=1
    )
    own_gain = lax.dynamic_slice(gain_out, (q * cw,), (cw,))
    own_heads = lax.dynamic_slice(head_params, (0, q * hq), (3, hq))
    heads = jnp.pad(
        jnp.stack([own_heads[0], -jnp.exp(own_heads[1])]), ((0, 6), (0, LANES - hq))
    )
    skip = jnp.repeat(own_heads[2], P_SIZE).reshape(1, cw)
    spread = (
        jnp.arange(LANES)[:, None] == (jnp.arange(cw) // P_SIZE)[None, :]
    ).astype(BF16)

    normed, px, y, states, z, u_blocks, wz, wo = forward(
        1, hidden.reshape(length, D), wx.reshape(D, cc + LANES), gate, wo, gain_in.reshape(1, D),
        own_gain.reshape(1, cw), taps, heads, skip, spread,
    )
    wx, wz = wx.reshape(D, cc + LANES), wz.reshape(D, cw)
    u, wo = swap_out(2, u_blocks.reshape(parts, rows, cw + LANES), wo)
    wo = wo.reshape(INNER, D)
    sig = jax.nn.sigmoid(z)
    gate = z * sig
    gated = y * gate
    channel = q * cw + jnp.arange(cw)

    cotangent = out_grads[:, 0]
    block_out, back_blocks, mixed = widths(u, wo, cotangent, hidden_in[0])
    block_out = block_out[:, None]
    back_own, dwo_left, dwo_right = swap_back(3, back_blocks, u, mixed, groups)
    back_own = back_own.reshape(length, cw + LANES)

    coefs = unpack_terms(back_own[:, cw:], LEVELS)
    pull = coefs[:, LEVELS - 1 :]
    for k in reversed(range(LEVELS - 1)):
        pull = jnp.where(channel[None, :] < level_width(k), coefs[:, k : k + 1], pull)
    back = back_own[:, :cw].astype(F32)
    dgated = own_gain * back - gated * pull
    dgain_out = jnp.sum(back * gated, axis=0)
    dz = (dgated * y * (sig + gate * (1.0 - sig))).astype(BF16)
    dy = dgated * gate
    dwz = dot(normed, dz, TN).astype(BF16)
    dwz = dwz.reshape(line, 2, parts * in_rows, cw)
    dpx, dtaps, dheads, dskip, dwo_left, dwz = scan_backward(
        5, px, taps, heads, skip, spread, spread.T, dy, y, states, dwo_left, dwz
    )
    skip_grad = jnp.sum(dskip[0].reshape(hq, P_SIZE), axis=-1)
    small = jnp.concatenate(
        [dtaps[: TAPS + 1].reshape(-1), dgain_out, dheads[0, :hq], dheads[1, :hq], skip_grad]
    )
    small_rows = -(-small.shape[0] // (8 * LANES)) * 8
    small = jnp.pad(small, (0, small_rows * LANES - small.shape[0])).reshape(small_rows, LANES)
    x_part, left_part, right_part, z_part, dnormed, small = sum_to_owners(
        4, normed, dwo_left, dwo_right, dwz.reshape(parts, in_rows, cw), small, dz, dpx, wz, wx
    )
    hidden_grad, chan_total, head_total, norm = gradient_norm(
        6, x_part, z_part, left_part, right_part, dnormed, small, hidden_in[0],
        gain_in.reshape(1, D), cotangent, groups,
    )
    (
        hidden_grad, w_in_new, w_in_m_new, w_in_v_new, w_in_copy,
        w_out_new, w_out_m_new, w_out_v_new, w_out_copy,
    ) = update_weights(
        norm, x_part, z_part, left_part, right_part, hidden_grad,
        (w_in, w_in_m, w_in_v, w_out, w_out_m, w_out_v),
    )
    hidden_grad = hidden_grad[None]
    grad_norm, clip_factor = norm[0, 0], norm[1, 0]
    owner = group * parts + q
    chan_part = lax.dynamic_slice(chan_total.reshape(-1), (owner * chan_len,), (chan_len,))
    head_total = head_total[:parts, : 3 * hq].reshape(parts, 3, hq)
    head_total = head_total.transpose(1, 0, 2).reshape(3, H)
    chan_new, chan_m_new, chan_v_new = adam_tile(
        chan_params, clip_factor * chan_part, chan_m, chan_v, 0.2, 0.0
    )
    head_new, head_m_new, head_v_new = adam_tile(
        head_params, clip_factor * head_total, head_m, head_v, 1.0, 0.0
    )
    return (
        block_out, hidden_grad, grad_norm,
        w_in_new, w_in_m_new, w_in_v_new, w_in_copy,
        w_out_new, w_out_m_new, w_out_v_new, w_out_copy,
        chan_new, chan_m_new, chan_v_new, head_new, head_m_new, head_v_new,
    )


def solution(mesh):
    rows = P(("dp", "seq"), None)
    flat = P(("dp", "seq"))
    in_specs = (
        P("dp", "seq", None),
        P(None, "dp", "seq", None),
        *([rows] * 6),
        *([flat] * 3),
        *([P()] * 3),
    )
    out_specs = (
        P(None, "dp", "seq", None),
        P("dp", "seq", None),
        P(),
        *([rows] * 8),
        *([flat] * 3),
        *([P()] * 3),
    )
    return jax.shard_map(
        on_device, mesh=mesh, in_specs=in_specs, out_specs=out_specs, check_vma=False
    )
```

```python
import functools

import jax
import jax.numpy as jnp
from jax import lax
from jax.experimental import pallas as pl
from jax.experimental.pallas import tpu as pltpu
from jax.sharding import PartitionSpec as P

D = 2048
INNER = 4096
H = 64
P_SIZE = 64
N = 128
TAPS = 4
STEP = 10
E_IN = 8512
CONV_CH = 4352
LANES = 128
CHUNK = 128
LEVELS = 4

EXACT = lax.Precision.HIGHEST
EPS_IN = 1e-06
EPS_OUT = 1e-05
ADAM_EPS = 1e-08
BETA = 0.5
CLIP = 1.0
F32 = jnp.float32
BF16 = jnp.bfloat16
MASKED = -1e30


def level_width(level):
    return INNER * 2**level // 8


SEGMENTS = tuple(
    (0 if level == 0 else level_width(level - 1), level_width(level)) for level in range(LEVELS)
)


def dot(a, b, dims=((1,), (0,)), precision=None):
    return lax.dot_general(a, b, (dims, ((), ())), precision=precision, preferred_element_type=F32)


NT = ((1,), (1,))
TN = ((0,), (0,))


def softplus(v):
    return jnp.maximum(v, 0.0) + jnp.log1p(jnp.exp(-jnp.abs(v)))


def two_terms(v):
    high = v.astype(BF16)
    return high, (v - high.astype(F32)).astype(BF16)


def spread_heads(v, spread):
    high, rest = two_terms(v)
    return dot(high, spread) + dot(rest, spread)


def own_heads_first(dt_raw, hq, back=False):
    by = lax.axis_index("seq") * hq
    return pltpu.roll(dt_raw, by if back else lax.rem(LANES - by, LANES), 1)


def rates(dt_raw, heads):
    step = softplus(dt_raw + heads[0:1, :])
    return step, step * heads[1:2, :]


def triangle(size):
    row = lax.broadcasted_iota(jnp.int32, (size, size), 0)
    col = lax.broadcasted_iota(jnp.int32, (size, size), 1)
    return row, col


def conv_block(taps, xbuf, lanes):
    out = taps[TAPS : TAPS + 1, lanes]
    for tap in range(TAPS):
        out = out + taps[tap : tap + 1, lanes] * xbuf[5 + tap : 5 + tap + CHUNK, lanes]
    return out


def pair_decay(cum, cum_t, causal, head):
    gap = cum[:, head : head + 1] - cum_t[head : head + 1, :]
    return jnp.exp(jnp.where(causal, gap, MASKED))


def scan_forward_step(cw, px, taps, heads, skip, spread, y, states, xbuf, state, xdt, carried):
    cc = cw + 2 * N
    xbuf[8 : 8 + CHUNK, :] = px[:, :cc]
    step, rate = rates(own_heads_first(px[:, cc:], cw // P_SIZE), heads)
    row, col = triangle(CHUNK)
    causal = row >= col
    cum = dot(causal.astype(F32), rate, precision=EXACT)
    cum_t = cum.T
    spread_m = spread[...]
    last = cum[CHUNK - 1 : CHUNK, :]
    step_x = spread_heads(step, spread_m)
    grow_x = spread_heads(jnp.exp(cum), spread_m)
    tail_x = spread_heads(jnp.exp(last - cum), spread_m)

    def activated(lanes):
        conv = conv_block(taps, xbuf, lanes)
        return conv * jax.nn.sigmoid(conv)

    state_in = activated(slice(cw, cw + N))
    state_out = activated(slice(cw + N, cw + 2 * N))
    scores = dot(state_out, state_in, NT, EXACT)
    states[...] = state[...].astype(BF16)
    carried[...] = dot(state_out.astype(BF16), state[...].astype(BF16))
    first = lax.broadcasted_iota(jnp.int32, (1, LANES), 1) < P_SIZE
    for pair in range(cw // LANES):
        lanes = slice(pair * LANES, (pair + 1) * LANES)
        x = activated(lanes)
        xd = (x * step_x[:, lanes]).astype(BF16).astype(F32)
        xdt[:, lanes] = (xd * tail_x[:, lanes]).astype(BF16)
        stacked = jnp.concatenate([jnp.where(first, xd, 0.0), jnp.where(first, 0.0, xd)], axis=0)
        mixing = jnp.concatenate(
            [
                (pair_decay(cum, cum_t, causal, 2 * pair + k) * scores).astype(BF16)
                for k in range(2)
            ],
            axis=1,
        )
        y[:, lanes] = (
            dot(mixing, stacked.astype(BF16))
            + grow_x[:, lanes] * carried[:, lanes]
            + skip[:, lanes] * x
        )
    state[...] = grow_x[CHUNK - 1 : CHUNK, :] * state[...] + dot(
        state_in.astype(BF16), xdt[...], TN
    )
    xbuf[0:8, :] = xbuf[CHUNK : CHUNK + 8, :]


def scan_backward_step(
    cw, start, px, halo, taps, heads, skip, spread, gather, dy, y, states,
    dpx, dtaps, dheads, dskip,
    xbuf, dstate, dcbuf, slope, xact, xd_s, dxd_s, acc_s,
):
    cc = cw + 2 * N
    xbuf[0:8, :] = jnp.where(start, 0.0, halo[:, :cc])
    xbuf[8 : 8 + CHUNK, :] = px[:, :cc]
    dt_raw = own_heads_first(px[:, cc:], cw // P_SIZE)
    step, rate = rates(dt_raw, heads)
    row, col = triangle(CHUNK)
    causal = row >= col
    cum = dot(causal.astype(F32), rate, precision=EXACT)
    cum_t = cum.T
    spread_m = spread[...]
    last = cum[CHUNK - 1 : CHUNK, :]
    step_x = spread_heads(step, spread_m)
    grow_x = spread_heads(jnp.exp(cum), spread_m)
    tail_x = spread_heads(jnp.exp(last - cum), spread_m)

    for block in range(cc // LANES):
        lanes = slice(block * LANES, (block + 1) * LANES)
        conv = conv_block(taps, xbuf, lanes)
        sig = jax.nn.sigmoid(conv)
        act = conv * sig
        xact[:, lanes] = act
        slope[:, lanes] = sig + act * (1.0 - sig)
    state_in = xact[:, cw : cw + N]
    state_out = xact[:, cw + N : cc]
    scores = dot(state_out, state_in, NT, EXACT)
    in_low = state_in.astype(BF16)
    out_low = state_out.astype(BF16)
    dstate_low = dstate[...].astype(BF16)
    acc_s[...] = jnp.zeros_like(acc_s)
    dxd_s[...] = tail_x * dot(in_low, dstate_low)
    dskip[0:1, :] += jnp.sum(xact[:, :cw] * dy[...], axis=0, keepdims=True)
    first = lax.broadcasted_iota(jnp.int32, (1, LANES), 1) < P_SIZE
    xd_s[...] = (xact[:, :cw] * step_x).astype(BF16)
    total = jnp.sum(xd_s[...].astype(F32) * dxd_s[...], axis=0, keepdims=True) + grow_x[
        CHUNK - 1 : CHUNK, :
    ] * jnp.sum(dstate[...] * states[...].astype(F32), axis=0, keepdims=True)
    dscores = jnp.zeros((CHUNK, CHUNK), F32)
    for pair in range(cw // LANES):
        lanes = slice(pair * LANES, (pair + 1) * LANES)
        dyp = dy[:, lanes]
        stacked = jnp.concatenate(
            [jnp.where(first, dyp, 0.0), jnp.where(first, 0.0, dyp)], axis=0
        ).astype(BF16)
        decays = [pair_decay(cum, cum_t, causal, 2 * pair + k) for k in range(2)]
        mixing = jnp.concatenate([(decay * scores).astype(BF16) for decay in decays], axis=0)
        dxd_s[:, lanes] += dot(mixing, stacked, TN)
        dmix = dot(stacked, xd_s[:, lanes], NT)
        dscores = dscores + decays[0] * dmix[:CHUNK] + decays[1] * dmix[CHUNK:]
    dy_low = dy[...].astype(BF16)
    dy_f = dy_low.astype(F32)
    xd_f = xd_s[...].astype(F32)
    dxd = dxd_s[...]
    y_scan = y[...] - skip[...] * xact[:, :cw]
    final = lax.broadcasted_iota(jnp.int32, (CHUNK, 1), 0) == CHUNK - 1
    gather_m = gather[...]
    dcum = spread_heads(dy_f * y_scan - xd_f * dxd + jnp.where(final, total, 0.0), gather_m)
    dstep = spread_heads(xact[:, :cw] * dxd, gather_m)
    drate = dot((row <= col).astype(F32), dcum, precision=EXACT)
    dstep = dstep + drate * heads[1:2, :]
    ddt = dstep * jax.nn.sigmoid(dt_raw + heads[0:1, :])
    dheads[0:1, :] += jnp.sum(ddt, axis=0, keepdims=True)
    dheads[1:2, :] += jnp.sum(drate * rate, axis=0, keepdims=True)
    grown = (grow_x * dy_f).astype(BF16)
    dscores_low = dscores.astype(BF16)
    dout = dot(dscores_low, in_low) + dot(grown, states[...], NT)
    din = dot(dscores_low, out_low, TN) + dot((tail_x * xd_f).astype(BF16), dstate_low, NT)
    dstate[...] = grow_x[CHUNK - 1 : CHUNK, :] * dstate[...] + dot(out_low, grown, TN)
    dcbuf[:CHUNK, :cw] = (step_x * dxd + skip[...] * dy[...]) * slope[:, :cw]
    dcbuf[:CHUNK, cw : cw + N] = din * slope[:, cw : cw + N]
    dcbuf[:CHUNK, cw + N :] = dout * slope[:, cw + N :]
    for block in range(cc // LANES):
        lanes = slice(block * LANES, (block + 1) * LANES)
        dconv = dcbuf[:CHUNK, lanes]
        dtaps[TAPS : TAPS + 1, lanes] += jnp.sum(dconv, axis=0, keepdims=True)
        back = taps[TAPS - 1 : TAPS, lanes] * dconv
        for tap in range(TAPS):
            dtaps[tap : tap + 1, lanes] += jnp.sum(
                dconv * xbuf[5 + tap : 5 + tap + CHUNK, lanes], axis=0, keepdims=True
            )
            if tap < TAPS - 1:
                reach = TAPS - 1 - tap
                back = back + taps[tap : tap + 1, lanes] * dcbuf[reach : reach + CHUNK, lanes]
        dpx[:, lanes] = back.astype(BF16)
    ours = lax.broadcasted_iota(jnp.int32, (1, LANES), 1) < cw // P_SIZE
    ddt = own_heads_first(jnp.where(ours, ddt, 0.0), cw // P_SIZE, back=True)
    dpx[:, cc:] = ddt.astype(BF16)
    dcbuf[CHUNK : CHUNK + 8, :] = dcbuf[0:8, :]


WIDE = 512


MESH = pl.DeviceIdType.MESH


def remote(src, dst, sends, recvs, index, device):
    return pltpu.make_async_remote_copy(
        src_ref=src,
        dst_ref=dst,
        send_sem=sends.at[index],
        recv_sem=recvs.at[index],
        device_id=device,
        device_id_type=MESH,
    )


def greet(devices):
    barrier = pltpu.get_barrier_semaphore()
    for device in devices:
        pl.semaphore_signal(barrier, inc=1, device_id=device, device_id_type=MESH)
    pl.semaphore_wait(barrier, len(devices))


def seq_peers(parts):
    group, q = lax.axis_index("dp"), lax.axis_index("seq")
    return [(group, lax.rem(q + k, parts)) for k in range(1, parts)]


def dp_peers(groups):
    group, q = lax.axis_index("dp"), lax.axis_index("seq")
    return [(lax.rem(group + k, groups), q) for k in range(1, groups)]


def all_peers(groups, parts):
    devices = groups * parts
    me = lax.axis_index("dp") * parts + lax.axis_index("seq")
    peers = []
    for k in range(1, devices):
        other = lax.rem(me + k, devices)
        peers.append((other // parts, lax.rem(other, parts)))
    return peers


CHAN_ROWS = ((TAPS + 1) * CONV_CH + D + INNER) // LANES


def adam_tile(weight, gradient, moment, second, step_rate, weight_decay):
    new_moment = BETA * moment + (1.0 - BETA) * gradient
    new_second = BETA * second + (1.0 - BETA) * gradient * gradient
    correction = 1.0 - BETA**STEP
    update = new_moment / correction / (jnp.sqrt(new_second / correction) + ADAM_EPS)
    return weight - step_rate * (update + weight_decay * weight), new_moment, new_second


def total_of(value):
    return jnp.sum(jnp.sum(value, axis=1, keepdims=True), axis=0, keepdims=True)


def norm_kernel(
    groups, parts,
    part_h, gate_h, left_h, right_h, back_h, small_h, hidden_h, gain, cotangent,
    hidden_grad, chan, head, norm,
    part, gate, left, right, back, small, hidden,
    cot_v, block, near, all_block, all_near, sends, recvs, near_s, near_r, load, local,
):
    group, q = lax.axis_index("dp"), lax.axis_index("seq")
    me = group * parts + q
    cw = INNER // parts
    cc = cw + 2 * N
    everyone = all_peers(groups, parts)
    fetches = [
        pltpu.make_async_copy(source, target, load.at[k])
        for k, (source, target) in enumerate(
            [(back_h, back), (hidden_h, hidden), (part_h, part), (gate_h, gate),
             (left_h, left), (right_h, right), (small_h, small), (cotangent, cot_v)]
        )
    ]
    for copy in fetches:
        copy.start()
    barrier = pltpu.get_barrier_semaphore()
    for device in everyone:
        pl.semaphore_signal(barrier, inc=1, device_id=device, device_id_type=MESH)
    for copy in fetches[:7]:
        copy.wait()
    total = small[0]
    for k in range(1, groups):
        total = total + small[k]
    near[...] = total
    rows = 32

    def summed(at):
        down = back[at, :]
        tokens = hidden[at, :].astype(F32)
        mean = jnp.sum(tokens * tokens, axis=-1, keepdims=True) / D
        return down, tokens, lax.rsqrt(mean + EPS_IN)

    def gain_rows(i, dgain):
        at = pl.ds(pl.multiple_of(i * rows, rows), rows)
        down, tokens, scale = summed(at)
        return dgain + jnp.sum(down * tokens * scale, axis=0, keepdims=True)

    dgain = lax.fori_loop(0, hidden.shape[0] // rows, gain_rows, jnp.zeros((1, D), F32))
    tail = part[0, :, cw : cc + H].astype(F32)
    for k in range(1, parts):
        tail = tail + part[k, :, cw : cc + H].astype(F32)
    squares = total_of(tail * tail)
    for k in range(parts):
        x = part[k, :, :cw].astype(F32)
        g = gate[k].astype(F32)
        squares = squares + total_of(x * x + g * g)
    squares = squares + total_of(left[...] * left[...] + right[...] * right[...])
    for k in range(D // LANES):
        block[k : k + 1, :] = dgain[:, k * LANES : (k + 1) * LANES]
    block[D // LANES :, :] = jnp.broadcast_to(squares, (8, LANES))
    pl.semaphore_wait(barrier, len(everyone))
    copies = [
        remote(block, all_block.at[me], sends, recvs, k, peer) for k, peer in enumerate(everyone)
    ]
    copies += [
        remote(near, all_near.at[q], near_s, near_r, k, peer)
        for k, peer in enumerate(seq_peers(parts))
    ]
    copies += [
        pltpu.make_async_copy(block, all_block.at[me], local.at[0]),
        pltpu.make_async_copy(near, all_near.at[q], local.at[1]),
    ]
    for copy in copies:
        copy.start()
    fetches[7].wait()

    def grad_rows(i, carry):
        at = pl.ds(pl.multiple_of(i * rows, rows), rows)
        down, tokens, scale = summed(at)
        scaled = down * gain[...]
        inner = jnp.sum(scaled * tokens, axis=-1, keepdims=True) / D
        direct = cot_v[0, at, :].astype(F32)
        for k in range(1, LEVELS):
            direct = direct + cot_v[k, at, :].astype(F32)
        hidden_grad[at, :] = (
            scale * scaled - tokens * (scale * scale * scale * inner) + direct
        )
        return carry

    lax.fori_loop(0, hidden.shape[0] // rows, grad_rows, 0)
    for copy in copies:
        copy.wait()
    total = jnp.sum(all_block[...], axis=0)
    own, wide = cw // LANES, cc // LANES
    span = CONV_CH // LANES
    for tap in range(TAPS + 1):
        for k in range(parts):
            at = tap * span + k * own
            chan[at : at + own, :] = all_near[k, tap * wide : tap * wide + own, :]
        shared = all_near[0, tap * wide + own : (tap + 1) * wide, :]
        for k in range(1, parts):
            shared = shared + all_near[k, tap * wide + own : (tap + 1) * wide, :]
        chan[tap * span + INNER // LANES : (tap + 1) * span, :] = shared
    at = (TAPS + 1) * span
    chan[at : at + D // LANES, :] = total[: D // LANES]
    at = at + D // LANES
    for k in range(parts):
        first = (TAPS + 1) * wide
        chan[at + k * own : at + (k + 1) * own, :] = all_near[k, first : first + own, :]
        head[k : k + 1, :] = all_near[k, first + own : first + own + 1, :]
    squares = (
        total[D // LANES : D // LANES + 1, :1]
        + total_of(chan[:CHAN_ROWS, :] * chan[:CHAN_ROWS, :])
        + total_of(head[:parts, :] * head[:parts, :])
    )
    grad_norm = jnp.sqrt(squares)
    norm[0:1, :] = jnp.broadcast_to(grad_norm, (1, LANES))
    norm[1:2, :] = jnp.broadcast_to(jnp.minimum(1.0, CLIP / grad_norm), (1, LANES))


def gradient_norm(
    collective_id, part, gate, left, right, back, small, hidden, gain, cotangent, groups
):
    parts = part.shape[0]
    devices = groups * parts
    sem = pltpu.SemaphoreType.DMA
    vmem = pl.BlockSpec(memory_space=pltpu.VMEM)
    hbm = pl.BlockSpec(memory_space=pltpu.HBM)
    block = (D // LANES + 8, LANES)
    chan_rows = -(-CHAN_ROWS // 8) * 8
    return pl.pallas_call(
        functools.partial(norm_kernel, groups, parts),
        in_specs=[*([hbm] * 7), vmem, hbm],
        out_specs=[vmem] * 4,
        out_shape=[
            jax.ShapeDtypeStruct(hidden.shape, F32),
            jax.ShapeDtypeStruct((chan_rows, LANES), F32),
            jax.ShapeDtypeStruct((8, LANES), F32),
            jax.ShapeDtypeStruct((8, LANES), F32),
        ],
        scratch_shapes=[
            *[pltpu.VMEM(a.shape, a.dtype) for a in (part, gate, left, right, back, small, hidden)],
            pltpu.VMEM(cotangent.shape, BF16),
            pltpu.VMEM(block, F32),
            pltpu.VMEM(small.shape[1:], F32),
            pltpu.VMEM((devices,) + block, F32),
            pltpu.VMEM((parts,) + small.shape[1:], F32),
            sem((devices - 1,)), sem((devices - 1,)), sem((parts - 1,)), sem((parts - 1,)),
            sem((8,)), sem((2,)),
        ],
        compiler_params=pltpu.CompilerParams(
            collective_id=collective_id, has_side_effects=True, vmem_limit_bytes=63 * 2**20
        ),
        name="gradient_norm",
    )(part, gate, left, right, back, small, hidden, gain, cotangent)


BLOCKS = 4


def update_kernel(
    parts, norm, part_h, gate_h, left_h, right_h, hidden_grad, *refs
):
    ins, refs = refs[:6], refs[6:]
    hidden_out, outs, refs = refs[0], refs[1:9], refs[9:]
    held, made = refs[:6], refs[6:14]
    part, gate, left, right, hidden_v, load, store, grads = refs[14:]
    clip = norm[1:2, :1]
    cw = INNER // parts
    cc = cw + 2 * N
    fetches = [
        pltpu.make_async_copy(source, target, grads.at[k])
        for k, (source, target) in enumerate(
            [(part_h, part), (gate_h, gate), (left_h, left), (right_h, right),
             (hidden_grad, hidden_v)]
        )
    ]
    for copy in fetches:
        copy.start()

    def at(a, i):
        rows = ins[a].shape[0] // BLOCKS
        return pl.ds(i * rows, rows)

    loads = [
        [
            pltpu.make_async_copy(ins[a].at[at(a, i)], held[a].at[at(a, i)], load.at[a * BLOCKS + i])
            for a in range(6)
        ]
        for i in range(BLOCKS)
    ]
    for weight in (0, 3):
        for i in range(BLOCKS):
            for a in range(weight, weight + 3):
                loads[i][a].start()
    stores = []

    def update(weight, rows, lanes, gradient, rate, decay):
        first = 0 if weight == 0 else 4
        new, moment, second = adam_tile(
            held[weight][rows, lanes], clip * gradient, held[weight + 1][rows, lanes],
            held[weight + 2][rows, lanes], rate, decay,
        )
        made[first][rows, lanes] = new
        made[first + 1][rows, lanes] = moment
        made[first + 2][rows, lanes] = second
        made[first + 3][rows, lanes] = new.astype(BF16)

    def send(first, rows, i):
        for a in range(first, first + 4):
            copy = pltpu.make_async_copy(
                made[a].at[rows], outs[a].at[rows], store.at[a * BLOCKS + i]
            )
            copy.start()
            stores.append(copy)

    for copy in fetches[:4]:
        copy.wait()
    for i in range(BLOCKS):
        rows = at(0, i)
        for a in range(3):
            loads[i][a].wait()
        for source, first in ((gate, 0), (part, INNER)):

            def step(k, carry, source=source, first=first, rows=rows):
                to = pl.ds(pl.multiple_of(first + k * cw, cw), cw)
                update(0, rows, to, source[k, rows, :cw].astype(F32), 0.02, 0.1)
                return carry

            lax.fori_loop(0, parts, step, 0)
        tail = part[0, rows, cw : cc + H].astype(F32)
        for k in range(1, parts):
            tail = tail + part[k, rows, cw : cc + H].astype(F32)
        update(0, rows, slice(2 * INNER, E_IN), tail, 0.02, 0.1)
        send(0, rows, i)
    fetches[4].wait()
    pass_on = pltpu.make_async_copy(hidden_v, hidden_out, grads.at[5])
    pass_on.start()
    half = D // 2
    for i in range(BLOCKS):
        rows = at(3, i)
        for a in range(3, 6):
            loads[i][a].wait()
        update(3, rows, slice(0, half), left[rows, :], 0.03, 0.1)
        update(3, rows, slice(half, D), right[rows, :], 0.03, 0.1)
        send(4, rows, i)
    pass_on.wait()
    for copy in stores:
        copy.wait()


def update_weights(norm, part, gate, left, right, hidden_grad, weights):
    parts = part.shape[0]
    w_in, w_out = weights[0], weights[3]
    sem = pltpu.SemaphoreType.DMA
    vmem = pl.BlockSpec(memory_space=pltpu.VMEM)
    hbm = pl.BlockSpec(memory_space=pltpu.HBM)
    made = [
        jax.ShapeDtypeStruct(w.shape, dtype) for w in (w_in, w_out) for dtype in (F32, F32, F32, BF16)
    ]
    return pl.pallas_call(
        functools.partial(update_kernel, parts),
        in_specs=[vmem, *([hbm] * 11)],
        out_specs=[hbm] * 9,
        out_shape=[jax.ShapeDtypeStruct(hidden_grad.shape, F32), *made],
        scratch_shapes=[
            *[pltpu.VMEM(w.shape, F32) for w in weights],
            *[pltpu.VMEM(m.shape, m.dtype) for m in made],
            *[pltpu.VMEM(a.shape, a.dtype) for a in (part, gate, left, right, hidden_grad)],
            sem((6 * BLOCKS,)), sem((8 * BLOCKS,)), sem((6,)),
        ],
        compiler_params=pltpu.CompilerParams(vmem_limit_bytes=63 * 2**20),
        name="update_weights",
    )(norm, part, gate, left, right, hidden_grad, *weights)


class LineGather:
    def __init__(self, line, z, core, q, slot, own, sends, recvs):
        self.line, self.z, self.core, self.q = line, z, core, q
        self.slot, self.own, self.sends, self.recvs = slot, own, sends, recvs

    def along(self, from_z, up, first=False):
        to = self.z + 1 if up else self.z - 1
        return remote(
            self.own if first else self.slot(from_z),
            self.slot(from_z),
            self.sends.at[0 if up else 1],
            self.recvs.at[0 if up else 1],
            from_z,
            (2 * to + self.core, self.q),
        )

    def step(self, t, got=None):
        line, z = self.line, self.z
        low, high = z - t, z + t
        if t == 0:

            @pl.when(z < line - 1)
            def _():
                self.along(z, True, True).start()

            @pl.when(z > 0)
            def _():
                self.along(z, False, True).start()

            return

        @pl.when(low >= 0)
        def _():
            self.along(low, True).wait_recv()

            @pl.when(z < line - 1)
            def _():
                self.along(low, True).start()

            if got is not None:
                got(low)

        @pl.when(high <= line - 1)
        def _():
            self.along(high, False).wait_recv()

            @pl.when(z > 0)
            def _():
                self.along(high, False).start()

            if got is not None:
                got(high)

    def sent(self):
        for from_z in range(self.line):

            @pl.when((from_z <= self.z) & (self.z < self.line - 1))
            def _():
                self.along(from_z, True).wait_send()

            @pl.when((from_z >= self.z) & (self.z > 0))
            def _():
                self.along(from_z, False).wait_send()


def collect_kernel(
    groups, parts, hidden, w_in, w_own, chan, hid_out, w_out, gate_out, chan_out, wo_out,
    blocks, gates, low, chan_s, chan_r, hid_s, hid_r, swap_s, swap_r, gate_s, gate_r,
    wo_s, wo_r, line_s, line_r, lwo_s, lwo_r, core_s, core_r, local,
):
    line = groups // 2
    cw = INNER // parts
    cc = cw + 2 * N
    group, q = lax.axis_index("dp"), lax.axis_index("seq")
    z, core = group // 2, lax.rem(group, 2)
    sibling = (2 * z + 1 - core, q)
    peers = seq_peers(parts)
    everyone = all_peers(groups, parts)
    shared = w_in[:, 2 * INNER :].astype(BF16)
    for part in range(parts):
        at = INNER + part * cw
        blocks[part, :, :cw] = w_in[:, at : at + cw].astype(BF16)
        blocks[part, :, cw : cc + H] = shared
        blocks[part, :, cc + H :] = jnp.zeros((w_in.shape[0], LANES - H), BF16)
    low[...] = w_own[...].astype(BF16)
    greet(everyone)
    swaps = []
    for k, peer in enumerate(peers):
        copy = remote(blocks.at[peer[1]], w_out.at[group, q], swap_s, swap_r, k, peer)
        copy.start()
        swaps.append(copy)
    outs = LineGather(
        line, z, core, q, lambda from_z: wo_out.at[2 * from_z + core, q], low, lwo_s, lwo_r
    )
    outs.step(0)
    own = [
        pltpu.make_async_copy(blocks.at[q], w_out.at[group, q], local.at[0]),
        pltpu.make_async_copy(hidden, hid_out.at[q], local.at[1]),
        pltpu.make_async_copy(chan, chan_out.at[group * parts + q], local.at[2]),
        pltpu.make_async_copy(low, wo_out.at[group, q], local.at[3]),
    ]
    for copy in own:
        copy.start()
    waiting = []
    for k, peer in enumerate(everyone):
        copy = remote(chan, chan_out.at[group * parts + q], chan_s, chan_r, k, peer)
        copy.start()
        waiting.append(copy)
    for part in range(parts):
        gates[part] = w_in[:, part * cw : (part + 1) * cw].astype(BF16)
    copy = pltpu.make_async_copy(gates.at[q], gate_out.at[q], local.at[4])
    copy.start()
    own.append(copy)
    own[0].wait()
    for copy in swaps:
        copy.wait()
    for k, peer in enumerate(peers):
        for source, target, sends, recvs in (
            (hidden, hid_out.at[q], hid_s, hid_r),
            (gates.at[peer[1]], gate_out.at[q], gate_s, gate_r),
            (low, wo_out.at[group, q], wo_s, wo_r),
        ):
            copy = remote(source, target, sends, recvs, k, peer)
            copy.start()
            waiting.append(copy)

    def across(from_z):
        block = w_out.at[2 * from_z + core]
        return remote(block, block, core_s, core_r, from_z, sibling)

    ins = LineGather(
        line, z, core, q, lambda from_z: w_out.at[2 * from_z + core], w_out.at[group],
        line_s, line_r,
    )
    across(z).start()
    ins.step(0)
    for t in range(1, line):
        ins.step(t, lambda from_z: across(from_z).start())
        if t == line - 2 or line == 2:
            for s in range(1, line):
                outs.step(s)
    ins.sent()
    outs.sent()
    for from_z in range(line):
        across(from_z).wait_send()
        block = w_out.at[2 * from_z + 1 - core]
        remote(block, block, core_s, core_r, from_z, sibling).wait_recv()
    for copy in own[1:] + waiting:
        copy.wait()


def collect(collective_id, hidden, w_in, w_own, chan, groups, parts):
    rows = w_in.shape[0]
    line = groups // 2
    cw = INNER // parts
    width = cw + 2 * N + LANES
    sem = pltpu.SemaphoreType.DMA
    hbm = pl.BlockSpec(memory_space=pltpu.HBM)
    vmem = pl.BlockSpec(memory_space=pltpu.VMEM)
    return pl.pallas_call(
        functools.partial(collect_kernel, groups, parts),
        in_specs=[hbm, vmem, vmem, hbm],
        out_specs=[hbm] * 5,
        out_shape=[
            jax.ShapeDtypeStruct((parts,) + hidden.shape, hidden.dtype),
            jax.ShapeDtypeStruct((groups, parts, rows, width), BF16),
            jax.ShapeDtypeStruct((parts, rows, cw), BF16),
            jax.ShapeDtypeStruct((groups * parts,) + chan.shape, chan.dtype),
            jax.ShapeDtypeStruct((groups, parts) + w_own.shape, BF16),
        ],
        scratch_shapes=[
            pltpu.VMEM((parts, rows, width), BF16),
            pltpu.VMEM((parts, rows, cw), BF16),
            pltpu.VMEM(w_own.shape, BF16),
            *([sem((groups * parts - 1,))] * 2),
            *([sem((parts - 1,))] * 8),
            *([sem((2, line))] * 4),
            sem((line,)), sem((line,)), sem((5,)),
        ],
        compiler_params=pltpu.CompilerParams(
            collective_id=collective_id, has_side_effects=True, vmem_limit_bytes=48 * 2**20
        ),
        name="collect",
    )(hidden, w_in, w_own, chan)


def forward_kernel(
    groups, parts, cw,
    hidden_h, wx_h, gate_h, wo_in, gain_in, gain_out, taps, heads, skip, spread,
    normed_h, px_h, y_h, states_h, z_h, u_h, wz_h, wo,
    hidden, wx, wz, normed, px, y, states, zs, us, xbuf, state, xdt, carried,
    line_s, line_r, core_s, core_r, out_s, out_r, load, store,
):
    line = groups // 2
    cc = cw + 2 * N
    length = px.shape[0]
    chunks = length // CHUNK
    group, q = lax.axis_index("dp"), lax.axis_index("seq")
    z, core = group // 2, lax.rem(group, 2)
    sibling = (2 * z + 1 - core, q)
    peers = seq_peers(parts)
    loads = [
        pltpu.make_async_copy(source, target, load.at[k])
        for k, (source, target) in enumerate(
            [(hidden_h, hidden), (wx_h, wx), (gate_h, wz.at[group])]
        )
    ]
    for copy in loads:
        copy.start()
    greet(peers + dp_peers(groups))

    places = [lax.rem(z + k, line) for k in range(1, line)]

    def plane(k, k_to, device, block):
        return remote(block, block, out_s, out_r, k * (parts + 1) + k_to, device)

    if parts == 4:
        near = [q + 1 - 2 * lax.rem(q, 2), lax.rem(q + 2, 4)]
        half = wo.shape[2] // 2

    def early(k):
        block = wo.at[2 * places[k] + core, q]
        if parts == 4:
            return [plane(k, h, (group, near[h]), block) for h in range(2)]
        return [plane(k, j, peer, block) for j, peer in enumerate(peers)]

    def late(k, h):
        rows = pl.ds(h * half, half)
        block = wo.at[2 * places[k] + core, near[h], rows]
        return plane(k, 2 + h, (group, near[1 - h]), block)

    for k in range(line - 1):
        for copy in early(k):
            copy.start()

    def across(from_z):
        block = wz.at[2 * from_z + core]
        return remote(block, block, core_s, core_r, from_z, sibling)

    gates = LineGather(
        line, z, core, q, lambda from_z: wz.at[2 * from_z + core], wz.at[group], line_s, line_r
    )
    loads[2].wait()
    across(z).start()
    gates.step(0)
    loads[0].wait()

    def norm_rows(i, carry):
        rows = pl.ds(pl.multiple_of(i * 32, 32), 32)
        tokens = hidden[rows, :].astype(F32)
        mean = jnp.sum(tokens * tokens, axis=-1, keepdims=True) / D
        normed[rows, :] = (tokens * lax.rsqrt(mean + EPS_IN) * gain_in[...]).astype(BF16)
        return carry

    lax.fori_loop(0, length // 32, norm_rows, 0)
    loads[1].wait()
    tall = 256

    def project_rows(i, carry):
        rows = pl.ds(pl.multiple_of(i * tall, tall), tall)
        px[rows, :] = dot(normed[rows, :], wx[...])
        return carry

    lax.fori_loop(0, length // tall, project_rows, 0)
    stores = [
        pltpu.make_async_copy(normed, normed_h, store.at[0]),
        pltpu.make_async_copy(px, px_h, store.at[1]),
    ]
    for copy in stores:
        copy.start()
    state[...] = jnp.zeros_like(state)
    xbuf[0:8, :] = jnp.zeros((8, cc), F32)

    def scan_rows(i, carry):
        for t in range(1, line):

            @pl.when(i == min(3 * (t - 1), chunks - 1))
            def _(t=t):
                gates.step(t, lambda from_z: across(from_z).start())

        rows = pl.ds(pl.multiple_of(i * CHUNK, CHUNK), CHUNK)
        scan_forward_step(
            cw, px.at[rows], taps, heads, skip, spread, y.at[rows], states.at[i],
            xbuf, state, xdt, carried,
        )
        return carry

    lax.fori_loop(0, chunks, scan_rows, 0)
    for source, target, at in ((y, y_h, 2), (states, states_h, 3)):
        copy = pltpu.make_async_copy(source, target, store.at[at])
        copy.start()
        stores.append(copy)
    if parts == 4:
        for k in range(line - 1):
            for copy in early(k):
                copy.wait()
            for h in range(2):
                late(k, h).start()
    for from_z in range(line):
        across(from_z).wait_send()
        block = wz.at[2 * from_z + 1 - core]
        remote(block, block, core_s, core_r, from_z, sibling).wait_recv()
    gates.sent()
    copy = pltpu.make_async_copy(wz, wz_h, store.at[4])
    copy.start()
    stores.append(copy)
    lane = lax.broadcasted_iota(jnp.int32, (1, LANES), 1)
    wide = 512

    def gate_rows(i, carry):
        rows = pl.ds(pl.multiple_of(i * tall, tall), tall)
        weights = wz[...].reshape(D, cw)
        gate_in = dot(normed[rows, :], weights)
        zs[rows, :] = gate_in
        gated = y[rows, :] * (gate_in * jax.nn.sigmoid(gate_in))
        us[rows, :cw] = (gated * gain_out[...]).astype(BF16)
        highs = jnp.zeros((tall, LANES), F32)
        rests = jnp.zeros((tall, LANES), F32)
        for b in range(cw // wide):
            block = gated[:, b * wide : (b + 1) * wide]
            total = jnp.sum(block * block, axis=-1, keepdims=True)
            level = level_of(q * cw + b * wide, wide)
            highs = highs + jnp.where(lane == level, total, 0.0)
            rests = rests + jnp.where(lane == level + LEVELS, total, 0.0)
        rests = rests - rests.astype(BF16).astype(F32)
        us[rows, cw:] = jnp.where(lane < LEVELS, highs, rests).astype(BF16)
        return carry

    lax.fori_loop(0, length // tall, gate_rows, 0)
    for source, target, at in ((zs, z_h, 5), (us, u_h, 6)):
        copy = pltpu.make_async_copy(source, target, store.at[at])
        copy.start()
        stores.append(copy)
    for k in range(line - 1):
        if parts == 4:
            for h in range(2):
                late(k, h).wait()
        else:
            for copy in early(k):
                copy.wait()
    for copy in stores:
        copy.wait()


def forward(collective_id, hidden, wx, gate, wo, gain_in, gain_out, taps, heads, skip, spread):
    groups, parts = wo.shape[:2]
    line = groups // 2
    length = hidden.shape[0]
    rows, cw = gate.shape[1:]
    cc = cw + 2 * N
    width = cc + LANES
    chunks = length // CHUNK
    sem = pltpu.SemaphoreType.DMA
    hbm = pl.BlockSpec(memory_space=pltpu.HBM)
    vmem = pl.BlockSpec(memory_space=pltpu.VMEM)
    made = [
        jax.ShapeDtypeStruct((length, D), BF16),
        jax.ShapeDtypeStruct((length, width), F32),
        jax.ShapeDtypeStruct((length, cw), F32),
        jax.ShapeDtypeStruct((chunks, N, cw), BF16),
        jax.ShapeDtypeStruct((length, cw), F32),
        jax.ShapeDtypeStruct((length, cw + LANES), BF16),
    ]
    wz = jax.ShapeDtypeStruct((groups, parts, rows, cw), BF16)
    return pl.pallas_call(
        functools.partial(forward_kernel, groups, parts, cw),
        in_specs=[*([hbm] * 4), *([vmem] * 6)],
        out_specs=[hbm] * 8,
        out_shape=[*made, wz, jax.ShapeDtypeStruct(wo.shape, BF16)],
        input_output_aliases={3: 7},
        scratch_shapes=[
            pltpu.VMEM(hidden.shape, BF16),
            pltpu.VMEM(wx.shape, BF16),
            pltpu.VMEM(wz.shape, BF16),
            *[pltpu.VMEM(m.shape, m.dtype) for m in made],
            pltpu.VMEM((CHUNK + 8, cc), F32),
            pltpu.VMEM((N, cw), F32),
            pltpu.VMEM((CHUNK, cw), BF16),
            pltpu.VMEM((CHUNK, cw), F32),
            sem((2, line)), sem((2, line)), sem((line,)), sem((line,)),
            sem(((line - 1) * (parts + 1),)), sem(((line - 1) * (parts + 1),)),
            sem((3,)), sem((7,)),
        ],
        compiler_params=pltpu.CompilerParams(
            collective_id=collective_id, has_side_effects=True, vmem_limit_bytes=63 * 2**20
        ),
        name="forward",
    )(hidden, wx, gate, wo, gain_in, gain_out, taps, heads, skip, spread)


def add_blocks(out, a, b, rows, steps):
    def step(i, carry):
        at = pl.ds(pl.multiple_of(i * rows, rows), rows)
        out[at] = (a[at].astype(F32) + b[at].astype(F32)).astype(out.dtype)
        return carry

    lax.fori_loop(0, steps, step, 0)


def level_of(channel, width):
    return sum((channel >= level_width(k)).astype(jnp.int32) for k in range(LEVELS - 1))


def mirror_peers(parts):
    group, q = lax.axis_index("dp"), lax.axis_index("seq")
    if parts != 4:
        return seq_peers(parts)
    return [(group, 3 - q), (group, q + 1 - 2 * lax.rem(q, 2)), (group, lax.rem(q + 2, 4))]


def middle_kernel(
    groups, parts, cw,
    u_h, wo_in, cot_h, tokens_h,
    back_h, coef_h, block_h, left_h, right_h, wo,
    u, cot, tokens, mixed, branch, norms, pulls, back, coefs, weights, sent, held, left, right,
    u_s, u_r, wo_s, wo_r, back_s, back_r, coef_s, coef_r, core_s, core_r, fetch, load, store, local,
):
    line = groups // 2
    group, q = lax.axis_index("dp"), lax.axis_index("seq")
    z, core = group // 2, lax.rem(group, 2)
    sibling = (2 * z + 1 - core, q)
    peers = mirror_peers(parts)
    loads = [
        pltpu.make_async_copy(u_h.at[q], u.at[q], load.at[0]),
        pltpu.make_async_copy(cot_h, cot, load.at[1]),
        pltpu.make_async_copy(tokens_h, tokens, load.at[2]),
    ]
    for copy in loads:
        copy.start()
    greet(peers + [sibling])
    swaps = [remote(u_h.at[peer[1]], u.at[q], u_s, u_r, k, peer) for k, peer in enumerate(peers)]
    for copy in swaps:
        copy.start()

    def parity(d, of):
        block = wo.at[2 * d + of]
        return remote(block, block, wo_s, wo_r, d, sibling)

    for d in range(line):
        parity(d, core).start()
    for copy in loads + swaps:
        copy.wait()

    terms = u[0, :, cw:].astype(F32)
    for part in range(1, parts):
        terms = terms + u[part, :, cw:].astype(F32)
    squares = jnp.zeros((terms.shape[0], 1), F32)
    for k in range(LEVELS):
        squares = squares + terms[:, k : k + 1] + terms[:, LEVELS + k : LEVELS + k + 1]
        norms[:, k : k + 1] = lax.rsqrt(squares / level_width(k) + EPS_OUT)
    rows = 32

    def mix_rows(i, carry):
        at = pl.ds(pl.multiple_of(i * rows, rows), rows)
        running = norms[at, LEVELS - 1 : LEVELS] * cot[LEVELS - 1, at, :].astype(F32)
        mixed[LEVELS - 1, at, :] = running.astype(BF16)
        for k in reversed(range(LEVELS - 1)):
            running = running + norms[at, k : k + 1] * cot[k, at, :].astype(F32)
            mixed[k, at, :] = running.astype(BF16)
        return carry

    lax.fori_loop(0, tokens.shape[0] // rows, mix_rows, 0)
    for d in range(line):
        parity(d, core).wait_send()
        parity(d, 1 - core).wait_recv()

    width = INNER // groups
    per = WIDE // width
    slots = weights.shape[0]
    dests = [peer[1] for peer in peers] + [q]
    firsts = [dest * cw + b * WIDE for dest in dests for b in range(cw // WIDE)]
    firsts += [b * WIDE for b in range(INNER // WIDE)]

    def get(i):
        return pltpu.make_async_copy(
            wo.at[pl.ds(firsts[i] // width, per)], weights.at[i % slots], fetch.at[i % slots]
        )

    def block_of(i):
        get(i).wait()
        return weights[i % slots].reshape(WIDE, D)

    for i in range(slots - 1):
        get(i).start()
    outgoing = []
    for i in range(len(dests) * (cw // WIDE)):
        get(i + slots - 1).start()
        at, b = divmod(i, cw // WIDE)
        lanes = slice(b * WIDE, (b + 1) * WIDE)
        level = level_of(firsts[i], WIDE)
        back[dests[at], :, lanes] = dot(mixed[level], block_of(i), NT).astype(BF16)
        if b == cw // WIDE - 1:
            if at < len(peers):
                copy = remote(back.at[dests[at]], back_h.at[q], back_s, back_r, at, peers[at])
            else:
                copy = pltpu.make_async_copy(back.at[q], back_h.at[q], local.at[0])
            copy.start()
            outgoing.append(copy)
    first = len(dests) * (cw // WIDE)
    branch[...] = jnp.zeros_like(branch)
    for b in range(INNER // WIDE):
        if first + b + slots - 1 < len(firsts):
            get(first + b + slots - 1).start()
        part, at = divmod(b * WIDE, cw)
        branch[...] += dot(u[part, :, at : at + WIDE], block_of(first + b))
        for k in range(LEVELS):
            if level_width(k) == (b + 1) * WIDE:

                def level_rows(i, carry, k=k):
                    at = pl.ds(pl.multiple_of(i * rows, rows), rows)
                    norm = norms[at, k : k + 1]
                    total = branch[at, :]
                    inner = jnp.sum(cot[k, at, :].astype(F32) * total, axis=-1, keepdims=True)
                    pulls[at, k : k + 1] = norm * norm * norm * (inner / level_width(k))
                    cot[k, at, :] = (tokens[at, :].astype(F32) + norm * total).astype(BF16)
                    return carry

                lax.fori_loop(0, tokens.shape[0] // rows, level_rows, 0)
                copy = pltpu.make_async_copy(cot.at[k], block_h.at[k], store.at[k])
                copy.start()
                outgoing.append(copy)
    coef = jnp.zeros((tokens.shape[0], 1), F32)
    lane = lax.broadcasted_iota(jnp.int32, (1, LANES), 1)
    packed = jnp.zeros((tokens.shape[0], LANES), F32)
    for k in reversed(range(LEVELS)):
        coef = coef + pulls[:, k : k + 1]
        high, rest = two_terms(coef)
        packed = jnp.where(lane == k, high.astype(F32), packed)
        packed = jnp.where(lane == LEVELS + k, rest.astype(F32), packed)
    coefs[...] = packed.astype(BF16)
    for k, peer in enumerate(peers):
        copy = remote(coefs, coef_h.at[q], coef_s, coef_r, k, peer)
        copy.start()
        outgoing.append(copy)
    copy = pltpu.make_async_copy(coefs, coef_h.at[q], local.at[1])
    copy.start()
    outgoing.append(copy)

    share = width // parts
    tile = 512
    halves = D // 2 // tile

    def product(of, j):
        channel = of * width
        lanes = pl.ds(pl.multiple_of(lax.rem(channel, cw), width), width)
        cols = pl.ds(pl.multiple_of(j * tile, tile), tile)
        return dot(u[channel // cw, :, lanes], mixed[level_of(channel, width), :, cols], TN)

    cores = []
    for d in range(line):

        def send_step(j, carry, d=d):
            cols = pl.ds(pl.multiple_of(j * tile, tile), tile)
            sent[d, :, cols] = product(2 * d + 1 - core, j).astype(BF16)
            return carry

        lax.fori_loop(0, 2 * halves, send_step, 0)
        copy = remote(sent.at[d], held.at[d], core_s, core_r, d, sibling)
        copy.start()
        cores.append(copy)
    for d in range(line):
        cores[d].wait_recv()
        for out, target, first, at in ((left, left_h, 0, 0), (right, right_h, halves, 1)):

            def keep_step(j, carry, d=d, out=out, first=first):
                cols = pl.ds(pl.multiple_of((j + first) * tile, tile), tile)
                to = pl.ds(pl.multiple_of(j * tile, tile), tile)
                total = product(2 * d + core, j + first) + held[d, :, cols].astype(F32)
                total = total.astype(BF16)
                for part in range(parts):
                    out[part, d, :, to] = total[part * share : (part + 1) * share]
                return carry

            lax.fori_loop(0, halves, keep_step, 0)
            copy = pltpu.make_async_copy(
                out.at[:, d], target.at[:, d], store.at[LEVELS + 2 * d + at]
            )
            copy.start()
            outgoing.append(copy)
    for copy in cores:
        copy.wait_send()
    for copy in outgoing:
        copy.wait()


def middle(collective_id, u, wo, cotangent, tokens):
    groups, parts, share = wo.shape[:3]
    line = groups // 2
    rows, wide = u.shape[1:]
    cw = wide - LANES
    width = share * parts
    sem = pltpu.SemaphoreType.DMA
    hbm = pl.BlockSpec(memory_space=pltpu.HBM)
    half = (parts, line, share, D // 2)
    return pl.pallas_call(
        functools.partial(middle_kernel, groups, parts, cw),
        in_specs=[hbm] * 4,
        out_specs=[hbm] * 6,
        out_shape=[
            jax.ShapeDtypeStruct((parts, rows, cw), BF16),
            jax.ShapeDtypeStruct((parts, rows, LANES), BF16),
            jax.ShapeDtypeStruct(cotangent.shape, BF16),
            jax.ShapeDtypeStruct(half, BF16),
            jax.ShapeDtypeStruct(half, BF16),
            jax.ShapeDtypeStruct(wo.shape, BF16),
        ],
        input_output_aliases={1: 5},
        scratch_shapes=[
            pltpu.VMEM(u.shape, BF16),
            pltpu.VMEM(cotangent.shape, BF16),
            pltpu.VMEM(tokens.shape, BF16),
            pltpu.VMEM(cotangent.shape, BF16),
            pltpu.VMEM((rows, D), F32),
            pltpu.VMEM((rows, LANES), F32),
            pltpu.VMEM((rows, LANES), F32),
            pltpu.VMEM((parts, rows, cw), BF16),
            pltpu.VMEM((rows, LANES), BF16),
            pltpu.VMEM((3, WIDE // width, parts, share, D), BF16),
            pltpu.VMEM((line, width, D), BF16),
            pltpu.VMEM((line, width, D), BF16),
            pltpu.VMEM(half, BF16),
            pltpu.VMEM(half, BF16),
            sem((parts - 1,)), sem((parts - 1,)), sem((line,)), sem((line,)),
            *([sem((parts - 1,))] * 4),
            sem((line,)), sem((line,)), sem((3,)), sem((3,)), sem((LEVELS + 2 * line,)), sem((2,)),
        ],
        compiler_params=pltpu.CompilerParams(
            collective_id=collective_id, has_side_effects=True, vmem_limit_bytes=63 * 2**20
        ),
        name="middle",
    )(u, wo, cotangent, tokens)


def sum_blocks(out, blocks, rows):
    def step(i, carry):
        at = pl.ds(pl.multiple_of(i * rows, rows), rows)
        total = blocks[0][at].astype(F32)
        for block in blocks[1:]:
            total = total + block[at].astype(F32)
        out[at] = total.astype(out.dtype)
        return carry

    lax.fori_loop(0, out.shape[0] // rows, step, 0)


class PlaneSum:
    def __init__(self, parts, group, q, blocks, first, second, sends, recvs):
        self.parts, self.group, self.q = parts, group, q
        self.blocks, self.first, self.second = blocks, first, second
        self.sends, self.recvs = sends, recvs
        self.half = blocks.shape[1] // 2
        if parts == 4:
            self.near = [q + 1 - 2 * lax.rem(q, 2), lax.rem(q + 2, 4)]
            self.far = 3 - q

    @staticmethod
    def scratch(parts, shape, dtype):
        if parts == 4:
            half = (shape[0] // 2,) + shape[1:]
            first, second, count = (2, 2) + half, (2, 2) + half, 6
        else:
            first, second, count = (parts - 1,) + shape, (1, 16, LANES), parts - 1
        sem = pltpu.SemaphoreType.DMA
        return [pltpu.VMEM(first, dtype), pltpu.VMEM(second, dtype), sem((count,)), sem((count,))]

    def piece(self, of, h):
        return self.blocks.at[of, pl.ds(h * self.half, self.half)]

    def early(self, h):
        if self.parts != 4:
            return []
        near = self.near[h]
        to = (self.group, near)
        return [
            remote(self.piece(of, h), self.first.at[h, k], self.sends, self.recvs, 2 * h + k, to)
            for k, of in enumerate((near, self.far))
        ]

    def late(self, h):
        to = (self.group, self.near[1 - h])
        return remote(
            self.second.at[h, 0], self.second.at[h, 1], self.sends, self.recvs, 4 + h, to
        )

    def direct(self):
        peers = seq_peers(self.parts)
        return [
            remote(self.blocks.at[peer[1]], self.first.at[k], self.sends, self.recvs, k, peer)
            for k, peer in enumerate(peers)
        ]

    def start(self, h):
        for copy in self.early(h):
            copy.start()
        if self.parts != 4 and h == 1:
            for copy in self.direct():
                copy.start()

    def turn(self, rows):
        if self.parts != 4:
            return
        for h in range(2):
            for copy in self.early(h):
                copy.wait()
            beyond = self.piece(self.near[1 - h], h)
            each(self.second.at[h, 0], [beyond, self.first.at[h, 1]], rows)
            self.late(h).start()

    def finish(self, out, rows):
        if self.parts != 4:
            for copy in self.direct():
                copy.wait()
            each(
                out,
                [self.blocks.at[self.q]] + [self.first.at[k] for k in range(self.parts - 1)],
                rows,
            )
            return
        for h in range(2):
            self.late(h).wait()
            each(
                out.at[pl.ds(h * self.half, self.half)],
                [self.piece(self.q, h), self.first.at[h, 0], self.second.at[h, 1]],
                rows,
            )


def each(out, blocks, rows):
    if len(out.shape) == 2:
        sum_blocks(out, blocks, rows)
        return
    for d in range(out.shape[0]):
        sum_blocks(out.at[d], [block.at[d] for block in blocks], rows)


class LineSum:
    def __init__(self, line, z, core, q, acc, up, down, up_s, up_r, down_s, down_r, rows, steps):
        self.line, self.z, self.core, self.q = line, z, core, q
        self.acc, self.up, self.down = acc, up, down
        self.up_s, self.up_r, self.down_s, self.down_r = up_s, up_r, down_s, down_r
        self.rows, self.steps = rows, steps

    def ahead(self, d, first):
        block = self.acc.at[d] if first else self.up.at[d]
        to = (2 * (self.z + 1) + self.core, self.q)
        return remote(block, self.up.at[d], self.up_s, self.up_r, d, to)

    def behind(self, d, first):
        block = self.acc.at[d] if first else self.down.at[d]
        to = (2 * (self.z - 1) + self.core, self.q)
        return remote(block, self.down.at[d], self.down_s, self.down_r, d, to)

    def add(self, into, d):
        add_blocks(into.at[d], into.at[d], self.acc.at[d], self.rows, self.steps)

    def step(self, t):
        line, z = self.line, self.z
        far, near = line - 1 - t + z, t - (line - 1 - z)

        @pl.when(z == 0)
        def _():
            self.ahead(line - 1 - t, True).start()

        @pl.when((z > 0) & (z <= t))
        def _():
            self.ahead(far, False).wait_recv()
            self.add(self.up, far)
            self.ahead(far, False).start()

        @pl.when(z == line - 1)
        def _():
            self.behind(t, True).start()

        @pl.when((z < line - 1) & (line - 1 - z <= t))
        def _():
            self.behind(near, False).wait_recv()
            self.add(self.down, near)
            self.behind(near, False).start()

    def sent(self, t):
        line, z = self.line, self.z
        far, near = line - 1 - t + z, t - (line - 1 - z)

        @pl.when(z == 0)
        def _():
            self.ahead(line - 1 - t, True).wait_send()

        @pl.when((z > 0) & (z <= t))
        def _():
            self.ahead(far, False).wait_send()

        @pl.when(z == line - 1)
        def _():
            self.behind(t, True).wait_send()

        @pl.when((z < line - 1) & (line - 1 - z <= t))
        def _():
            self.behind(near, False).wait_send()

    def finish(self, out):
        line, z = self.line, self.z

        @pl.when(z == 0)
        def _():
            self.behind(z, False).wait_recv()
            add_blocks(out, self.acc.at[z], self.down.at[z], self.rows, self.steps)

        @pl.when(z == line - 1)
        def _():
            self.ahead(z, False).wait_recv()
            add_blocks(out, self.acc.at[z], self.up.at[z], self.rows, self.steps)

        @pl.when((z > 0) & (z < line - 1))
        def _():
            self.ahead(z, False).wait_recv()
            self.add(self.up, z)
            self.behind(z, False).wait_recv()
            add_blocks(out, self.up.at[z], self.down.at[z], self.rows, self.steps)


def backward_kernel(
    groups, parts, cw,
    back_h, coefs_h, normed_h, px_h, y_h, z_h, states_h, wide_h,
    gain, taps, heads, skip, spread, gather,
    dz_h, dpx_h, small, wide_sum, gate_sum,
    dz, coefs, normed, px, y, dy, states, wide, dpx, dtaps, dheads, dskip, dgain,
    xbuf, dstate, dcbuf, slope, xact, xd_s, dxd_s, acc_s,
    first, second, wide_s, wide_r, gate_made, gate_held, gate_acc, gate_up, gate_down,
    core_s, core_r, up_s, up_r, down_s, down_r, load, store,
):
    line = groups // 2
    cc = cw + 2 * N
    length = y.shape[0]
    chunks = length // CHUNK
    group, q = lax.axis_index("dp"), lax.axis_index("seq")
    z, core = group // 2, lax.rem(group, 2)
    sibling = (2 * z + 1 - core, q)
    loads = [
        pltpu.make_async_copy(source, target, load.at[k])
        for k, (source, target) in enumerate(
            [(wide_h, wide), (back_h, dz), (coefs_h, coefs), (y_h, y), (z_h, dy),
             (normed_h, normed), (px_h, px), (states_h, states)]
        )
    ]
    for copy in loads:
        copy.start()
    greet(seq_peers(parts) + dp_peers(groups))
    plane = PlaneSum(parts, group, q, wide, first, second, wide_s, wide_r)
    loads[0].wait()
    plane.start(0)
    plane.start(1)
    for copy in loads[1:5]:
        copy.wait()

    rows = 32
    lane = lax.broadcasted_iota(jnp.int32, (1, LANES), 1)
    dgain[...] = jnp.zeros_like(dgain)

    def gate_rows(i, carry):
        at = pl.ds(pl.multiple_of(i * rows, rows), rows)
        coef = coefs[at, :].astype(F32)
        for b in range(cw // WIDE):
            lanes = slice(b * WIDE, (b + 1) * WIDE)
            level = level_of(q * cw + b * WIDE, WIDE)
            ours = (lane == level) | (lane == level + LEVELS)
            pull = jnp.sum(jnp.where(ours, coef, 0.0), axis=-1, keepdims=True)
            gate_in = dy[at, lanes]
            sig = jax.nn.sigmoid(gate_in)
            gate = gate_in * sig
            y_at = y[at, lanes]
            gated = y_at * gate
            back = dz[at, lanes].astype(F32)
            dgated = gain[:, lanes] * back - gated * pull
            dgain[0:1, lanes] += jnp.sum(back * gated, axis=0, keepdims=True)
            dz[at, lanes] = (dgated * y_at * (sig + gate * (1.0 - sig))).astype(BF16)
            dy[at, lanes] = dgated * gate
        return carry

    lax.fori_loop(0, length // rows, gate_rows, 0)
    dz_out = pltpu.make_async_copy(dz, dz_h, store.at[0])
    dz_out.start()
    loads[5].wait()
    span = gate_acc.shape[1]

    def dweight(of, out):
        at = pl.ds(pl.multiple_of(of * span, span), span)
        out[...] = dot(normed[:, at], dz[...], TN).astype(BF16)

    def core_copy(d):
        return remote(gate_made.at[d], gate_held.at[d], core_s, core_r, d, sibling)

    order = [d for k in range(line // 2) for d in (line - 1 - k, k)]
    for d in order:
        dweight(2 * d + 1 - core, gate_made.at[d])
        core_copy(d).start()
    for d in order:
        dweight(2 * d + core, gate_acc.at[d])
        core_copy(d).wait()
        add_blocks(gate_acc.at[d], gate_acc.at[d], gate_held.at[d], span // 4, 4)
    gates = LineSum(
        line, z, core, q, gate_acc, gate_up, gate_down, up_s, up_r, down_s, down_r, span // 4, 4
    )
    gates.step(0)
    dstate[...] = jnp.zeros_like(dstate)
    dcbuf[CHUNK : CHUNK + 8, :] = jnp.zeros((8, cc), F32)
    dtaps[...] = jnp.zeros_like(dtaps)
    dheads[...] = jnp.zeros_like(dheads)
    dskip[...] = jnp.zeros_like(dskip)
    for copy in loads[6:]:
        copy.wait()

    def scan_rows(i, carry):
        for t in range(1, line - 1):

            @pl.when(i == min(4 * t - 1, chunks - 1))
            def _(t=t):
                gates.sent(t - 1)
                gates.step(t)

        @pl.when(i == 2)
        def _():
            plane.turn(32)

        at = chunks - 1 - i
        here = pl.ds(pl.multiple_of(at * CHUNK, CHUNK), CHUNK)
        before = pl.ds(pl.multiple_of(jnp.maximum(at * CHUNK - 8, 0), 8), 8)
        scan_backward_step(
            cw, at == 0, px.at[here], px.at[before], taps, heads, skip, spread, gather,
            dy.at[here], y.at[here], states.at[at], dpx.at[here], dtaps, dheads, dskip,
            xbuf, dstate, dcbuf, slope, xact, xd_s, dxd_s, acc_s,
        )
        return carry

    lax.fori_loop(0, chunks, scan_rows, 0)
    dpx_out = pltpu.make_async_copy(dpx, dpx_h, store.at[1])
    dpx_out.start()
    small[...] = jnp.zeros_like(small)
    wide_rows, own_rows = cc // LANES, cw // LANES
    for tap in range(TAPS + 1):
        for b in range(wide_rows):
            to = tap * wide_rows + b
            small[to : to + 1, :] = dtaps[tap : tap + 1, b * LANES : (b + 1) * LANES]
    to = (TAPS + 1) * wide_rows
    for b in range(own_rows):
        small[to + b : to + b + 1, :] = dgain[0:1, b * LANES : (b + 1) * LANES]
    hq = cw // P_SIZE
    skips = spread_heads(dskip[...], gather[...])
    small[to + own_rows : to + own_rows + 1, :] = (
        dheads[0:1, :]
        + pltpu.roll(dheads[...], hq, 1)[1:2, :]
        + pltpu.roll(skips, 2 * hq, 1)[0:1, :]
    )
    plane.finish(wide_sum, 32)
    gates.finish(gate_sum)
    gates.sent(line - 2)
    dz_out.wait()
    dpx_out.wait()


def backward(
    collective_id, back, coefs, normed, px, y, z, states, wide, gain, taps, heads, skip, spread
):
    parts, line = wide.shape[:2]
    length, width = px.shape
    cw = skip.shape[1]
    cc = cw + 2 * N
    span = D // (2 * line)
    sem = pltpu.SemaphoreType.DMA
    vmem = pl.BlockSpec(memory_space=pltpu.VMEM)
    hbm = pl.BlockSpec(memory_space=pltpu.HBM)
    small_rows = (TAPS + 1) * (cc // LANES) + cw // LANES + 1
    small_rows = -(-small_rows // 8) * 8
    return pl.pallas_call(
        functools.partial(backward_kernel, 2 * line, parts, cw),
        in_specs=[*([hbm] * 8), *([vmem] * 6)],
        out_specs=[hbm, hbm, vmem, vmem, vmem],
        out_shape=[
            jax.ShapeDtypeStruct((length, cw), BF16),
            jax.ShapeDtypeStruct((length, width), BF16),
            jax.ShapeDtypeStruct((small_rows, LANES), F32),
            jax.ShapeDtypeStruct(wide.shape[1:], BF16),
            jax.ShapeDtypeStruct((span, cw), BF16),
        ],
        scratch_shapes=[
            *[pltpu.VMEM(a.shape, a.dtype) for a in (back, coefs, normed, px, y, z, states, wide)],
            pltpu.VMEM((length, width), BF16),
            pltpu.VMEM((8, cc), F32),
            pltpu.VMEM((8, LANES), F32),
            pltpu.VMEM((8, cw), F32),
            pltpu.VMEM((8, cw), F32),
            pltpu.VMEM((CHUNK + 8, cc), F32),
            pltpu.VMEM((N, cw), F32),
            pltpu.VMEM((CHUNK + 8, cc), F32),
            pltpu.VMEM((CHUNK, cc), F32),
            pltpu.VMEM((CHUNK, cc), F32),
            pltpu.VMEM((CHUNK, cw), BF16),
            pltpu.VMEM((CHUNK, cw), F32),
            pltpu.VMEM((CHUNK, CHUNK), F32),
            *PlaneSum.scratch(parts, wide.shape[1:], BF16),
            *([pltpu.VMEM((line, span, cw), BF16)] * 5),
            *([sem((line,))] * 6),
            sem((8,)), sem((2,)),
        ],
        compiler_params=pltpu.CompilerParams(
            collective_id=collective_id, has_side_effects=True, vmem_limit_bytes=63 * 2**20
        ),
        name="backward",
    )(back, coefs, normed, px, y, z, states, wide, gain, taps, heads, skip, spread, spread.T)


def owners_kernel(
    groups, parts, rows,
    normed, left, right, gate, small, dz, dpx, wz, wx,
    part, left_out, right_out, gate_out, back_out, small_all,
    made, held, acc, up, down, final, left_up, left_down, right_acc, right_up, right_down,
    normed_v, dz_v, dpx_v, wz_v, wx_v, back, back_sum,
    right_1, right_2, right_s, right_r, back_1, back_2, back_s, back_r,
    core_s, core_r, up_s, up_r, down_s, down_r, lup_s, lup_r, ldown_s, ldown_r,
    rup_s, rup_r, rdown_s, rdown_r, part_s, part_r, gate_s, gate_r, small_s, small_r,
    load, local,
):
    line = groups // 2
    span = parts * rows
    group, q = lax.axis_index("dp"), lax.axis_index("seq")
    z, core = group // 2, lax.rem(group, 2)
    sibling = (2 * z + 1 - core, q)
    peers, others = seq_peers(parts), dp_peers(groups)
    tokens = back.shape[1]
    loads = [
        pltpu.make_async_copy(source, target, load.at[k])
        for k, (source, target) in enumerate(
            [(normed, normed_v), (dpx, dpx_v), (dz, dz_v), (wz, wz_v), (wx, wx_v)]
        )
    ]
    for copy in loads:
        copy.start()
    greet(peers + others)
    half_rows = left.shape[1] // 2
    lefts = LineSum(
        line, z, core, q, left, left_up, left_down, lup_s, lup_r, ldown_s, ldown_r, half_rows, 2
    )
    rights = LineSum(
        line, z, core, q, right_acc, right_up, right_down, rup_s, rup_r, rdown_s, rdown_r,
        half_rows, 2,
    )
    wholes = LineSum(
        line, z, core, q, acc, up, down, up_s, up_r, down_s, down_r, rows, parts
    )
    lefts.step(0)
    right_plane = PlaneSum(parts, group, q, right, right_1, right_2, right_s, right_r)
    back_plane = PlaneSum(parts, group, q, back, back_1, back_2, back_s, back_r)
    right_plane.start(0)
    right_plane.start(1)
    waiting = []
    for k, peer in enumerate(peers):
        copy = remote(gate.at[peer[1]], gate_out.at[q], gate_s, gate_r, k, peer)
        copy.start()
        waiting.append(copy)
    for k, peer in enumerate(others):
        copy = remote(small, small_all.at[group], small_s, small_r, k, peer)
        copy.start()
        waiting.append(copy)
    own = [
        pltpu.make_async_copy(gate.at[q], gate_out.at[q], local.at[0]),
        pltpu.make_async_copy(small, small_all.at[group], local.at[1]),
    ]
    for copy in own:
        copy.start()
    loads[0].wait()
    loads[1].wait()
    tile = 512

    def dweight(of, out):
        at = pl.ds(pl.multiple_of(of * span, span), span)
        out[...] = dot(normed_v[:, at], dpx_v[...], TN).astype(BF16)

    cores = {}
    order = [d for k in range(line // 2) for d in (line - 1 - k, k)]

    def share_core(d):
        dweight(2 * d + 1 - core, made.at[d])
        copy = remote(made.at[d], held.at[d], core_s, core_r, d, sibling)
        copy.start()
        cores[d] = copy

    def sum_core(d):
        dweight(2 * d + core, acc.at[d])
        cores[d].wait()
        add_blocks(acc.at[d], acc.at[d], held.at[d], rows, parts)

    share_core(order[0])
    lefts.sent(0)
    lefts.step(1)
    share_core(order[1])
    sum_core(order[0])
    for t in range(2, line - 1):
        lefts.sent(t - 1)
        lefts.step(t)
    sum_core(order[1])
    wholes.step(0)
    for d in order[2:]:
        share_core(d)
    for d in order[2:]:
        sum_core(d)
    for copy in loads[2:]:
        copy.wait()

    def dnormed(of):
        at = pl.ds(pl.multiple_of(of * tokens, tokens), tokens)

        def step(j, carry):
            cols = pl.ds(pl.multiple_of(j * tile, tile), tile)
            back[of, :, cols] = (
                dot(dz_v[at, :], wz_v[cols, :], NT) + dot(dpx_v[at, :], wx_v[cols, :], NT)
            ).astype(BF16)
            return carry

        lax.fori_loop(0, D // tile, step, 0)

    right_plane.turn(32)
    if parts == 4:
        dnormed(back_plane.far)
        dnormed(back_plane.near[0])
        back_plane.start(0)
    wholes.sent(0)
    wholes.step(1)
    if parts == 4:
        dnormed(back_plane.near[1])
    else:
        for peer in peers:
            dnormed(peer[1])
    back_plane.start(1)
    dnormed(q)
    right_plane.finish(right_acc, 32)
    for t in range(2, line - 1):
        wholes.sent(t - 1)
        wholes.step(t)
    back_plane.turn(32)
    lefts.finish(left_out)
    lefts.sent(line - 2)
    wholes.sent(line - 2)
    rights.step(0)
    wholes.finish(final)
    for k, peer in enumerate(peers):
        block = final.at[pl.ds(pl.multiple_of(peer[1] * rows, rows), rows)]
        copy = remote(block, part.at[q], part_s, part_r, k, peer)
        copy.start()
        waiting.append(copy)
    copy = pltpu.make_async_copy(
        final.at[pl.ds(pl.multiple_of(q * rows, rows), rows)], part.at[q], local.at[2]
    )
    copy.start()
    own.append(copy)
    rights.sent(0)
    rights.step(1)
    back_plane.finish(back_sum, 32)
    copy = pltpu.make_async_copy(back_sum, back_out, local.at[3])
    copy.start()
    own.append(copy)
    for t in range(2, line - 1):
        rights.sent(t - 1)
        rights.step(t)
    rights.finish(right_out)
    rights.sent(line - 2)
    for copy in own + waiting:
        copy.wait()


def sum_to_owners(collective_id, normed, left, right, gate, small, dz, dpx, wz, wx):
    parts, line, out_rows, half = right.shape
    groups = 2 * line
    rows = gate.shape[1]
    span, width = rows * parts, dpx.shape[1]
    tokens = dz.shape[0] // parts
    sem = pltpu.SemaphoreType.DMA
    vmem = pl.BlockSpec(memory_space=pltpu.VMEM)
    hbm = pl.BlockSpec(memory_space=pltpu.HBM)
    return pl.pallas_call(
        functools.partial(owners_kernel, groups, parts, rows),
        in_specs=[hbm, vmem, vmem, hbm, vmem, hbm, hbm, hbm, hbm],
        out_specs=[hbm, vmem, vmem, hbm, hbm, vmem],
        out_shape=[
            jax.ShapeDtypeStruct((parts, rows, width), BF16),
            *([jax.ShapeDtypeStruct((out_rows, half), F32)] * 2),
            jax.ShapeDtypeStruct(gate.shape, BF16),
            jax.ShapeDtypeStruct((tokens, D), F32),
            jax.ShapeDtypeStruct((groups,) + small.shape, F32),
        ],
        scratch_shapes=[
            *([pltpu.VMEM((line, span, width), BF16)] * 5),
            pltpu.VMEM((span, width), BF16),
            *([pltpu.VMEM(left.shape, BF16)] * 5),
            *[pltpu.VMEM(a.shape, BF16) for a in (normed, dz, dpx, wz, wx)],
            pltpu.VMEM((parts, tokens, D), BF16),
            pltpu.VMEM((tokens, D), F32),
            *PlaneSum.scratch(parts, right.shape[1:], BF16),
            *PlaneSum.scratch(parts, (tokens, D), BF16),
            *([sem((line,))] * 14),
            *([sem((parts - 1,))] * 4),
            *([sem((groups - 1,))] * 2),
            sem((5,)),
            sem((4,)),
        ],
        compiler_params=pltpu.CompilerParams(
            collective_id=collective_id, has_side_effects=True, vmem_limit_bytes=63 * 2**20
        ),
        name="sum_to_owners",
    )(normed, left, right, gate, small, dz, dpx, wz, wx)


def on_device(
    hidden_in, out_grads, w_in, w_in_m, w_in_v, w_out, w_out_m, w_out_v,
    chan_params, chan_m, chan_v, head_params, head_m, head_v,
):
    parts = lax.axis_size("seq")
    groups = lax.axis_size("dp")
    q = lax.axis_index("seq")
    rows = hidden_in.shape[1]
    length = rows * parts
    cw = INNER // parts
    hq = H // parts
    cc = cw + 2 * N
    in_rows = w_in.shape[0]
    out_rows = w_out.shape[0]

    chan_len = chan_params.shape[0]
    chan_rows = -(-chan_len // (8 * LANES)) * 8
    chan_block = jnp.pad(
        lax.reduce_precision(chan_params, 8, 7), (0, chan_rows * LANES - chan_len)
    ).reshape(chan_rows, LANES)
    hidden, wx, gate, chan_full, wo = collect(
        0, hidden_in[0], w_in, w_out, chan_block, groups, parts
    )
    chan_full = chan_full.reshape(groups * parts, chan_rows * LANES)[:, :chan_len].reshape(-1)
    line = groups // 2
    group = lax.axis_index("dp")

    conv_taps = chan_full[: TAPS * CONV_CH].reshape(TAPS, CONV_CH)
    conv_bias = chan_full[TAPS * CONV_CH : (TAPS + 1) * CONV_CH].reshape(1, CONV_CH)
    offset = (TAPS + 1) * CONV_CH
    gain_in = chan_full[offset : offset + D]
    gain_out = chan_full[offset + D : offset + D + INNER]
    taps_all = jnp.concatenate(
        [conv_taps, conv_bias, jnp.zeros((8 - TAPS - 1, CONV_CH), F32)], axis=0
    )
    taps = jnp.concatenate(
        [lax.dynamic_slice(taps_all, (0, q * cw), (8, cw)), taps_all[:, INNER:]], axis=1
    )
    own_gain = lax.dynamic_slice(gain_out, (q * cw,), (cw,))
    own_heads = lax.dynamic_slice(head_params, (0, q * hq), (3, hq))
    heads = jnp.pad(
        jnp.stack([own_heads[0], -jnp.exp(own_heads[1])]), ((0, 6), (0, LANES - hq))
    )
    skip = jnp.repeat(own_heads[2], P_SIZE).reshape(1, cw)
    spread = (
        jnp.arange(LANES)[:, None] == (jnp.arange(cw) // P_SIZE)[None, :]
    ).astype(BF16)

    normed, px, y, states, z, u_blocks, wz, wo = forward(
        1, hidden.reshape(length, D), wx.reshape(D, cc + LANES), gate, wo, gain_in.reshape(1, D),
        own_gain.reshape(1, cw), taps, heads, skip, spread,
    )
    wx, wz = wx.reshape(D, cc + LANES), wz.reshape(D, cw)
    cotangent = out_grads[:, 0]
    back_own, coefs, block_out, dwo_left, dwo_right, _ = middle(
        2, u_blocks.reshape(parts, rows, cw + LANES), wo, cotangent, hidden_in[0]
    )
    block_out = block_out[:, None]

    dz, dpx, small, dwo_left, dwz = backward(
        5, back_own.reshape(length, cw), coefs.reshape(length, LANES), normed, px, y, z, states,
        dwo_left, own_gain.reshape(1, cw), taps, heads, skip, spread,
    )
    x_part, left_part, right_part, z_part, dnormed, small = sum_to_owners(
        4, normed, dwo_left, dwo_right, dwz.reshape(parts, in_rows, cw), small, dz, dpx, wz, wx
    )
    hidden_grad, chan_total, head_total, norm = gradient_norm(
        6, x_part, z_part, left_part, right_part, dnormed, small, hidden_in[0],
        gain_in.reshape(1, D), cotangent, groups,
    )
    (
        hidden_grad, w_in_new, w_in_m_new, w_in_v_new, w_in_copy,
        w_out_new, w_out_m_new, w_out_v_new, w_out_copy,
    ) = update_weights(
        norm, x_part, z_part, left_part, right_part, hidden_grad,
        (w_in, w_in_m, w_in_v, w_out, w_out_m, w_out_v),
    )
    hidden_grad = hidden_grad[None]
    grad_norm, clip_factor = norm[0, 0], norm[1, 0]
    owner = group * parts + q
    chan_part = lax.dynamic_slice(chan_total.reshape(-1), (owner * chan_len,), (chan_len,))
    head_total = head_total[:parts, : 3 * hq].reshape(parts, 3, hq)
    head_total = head_total.transpose(1, 0, 2).reshape(3, H)
    chan_new, chan_m_new, chan_v_new = adam_tile(
        chan_params, clip_factor * chan_part, chan_m, chan_v, 0.2, 0.0
    )
    head_new, head_m_new, head_v_new = adam_tile(
        head_params, clip_factor * head_total, head_m, head_v, 1.0, 0.0
    )
    return (
        block_out, hidden_grad, grad_norm,
        w_in_new, w_in_m_new, w_in_v_new, w_in_copy,
        w_out_new, w_out_m_new, w_out_v_new, w_out_copy,
        chan_new, chan_m_new, chan_v_new, head_new, head_m_new, head_v_new,
    )


def solution(mesh):
    rows = P(("dp", "seq"), None)
    flat = P(("dp", "seq"))
    in_specs = (
        P("dp", "seq", None),
        P(None, "dp", "seq", None),
        *([rows] * 6),
        *([flat] * 3),
        *([P()] * 3),
    )
    out_specs = (
        P(None, "dp", "seq", None),
        P("dp", "seq", None),
        P(),
        *([rows] * 8),
        *([flat] * 3),
        *([P()] * 3),
    )
    return jax.shard_map(
        on_device, mesh=mesh, in_specs=in_specs, out_specs=out_specs, check_vma=False
    )
```

```python
import functools

import jax
import jax.numpy as jnp
from jax import lax
from jax.experimental import pallas as pl
from jax.experimental.pallas import tpu as pltpu
from jax.sharding import PartitionSpec as P

D = 2048
INNER = 4096
H = 64
P_SIZE = 64
N = 128
TAPS = 4
STEP = 10
E_IN = 8512
CONV_CH = 4352
LANES = 128
CHUNK = 128
LEVELS = 4

EXACT = lax.Precision.HIGHEST
EPS_IN = 1e-06
EPS_OUT = 1e-05
ADAM_EPS = 1e-08
BETA = 0.5
CLIP = 1.0
F32 = jnp.float32
BF16 = jnp.bfloat16
MASKED = -1e30


def level_width(level):
    return INNER * 2**level // 8


SEGMENTS = tuple(
    (0 if level == 0 else level_width(level - 1), level_width(level)) for level in range(LEVELS)
)


def dot(a, b, dims=((1,), (0,)), precision=None):
    return lax.dot_general(a, b, (dims, ((), ())), precision=precision, preferred_element_type=F32)


NT = ((1,), (1,))
TN = ((0,), (0,))


def softplus(v):
    return jnp.maximum(v, 0.0) + jnp.log1p(jnp.exp(-jnp.abs(v)))


def two_terms(v):
    high = v.astype(BF16)
    return high, (v - high.astype(F32)).astype(BF16)


def spread_heads(v, spread):
    high, rest = two_terms(v)
    return dot(high, spread) + dot(rest, spread)


def own_heads_first(dt_raw, hq, back=False):
    by = lax.axis_index("seq") * hq
    return pltpu.roll(dt_raw, by if back else lax.rem(LANES - by, LANES), 1)


def rates(dt_raw, heads):
    step = softplus(dt_raw + heads[0:1, :])
    return step, step * heads[1:2, :]


def triangle(size):
    row = lax.broadcasted_iota(jnp.int32, (size, size), 0)
    col = lax.broadcasted_iota(jnp.int32, (size, size), 1)
    return row, col


def conv_block(taps, xbuf, lanes):
    out = taps[TAPS : TAPS + 1, lanes]
    for tap in range(TAPS):
        out = out + taps[tap : tap + 1, lanes] * xbuf[5 + tap : 5 + tap + CHUNK, lanes]
    return out


def pair_decay(cum, cum_t, causal, head):
    gap = cum[:, head : head + 1] - cum_t[head : head + 1, :]
    return jnp.exp(jnp.where(causal, gap, MASKED))


def scan_forward_step(cw, px, taps, heads, skip, spread, y, states, xbuf, state, xdt, carried):
    cc = cw + 2 * N
    xbuf[8 : 8 + CHUNK, :] = px[:, :cc]
    step, rate = rates(own_heads_first(px[:, cc:], cw // P_SIZE), heads)
    row, col = triangle(CHUNK)
    causal = row >= col
    cum = dot(causal.astype(F32), rate, precision=EXACT)
    cum_t = cum.T
    spread_m = spread[...]
    last = cum[CHUNK - 1 : CHUNK, :]
    step_x = spread_heads(step, spread_m)
    grow_x = spread_heads(jnp.exp(cum), spread_m)
    tail_x = spread_heads(jnp.exp(last - cum), spread_m)

    def activated(lanes):
        conv = conv_block(taps, xbuf, lanes)
        return conv * jax.nn.sigmoid(conv)

    state_in = activated(slice(cw, cw + N))
    state_out = activated(slice(cw + N, cw + 2 * N))
    scores = dot(state_out, state_in, NT, EXACT)
    states[...] = state[...].astype(BF16)
    carried[...] = dot(state_out.astype(BF16), state[...].astype(BF16))
    first = lax.broadcasted_iota(jnp.int32, (1, LANES), 1) < P_SIZE
    for pair in range(cw // LANES):
        lanes = slice(pair * LANES, (pair + 1) * LANES)
        x = activated(lanes)
        xd = (x * step_x[:, lanes]).astype(BF16).astype(F32)
        xdt[:, lanes] = (xd * tail_x[:, lanes]).astype(BF16)
        stacked = jnp.concatenate([jnp.where(first, xd, 0.0), jnp.where(first, 0.0, xd)], axis=0)
        mixing = jnp.concatenate(
            [
                (pair_decay(cum, cum_t, causal, 2 * pair + k) * scores).astype(BF16)
                for k in range(2)
            ],
            axis=1,
        )
        y[:, lanes] = (
            dot(mixing, stacked.astype(BF16))
            + grow_x[:, lanes] * carried[:, lanes]
            + skip[:, lanes] * x
        )
    state[...] = grow_x[CHUNK - 1 : CHUNK, :] * state[...] + dot(
        state_in.astype(BF16), xdt[...], TN
    )
    xbuf[0:8, :] = xbuf[CHUNK : CHUNK + 8, :]


def scan_backward_step(
    cw, start, px, halo, taps, heads, skip, spread, gather, dy, y, states,
    dpx, dtaps, dheads, dskip,
    xbuf, dstate, dcbuf, slope, xact, xd_s, dxd_s, acc_s,
):
    cc = cw + 2 * N
    xbuf[0:8, :] = jnp.where(start, 0.0, halo[:, :cc])
    xbuf[8 : 8 + CHUNK, :] = px[:, :cc]
    dt_raw = own_heads_first(px[:, cc:], cw // P_SIZE)
    step, rate = rates(dt_raw, heads)
    row, col = triangle(CHUNK)
    causal = row >= col
    cum = dot(causal.astype(F32), rate, precision=EXACT)
    cum_t = cum.T
    spread_m = spread[...]
    last = cum[CHUNK - 1 : CHUNK, :]
    step_x = spread_heads(step, spread_m)
    grow_x = spread_heads(jnp.exp(cum), spread_m)
    tail_x = spread_heads(jnp.exp(last - cum), spread_m)

    for block in range(cc // LANES):
        lanes = slice(block * LANES, (block + 1) * LANES)
        conv = conv_block(taps, xbuf, lanes)
        sig = jax.nn.sigmoid(conv)
        act = conv * sig
        xact[:, lanes] = act
        slope[:, lanes] = sig + act * (1.0 - sig)
    state_in = xact[:, cw : cw + N]
    state_out = xact[:, cw + N : cc]
    scores = dot(state_out, state_in, NT, EXACT)
    in_low = state_in.astype(BF16)
    out_low = state_out.astype(BF16)
    dstate_low = dstate[...].astype(BF16)
    acc_s[...] = jnp.zeros_like(acc_s)
    dxd_s[...] = tail_x * dot(in_low, dstate_low)
    dskip[0:1, :] += jnp.sum(xact[:, :cw] * dy[...], axis=0, keepdims=True)
    first = lax.broadcasted_iota(jnp.int32, (1, LANES), 1) < P_SIZE
    xd_s[...] = (xact[:, :cw] * step_x).astype(BF16)
    total = jnp.sum(xd_s[...].astype(F32) * dxd_s[...], axis=0, keepdims=True) + grow_x[
        CHUNK - 1 : CHUNK, :
    ] * jnp.sum(dstate[...] * states[...].astype(F32), axis=0, keepdims=True)
    dscores = jnp.zeros((CHUNK, CHUNK), F32)
    for pair in range(cw // LANES):
        lanes = slice(pair * LANES, (pair + 1) * LANES)
        dyp = dy[:, lanes]
        stacked = jnp.concatenate(
            [jnp.where(first, dyp, 0.0), jnp.where(first, 0.0, dyp)], axis=0
        ).astype(BF16)
        decays = [pair_decay(cum, cum_t, causal, 2 * pair + k) for k in range(2)]
        mixing = jnp.concatenate([(decay * scores).astype(BF16) for decay in decays], axis=0)
        dxd_s[:, lanes] += dot(mixing, stacked, TN)
        dmix = dot(stacked, xd_s[:, lanes], NT)
        dscores = dscores + decays[0] * dmix[:CHUNK] + decays[1] * dmix[CHUNK:]
    dy_low = dy[...].astype(BF16)
    dy_f = dy_low.astype(F32)
    xd_f = xd_s[...].astype(F32)
    dxd = dxd_s[...]
    y_scan = y[...] - skip[...] * xact[:, :cw]
    final = lax.broadcasted_iota(jnp.int32, (CHUNK, 1), 0) == CHUNK - 1
    gather_m = gather[...]
    dcum = spread_heads(dy_f * y_scan - xd_f * dxd + jnp.where(final, total, 0.0), gather_m)
    dstep = spread_heads(xact[:, :cw] * dxd, gather_m)
    drate = dot((row <= col).astype(F32), dcum, precision=EXACT)
    dstep = dstep + drate * heads[1:2, :]
    ddt = dstep * jax.nn.sigmoid(dt_raw + heads[0:1, :])
    dheads[0:1, :] += jnp.sum(ddt, axis=0, keepdims=True)
    dheads[1:2, :] += jnp.sum(drate * rate, axis=0, keepdims=True)
    grown = (grow_x * dy_f).astype(BF16)
    dscores_low = dscores.astype(BF16)
    dout = dot(dscores_low, in_low) + dot(grown, states[...], NT)
    din = dot(dscores_low, out_low, TN) + dot((tail_x * xd_f).astype(BF16), dstate_low, NT)
    dstate[...] = grow_x[CHUNK - 1 : CHUNK, :] * dstate[...] + dot(out_low, grown, TN)
    dcbuf[:CHUNK, :cw] = (step_x * dxd + skip[...] * dy[...]) * slope[:, :cw]
    dcbuf[:CHUNK, cw : cw + N] = din * slope[:, cw : cw + N]
    dcbuf[:CHUNK, cw + N :] = dout * slope[:, cw + N :]
    for block in range(cc // LANES):
        lanes = slice(block * LANES, (block + 1) * LANES)
        dconv = dcbuf[:CHUNK, lanes]
        dtaps[TAPS : TAPS + 1, lanes] += jnp.sum(dconv, axis=0, keepdims=True)
        back = taps[TAPS - 1 : TAPS, lanes] * dconv
        for tap in range(TAPS):
            dtaps[tap : tap + 1, lanes] += jnp.sum(
                dconv * xbuf[5 + tap : 5 + tap + CHUNK, lanes], axis=0, keepdims=True
            )
            if tap < TAPS - 1:
                reach = TAPS - 1 - tap
                back = back + taps[tap : tap + 1, lanes] * dcbuf[reach : reach + CHUNK, lanes]
        dpx[:, lanes] = back.astype(BF16)
    ours = lax.broadcasted_iota(jnp.int32, (1, LANES), 1) < cw // P_SIZE
    ddt = own_heads_first(jnp.where(ours, ddt, 0.0), cw // P_SIZE, back=True)
    dpx[:, cc:] = ddt.astype(BF16)
    dcbuf[CHUNK : CHUNK + 8, :] = dcbuf[0:8, :]


WIDE = 512
LEFT = 1280


MESH = pl.DeviceIdType.MESH


def remote(src, dst, sends, recvs, index, device):
    return pltpu.make_async_remote_copy(
        src_ref=src,
        dst_ref=dst,
        send_sem=sends.at[index],
        recv_sem=recvs.at[index],
        device_id=device,
        device_id_type=MESH,
    )


def greet(devices):
    barrier = pltpu.get_barrier_semaphore()
    for device in devices:
        pl.semaphore_signal(barrier, inc=1, device_id=device, device_id_type=MESH)
    pl.semaphore_wait(barrier, len(devices))


def seq_peers(parts):
    group, q = lax.axis_index("dp"), lax.axis_index("seq")
    return [(group, lax.rem(q + k, parts)) for k in range(1, parts)]


def dp_peers(groups):
    group, q = lax.axis_index("dp"), lax.axis_index("seq")
    return [(lax.rem(group + k, groups), q) for k in range(1, groups)]


def all_peers(groups, parts):
    devices = groups * parts
    me = lax.axis_index("dp") * parts + lax.axis_index("seq")
    peers = []
    for k in range(1, devices):
        other = lax.rem(me + k, devices)
        peers.append((other // parts, lax.rem(other, parts)))
    return peers


CHAN_ROWS = ((TAPS + 1) * CONV_CH + D + INNER) // LANES


def adam_tile(weight, gradient, moment, second, step_rate, weight_decay):
    new_moment = BETA * moment + (1.0 - BETA) * gradient
    new_second = BETA * second + (1.0 - BETA) * gradient * gradient
    correction = 1.0 - BETA**STEP
    update = new_moment / correction / (jnp.sqrt(new_second / correction) + ADAM_EPS)
    return weight - step_rate * (update + weight_decay * weight), new_moment, new_second


def total_of(value):
    return jnp.sum(jnp.sum(value, axis=1, keepdims=True), axis=0, keepdims=True)


def norm_kernel(
    groups, parts,
    part_h, rest_h, gate_h, left_h, right_h, back_h, small_h, hidden_h, gain, cotangent,
    hidden_grad, chan, head, norm,
    part, rest, gate, left, right, back, small, hidden,
    cot_v, block, near, all_block, all_near, sends, recvs, near_s, near_r, load, local,
):
    group, q = lax.axis_index("dp"), lax.axis_index("seq")
    me = group * parts + q
    cw = INNER // parts
    cc = cw + 2 * N
    everyone = all_peers(groups, parts)
    fetches = [
        pltpu.make_async_copy(source, target, load.at[k])
        for k, (source, target) in enumerate(
            [(back_h, back), (hidden_h, hidden), (part_h, part), (gate_h, gate),
             (left_h, left), (right_h, right), (small_h, small), (rest_h, rest),
             (cotangent, cot_v)]
        )
    ]
    for copy in fetches:
        copy.start()
    barrier = pltpu.get_barrier_semaphore()
    for device in everyone:
        pl.semaphore_signal(barrier, inc=1, device_id=device, device_id_type=MESH)
    for copy in fetches[:8]:
        copy.wait()
    total = small[0]
    for k in range(1, groups):
        total = total + small[k]
    near[...] = total
    rows = 32

    def summed(at):
        down = back[at, :]
        tokens = hidden[at, :].astype(F32)
        mean = jnp.sum(tokens * tokens, axis=-1, keepdims=True) / D
        return down, tokens, lax.rsqrt(mean + EPS_IN)

    def gain_rows(i, dgain):
        at = pl.ds(pl.multiple_of(i * rows, rows), rows)
        down, tokens, scale = summed(at)
        return dgain + jnp.sum(down * tokens * scale, axis=0, keepdims=True)

    dgain = lax.fori_loop(0, hidden.shape[0] // rows, gain_rows, jnp.zeros((1, D), F32))
    tail = rest[:, : 2 * N + H]
    squares = total_of(tail * tail)
    for k in range(parts):
        x = part[k].astype(F32)
        g = gate[k].astype(F32)
        squares = squares + total_of(x * x + g * g)
    squares = squares + total_of(left[...] * left[...]) + total_of(right[...] * right[...])
    for k in range(D // LANES):
        block[k : k + 1, :] = dgain[:, k * LANES : (k + 1) * LANES]
    block[D // LANES :, :] = jnp.broadcast_to(squares, (8, LANES))
    pl.semaphore_wait(barrier, len(everyone))
    copies = [
        remote(block, all_block.at[me], sends, recvs, k, peer) for k, peer in enumerate(everyone)
    ]
    copies += [
        remote(near, all_near.at[q], near_s, near_r, k, peer)
        for k, peer in enumerate(seq_peers(parts))
    ]
    copies += [
        pltpu.make_async_copy(block, all_block.at[me], local.at[0]),
        pltpu.make_async_copy(near, all_near.at[q], local.at[1]),
    ]
    for copy in copies:
        copy.start()
    fetches[8].wait()

    def grad_rows(i, carry):
        at = pl.ds(pl.multiple_of(i * rows, rows), rows)
        down, tokens, scale = summed(at)
        scaled = down * gain[...]
        inner = jnp.sum(scaled * tokens, axis=-1, keepdims=True) / D
        direct = cot_v[0, at, :].astype(F32)
        for k in range(1, LEVELS):
            direct = direct + cot_v[k, at, :].astype(F32)
        hidden_grad[at, :] = (
            scale * scaled - tokens * (scale * scale * scale * inner) + direct
        )
        return carry

    lax.fori_loop(0, hidden.shape[0] // rows, grad_rows, 0)
    for copy in copies:
        copy.wait()
    total = jnp.sum(all_block[...], axis=0)
    own, wide = cw // LANES, cc // LANES
    span = CONV_CH // LANES
    for tap in range(TAPS + 1):
        for k in range(parts):
            at = tap * span + k * own
            chan[at : at + own, :] = all_near[k, tap * wide : tap * wide + own, :]
        shared = all_near[0, tap * wide + own : (tap + 1) * wide, :]
        for k in range(1, parts):
            shared = shared + all_near[k, tap * wide + own : (tap + 1) * wide, :]
        chan[tap * span + INNER // LANES : (tap + 1) * span, :] = shared
    at = (TAPS + 1) * span
    chan[at : at + D // LANES, :] = total[: D // LANES]
    at = at + D // LANES
    for k in range(parts):
        first = (TAPS + 1) * wide
        chan[at + k * own : at + (k + 1) * own, :] = all_near[k, first : first + own, :]
        head[k : k + 1, :] = all_near[k, first + own : first + own + 1, :]
    squares = (
        total[D // LANES : D // LANES + 1, :1]
        + total_of(chan[:CHAN_ROWS, :] * chan[:CHAN_ROWS, :])
        + total_of(head[:parts, :] * head[:parts, :])
    )
    grad_norm = jnp.sqrt(squares)
    norm[0:1, :] = jnp.broadcast_to(grad_norm, (1, LANES))
    norm[1:2, :] = jnp.broadcast_to(jnp.minimum(1.0, CLIP / grad_norm), (1, LANES))


def gradient_norm(
    collective_id, part, rest, gate, left, right, back, small, hidden, gain, cotangent, groups
):
    parts = part.shape[0]
    devices = groups * parts
    sem = pltpu.SemaphoreType.DMA
    vmem = pl.BlockSpec(memory_space=pltpu.VMEM)
    hbm = pl.BlockSpec(memory_space=pltpu.HBM)
    block = (D // LANES + 8, LANES)
    chan_rows = -(-CHAN_ROWS // 8) * 8
    return pl.pallas_call(
        functools.partial(norm_kernel, groups, parts),
        in_specs=[*([hbm] * 8), vmem, hbm],
        out_specs=[vmem] * 4,
        out_shape=[
            jax.ShapeDtypeStruct(hidden.shape, F32),
            jax.ShapeDtypeStruct((chan_rows, LANES), F32),
            jax.ShapeDtypeStruct((8, LANES), F32),
            jax.ShapeDtypeStruct((8, LANES), F32),
        ],
        scratch_shapes=[
            *[
                pltpu.VMEM(a.shape, a.dtype)
                for a in (part, rest, gate, left, right, back, small, hidden)
            ],
            pltpu.VMEM(cotangent.shape, BF16),
            pltpu.VMEM(block, F32),
            pltpu.VMEM(small.shape[1:], F32),
            pltpu.VMEM((devices,) + block, F32),
            pltpu.VMEM((parts,) + small.shape[1:], F32),
            sem((devices - 1,)), sem((devices - 1,)), sem((parts - 1,)), sem((parts - 1,)),
            sem((9,)), sem((2,)),
        ],
        compiler_params=pltpu.CompilerParams(
            collective_id=collective_id, has_side_effects=True, vmem_limit_bytes=63 * 2**20
        ),
        name="gradient_norm",
    )(part, rest, gate, left, right, back, small, hidden, gain, cotangent)


BLOCKS = 4


def update_kernel(
    parts, norm, part_h, rest_h, gate_h, left_h, right_h, hidden_grad, block, *refs
):
    ins, refs = refs[:6], refs[6:]
    hidden_out, block_out, outs, refs = refs[0], refs[1], refs[2:10], refs[10:]
    held, made = refs[:6], refs[6:14]
    part, rest, gate, left, right, hidden_v, block_v, load, store, grads = refs[14:]
    clip = norm[1:2, :1]
    cw = INNER // parts
    fetches = [
        pltpu.make_async_copy(source, target, grads.at[k])
        for k, (source, target) in enumerate(
            [(part_h, part), (gate_h, gate), (left_h, left), (right_h, right), (rest_h, rest),
             (hidden_grad, hidden_v), (block, block_v)]
        )
    ]
    for copy in fetches[:5]:
        copy.start()

    def at(a, i):
        rows = ins[a].shape[0] // BLOCKS
        return pl.ds(i * rows, rows)

    loads = [
        [
            pltpu.make_async_copy(ins[a].at[at(a, i)], held[a].at[at(a, i)], load.at[a * BLOCKS + i])
            for a in range(6)
        ]
        for i in range(BLOCKS)
    ]
    for weight in (0, 3):
        for i in range(BLOCKS):
            for a in range(weight, weight + 3):
                loads[i][a].start()
    for copy in fetches[5:]:
        copy.start()
    stores = []

    def update(weight, rows, lanes, gradient, rate, decay):
        first = 0 if weight == 0 else 4
        new, moment, second = adam_tile(
            held[weight][rows, lanes], clip * gradient, held[weight + 1][rows, lanes],
            held[weight + 2][rows, lanes], rate, decay,
        )
        made[first][rows, lanes] = new
        made[first + 1][rows, lanes] = moment
        made[first + 2][rows, lanes] = second
        made[first + 3][rows, lanes] = new.astype(BF16)

    def send(first, rows, i):
        for a in range(first, first + 4):
            copy = pltpu.make_async_copy(
                made[a].at[rows], outs[a].at[rows], store.at[a * BLOCKS + i]
            )
            copy.start()
            stores.append(copy)

    for copy in fetches[:5]:
        copy.wait()
    for i in range(BLOCKS):
        rows = at(0, i)
        for a in range(3):
            loads[i][a].wait()
        for source, first in ((gate, 0), (part, INNER)):

            def step(k, carry, source=source, first=first, rows=rows):
                to = pl.ds(pl.multiple_of(first + k * cw, cw), cw)
                update(0, rows, to, source[k, rows, :cw].astype(F32), 0.02, 0.1)
                return carry

            lax.fori_loop(0, parts, step, 0)
        update(0, rows, slice(2 * INNER, E_IN), rest[rows, : 2 * N + H], 0.02, 0.1)
        send(0, rows, i)
    fetches[5].wait()
    fetches[6].wait()
    for source, target, k in ((hidden_v, hidden_out, 7), (block_v, block_out, 8)):
        copy = pltpu.make_async_copy(source, target, grads.at[k])
        copy.start()
        stores.append(copy)
    for i in range(BLOCKS):
        rows = at(3, i)
        for a in range(3, 6):
            loads[i][a].wait()
        update(3, rows, slice(0, LEFT), left[rows, :], 0.03, 0.1)
        update(3, rows, slice(LEFT, D), right[rows, :], 0.03, 0.1)
        send(4, rows, i)
    for copy in stores:
        copy.wait()


def update_weights(norm, part, rest, gate, left, right, hidden_grad, block, weights):
    parts = part.shape[0]
    w_in, w_out = weights[0], weights[3]
    sem = pltpu.SemaphoreType.DMA
    vmem = pl.BlockSpec(memory_space=pltpu.VMEM)
    hbm = pl.BlockSpec(memory_space=pltpu.HBM)
    made = [
        jax.ShapeDtypeStruct(w.shape, dtype) for w in (w_in, w_out) for dtype in (F32, F32, F32, BF16)
    ]
    return pl.pallas_call(
        functools.partial(update_kernel, parts),
        in_specs=[vmem, *([hbm] * 13)],
        out_specs=[hbm] * 10,
        out_shape=[
            jax.ShapeDtypeStruct(hidden_grad.shape, F32),
            jax.ShapeDtypeStruct(block.shape, BF16),
            *made,
        ],
        scratch_shapes=[
            *[pltpu.VMEM(w.shape, F32) for w in weights],
            *[pltpu.VMEM(m.shape, m.dtype) for m in made],
            *[
                pltpu.VMEM(a.shape, a.dtype)
                for a in (part, rest, gate, left, right, hidden_grad, block)
            ],
            sem((6 * BLOCKS,)), sem((8 * BLOCKS,)), sem((9,)),
        ],
        compiler_params=pltpu.CompilerParams(vmem_limit_bytes=63 * 2**20),
        name="update_weights",
    )(norm, part, rest, gate, left, right, hidden_grad, block, *weights)


class LineGather:
    def __init__(self, line, z, core, q, slot, own, sends, recvs):
        self.line, self.z, self.core, self.q = line, z, core, q
        self.slot, self.own, self.sends, self.recvs = slot, own, sends, recvs

    def along(self, from_z, up, first=False):
        to = self.z + 1 if up else self.z - 1
        return remote(
            self.own if first else self.slot(from_z),
            self.slot(from_z),
            self.sends.at[0 if up else 1],
            self.recvs.at[0 if up else 1],
            from_z,
            (2 * to + self.core, self.q),
        )

    def push(self, t):
        z, line = self.z, self.line

        @pl.when((z - t >= 0) & (z < line - 1))
        def _():
            self.along(z - t, True, t == 0).start()

        @pl.when((z + t <= line - 1) & (z > 0))
        def _():
            self.along(z + t, False, t == 0).start()

    def pushed(self, t):
        z, line = self.z, self.line

        @pl.when((z - t >= 0) & (z < line - 1))
        def _():
            self.along(z - t, True, t == 0).wait_send()

        @pl.when((z + t <= line - 1) & (z > 0))
        def _():
            self.along(z + t, False, t == 0).wait_send()

    def step(self, t, got=None, push=True):
        z, line = self.z, self.line

        @pl.when(z - t >= 0)
        def _():
            self.along(z - t, True).wait_recv()

            if push:

                @pl.when(z < line - 1)
                def _():
                    self.along(z - t, True).start()

            if got is not None:
                got(z - t)

        @pl.when(z + t <= line - 1)
        def _():
            self.along(z + t, False).wait_recv()

            if push:

                @pl.when(z > 0)
                def _():
                    self.along(z + t, False).start()

            if got is not None:
                got(z + t)


class LineGathers:
    def __init__(self, line, z, core, q, slot, own, sends, recvs):
        half = own.shape[0] // 2
        self.line = line
        self.halves = []
        for h in range(2):
            rows = pl.ds(h * half, half)
            self.halves.append(
                LineGather(
                    line, z, core, q, lambda from_z, rows=rows: slot(from_z).at[rows],
                    own.at[rows], sends.at[h], recvs.at[h],
                )
            )

    def push(self, t):
        for part in self.halves:
            part.push(t)

    def step(self, t, got=None, push=True):
        self.halves[0].step(t, None, push)
        self.halves[1].step(t, got, push)

    def pushed(self):
        for t in range(self.line - 1):
            for part in self.halves:
                part.pushed(t)


class PlaneGather:
    def __init__(self, parts, slot, own, sends, recvs, base=0):
        self.parts, self.slot, self.own = parts, slot, own
        self.sends, self.recvs, self.base = sends, recvs, base
        self.group, self.q = lax.axis_index("dp"), lax.axis_index("seq")
        if parts == 4:
            self.near = [self.q + 1 - 2 * lax.rem(self.q, 2), lax.rem(self.q + 2, 4)]
            self.half = own.shape[0] // 2

    def early(self):
        to = self.near if self.parts == 4 else [peer[1] for peer in seq_peers(self.parts)]
        return [
            remote(
                self.own, self.slot(self.q), self.sends, self.recvs, self.base + k, (self.group, d)
            )
            for k, d in enumerate(to)
        ]

    def late(self):
        if self.parts != 4:
            return []
        copies = []
        for h in range(2):
            block = self.slot(self.near[h]).at[pl.ds(h * self.half, self.half)]
            to = (self.group, self.near[1 - h])
            copies.append(remote(block, block, self.sends, self.recvs, self.base + 2 + h, to))
        return copies

    def start(self):
        for copy in self.early():
            copy.start()

    def turn(self):
        if self.parts == 4:
            for copy in self.early():
                copy.wait()
            for copy in self.late():
                copy.start()

    def finish(self):
        for copy in self.late() if self.parts == 4 else self.early():
            copy.wait()


def collect_kernel(
    groups, parts, hidden, w_in, w_own, chan, hid_out, w_out, gate_out, chan_out, wo_out,
    blocks, gates, low, chan_s, chan_r, hid_s, hid_r, swap_s, swap_r, gate_s, gate_r,
    wo_s, wo_r, line_s, line_r, lwo_s, lwo_r, core_s, core_r, local,
):
    line = groups // 2
    cw = INNER // parts
    cc = cw + 2 * N
    group, q = lax.axis_index("dp"), lax.axis_index("seq")
    z, core = group // 2, lax.rem(group, 2)
    sibling = (2 * z + 1 - core, q)
    peers = seq_peers(parts)
    everyone = all_peers(groups, parts)
    shared = w_in[:, 2 * INNER :].astype(BF16)
    for part in range(parts):
        at = INNER + part * cw
        blocks[part, :, :cw] = w_in[:, at : at + cw].astype(BF16)
        blocks[part, :, cw : cc + H] = shared
        blocks[part, :, cc + H :] = jnp.zeros((w_in.shape[0], LANES - H), BF16)
    low[...] = w_own[...].astype(BF16)
    greet(everyone)
    swaps = []
    for k, peer in enumerate(peers):
        copy = remote(blocks.at[peer[1]], w_out.at[group, q], swap_s, swap_r, k, peer)
        copy.start()
        swaps.append(copy)
    outs = LineGather(
        line, z, core, q, lambda from_z: wo_out.at[2 * from_z + core, q], low, lwo_s, lwo_r
    )
    outs.push(0)
    own = [
        pltpu.make_async_copy(blocks.at[q], w_out.at[group, q], local.at[0]),
        pltpu.make_async_copy(hidden, hid_out.at[q], local.at[1]),
        pltpu.make_async_copy(chan, chan_out.at[group * parts + q], local.at[2]),
        pltpu.make_async_copy(low, wo_out.at[group, q], local.at[3]),
    ]
    for copy in own:
        copy.start()
    waiting = []
    for k, peer in enumerate(everyone):
        copy = remote(chan, chan_out.at[group * parts + q], chan_s, chan_r, k, peer)
        copy.start()
        waiting.append(copy)
    for part in range(parts):
        gates[part] = w_in[:, part * cw : (part + 1) * cw].astype(BF16)
    copy = pltpu.make_async_copy(gates.at[q], gate_out.at[q], local.at[4])
    copy.start()
    own.append(copy)
    own[0].wait()
    for copy in swaps:
        copy.wait()
    hids = PlaneGather(parts, lambda of: hid_out.at[of], hidden, hid_s, hid_r)
    lows = PlaneGather(parts, lambda of: wo_out.at[group, of], low, wo_s, wo_r)
    hids.start()

    def across(from_z):
        block = w_out.at[2 * from_z + core]
        return remote(block, block, core_s, core_r, from_z, sibling)

    ins = LineGathers(
        line, z, core, q, lambda from_z: w_out.at[2 * from_z + core], w_out.at[group],
        line_s, line_r,
    )
    across(z).start()
    ins.push(0)
    lows.start()
    for t in range(1, line):
        ins.step(t, lambda from_z: across(from_z).start(), t < line - 1)
        if t == line - 2:
            outs.step(1)
            hids.turn()
            lows.turn()
            for k, peer in enumerate(peers):
                copy = remote(gates.at[peer[1]], gate_out.at[q], gate_s, gate_r, k, peer)
                copy.start()
                waiting.append(copy)
    ins.pushed()
    outs.step(2, None, False)
    outs.pushed(0)
    outs.pushed(1)
    hids.finish()
    lows.finish()
    for from_z in range(line):
        across(from_z).wait_send()
        block = w_out.at[2 * from_z + 1 - core]
        remote(block, block, core_s, core_r, from_z, sibling).wait_recv()
    for copy in own[1:] + waiting:
        copy.wait()


def collect(collective_id, hidden, w_in, w_own, chan, groups, parts):
    rows = w_in.shape[0]
    line = groups // 2
    cw = INNER // parts
    width = cw + 2 * N + LANES
    sem = pltpu.SemaphoreType.DMA
    hbm = pl.BlockSpec(memory_space=pltpu.HBM)
    vmem = pl.BlockSpec(memory_space=pltpu.VMEM)
    return pl.pallas_call(
        functools.partial(collect_kernel, groups, parts),
        in_specs=[hbm, vmem, vmem, hbm],
        out_specs=[hbm] * 5,
        out_shape=[
            jax.ShapeDtypeStruct((parts,) + hidden.shape, hidden.dtype),
            jax.ShapeDtypeStruct((groups, parts, rows, width), BF16),
            jax.ShapeDtypeStruct((parts, rows, cw), BF16),
            jax.ShapeDtypeStruct((groups * parts,) + chan.shape, chan.dtype),
            jax.ShapeDtypeStruct((groups, parts) + w_own.shape, BF16),
        ],
        scratch_shapes=[
            pltpu.VMEM((parts, rows, width), BF16),
            pltpu.VMEM((parts, rows, cw), BF16),
            pltpu.VMEM(w_own.shape, BF16),
            *([sem((groups * parts - 1,))] * 2),
            *([sem((parts + 1,))] * 8),
            *([sem((2, 2, line))] * 2), *([sem((2, line))] * 2),
            sem((line,)), sem((line,)), sem((5,)),
        ],
        compiler_params=pltpu.CompilerParams(
            collective_id=collective_id, has_side_effects=True, vmem_limit_bytes=48 * 2**20
        ),
        name="collect",
    )(hidden, w_in, w_own, chan)


def forward_kernel(
    groups, parts, cw,
    hidden_h, wx_h, gate_h, wo_in, gain_in, gain_out, taps, heads, skip, spread,
    normed_h, px_h, y_h, states_h, z_h, u_h, wz_h, wo,
    hidden, wx, wz, normed, px, y, states, zs, us, xbuf, state, xdt, carried,
    line_s, line_r, lwo_s, lwo_r, core_s, core_r, wo_s, wo_r, out_s, out_r, u_s, u_r, load, store,
):
    line = groups // 2
    cc = cw + 2 * N
    length = px.shape[0]
    chunks = length // CHUNK
    group, q = lax.axis_index("dp"), lax.axis_index("seq")
    z, core = group // 2, lax.rem(group, 2)
    sibling = (2 * z + 1 - core, q)
    peers = mirror_peers(parts)
    loads = [
        pltpu.make_async_copy(source, target, load.at[k])
        for k, (source, target) in enumerate(
            [(hidden_h, hidden), (wx_h, wx), (gate_h, wz.at[group])]
        )
    ]
    for copy in loads:
        copy.start()
    greet(peers + dp_peers(groups))

    outs = LineGather(
        line, z, core, q, lambda from_z: wo.at[2 * from_z + core, q], wo.at[group, q], lwo_s, lwo_r
    )

    def planes(t, act):
        for from_z, there in ((z - t, z - t >= 0), (z + t, z + t <= line - 1)):

            @pl.when(there)
            def _(from_z=from_z):
                block = wo.at[2 * from_z + core]
                act(
                    PlaneGather(
                        parts, lambda of: block.at[of], block.at[q], out_s, out_r,
                        from_z * (parts + 1),
                    )
                )

    outs.push(2)
    planes(1, PlaneGather.start)
    planes(2, PlaneGather.start)

    def across(from_z):
        block = wz.at[2 * from_z + core]
        return remote(block, block, core_s, core_r, from_z, sibling)

    gates = LineGathers(
        line, z, core, q, lambda from_z: wz.at[2 * from_z + core], wz.at[group], line_s, line_r
    )
    loads[2].wait()
    across(z).start()
    gates.push(0)
    loads[0].wait()

    def norm_rows(i, carry):
        rows = pl.ds(pl.multiple_of(i * 32, 32), 32)
        tokens = hidden[rows, :].astype(F32)
        mean = jnp.sum(tokens * tokens, axis=-1, keepdims=True) / D
        normed[rows, :] = (tokens * lax.rsqrt(mean + EPS_IN) * gain_in[...]).astype(BF16)
        return carry

    lax.fori_loop(0, length // 32, norm_rows, 0)
    loads[1].wait()
    tall = 256

    def project_rows(i, carry):
        rows = pl.ds(pl.multiple_of(i * tall, tall), tall)
        px[rows, :] = dot(normed[rows, :], wx[...])
        return carry

    lax.fori_loop(0, length // tall, project_rows, 0)
    stores = [
        pltpu.make_async_copy(normed, normed_h, store.at[0]),
        pltpu.make_async_copy(px, px_h, store.at[1]),
    ]
    for copy in stores:
        copy.start()
    state[...] = jnp.zeros_like(state)
    xbuf[0:8, :] = jnp.zeros((8, cc), F32)

    def scan_rows(i, carry):
        for t in range(1, line - 1):

            @pl.when(i == min(5 * t - 4, chunks - 1))
            def _(t=t):
                gates.step(t, lambda from_z: across(from_z).start(), t < line - 1)

        for t in range(3, line):

            @pl.when(i == min(2 * t - 3, chunks - 1))
            def _(t=t):
                outs.step(t, None, t < line - 1)
                planes(t, PlaneGather.start)

        rows = pl.ds(pl.multiple_of(i * CHUNK, CHUNK), CHUNK)
        scan_forward_step(
            cw, px.at[rows], taps, heads, skip, spread, y.at[rows], states.at[i],
            xbuf, state, xdt, carried,
        )
        return carry

    lax.fori_loop(0, chunks, scan_rows, 0)
    for source, target, at in ((y, y_h, 2), (states, states_h, 3)):
        copy = pltpu.make_async_copy(source, target, store.at[at])
        copy.start()
        stores.append(copy)
    for t in range(1, line):
        planes(t, PlaneGather.turn)
    gates.step(line - 1, lambda from_z: across(from_z).start(), False)
    for from_z in range(line):
        across(from_z).wait_send()
        block = wz.at[2 * from_z + 1 - core]
        remote(block, block, core_s, core_r, from_z, sibling).wait_recv()
    gates.pushed()
    for t in range(2, line - 1):
        outs.pushed(t)
    copy = pltpu.make_async_copy(wz, wz_h, store.at[4])
    copy.start()
    stores.append(copy)
    lane = lax.broadcasted_iota(jnp.int32, (1, LANES), 1)
    wide = 512

    def gate_rows(rows):
        gate_in = dot(normed[rows, :], wz[...].reshape(D, cw))
        zs[rows, :] = gate_in
        gated = y[rows, :] * (gate_in * jax.nn.sigmoid(gate_in))
        us[rows, :cw] = (gated * gain_out[...]).astype(BF16)
        highs = jnp.zeros((tall, LANES), F32)
        rests = jnp.zeros((tall, LANES), F32)
        for b in range(cw // wide):
            block = gated[:, b * wide : (b + 1) * wide]
            total = jnp.sum(block * block, axis=-1, keepdims=True)
            level = level_of(q * cw + b * wide, wide)
            highs = highs + jnp.where(lane == level, total, 0.0)
            rests = rests + jnp.where(lane == level + LEVELS, total, 0.0)
        rests = rests - rests.astype(BF16).astype(F32)
        us[rows, cw:] = jnp.where(lane < LEVELS, highs, rests).astype(BF16)

    waiting = []
    tokens = length // parts
    for k, dest in enumerate([peer[1] for peer in peers] + [q]):

        def block_rows(i, carry, dest=dest):
            gate_rows(pl.ds(pl.multiple_of(dest * tokens + i * tall, tall), tall))
            return carry

        lax.fori_loop(0, tokens // tall, block_rows, 0)
        ours = us.at[pl.ds(pl.multiple_of(dest * tokens, tokens), tokens)]
        if k < len(peers):
            copy = remote(ours, u_h.at[q], u_s, u_r, k, peers[k])
        else:
            copy = pltpu.make_async_copy(ours, u_h.at[q], store.at[6])
        copy.start()
        waiting.append(copy)
    copy = pltpu.make_async_copy(zs, z_h, store.at[5])
    copy.start()
    stores.append(copy)

    def parity(d, of):
        block = wo.at[2 * d + of]
        return remote(block, block, wo_s, wo_r, d, sibling)

    for t in range(1, line):
        planes(t, PlaneGather.finish)
    for d in range(line):
        parity(d, core).start()
    for copy in waiting + stores:
        copy.wait()
    for d in range(line):
        parity(d, core).wait_send()
        parity(d, 1 - core).wait_recv()


def forward(collective_id, hidden, wx, gate, wo, gain_in, gain_out, taps, heads, skip, spread):
    groups, parts = wo.shape[:2]
    line = groups // 2
    length = hidden.shape[0]
    rows, cw = gate.shape[1:]
    cc = cw + 2 * N
    width = cc + LANES
    chunks = length // CHUNK
    sem = pltpu.SemaphoreType.DMA
    hbm = pl.BlockSpec(memory_space=pltpu.HBM)
    vmem = pl.BlockSpec(memory_space=pltpu.VMEM)
    u = jax.ShapeDtypeStruct((parts, length // parts, cw + LANES), BF16)
    made = [
        jax.ShapeDtypeStruct((length, D), BF16),
        jax.ShapeDtypeStruct((length, width), F32),
        jax.ShapeDtypeStruct((length, cw), F32),
        jax.ShapeDtypeStruct((chunks, N, cw), BF16),
        jax.ShapeDtypeStruct((length, cw), F32),
        jax.ShapeDtypeStruct((length, cw + LANES), BF16),
    ]
    wz = jax.ShapeDtypeStruct((groups, parts, rows, cw), BF16)
    return pl.pallas_call(
        functools.partial(forward_kernel, groups, parts, cw),
        in_specs=[*([hbm] * 4), *([vmem] * 6)],
        out_specs=[hbm] * 8,
        out_shape=[*made[:-1], u, wz, jax.ShapeDtypeStruct(wo.shape, BF16)],
        input_output_aliases={3: 7},
        scratch_shapes=[
            pltpu.VMEM(hidden.shape, BF16),
            pltpu.VMEM(wx.shape, BF16),
            pltpu.VMEM(wz.shape, BF16),
            *[pltpu.VMEM(m.shape, m.dtype) for m in made],
            pltpu.VMEM((CHUNK + 8, cc), F32),
            pltpu.VMEM((N, cw), F32),
            pltpu.VMEM((CHUNK, cw), BF16),
            pltpu.VMEM((CHUNK, cw), F32),
            *([sem((2, 2, line))] * 2), *([sem((2, line))] * 2),
            *([sem((line,))] * 4),
            sem((line * (parts + 1),)), sem((line * (parts + 1),)),
            sem((parts - 1,)), sem((parts - 1,)),
            sem((3,)), sem((7,)),
        ],
        compiler_params=pltpu.CompilerParams(
            collective_id=collective_id, has_side_effects=True, vmem_limit_bytes=63 * 2**20
        ),
        name="forward",
    )(hidden, wx, gate, wo, gain_in, gain_out, taps, heads, skip, spread)


def add_blocks(out, a, b, rows, steps):
    def step(i, carry):
        at = pl.ds(pl.multiple_of(i * rows, rows), rows)
        out[at] = (a[at].astype(F32) + b[at].astype(F32)).astype(out.dtype)
        return carry

    lax.fori_loop(0, steps, step, 0)


def level_of(channel, width):
    return sum((channel >= level_width(k)).astype(jnp.int32) for k in range(LEVELS - 1))


def mirror_peers(parts):
    group, q = lax.axis_index("dp"), lax.axis_index("seq")
    if parts != 4:
        return seq_peers(parts)
    return [(group, 3 - q), (group, q + 1 - 2 * lax.rem(q, 2)), (group, lax.rem(q + 2, 4))]


def middle_kernel(
    groups, parts, cw,
    u_h, wo, cot_h, tokens_h,
    back_h, coef_h, block_h, left_h, right_h,
    u, cot, tokens, mixed, branch, norms, pulls, back, coefs, weights, sent, held, left, right,
    back_s, back_r, coef_s, coef_r, core_s, core_r, fetch, load, store, local,
):
    line = groups // 2
    group, q = lax.axis_index("dp"), lax.axis_index("seq")
    z, core = group // 2, lax.rem(group, 2)
    sibling = (2 * z + 1 - core, q)
    peers = mirror_peers(parts)
    loads = [
        pltpu.make_async_copy(u_h, u, load.at[0]),
        pltpu.make_async_copy(cot_h, cot, load.at[1]),
        pltpu.make_async_copy(tokens_h, tokens, load.at[2]),
    ]
    for copy in loads:
        copy.start()
    greet(peers + [sibling])
    for copy in loads:
        copy.wait()

    terms = u[0, :, cw:].astype(F32)
    for part in range(1, parts):
        terms = terms + u[part, :, cw:].astype(F32)
    squares = jnp.zeros((terms.shape[0], 1), F32)
    for k in range(LEVELS):
        squares = squares + terms[:, k : k + 1] + terms[:, LEVELS + k : LEVELS + k + 1]
        norms[:, k : k + 1] = lax.rsqrt(squares / level_width(k) + EPS_OUT)
    rows = 32

    def mix_rows(i, carry):
        at = pl.ds(pl.multiple_of(i * rows, rows), rows)
        running = norms[at, LEVELS - 1 : LEVELS] * cot[LEVELS - 1, at, :].astype(F32)
        mixed[LEVELS - 1, at, :] = running.astype(BF16)
        for k in reversed(range(LEVELS - 1)):
            running = running + norms[at, k : k + 1] * cot[k, at, :].astype(F32)
            mixed[k, at, :] = running.astype(BF16)
        return carry

    lax.fori_loop(0, tokens.shape[0] // rows, mix_rows, 0)

    width = INNER // groups
    per = WIDE // width
    slots = weights.shape[0]
    dests = [peer[1] for peer in peers] + [q]
    firsts = [dest * cw + b * WIDE for dest in dests for b in range(cw // WIDE)]
    firsts += [b * WIDE for b in range(INNER // WIDE)]

    def get(i):
        return pltpu.make_async_copy(
            wo.at[pl.ds(firsts[i] // width, per)], weights.at[i % slots], fetch.at[i % slots]
        )

    def block_of(i):
        get(i).wait()
        return weights[i % slots].reshape(WIDE, D)

    for i in range(slots - 1):
        get(i).start()
    outgoing = []
    for i in range(len(dests) * (cw // WIDE)):
        get(i + slots - 1).start()
        at, b = divmod(i, cw // WIDE)
        lanes = slice(b * WIDE, (b + 1) * WIDE)
        level = level_of(firsts[i], WIDE)
        back[dests[at], :, lanes] = dot(mixed[level], block_of(i), NT).astype(BF16)
        if b == cw // WIDE - 1:
            if at < len(peers):
                copy = remote(back.at[dests[at]], back_h.at[q], back_s, back_r, at, peers[at])
            else:
                copy = pltpu.make_async_copy(back.at[q], back_h.at[q], local.at[0])
            copy.start()
            outgoing.append(copy)
    first = len(dests) * (cw // WIDE)
    branch[...] = jnp.zeros_like(branch)
    for b in range(INNER // WIDE):
        if first + b + slots - 1 < len(firsts):
            get(first + b + slots - 1).start()
        part, at = divmod(b * WIDE, cw)
        branch[...] += dot(u[part, :, at : at + WIDE], block_of(first + b))
        for k in range(LEVELS):
            if level_width(k) == (b + 1) * WIDE:

                def level_rows(i, carry, k=k):
                    at = pl.ds(pl.multiple_of(i * rows, rows), rows)
                    norm = norms[at, k : k + 1]
                    total = branch[at, :]
                    inner = jnp.sum(cot[k, at, :].astype(F32) * total, axis=-1, keepdims=True)
                    pulls[at, k : k + 1] = norm * norm * norm * (inner / level_width(k))
                    cot[k, at, :] = (tokens[at, :].astype(F32) + norm * total).astype(BF16)
                    return carry

                lax.fori_loop(0, tokens.shape[0] // rows, level_rows, 0)
                copy = pltpu.make_async_copy(cot.at[k], block_h.at[k], store.at[k])
                copy.start()
                outgoing.append(copy)
    coef = jnp.zeros((tokens.shape[0], 1), F32)
    lane = lax.broadcasted_iota(jnp.int32, (1, LANES), 1)
    packed = jnp.zeros((tokens.shape[0], LANES), F32)
    for k in reversed(range(LEVELS)):
        coef = coef + pulls[:, k : k + 1]
        high, rest = two_terms(coef)
        packed = jnp.where(lane == k, high.astype(F32), packed)
        packed = jnp.where(lane == LEVELS + k, rest.astype(F32), packed)
    coefs[...] = packed.astype(BF16)
    for k, peer in enumerate(peers):
        copy = remote(coefs, coef_h.at[q], coef_s, coef_r, k, peer)
        copy.start()
        outgoing.append(copy)
    copy = pltpu.make_async_copy(coefs, coef_h.at[q], local.at[1])
    copy.start()
    outgoing.append(copy)

    share = width // parts
    tile = 256
    turns = LEFT // tile

    def product(of, j):
        channel = of * width
        lanes = pl.ds(pl.multiple_of(lax.rem(channel, cw), width), width)
        cols = pl.ds(pl.multiple_of(j * tile, tile), tile)
        return dot(u[channel // cw, :, lanes], mixed[level_of(channel, width), :, cols], TN)

    cores = []
    for d in range(line):

        def send_step(j, carry, d=d):
            cols = pl.ds(pl.multiple_of(j * tile, tile), tile)
            sent[d, :, cols] = product(2 * d + 1 - core, j).astype(BF16)
            return carry

        lax.fori_loop(0, D // tile, send_step, 0)
        copy = remote(sent.at[d], held.at[d], core_s, core_r, d, sibling)
        copy.start()
        cores.append(copy)
    for d in range(line):
        cores[d].wait_recv()
        for out, target, first, at in ((left, left_h, 0, 0), (right, right_h, turns, 1)):

            def keep_step(j, carry, d=d, out=out, first=first):
                cols = pl.ds(pl.multiple_of((j + first) * tile, tile), tile)
                to = pl.ds(pl.multiple_of(j * tile, tile), tile)
                total = product(2 * d + core, j + first) + held[d, :, cols].astype(F32)
                total = total.astype(BF16)
                for part in range(parts):
                    out[part, d, :, to] = total[part * share : (part + 1) * share]
                return carry

            lax.fori_loop(0, out.shape[-1] // tile, keep_step, 0)
            copy = pltpu.make_async_copy(
                out.at[:, d], target.at[:, d], store.at[LEVELS + 2 * d + at]
            )
            copy.start()
            outgoing.append(copy)
    for copy in cores:
        copy.wait_send()
    for copy in outgoing:
        copy.wait()


def middle(collective_id, u, wo, cotangent, tokens):
    groups, parts, share = wo.shape[:3]
    line = groups // 2
    rows, wide = u.shape[1:]
    cw = wide - LANES
    width = share * parts
    sem = pltpu.SemaphoreType.DMA
    hbm = pl.BlockSpec(memory_space=pltpu.HBM)
    left = (parts, line, share, LEFT)
    right = (parts, line, share, D - LEFT)
    return pl.pallas_call(
        functools.partial(middle_kernel, groups, parts, cw),
        in_specs=[hbm] * 4,
        out_specs=[hbm] * 5,
        out_shape=[
            jax.ShapeDtypeStruct((parts, rows, cw), BF16),
            jax.ShapeDtypeStruct((parts, rows, LANES), BF16),
            jax.ShapeDtypeStruct(cotangent.shape, BF16),
            jax.ShapeDtypeStruct(left, BF16),
            jax.ShapeDtypeStruct(right, BF16),
        ],
        scratch_shapes=[
            pltpu.VMEM(u.shape, BF16),
            pltpu.VMEM(cotangent.shape, BF16),
            pltpu.VMEM(tokens.shape, BF16),
            pltpu.VMEM(cotangent.shape, BF16),
            pltpu.VMEM((rows, D), F32),
            pltpu.VMEM((rows, LANES), F32),
            pltpu.VMEM((rows, LANES), F32),
            pltpu.VMEM((parts, rows, cw), BF16),
            pltpu.VMEM((rows, LANES), BF16),
            pltpu.VMEM((3, WIDE // width, parts, share, D), BF16),
            pltpu.VMEM((line, width, D), BF16),
            pltpu.VMEM((line, width, D), BF16),
            pltpu.VMEM(left, BF16),
            pltpu.VMEM(right, BF16),
            *([sem((parts - 1,))] * 4),
            sem((line,)), sem((line,)), sem((3,)), sem((3,)), sem((LEVELS + 2 * line,)), sem((2,)),
        ],
        compiler_params=pltpu.CompilerParams(
            collective_id=collective_id, has_side_effects=True, vmem_limit_bytes=63 * 2**20
        ),
        name="middle",
    )(u, wo, cotangent, tokens)


def sum_blocks(out, blocks, rows):
    def step(i, carry):
        at = pl.ds(pl.multiple_of(i * rows, rows), rows)
        total = blocks[0][at].astype(F32)
        for block in blocks[1:]:
            total = total + block[at].astype(F32)
        out[at] = total.astype(out.dtype)
        return carry

    lax.fori_loop(0, out.shape[0] // rows, step, 0)


class PlaneSum:
    def __init__(self, parts, group, q, blocks, first, second, sends, recvs, source=None):
        self.parts, self.group, self.q = parts, group, q
        self.source = blocks if source is None else source
        self.blocks, self.first, self.second = blocks, first, second
        self.sends, self.recvs = sends, recvs
        self.half = blocks.shape[1] // 2
        if parts == 4:
            self.near = [q + 1 - 2 * lax.rem(q, 2), lax.rem(q + 2, 4)]
            self.far = 3 - q

    @staticmethod
    def scratch(parts, shape, dtype):
        if parts == 4:
            half = (shape[0] // 2,) + shape[1:]
            first, second, count = (2, 2) + half, (2, 2) + half, 6
        else:
            first, second, count = (parts - 1,) + shape, (1, 16, LANES), parts - 1
        sem = pltpu.SemaphoreType.DMA
        return [pltpu.VMEM(first, dtype), pltpu.VMEM(second, dtype), sem((count,)), sem((count,))]

    def piece(self, of, h, source=None):
        blocks = self.blocks if source is None else source
        return blocks.at[of, pl.ds(h * self.half, self.half)]

    def early(self, h):
        if self.parts != 4:
            return []
        near = self.near[h]
        to = (self.group, near)
        return [
            remote(
                self.piece(of, h, self.source), self.first.at[h, k],
                self.sends, self.recvs, 2 * h + k, to,
            )
            for k, of in enumerate((near, self.far))
        ]

    def late(self, h):
        to = (self.group, self.near[1 - h])
        return remote(
            self.second.at[h, 0], self.second.at[h, 1], self.sends, self.recvs, 4 + h, to
        )

    def direct(self):
        peers = seq_peers(self.parts)
        return [
            remote(self.source.at[peer[1]], self.first.at[k], self.sends, self.recvs, k, peer)
            for k, peer in enumerate(peers)
        ]

    def start(self, h):
        for copy in self.early(h):
            copy.start()
        if self.parts != 4 and h == 1:
            for copy in self.direct():
                copy.start()

    def turn(self, rows):
        if self.parts != 4:
            return
        for h in range(2):
            for copy in self.early(h):
                copy.wait()
            beyond = self.piece(self.near[1 - h], h)
            each(self.second.at[h, 0], [beyond, self.first.at[h, 1]], rows)
            self.late(h).start()

    def finish(self, out, rows):
        if self.parts != 4:
            for copy in self.direct():
                copy.wait()
            each(
                out,
                [self.blocks.at[self.q]] + [self.first.at[k] for k in range(self.parts - 1)],
                rows,
            )
            return
        for h in range(2):
            self.late(h).wait()
            each(
                out.at[pl.ds(h * self.half, self.half)],
                [self.piece(self.q, h), self.first.at[h, 0], self.second.at[h, 1]],
                rows,
            )


def each(out, blocks, rows):
    if len(out.shape) == 2:
        sum_blocks(out, blocks, rows)
        return
    for d in range(out.shape[0]):
        sum_blocks(out.at[d], [block.at[d] for block in blocks], rows)


class LineSum:
    def __init__(self, line, z, core, q, acc, up, down, up_s, up_r, down_s, down_r, rows, steps):
        self.line, self.z, self.core, self.q = line, z, core, q
        self.acc, self.up, self.down = acc, up, down
        self.up_s, self.up_r, self.down_s, self.down_r = up_s, up_r, down_s, down_r
        self.rows, self.steps = rows, steps

    def ahead(self, d, first):
        block = self.acc.at[d] if first else self.up.at[d]
        to = (2 * (self.z + 1) + self.core, self.q)
        return remote(block, self.up.at[d], self.up_s, self.up_r, d, to)

    def behind(self, d, first):
        block = self.acc.at[d] if first else self.down.at[d]
        to = (2 * (self.z - 1) + self.core, self.q)
        return remote(block, self.down.at[d], self.down_s, self.down_r, d, to)

    def add(self, into, d):
        add_blocks(into.at[d], into.at[d], self.acc.at[d], self.rows, self.steps)

    def step(self, t):
        line, z = self.line, self.z
        far, near = line - 1 - t + z, t - (line - 1 - z)

        @pl.when(z == 0)
        def _():
            self.ahead(line - 1 - t, True).start()

        @pl.when((z > 0) & (z <= t))
        def _():
            self.ahead(far, False).wait_recv()
            self.add(self.up, far)
            self.ahead(far, False).start()

        @pl.when(z == line - 1)
        def _():
            self.behind(t, True).start()

        @pl.when((z < line - 1) & (line - 1 - z <= t))
        def _():
            self.behind(near, False).wait_recv()
            self.add(self.down, near)
            self.behind(near, False).start()

    def sent(self, t):
        line, z = self.line, self.z
        far, near = line - 1 - t + z, t - (line - 1 - z)

        @pl.when(z == 0)
        def _():
            self.ahead(line - 1 - t, True).wait_send()

        @pl.when((z > 0) & (z <= t))
        def _():
            self.ahead(far, False).wait_send()

        @pl.when(z == line - 1)
        def _():
            self.behind(t, True).wait_send()

        @pl.when((z < line - 1) & (line - 1 - z <= t))
        def _():
            self.behind(near, False).wait_send()

    def finish(self, out):
        line, z = self.line, self.z

        @pl.when(z == 0)
        def _():
            self.behind(z, False).wait_recv()
            add_blocks(out, self.acc.at[z], self.down.at[z], self.rows, self.steps)

        @pl.when(z == line - 1)
        def _():
            self.ahead(z, False).wait_recv()
            add_blocks(out, self.acc.at[z], self.up.at[z], self.rows, self.steps)

        @pl.when((z > 0) & (z < line - 1))
        def _():
            self.ahead(z, False).wait_recv()
            self.add(self.up, z)
            self.behind(z, False).wait_recv()
            add_blocks(out, self.up.at[z], self.down.at[z], self.rows, self.steps)


class LineSums:
    def __init__(self, line, z, core, q, acc, up, down, sems, rows):
        half = acc.shape[1] // 2
        self.line = line
        self.halves = [
            LineSum(
                line, z, core, q, *[a.at[:, pl.ds(h * half, half)] for a in (acc, up, down)],
                *[s.at[h] for s in sems], rows, half // rows,
            )
            for h in range(2)
        ]
        self.half = half

    def step(self, t):
        for part in self.halves:
            part.step(t)

    def finish(self, out):
        for h, part in enumerate(self.halves):
            part.finish(out.at[pl.ds(h * self.half, self.half)])

    def sent(self):
        for t in range(self.line - 1):
            for part in self.halves:
                part.sent(t)


def backward_kernel(
    groups, parts, cw,
    back_h, coefs_h, normed_h, px_h, y_h, z_h, states_h, wide_h,
    gain, taps, heads, skip, spread, gather,
    dz_h, dpx_h, small, wide_sum, gate_sum,
    dz, coefs, normed, px, y, dy, states, wide, dpx, dtaps, dheads, dskip, dgain,
    xbuf, dstate, dcbuf, slope, xact, xd_s, dxd_s, acc_s,
    first, second, wide_s, wide_r, gate_made, gate_held, gate_acc, gate_up, gate_down,
    core_s, core_r, up_s, up_r, down_s, down_r, load, store,
):
    line = groups // 2
    cc = cw + 2 * N
    length = y.shape[0]
    chunks = length // CHUNK
    group, q = lax.axis_index("dp"), lax.axis_index("seq")
    z, core = group // 2, lax.rem(group, 2)
    sibling = (2 * z + 1 - core, q)
    loads = [
        pltpu.make_async_copy(source, target, load.at[k])
        for k, (source, target) in enumerate(
            [(wide_h, wide), (back_h, dz), (coefs_h, coefs), (y_h, y), (z_h, dy),
             (normed_h, normed), (states_h, states)]
        )
    ]
    for copy in loads[1:5]:
        copy.start()

    def fetch(at, first=False):
        slot = lax.rem(at, 2)
        if first:
            return pltpu.make_async_copy(
                px_h.at[pl.ds(0, CHUNK)], px.at[0, pl.ds(8, CHUNK)], load.at[7]
            )
        rows = pl.ds(pl.multiple_of(at * CHUNK - 8, 8), CHUNK + 8)
        return pltpu.make_async_copy(px_h.at[rows], px.at[slot], load.at[7 + slot])

    greet(seq_peers(parts) + dp_peers(groups))
    plane = PlaneSum(parts, group, q, wide, first, second, wide_s, wide_r, wide_h)
    plane.start(0)
    plane.start(1)
    for copy in loads[1:5]:
        copy.wait()
    loads[5].start()
    loads[6].start()
    loads[0].start()
    fetch(chunks - 1).start()

    rows = 32
    lane = lax.broadcasted_iota(jnp.int32, (1, LANES), 1)
    dgain[...] = jnp.zeros_like(dgain)

    def gate_rows(i, carry):
        at = pl.ds(pl.multiple_of(i * rows, rows), rows)
        coef = coefs[at, :].astype(F32)
        for b in range(cw // WIDE):
            lanes = slice(b * WIDE, (b + 1) * WIDE)
            level = level_of(q * cw + b * WIDE, WIDE)
            ours = (lane == level) | (lane == level + LEVELS)
            pull = jnp.sum(jnp.where(ours, coef, 0.0), axis=-1, keepdims=True)
            gate_in = dy[at, lanes]
            sig = jax.nn.sigmoid(gate_in)
            gate = gate_in * sig
            y_at = y[at, lanes]
            gated = y_at * gate
            back = dz[at, lanes].astype(F32)
            dgated = gain[:, lanes] * back - gated * pull
            dgain[0:1, lanes] += jnp.sum(back * gated, axis=0, keepdims=True)
            dz[at, lanes] = (dgated * y_at * (sig + gate * (1.0 - sig))).astype(BF16)
            dy[at, lanes] = dgated * gate
        return carry

    lax.fori_loop(0, length // rows, gate_rows, 0)
    dz_out = pltpu.make_async_copy(dz, dz_h, store.at[0])
    dz_out.start()
    loads[5].wait()
    span = gate_acc.shape[1]

    def dweight(of, out):
        at = pl.ds(pl.multiple_of(of * span, span), span)
        out[...] = dot(normed[:, at], dz[...], TN).astype(BF16)

    def core_copy(d):
        return remote(gate_made.at[d], gate_held.at[d], core_s, core_r, d, sibling)

    order = [d for k in range(line // 2) for d in (line - 1 - k, k)]
    gates = LineSums(
        line, z, core, q, gate_acc, gate_up, gate_down, (up_s, up_r, down_s, down_r), span // 8
    )
    for some in (order[:2], order[2:]):
        for d in some:
            dweight(2 * d + 1 - core, gate_made.at[d])
            core_copy(d).start()
        for d in some:
            dweight(2 * d + core, gate_acc.at[d])
            core_copy(d).wait()
            add_blocks(gate_acc.at[d], gate_acc.at[d], gate_held.at[d], span // 4, 4)
        if some[0] == order[0]:
            gates.step(0)
    dstate[...] = jnp.zeros_like(dstate)
    dcbuf[CHUNK : CHUNK + 8, :] = jnp.zeros((8, cc), F32)
    dtaps[...] = jnp.zeros_like(dtaps)
    dheads[...] = jnp.zeros_like(dheads)
    dskip[...] = jnp.zeros_like(dskip)
    loads[6].wait()
    loads[0].wait()

    def scan_rows(i, carry):
        for t in range(1, line - 1):

            @pl.when(i == min(3 * t - 2, chunks - 1))
            def _(t=t):
                gates.step(t)

        @pl.when(i == 3)
        def _():
            plane.turn(32)

        at = chunks - 1 - i
        here = pl.ds(pl.multiple_of(at * CHUNK, CHUNK), CHUNK)

        @pl.when(at > 0)
        def _():
            fetch(at).wait()

        @pl.when(at == 0)
        def _():
            fetch(0, True).wait()

        @pl.when(at > 1)
        def _():
            fetch(at - 1).start()

        @pl.when(at == 1)
        def _():
            fetch(0, True).start()

        rows = px.at[lax.rem(at, 2)]
        scan_backward_step(
            cw, at == 0, rows.at[pl.ds(8, CHUNK)], rows.at[pl.ds(0, 8)], taps, heads, skip, spread, gather,
            dy.at[here], y.at[here], states.at[at], dpx.at[here], dtaps, dheads, dskip,
            xbuf, dstate, dcbuf, slope, xact, xd_s, dxd_s, acc_s,
        )
        return carry

    lax.fori_loop(0, chunks, scan_rows, 0)
    dpx_out = pltpu.make_async_copy(dpx, dpx_h, store.at[1])
    dpx_out.start()
    small[...] = jnp.zeros_like(small)
    wide_rows, own_rows = cc // LANES, cw // LANES
    for tap in range(TAPS + 1):
        for b in range(wide_rows):
            to = tap * wide_rows + b
            small[to : to + 1, :] = dtaps[tap : tap + 1, b * LANES : (b + 1) * LANES]
    to = (TAPS + 1) * wide_rows
    for b in range(own_rows):
        small[to + b : to + b + 1, :] = dgain[0:1, b * LANES : (b + 1) * LANES]
    hq = cw // P_SIZE
    skips = spread_heads(dskip[...], gather[...])
    small[to + own_rows : to + own_rows + 1, :] = (
        dheads[0:1, :]
        + pltpu.roll(dheads[...], hq, 1)[1:2, :]
        + pltpu.roll(skips, 2 * hq, 1)[0:1, :]
    )
    plane.finish(wide_sum, 32)
    gates.finish(gate_sum)
    gates.sent()
    dz_out.wait()
    dpx_out.wait()


def backward(
    collective_id, back, coefs, normed, px, y, z, states, wide, gain, taps, heads, skip, spread
):
    parts, line = wide.shape[:2]
    length, width = px.shape
    cw = skip.shape[1]
    cc = cw + 2 * N
    span = D // (2 * line)
    sem = pltpu.SemaphoreType.DMA
    vmem = pl.BlockSpec(memory_space=pltpu.VMEM)
    hbm = pl.BlockSpec(memory_space=pltpu.HBM)
    small_rows = (TAPS + 1) * (cc // LANES) + cw // LANES + 1
    small_rows = -(-small_rows // 8) * 8
    return pl.pallas_call(
        functools.partial(backward_kernel, 2 * line, parts, cw),
        in_specs=[*([hbm] * 8), *([vmem] * 6)],
        out_specs=[hbm, hbm, vmem, vmem, vmem],
        out_shape=[
            jax.ShapeDtypeStruct((length, cw), BF16),
            jax.ShapeDtypeStruct((length, width), BF16),
            jax.ShapeDtypeStruct((small_rows, LANES), F32),
            jax.ShapeDtypeStruct(wide.shape[1:], BF16),
            jax.ShapeDtypeStruct((span, cw), BF16),
        ],
        scratch_shapes=[
            *[pltpu.VMEM(a.shape, a.dtype) for a in (back, coefs, normed)],
            pltpu.VMEM((2, CHUNK + 8, width), F32),
            *[pltpu.VMEM(a.shape, a.dtype) for a in (y, z, states, wide)],
            pltpu.VMEM((length, width), BF16),
            pltpu.VMEM((8, cc), F32),
            pltpu.VMEM((8, LANES), F32),
            pltpu.VMEM((8, cw), F32),
            pltpu.VMEM((8, cw), F32),
            pltpu.VMEM((CHUNK + 8, cc), F32),
            pltpu.VMEM((N, cw), F32),
            pltpu.VMEM((CHUNK + 8, cc), F32),
            pltpu.VMEM((CHUNK, cc), F32),
            pltpu.VMEM((CHUNK, cc), F32),
            pltpu.VMEM((CHUNK, cw), BF16),
            pltpu.VMEM((CHUNK, cw), F32),
            pltpu.VMEM((CHUNK, CHUNK), F32),
            *PlaneSum.scratch(parts, wide.shape[1:], BF16),
            *([pltpu.VMEM((line, span, cw), BF16)] * 5),
            sem((line,)), sem((line,)), *([sem((2, line))] * 4),
            sem((9,)), sem((2,)),
        ],
        compiler_params=pltpu.CompilerParams(
            collective_id=collective_id, has_side_effects=True, vmem_limit_bytes=63 * 2**20
        ),
        name="backward",
    )(back, coefs, normed, px, y, z, states, wide, gain, taps, heads, skip, spread, spread.T)


def owners_kernel(
    groups, parts, rows, cw,
    normed, left, right, gate, small, dz, dpx, wz, wx,
    part, rest_out, left_out, right_out, gate_out, back_out, small_all,
    made, held, acc, up, down, final, left_up, left_down, right_acc, right_up, right_down,
    rest_made, rest_held, rest, rest_acc, rest_up, rest_down,
    normed_v, dz_v, dpx_v, wz_v, wx_v, back, back_sum,
    right_1, right_2, right_s, right_r, back_1, back_2, back_s, back_r,
    rest_1, rest_2, rest_s, rest_r,
    core_s, core_r, up_s, up_r, down_s, down_r, lup_s, lup_r, ldown_s, ldown_r,
    rup_s, rup_r, rdown_s, rdown_r, tup_s, tup_r, tdown_s, tdown_r, rcore_s, rcore_r,
    part_s, part_r, gate_s, gate_r, small_s, small_r, load, local,
):
    line = groups // 2
    span = parts * rows
    group, q = lax.axis_index("dp"), lax.axis_index("seq")
    z, core = group // 2, lax.rem(group, 2)
    sibling = (2 * z + 1 - core, q)
    peers, others = seq_peers(parts), dp_peers(groups)
    tokens = back.shape[1]
    loads = [
        pltpu.make_async_copy(source, target, load.at[k])
        for k, (source, target) in enumerate(
            [(normed, normed_v), (dpx, dpx_v), (dz, dz_v), (wz, wz_v), (wx, wx_v)]
        )
    ]
    for copy in loads[:2]:
        copy.start()
    greet(peers + others)
    half_rows = left.shape[1] // 2
    lefts = LineSum(
        line, z, core, q, left, left_up, left_down, lup_s, lup_r, ldown_s, ldown_r, half_rows, 2
    )
    rights = LineSum(
        line, z, core, q, right_acc, right_up, right_down, rup_s, rup_r, rdown_s, rdown_r,
        half_rows, 2,
    )
    wholes = LineSum(
        line, z, core, q, acc, up, down, up_s, up_r, down_s, down_r, rows, parts
    )
    lefts.step(0)
    right_plane = PlaneSum(parts, group, q, right, right_1, right_2, right_s, right_r)
    rest_plane = PlaneSum(parts, group, q, rest, rest_1, rest_2, rest_s, rest_r)
    rests = LineSum(
        line, z, core, q, rest_acc, rest_up, rest_down, tup_s, tup_r, tdown_s, tdown_r, rows, 1
    )
    back_plane = PlaneSum(parts, group, q, back, back_1, back_2, back_s, back_r)
    right_plane.start(0)
    right_plane.start(1)
    waiting = []
    for k, peer in enumerate(peers):
        copy = remote(gate.at[peer[1]], gate_out.at[q], gate_s, gate_r, k, peer)
        copy.start()
        waiting.append(copy)
    for k, peer in enumerate(others):
        copy = remote(small, small_all.at[group], small_s, small_r, k, peer)
        copy.start()
        waiting.append(copy)
    own = [
        pltpu.make_async_copy(gate.at[q], gate_out.at[q], local.at[0]),
        pltpu.make_async_copy(small, small_all.at[group], local.at[1]),
    ]
    for copy in own:
        copy.start()
    loads[0].wait()
    loads[1].wait()
    for copy in loads[2:]:
        copy.start()
    tile = 512

    def dweight(of):
        at = pl.ds(pl.multiple_of(of * span, span), span)
        return dot(normed_v[:, at], dpx_v[...], TN)

    cores = {}
    order = [d for k in range(line // 2) for d in (line - 1 - k, k)]

    def share_core(d):
        total = dweight(2 * d + 1 - core)
        made[d] = total[:, :cw].astype(BF16)
        rest_made[d] = total[:, cw:].astype(BF16)
        cores[d] = [
            remote(made.at[d], held.at[d], core_s, core_r, d, sibling),
            remote(rest_made.at[d], rest_held.at[d], rcore_s, rcore_r, d, sibling),
        ]
        for copy in cores[d]:
            copy.start()

    def sum_core(d):
        total = dweight(2 * d + core)
        for copy in cores[d]:
            copy.wait()
        acc[d] = (total[:, :cw] + held[d].astype(F32)).astype(BF16)
        others = (total[:, cw:] + rest_held[d].astype(F32)).astype(BF16)
        for k in range(parts):
            rest[k, d] = others[k * rows : (k + 1) * rows]

    share_core(order[0])
    lefts.sent(0)
    lefts.step(1)
    share_core(order[1])
    sum_core(order[0])
    for t in range(2, line - 1):
        lefts.sent(t - 1)
        lefts.step(t)
    sum_core(order[1])
    wholes.step(0)
    for d in order[2:]:
        share_core(d)
    for d in order[2:]:
        sum_core(d)
    rest_plane.start(0)
    rest_plane.start(1)
    for copy in loads[2:]:
        copy.wait()

    def dnormed(of):
        at = pl.ds(pl.multiple_of(of * tokens, tokens), tokens)

        def step(j, carry):
            cols = pl.ds(pl.multiple_of(j * tile, tile), tile)
            back[of, :, cols] = (
                dot(dz_v[at, :], wz_v[cols, :], NT) + dot(dpx_v[at, :], wx_v[cols, :], NT)
            ).astype(BF16)
            return carry

        lax.fori_loop(0, D // tile, step, 0)

    right_plane.turn(32)
    rest_plane.turn(rows)
    if parts == 4:
        dnormed(back_plane.far)
        dnormed(back_plane.near[0])
        back_plane.start(0)
    wholes.sent(0)
    wholes.step(1)
    if parts == 4:
        dnormed(back_plane.near[1])
    else:
        for peer in peers:
            dnormed(peer[1])
    back_plane.start(1)
    dnormed(q)
    right_plane.finish(right_acc, 32)
    rest_plane.finish(rest_acc, rows)
    rests.step(0)
    for t in range(2, line - 1):
        wholes.sent(t - 1)
        wholes.step(t)
        rests.sent(t - 2)
        rests.step(t - 1)
    back_plane.turn(32)
    lefts.finish(left_out)
    lefts.sent(line - 2)
    wholes.sent(line - 2)
    rests.sent(line - 3)
    rests.step(line - 2)
    rights.step(0)
    wholes.finish(final)
    for k, peer in enumerate(peers):
        block = final.at[pl.ds(pl.multiple_of(peer[1] * rows, rows), rows)]
        copy = remote(block, part.at[q], part_s, part_r, k, peer)
        copy.start()
        waiting.append(copy)
    copy = pltpu.make_async_copy(
        final.at[pl.ds(pl.multiple_of(q * rows, rows), rows)], part.at[q], local.at[2]
    )
    copy.start()
    own.append(copy)
    rights.sent(0)
    rights.step(1)
    back_plane.finish(back_sum, 32)
    copy = pltpu.make_async_copy(back_sum, back_out, local.at[3])
    copy.start()
    own.append(copy)
    for t in range(2, line - 1):
        rights.sent(t - 1)
        rights.step(t)
    rests.finish(rest_out)
    rests.sent(line - 2)
    rights.finish(right_out)
    rights.sent(line - 2)
    for copy in own + waiting:
        copy.wait()


def sum_to_owners(collective_id, normed, left, right, gate, small, dz, dpx, wz, wx):
    parts, line, out_rows, slim = right.shape
    groups = 2 * line
    rows, cw = gate.shape[1:]
    span = rows * parts
    extra = dpx.shape[1] - cw
    tokens = dz.shape[0] // parts
    sem = pltpu.SemaphoreType.DMA
    vmem = pl.BlockSpec(memory_space=pltpu.VMEM)
    hbm = pl.BlockSpec(memory_space=pltpu.HBM)
    right_sum = (line, out_rows, slim)
    rest = (parts, line, rows, extra)
    return pl.pallas_call(
        functools.partial(owners_kernel, groups, parts, rows, cw),
        in_specs=[hbm, vmem, vmem, hbm, vmem, hbm, hbm, hbm, hbm],
        out_specs=[hbm, vmem, vmem, vmem, hbm, hbm, vmem],
        out_shape=[
            jax.ShapeDtypeStruct((parts, rows, cw), BF16),
            jax.ShapeDtypeStruct((rows, extra), F32),
            jax.ShapeDtypeStruct((out_rows, left.shape[-1]), F32),
            jax.ShapeDtypeStruct((out_rows, slim), F32),
            jax.ShapeDtypeStruct(gate.shape, BF16),
            jax.ShapeDtypeStruct((tokens, D), F32),
            jax.ShapeDtypeStruct((groups,) + small.shape, F32),
        ],
        scratch_shapes=[
            *([pltpu.VMEM((line, span, cw), BF16)] * 5),
            pltpu.VMEM((span, cw), BF16),
            *([pltpu.VMEM(left.shape, BF16)] * 2),
            *([pltpu.VMEM(right_sum, BF16)] * 3),
            *([pltpu.VMEM((line, span, extra), BF16)] * 2),
            pltpu.VMEM(rest, BF16),
            *([pltpu.VMEM(rest[1:], BF16)] * 3),
            *[pltpu.VMEM(a.shape, BF16) for a in (normed, dz, dpx, wz, wx)],
            pltpu.VMEM((parts, tokens, D), BF16),
            pltpu.VMEM((tokens, D), F32),
            *PlaneSum.scratch(parts, right.shape[1:], BF16),
            *PlaneSum.scratch(parts, (tokens, D), BF16),
            *PlaneSum.scratch(parts, rest[1:], BF16),
            *([sem((line,))] * 20),
            *([sem((parts - 1,))] * 4),
            *([sem((groups - 1,))] * 2),
            sem((5,)),
            sem((4,)),
        ],
        compiler_params=pltpu.CompilerParams(
            collective_id=collective_id, has_side_effects=True, vmem_limit_bytes=63 * 2**20
        ),
        name="sum_to_owners",
    )(normed, left, right, gate, small, dz, dpx, wz, wx)


def on_device(
    hidden_in, out_grads, w_in, w_in_m, w_in_v, w_out, w_out_m, w_out_v,
    chan_params, chan_m, chan_v, head_params, head_m, head_v,
):
    parts = lax.axis_size("seq")
    groups = lax.axis_size("dp")
    q = lax.axis_index("seq")
    rows = hidden_in.shape[1]
    length = rows * parts
    cw = INNER // parts
    hq = H // parts
    cc = cw + 2 * N
    in_rows = w_in.shape[0]
    out_rows = w_out.shape[0]

    chan_len = chan_params.shape[0]
    chan_rows = -(-chan_len // (8 * LANES)) * 8
    chan_block = jnp.pad(
        lax.reduce_precision(chan_params, 8, 7), (0, chan_rows * LANES - chan_len)
    ).reshape(chan_rows, LANES)
    hidden, wx, gate, chan_full, wo = collect(
        0, hidden_in[0], w_in, w_out, chan_block, groups, parts
    )
    chan_full = chan_full.reshape(groups * parts, chan_rows * LANES)[:, :chan_len].reshape(-1)
    line = groups // 2
    group = lax.axis_index("dp")

    conv_taps = chan_full[: TAPS * CONV_CH].reshape(TAPS, CONV_CH)
    conv_bias = chan_full[TAPS * CONV_CH : (TAPS + 1) * CONV_CH].reshape(1, CONV_CH)
    offset = (TAPS + 1) * CONV_CH
    gain_in = chan_full[offset : offset + D]
    gain_out = chan_full[offset + D : offset + D + INNER]
    taps_all = jnp.concatenate(
        [conv_taps, conv_bias, jnp.zeros((8 - TAPS - 1, CONV_CH), F32)], axis=0
    )
    taps = jnp.concatenate(
        [lax.dynamic_slice(taps_all, (0, q * cw), (8, cw)), taps_all[:, INNER:]], axis=1
    )
    own_gain = lax.dynamic_slice(gain_out, (q * cw,), (cw,))
    own_heads = lax.dynamic_slice(head_params, (0, q * hq), (3, hq))
    heads = jnp.pad(
        jnp.stack([own_heads[0], -jnp.exp(own_heads[1])]), ((0, 6), (0, LANES - hq))
    )
    skip = jnp.repeat(own_heads[2], P_SIZE).reshape(1, cw)
    spread = (
        jnp.arange(LANES)[:, None] == (jnp.arange(cw) // P_SIZE)[None, :]
    ).astype(BF16)

    normed, px, y, states, z, u_blocks, wz, wo = forward(
        1, hidden.reshape(length, D), wx.reshape(D, cc + LANES), gate, wo, gain_in.reshape(1, D),
        own_gain.reshape(1, cw), taps, heads, skip, spread,
    )
    wx, wz = wx.reshape(D, cc + LANES), wz.reshape(D, cw)
    cotangent = out_grads[:, 0]
    back_own, coefs, block_out, dwo_left, dwo_right = middle(
        2, u_blocks, wo, cotangent, hidden_in[0]
    )

    dz, dpx, small, dwo_left, dwz = backward(
        5, back_own.reshape(length, cw), coefs.reshape(length, LANES), normed, px, y, z, states,
        dwo_left, own_gain.reshape(1, cw), taps, heads, skip, spread,
    )
    x_part, rest, left_part, right_part, z_part, dnormed, small = sum_to_owners(
        4, normed, dwo_left, dwo_right, dwz.reshape(parts, in_rows, cw), small, dz, dpx, wz, wx
    )
    hidden_grad, chan_total, head_total, norm = gradient_norm(
        6, x_part, rest, z_part, left_part, right_part, dnormed, small, hidden_in[0],
        gain_in.reshape(1, D), cotangent, groups,
    )
    (
        hidden_grad, block_out, w_in_new, w_in_m_new, w_in_v_new, w_in_copy,
        w_out_new, w_out_m_new, w_out_v_new, w_out_copy,
    ) = update_weights(
        norm, x_part, rest, z_part, left_part, right_part, hidden_grad, block_out,
        (w_in, w_in_m, w_in_v, w_out, w_out_m, w_out_v),
    )
    hidden_grad, block_out = hidden_grad[None], block_out[:, None]
    grad_norm, clip_factor = norm[0, 0], norm[1, 0]
    owner = group * parts + q
    chan_part = lax.dynamic_slice(chan_total.reshape(-1), (owner * chan_len,), (chan_len,))
    head_total = head_total[:parts, : 3 * hq].reshape(parts, 3, hq)
    head_total = head_total.transpose(1, 0, 2).reshape(3, H)
    chan_new, chan_m_new, chan_v_new = adam_tile(
        chan_params, clip_factor * chan_part, chan_m, chan_v, 0.2, 0.0
    )
    head_new, head_m_new, head_v_new = adam_tile(
        head_params, clip_factor * head_total, head_m, head_v, 1.0, 0.0
    )
    return (
        block_out, hidden_grad, grad_norm,
        w_in_new, w_in_m_new, w_in_v_new, w_in_copy,
        w_out_new, w_out_m_new, w_out_v_new, w_out_copy,
        chan_new, chan_m_new, chan_v_new, head_new, head_m_new, head_v_new,
    )


def solution(mesh):
    rows = P(("dp", "seq"), None)
    flat = P(("dp", "seq"))
    in_specs = (
        P("dp", "seq", None),
        P(None, "dp", "seq", None),
        *([rows] * 6),
        *([flat] * 3),
        *([P()] * 3),
    )
    out_specs = (
        P(None, "dp", "seq", None),
        P("dp", "seq", None),
        P(),
        *([rows] * 8),
        *([flat] * 3),
        *([P()] * 3),
    )
    return jax.shard_map(
        on_device, mesh=mesh, in_specs=in_specs, out_specs=out_specs, check_vma=False
    )
```

```python
import functools

import jax
import jax.numpy as jnp
from jax import lax
from jax.experimental import pallas as pl
from jax.experimental.pallas import tpu as pltpu
from jax.sharding import PartitionSpec as P

D = 2048
INNER = 4096
H = 64
P_SIZE = 64
N = 128
TAPS = 4
STEP = 10
E_IN = 8512
CONV_CH = 4352
LANES = 128
CHUNK = 128
LEVELS = 4

EXACT = lax.Precision.HIGHEST
EPS_IN = 1e-06
EPS_OUT = 1e-05
ADAM_EPS = 1e-08
BETA = 0.5
CLIP = 1.0
F32 = jnp.float32
BF16 = jnp.bfloat16
MASKED = -1e30


def level_width(level):
    return INNER * 2**level // 8


SEGMENTS = tuple(
    (0 if level == 0 else level_width(level - 1), level_width(level)) for level in range(LEVELS)
)


def dot(a, b, dims=((1,), (0,)), precision=None):
    return lax.dot_general(a, b, (dims, ((), ())), precision=precision, preferred_element_type=F32)


NT = ((1,), (1,))
TN = ((0,), (0,))


def softplus(v):
    return jnp.maximum(v, 0.0) + jnp.log1p(jnp.exp(-jnp.abs(v)))


def two_terms(v):
    high = v.astype(BF16)
    return high, (v - high.astype(F32)).astype(BF16)


def spread_heads(v, spread):
    high, rest = two_terms(v)
    return dot(high, spread) + dot(rest, spread)


def own_heads_first(dt_raw, hq, back=False):
    by = lax.axis_index("seq") * hq
    return pltpu.roll(dt_raw, by if back else lax.rem(LANES - by, LANES), 1)


def rates(dt_raw, heads):
    step = softplus(dt_raw + heads[0:1, :])
    return step, step * heads[1:2, :]


def triangle(size):
    row = lax.broadcasted_iota(jnp.int32, (size, size), 0)
    col = lax.broadcasted_iota(jnp.int32, (size, size), 1)
    return row, col


def conv_block(taps, xbuf, lanes):
    out = taps[TAPS : TAPS + 1, lanes]
    for tap in range(TAPS):
        out = out + taps[tap : tap + 1, lanes] * xbuf[5 + tap : 5 + tap + CHUNK, lanes]
    return out


def pair_decay(cum, cum_t, causal, head):
    gap = cum[:, head : head + 1] - cum_t[head : head + 1, :]
    return jnp.exp(jnp.where(causal, gap, MASKED))


def scan_forward_step(cw, px, taps, heads, skip, spread, y, states, xbuf, state, xdt, carried):
    cc = cw + 2 * N
    xbuf[8 : 8 + CHUNK, :] = px[:, :cc]
    step, rate = rates(own_heads_first(px[:, cc:], cw // P_SIZE), heads)
    row, col = triangle(CHUNK)
    causal = row >= col
    cum = dot(causal.astype(F32), rate, precision=EXACT)
    cum_t = cum.T
    spread_m = spread[...]
    last = cum[CHUNK - 1 : CHUNK, :]
    step_x = spread_heads(step, spread_m)
    grow_x = spread_heads(jnp.exp(cum), spread_m)
    tail_x = spread_heads(jnp.exp(last - cum), spread_m)

    def activated(lanes):
        conv = conv_block(taps, xbuf, lanes)
        return conv * jax.nn.sigmoid(conv)

    state_in = activated(slice(cw, cw + N))
    state_out = activated(slice(cw + N, cw + 2 * N))
    scores = dot(state_out, state_in, NT, EXACT)
    states[...] = state[...].astype(BF16)
    carried[...] = dot(state_out.astype(BF16), state[...].astype(BF16))
    first = lax.broadcasted_iota(jnp.int32, (1, LANES), 1) < P_SIZE
    for pair in range(cw // LANES):
        lanes = slice(pair * LANES, (pair + 1) * LANES)
        x = activated(lanes)
        xd = (x * step_x[:, lanes]).astype(BF16).astype(F32)
        xdt[:, lanes] = (xd * tail_x[:, lanes]).astype(BF16)
        stacked = jnp.concatenate([jnp.where(first, xd, 0.0), jnp.where(first, 0.0, xd)], axis=0)
        mixing = jnp.concatenate(
            [
                (pair_decay(cum, cum_t, causal, 2 * pair + k) * scores).astype(BF16)
                for k in range(2)
            ],
            axis=1,
        )
        y[:, lanes] = (
            dot(mixing, stacked.astype(BF16))
            + grow_x[:, lanes] * carried[:, lanes]
            + skip[:, lanes] * x
        )
    state[...] = grow_x[CHUNK - 1 : CHUNK, :] * state[...] + dot(
        state_in.astype(BF16), xdt[...], TN
    )
    xbuf[0:8, :] = xbuf[CHUNK : CHUNK + 8, :]


def scan_backward_step(
    cw, start, px, halo, taps, heads, skip, spread, gather, dy, y, states,
    dpx, dtaps, dheads, dskip,
    xbuf, dstate, dcbuf, slope, xact, xd_s, dxd_s, acc_s,
):
    cc = cw + 2 * N
    xbuf[0:8, :] = jnp.where(start, 0.0, halo[:, :cc])
    xbuf[8 : 8 + CHUNK, :] = px[:, :cc]
    dt_raw = own_heads_first(px[:, cc:], cw // P_SIZE)
    step, rate = rates(dt_raw, heads)
    row, col = triangle(CHUNK)
    causal = row >= col
    cum = dot(causal.astype(F32), rate, precision=EXACT)
    cum_t = cum.T
    spread_m = spread[...]
    last = cum[CHUNK - 1 : CHUNK, :]
    step_x = spread_heads(step, spread_m)
    grow_x = spread_heads(jnp.exp(cum), spread_m)
    tail_x = spread_heads(jnp.exp(last - cum), spread_m)

    for block in range(cc // LANES):
        lanes = slice(block * LANES, (block + 1) * LANES)
        conv = conv_block(taps, xbuf, lanes)
        sig = jax.nn.sigmoid(conv)
        act = conv * sig
        xact[:, lanes] = act
        slope[:, lanes] = sig + act * (1.0 - sig)
    state_in = xact[:, cw : cw + N]
    state_out = xact[:, cw + N : cc]
    scores = dot(state_out, state_in, NT, EXACT)
    in_low = state_in.astype(BF16)
    out_low = state_out.astype(BF16)
    dstate_low = dstate[...].astype(BF16)
    acc_s[...] = jnp.zeros_like(acc_s)
    dxd_s[...] = tail_x * dot(in_low, dstate_low)
    dskip[0:1, :] += jnp.sum(xact[:, :cw] * dy[...], axis=0, keepdims=True)
    first = lax.broadcasted_iota(jnp.int32, (1, LANES), 1) < P_SIZE
    xd_s[...] = (xact[:, :cw] * step_x).astype(BF16)
    total = jnp.sum(xd_s[...].astype(F32) * dxd_s[...], axis=0, keepdims=True) + grow_x[
        CHUNK - 1 : CHUNK, :
    ] * jnp.sum(dstate[...] * states[...].astype(F32), axis=0, keepdims=True)
    dscores = jnp.zeros((CHUNK, CHUNK), F32)
    for pair in range(cw // LANES):
        lanes = slice(pair * LANES, (pair + 1) * LANES)
        dyp = dy[:, lanes]
        stacked = jnp.concatenate(
            [jnp.where(first, dyp, 0.0), jnp.where(first, 0.0, dyp)], axis=0
        ).astype(BF16)
        decays = [pair_decay(cum, cum_t, causal, 2 * pair + k) for k in range(2)]
        mixing = jnp.concatenate([(decay * scores).astype(BF16) for decay in decays], axis=0)
        dxd_s[:, lanes] += dot(mixing, stacked, TN)
        dmix = dot(stacked, xd_s[:, lanes], NT)
        dscores = dscores + decays[0] * dmix[:CHUNK] + decays[1] * dmix[CHUNK:]
    dy_low = dy[...].astype(BF16)
    dy_f = dy_low.astype(F32)
    xd_f = xd_s[...].astype(F32)
    dxd = dxd_s[...]
    y_scan = y[...] - skip[...] * xact[:, :cw]
    final = lax.broadcasted_iota(jnp.int32, (CHUNK, 1), 0) == CHUNK - 1
    gather_m = gather[...]
    dcum = spread_heads(dy_f * y_scan - xd_f * dxd + jnp.where(final, total, 0.0), gather_m)
    dstep = spread_heads(xact[:, :cw] * dxd, gather_m)
    drate = dot((row <= col).astype(F32), dcum, precision=EXACT)
    dstep = dstep + drate * heads[1:2, :]
    ddt = dstep * jax.nn.sigmoid(dt_raw + heads[0:1, :])
    dheads[0:1, :] += jnp.sum(ddt, axis=0, keepdims=True)
    dheads[1:2, :] += jnp.sum(drate * rate, axis=0, keepdims=True)
    grown = (grow_x * dy_f).astype(BF16)
    dscores_low = dscores.astype(BF16)
    dout = dot(dscores_low, in_low) + dot(grown, states[...], NT)
    din = dot(dscores_low, out_low, TN) + dot((tail_x * xd_f).astype(BF16), dstate_low, NT)
    dstate[...] = grow_x[CHUNK - 1 : CHUNK, :] * dstate[...] + dot(out_low, grown, TN)
    dcbuf[:CHUNK, :cw] = (step_x * dxd + skip[...] * dy[...]) * slope[:, :cw]
    dcbuf[:CHUNK, cw : cw + N] = din * slope[:, cw : cw + N]
    dcbuf[:CHUNK, cw + N :] = dout * slope[:, cw + N :]
    for block in range(cc // LANES):
        lanes = slice(block * LANES, (block + 1) * LANES)
        dconv = dcbuf[:CHUNK, lanes]
        dtaps[TAPS : TAPS + 1, lanes] += jnp.sum(dconv, axis=0, keepdims=True)
        back = taps[TAPS - 1 : TAPS, lanes] * dconv
        for tap in range(TAPS):
            dtaps[tap : tap + 1, lanes] += jnp.sum(
                dconv * xbuf[5 + tap : 5 + tap + CHUNK, lanes], axis=0, keepdims=True
            )
            if tap < TAPS - 1:
                reach = TAPS - 1 - tap
                back = back + taps[tap : tap + 1, lanes] * dcbuf[reach : reach + CHUNK, lanes]
        dpx[:, lanes] = back.astype(BF16)
    ours = lax.broadcasted_iota(jnp.int32, (1, LANES), 1) < cw // P_SIZE
    ddt = own_heads_first(jnp.where(ours, ddt, 0.0), cw // P_SIZE, back=True)
    dpx[:, cc:] = ddt.astype(BF16)
    dcbuf[CHUNK : CHUNK + 8, :] = dcbuf[0:8, :]


WIDE = 512
LEFT = 1280
SPLIT = 256


MESH = pl.DeviceIdType.MESH


def remote(src, dst, sends, recvs, index, device):
    return pltpu.make_async_remote_copy(
        src_ref=src,
        dst_ref=dst,
        send_sem=sends.at[index],
        recv_sem=recvs.at[index],
        device_id=device,
        device_id_type=MESH,
    )


def greet(devices):
    barrier = pltpu.get_barrier_semaphore()
    for device in devices:
        pl.semaphore_signal(barrier, inc=1, device_id=device, device_id_type=MESH)
    pl.semaphore_wait(barrier, len(devices))


def seq_peers(parts):
    group, q = lax.axis_index("dp"), lax.axis_index("seq")
    return [(group, lax.rem(q + k, parts)) for k in range(1, parts)]


def dp_peers(groups):
    group, q = lax.axis_index("dp"), lax.axis_index("seq")
    return [(lax.rem(group + k, groups), q) for k in range(1, groups)]


def all_peers(groups, parts):
    devices = groups * parts
    me = lax.axis_index("dp") * parts + lax.axis_index("seq")
    peers = []
    for k in range(1, devices):
        other = lax.rem(me + k, devices)
        peers.append((other // parts, lax.rem(other, parts)))
    return peers


CHAN_ROWS = ((TAPS + 1) * CONV_CH + D + INNER) // LANES


def adam_tile(weight, gradient, moment, second, step_rate, weight_decay):
    new_moment = BETA * moment + (1.0 - BETA) * gradient
    new_second = BETA * second + (1.0 - BETA) * gradient * gradient
    correction = 1.0 - BETA**STEP
    update = new_moment / correction / (jnp.sqrt(new_second / correction) + ADAM_EPS)
    return weight - step_rate * (update + weight_decay * weight), new_moment, new_second


def total_of(value):
    return jnp.sum(jnp.sum(value, axis=1, keepdims=True), axis=0, keepdims=True)


def norm_kernel(
    groups, parts,
    part_h, rest_h, gate_h, left_h, right_h, back_h, small_h, hidden_h, gain, cotangent,
    hidden_grad, chan, head, norm,
    part, rest, gate, left, right, back, small, hidden,
    cot_v, block, near, all_block, all_near, sends, recvs, near_s, near_r, load, local,
):
    group, q = lax.axis_index("dp"), lax.axis_index("seq")
    me = group * parts + q
    cw = INNER // parts
    cc = cw + 2 * N
    everyone = all_peers(groups, parts)
    fetches = [
        pltpu.make_async_copy(source, target, load.at[k])
        for k, (source, target) in enumerate(
            [(back_h, back), (hidden_h, hidden), (part_h, part), (gate_h, gate),
             (left_h, left), (right_h, right), (small_h, small), (rest_h, rest),
             (cotangent, cot_v)]
        )
    ]
    for copy in fetches:
        copy.start()
    barrier = pltpu.get_barrier_semaphore()
    for device in everyone:
        pl.semaphore_signal(barrier, inc=1, device_id=device, device_id_type=MESH)
    for copy in fetches[:8]:
        copy.wait()
    total = small[0]
    for k in range(1, groups):
        total = total + small[k]
    near[...] = total
    rows = 32

    def summed(at):
        down = back[at, :]
        tokens = hidden[at, :].astype(F32)
        mean = jnp.sum(tokens * tokens, axis=-1, keepdims=True) / D
        return down, tokens, lax.rsqrt(mean + EPS_IN)

    def gain_rows(i, dgain):
        at = pl.ds(pl.multiple_of(i * rows, rows), rows)
        down, tokens, scale = summed(at)
        return dgain + jnp.sum(down * tokens * scale, axis=0, keepdims=True)

    dgain = lax.fori_loop(0, hidden.shape[0] // rows, gain_rows, jnp.zeros((1, D), F32))
    tail = rest[:, : 2 * N + H]
    squares = total_of(tail * tail)
    for k in range(parts):
        x = part[k].astype(F32)
        g = gate[k].astype(F32)
        squares = squares + total_of(x * x + g * g)
    squares = squares + total_of(left[...] * left[...]) + total_of(right[...] * right[...])
    for k in range(D // LANES):
        block[k : k + 1, :] = dgain[:, k * LANES : (k + 1) * LANES]
    block[D // LANES :, :] = jnp.broadcast_to(squares, (8, LANES))
    pl.semaphore_wait(barrier, len(everyone))
    copies = [
        remote(block, all_block.at[me], sends, recvs, k, peer) for k, peer in enumerate(everyone)
    ]
    copies += [
        remote(near, all_near.at[q], near_s, near_r, k, peer)
        for k, peer in enumerate(seq_peers(parts))
    ]
    copies += [
        pltpu.make_async_copy(block, all_block.at[me], local.at[0]),
        pltpu.make_async_copy(near, all_near.at[q], local.at[1]),
    ]
    for copy in copies:
        copy.start()
    fetches[8].wait()

    def grad_rows(i, carry):
        at = pl.ds(pl.multiple_of(i * rows, rows), rows)
        down, tokens, scale = summed(at)
        scaled = down * gain[...]
        inner = jnp.sum(scaled * tokens, axis=-1, keepdims=True) / D
        direct = cot_v[0, at, :].astype(F32)
        for k in range(1, LEVELS):
            direct = direct + cot_v[k, at, :].astype(F32)
        hidden_grad[at, :] = (
            scale * scaled - tokens * (scale * scale * scale * inner) + direct
        )
        return carry

    lax.fori_loop(0, hidden.shape[0] // rows, grad_rows, 0)
    for copy in copies:
        copy.wait()
    total = jnp.sum(all_block[...], axis=0)
    own, wide = cw // LANES, cc // LANES
    span = CONV_CH // LANES
    for tap in range(TAPS + 1):
        for k in range(parts):
            at = tap * span + k * own
            chan[at : at + own, :] = all_near[k, tap * wide : tap * wide + own, :]
        shared = all_near[0, tap * wide + own : (tap + 1) * wide, :]
        for k in range(1, parts):
            shared = shared + all_near[k, tap * wide + own : (tap + 1) * wide, :]
        chan[tap * span + INNER // LANES : (tap + 1) * span, :] = shared
    at = (TAPS + 1) * span
    chan[at : at + D // LANES, :] = total[: D // LANES]
    at = at + D // LANES
    for k in range(parts):
        first = (TAPS + 1) * wide
        chan[at + k * own : at + (k + 1) * own, :] = all_near[k, first : first + own, :]
        head[k : k + 1, :] = all_near[k, first + own : first + own + 1, :]
    squares = (
        total[D // LANES : D // LANES + 1, :1]
        + total_of(chan[:CHAN_ROWS, :] * chan[:CHAN_ROWS, :])
        + total_of(head[:parts, :] * head[:parts, :])
    )
    grad_norm = jnp.sqrt(squares)
    norm[0:1, :] = jnp.broadcast_to(grad_norm, (1, LANES))
    norm[1:2, :] = jnp.broadcast_to(jnp.minimum(1.0, CLIP / grad_norm), (1, LANES))


def gradient_norm(
    collective_id, part, rest, gate, left, right, back, small, hidden, gain, cotangent, groups
):
    parts = part.shape[0]
    devices = groups * parts
    sem = pltpu.SemaphoreType.DMA
    vmem = pl.BlockSpec(memory_space=pltpu.VMEM)
    hbm = pl.BlockSpec(memory_space=pltpu.HBM)
    block = (D // LANES + 8, LANES)
    chan_rows = -(-CHAN_ROWS // 8) * 8
    return pl.pallas_call(
        functools.partial(norm_kernel, groups, parts),
        in_specs=[*([hbm] * 8), vmem, hbm],
        out_specs=[vmem] * 4,
        out_shape=[
            jax.ShapeDtypeStruct(hidden.shape, F32),
            jax.ShapeDtypeStruct((chan_rows, LANES), F32),
            jax.ShapeDtypeStruct((8, LANES), F32),
            jax.ShapeDtypeStruct((8, LANES), F32),
        ],
        scratch_shapes=[
            *[
                pltpu.VMEM(a.shape, a.dtype)
                for a in (part, rest, gate, left, right, back, small, hidden)
            ],
            pltpu.VMEM(cotangent.shape, BF16),
            pltpu.VMEM(block, F32),
            pltpu.VMEM(small.shape[1:], F32),
            pltpu.VMEM((devices,) + block, F32),
            pltpu.VMEM((parts,) + small.shape[1:], F32),
            sem((devices - 1,)), sem((devices - 1,)), sem((parts - 1,)), sem((parts - 1,)),
            sem((9,)), sem((2,)),
        ],
        compiler_params=pltpu.CompilerParams(
            collective_id=collective_id, has_side_effects=True, vmem_limit_bytes=63 * 2**20
        ),
        name="gradient_norm",
    )(part, rest, gate, left, right, back, small, hidden, gain, cotangent)


BLOCKS = 4


def update_kernel(
    parts, norm, part_h, rest_h, gate_h, left_h, right_h, hidden_grad, block, *refs
):
    ins, refs = refs[:6], refs[6:]
    hidden_out, block_out, outs, refs = refs[0], refs[1], refs[2:10], refs[10:]
    held, made = refs[:6], refs[6:14]
    part, rest, gate, left, right, hidden_v, block_v, load, store, grads = refs[14:]
    clip = norm[1:2, :1]
    cw = INNER // parts
    fetches = [
        pltpu.make_async_copy(source, target, grads.at[k])
        for k, (source, target) in enumerate(
            [(part_h, part), (gate_h, gate), (left_h, left), (right_h, right), (rest_h, rest),
             (hidden_grad, hidden_v), (block, block_v)]
        )
    ]
    for copy in fetches[:5]:
        copy.start()

    def at(a, i):
        rows = ins[a].shape[0] // BLOCKS
        return pl.ds(i * rows, rows)

    loads = [
        [
            pltpu.make_async_copy(ins[a].at[at(a, i)], held[a].at[at(a, i)], load.at[a * BLOCKS + i])
            for a in range(6)
        ]
        for i in range(BLOCKS)
    ]
    for weight in (0, 3):
        for i in range(BLOCKS):
            for a in range(weight, weight + 3):
                loads[i][a].start()
    for copy in fetches[5:]:
        copy.start()
    stores = []

    def update(weight, rows, lanes, gradient, rate, decay):
        first = 0 if weight == 0 else 4
        new, moment, second = adam_tile(
            held[weight][rows, lanes], clip * gradient, held[weight + 1][rows, lanes],
            held[weight + 2][rows, lanes], rate, decay,
        )
        made[first][rows, lanes] = new
        made[first + 1][rows, lanes] = moment
        made[first + 2][rows, lanes] = second
        made[first + 3][rows, lanes] = new.astype(BF16)

    def send(first, rows, i):
        for a in range(first, first + 4):
            copy = pltpu.make_async_copy(
                made[a].at[rows], outs[a].at[rows], store.at[a * BLOCKS + i]
            )
            copy.start()
            stores.append(copy)

    for copy in fetches[:5]:
        copy.wait()
    for i in range(BLOCKS):
        rows = at(0, i)
        for a in range(3):
            loads[i][a].wait()
        for source, first in ((gate, 0), (part, INNER)):

            def step(k, carry, source=source, first=first, rows=rows):
                to = pl.ds(pl.multiple_of(first + k * cw, cw), cw)
                update(0, rows, to, source[k, rows, :cw].astype(F32), 0.02, 0.1)
                return carry

            lax.fori_loop(0, parts, step, 0)
        update(0, rows, slice(2 * INNER, E_IN), rest[rows, : 2 * N + H], 0.02, 0.1)
        send(0, rows, i)
    fetches[5].wait()
    fetches[6].wait()
    for source, target, k in ((hidden_v, hidden_out, 7), (block_v, block_out, 8)):
        copy = pltpu.make_async_copy(source, target, grads.at[k])
        copy.start()
        stores.append(copy)
    for i in range(BLOCKS):
        rows = at(3, i)
        for a in range(3, 6):
            loads[i][a].wait()
        update(3, rows, slice(0, LEFT), left[rows, :], 0.03, 0.1)
        update(3, rows, slice(LEFT, D), right[rows, :], 0.03, 0.1)
        send(4, rows, i)
    for copy in stores:
        copy.wait()


def update_weights(norm, part, rest, gate, left, right, hidden_grad, block, weights):
    parts = part.shape[0]
    w_in, w_out = weights[0], weights[3]
    sem = pltpu.SemaphoreType.DMA
    vmem = pl.BlockSpec(memory_space=pltpu.VMEM)
    hbm = pl.BlockSpec(memory_space=pltpu.HBM)
    made = [
        jax.ShapeDtypeStruct(w.shape, dtype) for w in (w_in, w_out) for dtype in (F32, F32, F32, BF16)
    ]
    return pl.pallas_call(
        functools.partial(update_kernel, parts),
        in_specs=[vmem, *([hbm] * 13)],
        out_specs=[hbm] * 10,
        out_shape=[
            jax.ShapeDtypeStruct(hidden_grad.shape, F32),
            jax.ShapeDtypeStruct(block.shape, BF16),
            *made,
        ],
        scratch_shapes=[
            *[pltpu.VMEM(w.shape, F32) for w in weights],
            *[pltpu.VMEM(m.shape, m.dtype) for m in made],
            *[
                pltpu.VMEM(a.shape, a.dtype)
                for a in (part, rest, gate, left, right, hidden_grad, block)
            ],
            sem((6 * BLOCKS,)), sem((8 * BLOCKS,)), sem((9,)),
        ],
        compiler_params=pltpu.CompilerParams(vmem_limit_bytes=63 * 2**20),
        name="update_weights",
    )(norm, part, rest, gate, left, right, hidden_grad, block, *weights)


WO_ALL, WO_REST = pl.ds(0, SPLIT), pl.ds(SPLIT, D - SPLIT)


class LineGather:
    def __init__(self, line, z, core, q, slot, own, sends, recvs):
        self.line, self.z, self.core, self.q = line, z, core, q
        self.slot, self.own, self.sends, self.recvs = slot, own, sends, recvs

    def along(self, from_z, up, first=False):
        to = self.z + 1 if up else self.z - 1
        return remote(
            self.own if first else self.slot(from_z),
            self.slot(from_z),
            self.sends.at[0 if up else 1],
            self.recvs.at[0 if up else 1],
            from_z,
            (2 * to + self.core, self.q),
        )

    def push(self, t):
        z, line = self.z, self.line

        @pl.when((z - t >= 0) & (z < line - 1))
        def _():
            self.along(z - t, True, t == 0).start()

        @pl.when((z + t <= line - 1) & (z > 0))
        def _():
            self.along(z + t, False, t == 0).start()

    def pushed(self, t):
        z, line = self.z, self.line

        @pl.when((z - t >= 0) & (z < line - 1))
        def _():
            self.along(z - t, True, t == 0).wait_send()

        @pl.when((z + t <= line - 1) & (z > 0))
        def _():
            self.along(z + t, False, t == 0).wait_send()

    def step(self, t, got=None, push=True):
        z, line = self.z, self.line

        @pl.when(z - t >= 0)
        def _():
            self.along(z - t, True).wait_recv()

            if push:

                @pl.when(z < line - 1)
                def _():
                    self.along(z - t, True).start()

            if got is not None:
                got(z - t)

        @pl.when(z + t <= line - 1)
        def _():
            self.along(z + t, False).wait_recv()

            if push:

                @pl.when(z > 0)
                def _():
                    self.along(z + t, False).start()

            if got is not None:
                got(z + t)


class LineGathers:
    def __init__(self, line, z, core, q, slot, own, sends, recvs):
        half = own.shape[0] // 2
        self.line = line
        self.halves = []
        for h in range(2):
            rows = pl.ds(h * half, half)
            self.halves.append(
                LineGather(
                    line, z, core, q, lambda from_z, rows=rows: slot(from_z).at[rows],
                    own.at[rows], sends.at[h], recvs.at[h],
                )
            )

    def push(self, t):
        for part in self.halves:
            part.push(t)

    def step(self, t, got=None, push=True):
        self.halves[0].step(t, None, push)
        self.halves[1].step(t, got, push)

    def pushed(self):
        for t in range(self.line - 1):
            for part in self.halves:
                part.pushed(t)


class PlaneGather:
    def __init__(self, parts, slot, own, sends, recvs, base=0):
        self.parts, self.slot, self.own = parts, slot, own
        self.sends, self.recvs, self.base = sends, recvs, base
        self.group, self.q = lax.axis_index("dp"), lax.axis_index("seq")
        if parts == 4:
            self.near = [self.q + 1 - 2 * lax.rem(self.q, 2), lax.rem(self.q + 2, 4)]
            self.half = own.shape[0] // 2

    def early(self):
        to = self.near if self.parts == 4 else [peer[1] for peer in seq_peers(self.parts)]
        return [
            remote(
                self.own, self.slot(self.q), self.sends, self.recvs, self.base + k, (self.group, d)
            )
            for k, d in enumerate(to)
        ]

    def late(self):
        if self.parts != 4:
            return []
        copies = []
        for h in range(2):
            block = self.slot(self.near[h]).at[pl.ds(h * self.half, self.half)]
            to = (self.group, self.near[1 - h])
            copies.append(remote(block, block, self.sends, self.recvs, self.base + 2 + h, to))
        return copies

    def start(self):
        for copy in self.early():
            copy.start()

    def turn(self):
        if self.parts == 4:
            for copy in self.early():
                copy.wait()
            for copy in self.late():
                copy.start()

    def finish(self):
        for copy in self.late() if self.parts == 4 else self.early():
            copy.wait()


def chan_rows_of(chan_len, devices):
    return -(-((devices - 1) * chan_len // LANES + 8) // 8) * 8


def unpack_chan(
    chan_len, parts, q, all_chan, full, hp, gain_in, gain_out, taps, heads, skip, spread, gather
):
    cw = INNER // parts
    hq = H // parts
    own, span, shared = cw // LANES, CONV_CH // LANES, 2 * N // LANES
    full[...] = jnp.zeros_like(full)
    for o in range(all_chan.shape[0]):
        at = o * chan_len // LANES
        full[at : at + 8, :] += all_chan[o]
    taps[...] = jnp.zeros_like(taps)
    for tap in range(TAPS + 1):
        for b in range(own):
            taps[tap : tap + 1, b * LANES : (b + 1) * LANES] = full[
                pl.ds(tap * span + q * own + b, 1), :
            ]
        for b in range(shared):
            at = tap * span + INNER // LANES + b
            taps[tap : tap + 1, cw + b * LANES : cw + (b + 1) * LANES] = full[at : at + 1, :]
    at = (TAPS + 1) * span
    for b in range(D // LANES):
        gain_in[:, b * LANES : (b + 1) * LANES] = full[at + b : at + b + 1, :]
    at = at + D // LANES
    for b in range(own):
        gain_out[:, b * LANES : (b + 1) * LANES] = full[pl.ds(at + q * own + b, 1), :]
    for out, axis in ((spread, 0), (gather, 1)):
        head = lax.broadcasted_iota(jnp.int32, out.shape, axis)
        channel = lax.broadcasted_iota(jnp.int32, out.shape, 1 - axis)
        inside = (channel >= head * P_SIZE) & (channel < (head + 1) * P_SIZE)
        out[...] = jnp.where(inside, 1.0, 0.0).astype(BF16)
    ours = own_heads_first(hp[...], hq)
    row = lax.broadcasted_iota(jnp.int32, ours.shape, 0)
    heads[...] = jnp.where(row == 0, ours, jnp.where(row == 1, -jnp.exp(ours), 0.0))
    skip[...] = spread_heads(ours, spread[...])[2:3, :]


def collect_kernel(
    groups, parts, chan_len, hidden, w_in_h, w_own_h, chan, hp,
    hid_out, w_out, gate_out, wo_out, gain_in, gain_out, taps, heads, skip, spread, gather,
    chan_out, full, w_in, w_own, blocks, gates, low, chan_s, chan_r, hid_s, hid_r, swap_s, swap_r, gate_s, gate_r,
    wo_s, wo_r, line_s, line_r, lwo_s, lwo_r, core_s, core_r, local,
):
    line = groups // 2
    cw = INNER // parts
    cc = cw + 2 * N
    group, q = lax.axis_index("dp"), lax.axis_index("seq")
    z, core = group // 2, lax.rem(group, 2)
    sibling = (2 * z + 1 - core, q)
    peers = seq_peers(parts)
    everyone = all_peers(groups, parts)
    loads = [
        pltpu.make_async_copy(w_in_h, w_in, local.at[5]),
        pltpu.make_async_copy(w_own_h, w_own, local.at[6]),
    ]
    for copy in loads:
        copy.start()
    barrier = pltpu.get_barrier_semaphore()
    for device in everyone:
        pl.semaphore_signal(barrier, inc=1, device_id=device, device_id_type=MESH)
    for copy in loads:
        copy.wait()
    shared = w_in[:, 2 * INNER :].astype(BF16)
    for part in range(parts):
        at = INNER + part * cw
        blocks[part, :, :cw] = w_in[:, at : at + cw].astype(BF16)
        blocks[part, :, cw : cc + H] = shared
        blocks[part, :, cc + H :] = jnp.zeros((w_in.shape[0], LANES - H), BF16)
    low[...] = w_own[...].astype(BF16)
    pl.semaphore_wait(barrier, len(everyone))
    swaps = []
    for k, peer in enumerate(peers):
        copy = remote(blocks.at[peer[1]], w_out.at[group, q], swap_s, swap_r, k, peer)
        copy.start()
        swaps.append(copy)
    outs = LineGather(
        line, z, core, q, lambda from_z: wo_out.at[2 * from_z + core, q, :, WO_REST],
        low.at[:, WO_REST], lwo_s, lwo_r,
    )
    outs.push(0)
    own = [
        pltpu.make_async_copy(blocks.at[q], w_out.at[group, q], local.at[0]),
        pltpu.make_async_copy(hidden, hid_out.at[q], local.at[1]),
        pltpu.make_async_copy(chan, chan_out.at[group * parts + q], local.at[2]),
        pltpu.make_async_copy(low, wo_out.at[group, q], local.at[3]),
    ]
    for copy in own:
        copy.start()
    waiting = []
    chans = [
        remote(chan, chan_out.at[group * parts + q], chan_s, chan_r, k, peer)
        for k, peer in enumerate(everyone)
    ]
    for copy in chans:
        copy.start()
    for part in range(parts):
        gates[part] = w_in[:, part * cw : (part + 1) * cw].astype(BF16)
    copy = pltpu.make_async_copy(gates.at[q], gate_out.at[q], local.at[4])
    copy.start()
    own.append(copy)
    own[0].wait()
    for copy in swaps:
        copy.wait()
    hids = PlaneGather(parts, lambda of: hid_out.at[of], hidden, hid_s, hid_r)
    lows = PlaneGather(parts, lambda of: wo_out.at[group, of], low, wo_s, wo_r)
    hids.start()

    def across(from_z):
        block = w_out.at[2 * from_z + core]
        return remote(block, block, core_s, core_r, from_z, sibling)

    ins = LineGathers(
        line, z, core, q, lambda from_z: w_out.at[2 * from_z + core], w_out.at[group],
        line_s, line_r,
    )
    across(z).start()
    ins.push(0)
    lows.start()
    for t in range(1, line):
        ins.step(t, lambda from_z: across(from_z).start(), t < line - 1)
        if t == 1:
            own[2].wait()
            for copy in chans:
                copy.wait()
            unpack_chan(
                chan_len, parts, q, chan_out, full, hp, gain_in, gain_out, taps, heads, skip,
                spread, gather,
            )
        if t == line - 2:
            outs.step(1)
            hids.turn()
            lows.turn()
            for k, peer in enumerate(peers):
                copy = remote(gates.at[peer[1]], gate_out.at[q], gate_s, gate_r, k, peer)
                copy.start()
                waiting.append(copy)
    ins.pushed()
    outs.step(2, None, False)
    outs.pushed(0)
    outs.pushed(1)
    hids.finish()
    lows.finish()
    for from_z in range(line):
        across(from_z).wait_send()
        block = w_out.at[2 * from_z + 1 - core]
        remote(block, block, core_s, core_r, from_z, sibling).wait_recv()
    for copy in own[1:2] + own[3:] + waiting:
        copy.wait()


def collect(collective_id, hidden, w_in, w_own, chan, hp, chan_len, groups, parts):
    rows = w_in.shape[0]
    line = groups // 2
    cw = INNER // parts
    width = cw + 2 * N + LANES
    sem = pltpu.SemaphoreType.DMA
    hbm = pl.BlockSpec(memory_space=pltpu.HBM)
    vmem = pl.BlockSpec(memory_space=pltpu.VMEM)
    return pl.pallas_call(
        functools.partial(collect_kernel, groups, parts, chan_len),
        in_specs=[hbm, hbm, hbm, vmem, vmem],
        out_specs=[*([hbm] * 4), *([vmem] * 7)],
        out_shape=[
            jax.ShapeDtypeStruct((parts,) + hidden.shape, hidden.dtype),
            jax.ShapeDtypeStruct((groups, parts, rows, width), BF16),
            jax.ShapeDtypeStruct((parts, rows, cw), BF16),
            jax.ShapeDtypeStruct((groups, parts) + w_own.shape, BF16),
            jax.ShapeDtypeStruct((1, D), F32),
            jax.ShapeDtypeStruct((1, cw), F32),
            jax.ShapeDtypeStruct((8, cw + 2 * N), F32),
            jax.ShapeDtypeStruct((8, LANES), F32),
            jax.ShapeDtypeStruct((1, cw), F32),
            jax.ShapeDtypeStruct((LANES, cw), BF16),
            jax.ShapeDtypeStruct((cw, LANES), BF16),
        ],
        scratch_shapes=[
            pltpu.VMEM((groups * parts,) + chan.shape, F32),
            pltpu.VMEM((chan_rows_of(chan_len, groups * parts), LANES), F32),
            pltpu.VMEM(w_in.shape, F32),
            pltpu.VMEM(w_own.shape, F32),
            pltpu.VMEM((parts, rows, width), BF16),
            pltpu.VMEM((parts, rows, cw), BF16),
            pltpu.VMEM(w_own.shape, BF16),
            *([sem((groups * parts - 1,))] * 2),
            *([sem((parts + 1,))] * 8),
            *([sem((2, 2, line))] * 2), *([sem((2, line))] * 2),
            sem((line,)), sem((line,)), sem((7,)),
        ],
        compiler_params=pltpu.CompilerParams(
            collective_id=collective_id, has_side_effects=True, vmem_limit_bytes=63 * 2**20
        ),
        name="collect",
    )(hidden, w_in, w_own, chan, hp)


def forward_kernel(
    groups, parts, cw,
    hidden_h, wx_h, gate_h, wo_in, gain_in, gain_out, taps, heads, skip, spread,
    normed_h, px_h, y_h, states_h, z_h, u_h, stat_h, wz_h, wo,
    hidden, wx, wz, normed, px, y, states, zs, us, stats, xbuf, state, xdt, carried,
    line_s, line_r, lwo_s, lwo_r, wide_s, wide_r, stat_s, stat_r, core_s, core_r, wo_s, wo_r, out_s, out_r, u_s, u_r, load, store,
):
    line = groups // 2
    cc = cw + 2 * N
    length = px.shape[0]
    chunks = length // CHUNK
    group, q = lax.axis_index("dp"), lax.axis_index("seq")
    z, core = group // 2, lax.rem(group, 2)
    sibling = (2 * z + 1 - core, q)
    peers = mirror_peers(parts)
    loads = [
        pltpu.make_async_copy(source, target, load.at[k])
        for k, (source, target) in enumerate(
            [(hidden_h, hidden), (wx_h, wx), (gate_h, wz.at[group])]
        )
    ]
    for copy in loads:
        copy.start()
    greet(peers + dp_peers(groups))

    outs = LineGather(
        line, z, core, q, lambda from_z: wo.at[2 * from_z + core, q, :, WO_REST],
        wo.at[group, q, :, WO_REST], lwo_s, lwo_r,
    )
    wides = LineGather(
        line, z, core, q, lambda from_z: wo.at[2 * from_z + core, :, :, WO_ALL],
        wo.at[group, :, :, WO_ALL], wide_s, wide_r,
    )

    def planes(t, act):
        for from_z, there in ((z - t, z - t >= 0), (z + t, z + t <= line - 1)):

            @pl.when(there)
            def _(from_z=from_z):
                block = wo.at[2 * from_z + core]
                act(
                    PlaneGather(
                        parts, lambda of: block.at[of, :, WO_REST], block.at[q, :, WO_REST],
                        out_s, out_r,
                        from_z * (parts + 1),
                    )
                )

    outs.push(2)
    planes(1, PlaneGather.start)
    planes(2, PlaneGather.start)

    def parity(from_z, of, columns):
        block = wo.at[2 * from_z + of, :, :, columns]
        at = from_z if columns is WO_REST else line + from_z
        return remote(block, block, wo_s, wo_r, at, sibling)

    def across_planes(t):
        planes(t, PlaneGather.finish)
        for from_z, there in ((z - t, z - t >= 0), (z + t, z + t <= line - 1)):

            @pl.when(there)
            def _(from_z=from_z):
                parity(from_z, core, WO_REST).start()

    def across_wide(from_z):
        parity(from_z, core, WO_ALL).start()

    across_wide(z)
    parity(z, core, WO_REST).start()

    def across(from_z):
        block = wz.at[2 * from_z + core]
        return remote(block, block, core_s, core_r, from_z, sibling)

    gates = LineGathers(
        line, z, core, q, lambda from_z: wz.at[2 * from_z + core], wz.at[group], line_s, line_r
    )
    loads[2].wait()
    across(z).start()
    gates.push(0)
    loads[0].wait()

    def norm_rows(i, carry):
        rows = pl.ds(pl.multiple_of(i * 32, 32), 32)
        tokens = hidden[rows, :].astype(F32)
        mean = jnp.sum(tokens * tokens, axis=-1, keepdims=True) / D
        normed[rows, :] = (tokens * lax.rsqrt(mean + EPS_IN) * gain_in[...]).astype(BF16)
        return carry

    lax.fori_loop(0, length // 32, norm_rows, 0)
    loads[1].wait()
    tall = 256

    def project_rows(i, carry):
        rows = pl.ds(pl.multiple_of(i * tall, tall), tall)
        px[rows, :] = dot(normed[rows, :], wx[...])
        return carry

    lax.fori_loop(0, length // tall, project_rows, 0)
    stores = [
        pltpu.make_async_copy(normed, normed_h, store.at[0]),
        pltpu.make_async_copy(px, px_h, store.at[1]),
    ]
    for copy in stores:
        copy.start()
    state[...] = jnp.zeros_like(state)
    xbuf[0:8, :] = jnp.zeros((8, cc), F32)

    def scan_rows(i, carry):
        for t in range(1, line - 1):

            @pl.when(i == min(5 * t - 4, chunks - 1))
            def _(t=t):
                gates.step(t, lambda from_z: across(from_z).start(), t < line - 1)
                if t == line - 2:
                    wides.push(0)

        for t in range(3, line):

            @pl.when(i == min(2 * t - 3, chunks - 1))
            def _(t=t):
                outs.step(t, None, t < line - 1)
                planes(t, PlaneGather.start)

        @pl.when(i == min(5, chunks - 1))
        def _():
            planes(1, PlaneGather.turn)
            planes(2, PlaneGather.turn)

        rows = pl.ds(pl.multiple_of(i * CHUNK, CHUNK), CHUNK)
        scan_forward_step(
            cw, px.at[rows], taps, heads, skip, spread, y.at[rows], states.at[i],
            xbuf, state, xdt, carried,
        )
        return carry

    lax.fori_loop(0, chunks, scan_rows, 0)
    for source, target, at in ((y, y_h, 2), (states, states_h, 3)):
        copy = pltpu.make_async_copy(source, target, store.at[at])
        copy.start()
        stores.append(copy)
    for t in range(3, line):
        planes(t, PlaneGather.turn)
    gates.step(line - 1, lambda from_z: across(from_z).start(), False)
    for from_z in range(line):
        across(from_z).wait_send()
        block = wz.at[2 * from_z + 1 - core]
        remote(block, block, core_s, core_r, from_z, sibling).wait_recv()
    gates.pushed()
    for t in range(2, line - 1):
        outs.pushed(t)
    copy = pltpu.make_async_copy(wz, wz_h, store.at[4])
    copy.start()
    stores.append(copy)
    lane = lax.broadcasted_iota(jnp.int32, (1, LANES), 1)
    wide = 512

    def gate_rows(rows):
        gate_in = dot(normed[rows, :], wz[...].reshape(D, cw))
        zs[rows, :] = gate_in
        gated = y[rows, :] * (gate_in * jax.nn.sigmoid(gate_in))
        us[rows, :] = (gated * gain_out[...]).astype(BF16)
        squares = jnp.zeros((tall, LANES), F32)
        for b in range(cw // wide):
            block = gated[:, b * wide : (b + 1) * wide]
            total = jnp.sum(block * block, axis=-1, keepdims=True)
            level = level_of(q * cw + b * wide, wide)
            squares = squares + jnp.where(lane == level, total, 0.0)
        stats[:, rows] = squares.T[:8, :]

    waiting = []
    tokens = length // parts
    for k, dest in enumerate([peer[1] for peer in peers] + [q]):

        def block_rows(i, carry, dest=dest):
            gate_rows(pl.ds(pl.multiple_of(dest * tokens + i * tall, tall), tall))
            return carry

        lax.fori_loop(0, tokens // tall, block_rows, 0)
        ours = us.at[pl.ds(pl.multiple_of(dest * tokens, tokens), tokens)]
        stat = stats.at[:, pl.ds(pl.multiple_of(dest * tokens, tokens), tokens)]
        if k < len(peers):
            some = [
                remote(ours, u_h.at[q], u_s, u_r, k, peers[k]),
                remote(stat, stat_h.at[q], stat_s, stat_r, k, peers[k]),
            ]
        else:
            some = [
                pltpu.make_async_copy(ours, u_h.at[q], store.at[6]),
                pltpu.make_async_copy(stat, stat_h.at[q], store.at[7]),
            ]
        for copy in some:
            copy.start()
        waiting += some
        if k == 0:
            wides.step(1, across_wide)
        if k == 1:
            for t in range(2, line - 1):
                wides.step(t, across_wide)
        if k in (1, 2):
            across_planes(k)
    copy = pltpu.make_async_copy(zs, z_h, store.at[5])
    copy.start()
    stores.append(copy)

    for t in range(3, line):
        across_planes(t)
    wides.step(line - 1, across_wide, False)
    for t in range(line - 1):
        wides.pushed(t)
    for copy in waiting + stores:
        copy.wait()
    for columns in (WO_REST, WO_ALL):
        for d in range(line):
            parity(d, core, columns).wait_send()
            parity(d, 1 - core, columns).wait_recv()


def forward(collective_id, hidden, wx, gate, wo, gain_in, gain_out, taps, heads, skip, spread):
    groups, parts = wo.shape[:2]
    line = groups // 2
    length = hidden.shape[0]
    rows, cw = gate.shape[1:]
    cc = cw + 2 * N
    width = cc + LANES
    chunks = length // CHUNK
    sem = pltpu.SemaphoreType.DMA
    hbm = pl.BlockSpec(memory_space=pltpu.HBM)
    vmem = pl.BlockSpec(memory_space=pltpu.VMEM)
    u = jax.ShapeDtypeStruct((parts, length // parts, cw), BF16)
    stat = jax.ShapeDtypeStruct((parts, 8, length // parts), F32)
    made = [
        jax.ShapeDtypeStruct((length, D), BF16),
        jax.ShapeDtypeStruct((length, width), F32),
        jax.ShapeDtypeStruct((length, cw), F32),
        jax.ShapeDtypeStruct((chunks, N, cw), BF16),
        jax.ShapeDtypeStruct((length, cw), F32),
        jax.ShapeDtypeStruct((length, cw), BF16),
        jax.ShapeDtypeStruct((8, length), F32),
    ]
    wz = jax.ShapeDtypeStruct((groups, parts, rows, cw), BF16)
    return pl.pallas_call(
        functools.partial(forward_kernel, groups, parts, cw),
        in_specs=[*([hbm] * 4), *([vmem] * 6)],
        out_specs=[hbm] * 9,
        out_shape=[*made[:-2], u, stat, wz, jax.ShapeDtypeStruct(wo.shape, BF16)],
        input_output_aliases={3: 8},
        scratch_shapes=[
            pltpu.VMEM(hidden.shape, BF16),
            pltpu.VMEM(wx.shape, BF16),
            pltpu.VMEM(wz.shape, BF16),
            *[pltpu.VMEM(m.shape, m.dtype) for m in made],
            pltpu.VMEM((CHUNK + 8, cc), F32),
            pltpu.VMEM((N, cw), F32),
            pltpu.VMEM((CHUNK, cw), BF16),
            pltpu.VMEM((CHUNK, cw), F32),
            *([sem((2, 2, line))] * 2), *([sem((2, line))] * 4),
            sem((parts - 1,)), sem((parts - 1,)),
            sem((line,)), sem((line,)), sem((2 * line,)), sem((2 * line,)),
            sem((line * (parts + 1),)), sem((line * (parts + 1),)),
            sem((parts - 1,)), sem((parts - 1,)),
            sem((3,)), sem((8,)),
        ],
        compiler_params=pltpu.CompilerParams(
            collective_id=collective_id, has_side_effects=True, vmem_limit_bytes=63 * 2**20
        ),
        name="forward",
    )(hidden, wx, gate, wo, gain_in, gain_out, taps, heads, skip, spread)


def add_blocks(out, a, b, rows, steps):
    def step(i, carry):
        at = pl.ds(pl.multiple_of(i * rows, rows), rows)
        out[at] = (a[at].astype(F32) + b[at].astype(F32)).astype(out.dtype)
        return carry

    lax.fori_loop(0, steps, step, 0)


def level_of(channel, width):
    return sum((channel >= level_width(k)).astype(jnp.int32) for k in range(LEVELS - 1))


def mirror_peers(parts):
    group, q = lax.axis_index("dp"), lax.axis_index("seq")
    if parts != 4:
        return seq_peers(parts)
    return [(group, 3 - q), (group, q + 1 - 2 * lax.rem(q, 2)), (group, lax.rem(q + 2, 4))]


def middle_kernel(
    groups, parts, cw,
    u_h, stat_h, wo, cot_h, tokens_h,
    back_h, coef_h, block_h, left_h, right_h,
    u, stats, cot, tokens, mixed, branch, norms, pulls, back, coefs, weights, sent, held, left, right,
    back_s, back_r, coef_s, coef_r, core_s, core_r, fetch, load, store, local,
):
    line = groups // 2
    group, q = lax.axis_index("dp"), lax.axis_index("seq")
    z, core = group // 2, lax.rem(group, 2)
    sibling = (2 * z + 1 - core, q)
    peers = mirror_peers(parts)
    loads = [
        pltpu.make_async_copy(stat_h, stats, load.at[3]),
        pltpu.make_async_copy(cot_h, cot, load.at[1]),
        pltpu.make_async_copy(u_h, u, load.at[0]),
        pltpu.make_async_copy(tokens_h, tokens, load.at[2]),
    ]
    for copy in loads:
        copy.start()
    greet(peers + [sibling])
    for copy in loads[:2]:
        copy.wait()

    terms = stats[0]
    for part in range(1, parts):
        terms = terms + stats[part]
    terms = jnp.concatenate([terms, jnp.zeros((LANES - 8, terms.shape[1]), F32)], axis=0).T
    squares = jnp.zeros((terms.shape[0], 1), F32)
    for k in range(LEVELS):
        squares = squares + terms[:, k : k + 1]
        norms[:, k : k + 1] = lax.rsqrt(squares / level_width(k) + EPS_OUT)
    rows = 32

    def mix_rows(i, carry):
        at = pl.ds(pl.multiple_of(i * rows, rows), rows)
        running = norms[at, LEVELS - 1 : LEVELS] * cot[LEVELS - 1, at, :].astype(F32)
        mixed[LEVELS - 1, at, :] = running.astype(BF16)
        for k in reversed(range(LEVELS - 1)):
            running = running + norms[at, k : k + 1] * cot[k, at, :].astype(F32)
            mixed[k, at, :] = running.astype(BF16)
        return carry

    lax.fori_loop(0, tokens.shape[0] // rows, mix_rows, 0)

    width = INNER // groups
    per = WIDE // width
    slots = weights.shape[0]
    dests = [peer[1] for peer in peers] + [q]
    firsts = [dest * cw + b * WIDE for dest in dests for b in range(cw // WIDE)]
    firsts += [b * WIDE for b in range(INNER // WIDE)]

    def get(i):
        return pltpu.make_async_copy(
            wo.at[pl.ds(firsts[i] // width, per)], weights.at[i % slots], fetch.at[i % slots]
        )

    def block_of(i):
        get(i).wait()
        return weights[i % slots].reshape(WIDE, D)

    for i in range(slots - 1):
        get(i).start()
    outgoing = []
    for i in range(len(dests) * (cw // WIDE)):
        get(i + slots - 1).start()
        at, b = divmod(i, cw // WIDE)
        lanes = slice(b * WIDE, (b + 1) * WIDE)
        level = level_of(firsts[i], WIDE)
        back[dests[at], :, lanes] = dot(mixed[level], block_of(i), NT).astype(BF16)
        if b == cw // WIDE - 1:
            if at < len(peers):
                copy = remote(back.at[dests[at]], back_h.at[q], back_s, back_r, at, peers[at])
            else:
                copy = pltpu.make_async_copy(back.at[q], back_h.at[q], local.at[0])
            copy.start()
            outgoing.append(copy)
    first = len(dests) * (cw // WIDE)
    for copy in loads[2:]:
        copy.wait()
    branch[...] = jnp.zeros_like(branch)
    for b in range(INNER // WIDE):
        if first + b + slots - 1 < len(firsts):
            get(first + b + slots - 1).start()
        part, at = divmod(b * WIDE, cw)
        branch[...] += dot(u[part, :, at : at + WIDE], block_of(first + b))
        for k in range(LEVELS):
            if level_width(k) == (b + 1) * WIDE:

                def level_rows(i, carry, k=k):
                    at = pl.ds(pl.multiple_of(i * rows, rows), rows)
                    norm = norms[at, k : k + 1]
                    total = branch[at, :]
                    inner = jnp.sum(cot[k, at, :].astype(F32) * total, axis=-1, keepdims=True)
                    pulls[at, k : k + 1] = norm * norm * norm * (inner / level_width(k))
                    cot[k, at, :] = (tokens[at, :].astype(F32) + norm * total).astype(BF16)
                    return carry

                lax.fori_loop(0, tokens.shape[0] // rows, level_rows, 0)
                copy = pltpu.make_async_copy(cot.at[k], block_h.at[k], store.at[k])
                copy.start()
                outgoing.append(copy)
    coef = jnp.zeros((tokens.shape[0], 1), F32)
    lane = lax.broadcasted_iota(jnp.int32, (1, LANES), 1)
    packed = jnp.zeros((tokens.shape[0], LANES), F32)
    for k in reversed(range(LEVELS)):
        coef = coef + pulls[:, k : k + 1]
        high, rest = two_terms(coef)
        packed = jnp.where(lane == k, high.astype(F32), packed)
        packed = jnp.where(lane == LEVELS + k, rest.astype(F32), packed)
    coefs[...] = packed.astype(BF16)
    for k, peer in enumerate(peers):
        copy = remote(coefs, coef_h.at[q], coef_s, coef_r, k, peer)
        copy.start()
        outgoing.append(copy)
    copy = pltpu.make_async_copy(coefs, coef_h.at[q], local.at[1])
    copy.start()
    outgoing.append(copy)

    share = width // parts
    tile = 256
    turns = LEFT // tile

    def product(of, j):
        channel = of * width
        lanes = pl.ds(pl.multiple_of(lax.rem(channel, cw), width), width)
        cols = pl.ds(pl.multiple_of(j * tile, tile), tile)
        return dot(u[channel // cw, :, lanes], mixed[level_of(channel, width), :, cols], TN)

    cores = []
    for d in range(line):

        def send_step(j, carry, d=d):
            cols = pl.ds(pl.multiple_of(j * tile, tile), tile)
            sent[d, :, cols] = product(2 * d + 1 - core, j).astype(BF16)
            return carry

        lax.fori_loop(0, D // tile, send_step, 0)
        copy = remote(sent.at[d], held.at[d], core_s, core_r, d, sibling)
        copy.start()
        cores.append(copy)
    for d in range(line):
        cores[d].wait_recv()
        for out, target, first, at in ((left, left_h, 0, 0), (right, right_h, turns, 1)):

            def keep_step(j, carry, d=d, out=out, first=first):
                cols = pl.ds(pl.multiple_of((j + first) * tile, tile), tile)
                to = pl.ds(pl.multiple_of(j * tile, tile), tile)
                total = product(2 * d + core, j + first) + held[d, :, cols].astype(F32)
                total = total.astype(BF16)
                for part in range(parts):
                    out[part, d, :, to] = total[part * share : (part + 1) * share]
                return carry

            lax.fori_loop(0, out.shape[-1] // tile, keep_step, 0)
            copy = pltpu.make_async_copy(
                out.at[:, d], target.at[:, d], store.at[LEVELS + 2 * d + at]
            )
            copy.start()
            outgoing.append(copy)
    for copy in cores:
        copy.wait_send()
    for copy in outgoing:
        copy.wait()


def middle(collective_id, u, stats, wo, cotangent, tokens):
    groups, parts, share = wo.shape[:3]
    line = groups // 2
    rows, cw = u.shape[1:]
    width = share * parts
    sem = pltpu.SemaphoreType.DMA
    hbm = pl.BlockSpec(memory_space=pltpu.HBM)
    left = (parts, line, share, LEFT)
    right = (parts, line, share, D - LEFT)
    return pl.pallas_call(
        functools.partial(middle_kernel, groups, parts, cw),
        in_specs=[hbm] * 5,
        out_specs=[hbm] * 5,
        out_shape=[
            jax.ShapeDtypeStruct((parts, rows, cw), BF16),
            jax.ShapeDtypeStruct((parts, rows, LANES), BF16),
            jax.ShapeDtypeStruct(cotangent.shape, BF16),
            jax.ShapeDtypeStruct(left, BF16),
            jax.ShapeDtypeStruct(right, BF16),
        ],
        scratch_shapes=[
            pltpu.VMEM(u.shape, BF16),
            pltpu.VMEM(stats.shape, F32),
            pltpu.VMEM(cotangent.shape, BF16),
            pltpu.VMEM(tokens.shape, BF16),
            pltpu.VMEM(cotangent.shape, BF16),
            pltpu.VMEM((rows, D), F32),
            pltpu.VMEM((rows, LANES), F32),
            pltpu.VMEM((rows, LANES), F32),
            pltpu.VMEM((parts, rows, cw), BF16),
            pltpu.VMEM((rows, LANES), BF16),
            pltpu.VMEM((3, WIDE // width, parts, share, D), BF16),
            pltpu.VMEM((line, width, D), BF16),
            pltpu.VMEM((line, width, D), BF16),
            pltpu.VMEM(left, BF16),
            pltpu.VMEM(right, BF16),
            *([sem((parts - 1,))] * 4),
            sem((line,)), sem((line,)), sem((3,)), sem((4,)), sem((LEVELS + 2 * line,)), sem((2,)),
        ],
        compiler_params=pltpu.CompilerParams(
            collective_id=collective_id, has_side_effects=True, vmem_limit_bytes=63 * 2**20
        ),
        name="middle",
    )(u, stats, wo, cotangent, tokens)


def sum_blocks(out, blocks, rows):
    def step(i, carry):
        at = pl.ds(pl.multiple_of(i * rows, rows), rows)
        total = blocks[0][at].astype(F32)
        for block in blocks[1:]:
            total = total + block[at].astype(F32)
        out[at] = total.astype(out.dtype)
        return carry

    lax.fori_loop(0, out.shape[0] // rows, step, 0)


class PlaneSum:
    def __init__(self, parts, group, q, blocks, first, second, sends, recvs, source=None):
        self.parts, self.group, self.q = parts, group, q
        self.source = blocks if source is None else source
        self.blocks, self.first, self.second = blocks, first, second
        self.sends, self.recvs = sends, recvs
        self.half = blocks.shape[1] // 2
        if parts == 4:
            self.near = [q + 1 - 2 * lax.rem(q, 2), lax.rem(q + 2, 4)]
            self.far = 3 - q

    @staticmethod
    def scratch(parts, shape, dtype):
        if parts == 4:
            half = (shape[0] // 2,) + shape[1:]
            first, second, count = (2, 2) + half, (2, 2) + half, 6
        else:
            first, second, count = (parts - 1,) + shape, (1, 16, LANES), parts - 1
        sem = pltpu.SemaphoreType.DMA
        return [pltpu.VMEM(first, dtype), pltpu.VMEM(second, dtype), sem((count,)), sem((count,))]

    def piece(self, of, h, source=None):
        blocks = self.blocks if source is None else source
        return blocks.at[of, pl.ds(h * self.half, self.half)]

    def early(self, h):
        if self.parts != 4:
            return []
        near = self.near[h]
        to = (self.group, near)
        return [
            remote(
                self.piece(of, h, self.source), self.first.at[h, k],
                self.sends, self.recvs, 2 * h + k, to,
            )
            for k, of in enumerate((near, self.far))
        ]

    def late(self, h):
        to = (self.group, self.near[1 - h])
        return remote(
            self.second.at[h, 0], self.second.at[h, 1], self.sends, self.recvs, 4 + h, to
        )

    def direct(self):
        peers = seq_peers(self.parts)
        return [
            remote(self.source.at[peer[1]], self.first.at[k], self.sends, self.recvs, k, peer)
            for k, peer in enumerate(peers)
        ]

    def start_far(self):
        for h in range(2):
            for copy in self.early(h)[1:]:
                copy.start()

    def start_near(self, h):
        for copy in self.early(h)[:1]:
            copy.start()

    def start(self, h):
        for copy in self.early(h):
            copy.start()
        if self.parts != 4 and h == 1:
            for copy in self.direct():
                copy.start()

    def turn(self, rows):
        if self.parts != 4:
            return
        for h in range(2):
            for copy in self.early(h):
                copy.wait()
            beyond = self.piece(self.near[1 - h], h)
            each(self.second.at[h, 0], [beyond, self.first.at[h, 1]], rows)
            self.late(h).start()

    def finish(self, out, rows):
        if self.parts != 4:
            for copy in self.direct():
                copy.wait()
            each(
                out,
                [self.blocks.at[self.q]] + [self.first.at[k] for k in range(self.parts - 1)],
                rows,
            )
            return
        for h in range(2):
            self.late(h).wait()
            each(
                out.at[pl.ds(h * self.half, self.half)],
                [self.piece(self.q, h), self.first.at[h, 0], self.second.at[h, 1]],
                rows,
            )


def each(out, blocks, rows):
    if len(out.shape) == 2:
        sum_blocks(out, blocks, rows)
        return
    for d in range(out.shape[0]):
        sum_blocks(out.at[d], [block.at[d] for block in blocks], rows)


class LineSum:
    def __init__(self, line, z, core, q, acc, up, down, up_s, up_r, down_s, down_r, rows, steps):
        self.line, self.z, self.core, self.q = line, z, core, q
        self.acc, self.up, self.down = acc, up, down
        self.up_s, self.up_r, self.down_s, self.down_r = up_s, up_r, down_s, down_r
        self.rows, self.steps = rows, steps

    def ahead(self, d, first):
        block = self.acc.at[d] if first else self.up.at[d]
        to = (2 * (self.z + 1) + self.core, self.q)
        return remote(block, self.up.at[d], self.up_s, self.up_r, d, to)

    def behind(self, d, first):
        block = self.acc.at[d] if first else self.down.at[d]
        to = (2 * (self.z - 1) + self.core, self.q)
        return remote(block, self.down.at[d], self.down_s, self.down_r, d, to)

    def add(self, into, d):
        add_blocks(into.at[d], into.at[d], self.acc.at[d], self.rows, self.steps)

    def step(self, t):
        line, z = self.line, self.z
        far, near = line - 1 - t + z, t - (line - 1 - z)

        @pl.when(z == 0)
        def _():
            self.ahead(line - 1 - t, True).start()

        @pl.when((z > 0) & (z <= t))
        def _():
            self.ahead(far, False).wait_recv()
            self.add(self.up, far)
            self.ahead(far, False).start()

        @pl.when(z == line - 1)
        def _():
            self.behind(t, True).start()

        @pl.when((z < line - 1) & (line - 1 - z <= t))
        def _():
            self.behind(near, False).wait_recv()
            self.add(self.down, near)
            self.behind(near, False).start()

    def sent(self, t):
        line, z = self.line, self.z
        far, near = line - 1 - t + z, t - (line - 1 - z)

        @pl.when(z == 0)
        def _():
            self.ahead(line - 1 - t, True).wait_send()

        @pl.when((z > 0) & (z <= t))
        def _():
            self.ahead(far, False).wait_send()

        @pl.when(z == line - 1)
        def _():
            self.behind(t, True).wait_send()

        @pl.when((z < line - 1) & (line - 1 - z <= t))
        def _():
            self.behind(near, False).wait_send()

    def finish(self, out):
        line, z = self.line, self.z

        @pl.when(z == 0)
        def _():
            self.behind(z, False).wait_recv()
            add_blocks(out, self.acc.at[z], self.down.at[z], self.rows, self.steps)

        @pl.when(z == line - 1)
        def _():
            self.ahead(z, False).wait_recv()
            add_blocks(out, self.acc.at[z], self.up.at[z], self.rows, self.steps)

        @pl.when((z > 0) & (z < line - 1))
        def _():
            self.ahead(z, False).wait_recv()
            self.add(self.up, z)
            self.behind(z, False).wait_recv()
            add_blocks(out, self.up.at[z], self.down.at[z], self.rows, self.steps)


class LineSums:
    def __init__(self, line, z, core, q, acc, up, down, sems, rows):
        half = acc.shape[1] // 2
        self.line = line
        self.halves = [
            LineSum(
                line, z, core, q, *[a.at[:, pl.ds(h * half, half)] for a in (acc, up, down)],
                *[s.at[h] for s in sems], rows, half // rows,
            )
            for h in range(2)
        ]
        self.half = half

    def step(self, t):
        for part in self.halves:
            part.step(t)

    def finish(self, out):
        for h, part in enumerate(self.halves):
            part.finish(out.at[pl.ds(h * self.half, self.half)])

    def sent(self):
        for t in range(self.line - 1):
            for part in self.halves:
                part.sent(t)


def backward_kernel(
    groups, parts, cw,
    back_h, coefs_h, normed_h, px_h, y_h, z_h, states_h, wide_h,
    gain, taps, heads, skip, spread, gather,
    dz_h, dpx_h, small, wide_sum, gate_sum,
    dz, coefs, normed, px, y, dy, states, wide, dpx, dtaps, dheads, dskip, dgain,
    xbuf, dstate, dcbuf, slope, xact, xd_s, dxd_s, acc_s,
    first, second, wide_s, wide_r, gate_made, gate_held, gate_acc, gate_up, gate_down,
    core_s, core_r, up_s, up_r, down_s, down_r, load, store,
):
    line = groups // 2
    cc = cw + 2 * N
    length = y.shape[0]
    chunks = length // CHUNK
    group, q = lax.axis_index("dp"), lax.axis_index("seq")
    z, core = group // 2, lax.rem(group, 2)
    sibling = (2 * z + 1 - core, q)
    loads = [
        pltpu.make_async_copy(source, target, load.at[k])
        for k, (source, target) in enumerate(
            [(wide_h, wide), (back_h, dz), (coefs_h, coefs), (y_h, y), (z_h, dy),
             (normed_h, normed), (states_h, states)]
        )
    ]
    for copy in loads[1:5]:
        copy.start()

    def fetch(at, first=False):
        slot = lax.rem(at, 2)
        if first:
            return pltpu.make_async_copy(
                px_h.at[pl.ds(0, CHUNK)], px.at[0, pl.ds(8, CHUNK)], load.at[7]
            )
        rows = pl.ds(pl.multiple_of(at * CHUNK - 8, 8), CHUNK + 8)
        return pltpu.make_async_copy(px_h.at[rows], px.at[slot], load.at[7 + slot])

    greet(seq_peers(parts) + dp_peers(groups))
    plane = PlaneSum(parts, group, q, wide, first, second, wide_s, wide_r, wide_h)
    plane.start(0)
    plane.start(1)
    for copy in loads[1:5]:
        copy.wait()
    loads[5].start()
    loads[6].start()
    loads[0].start()
    fetch(chunks - 1).start()

    rows = 32
    lane = lax.broadcasted_iota(jnp.int32, (1, LANES), 1)
    dgain[...] = jnp.zeros_like(dgain)

    def gate_rows(i, carry):
        at = pl.ds(pl.multiple_of(i * rows, rows), rows)
        coef = coefs[at, :].astype(F32)
        for b in range(cw // WIDE):
            lanes = slice(b * WIDE, (b + 1) * WIDE)
            level = level_of(q * cw + b * WIDE, WIDE)
            ours = (lane == level) | (lane == level + LEVELS)
            pull = jnp.sum(jnp.where(ours, coef, 0.0), axis=-1, keepdims=True)
            gate_in = dy[at, lanes]
            sig = jax.nn.sigmoid(gate_in)
            gate = gate_in * sig
            y_at = y[at, lanes]
            gated = y_at * gate
            back = dz[at, lanes].astype(F32)
            dgated = gain[:, lanes] * back - gated * pull
            dgain[0:1, lanes] += jnp.sum(back * gated, axis=0, keepdims=True)
            dz[at, lanes] = (dgated * y_at * (sig + gate * (1.0 - sig))).astype(BF16)
            dy[at, lanes] = dgated * gate
        return carry

    lax.fori_loop(0, length // rows, gate_rows, 0)
    dz_out = pltpu.make_async_copy(dz, dz_h, store.at[0])
    dz_out.start()
    loads[5].wait()
    span = gate_acc.shape[1]

    def dweight(of, out):
        at = pl.ds(pl.multiple_of(of * span, span), span)
        out[...] = dot(normed[:, at], dz[...], TN).astype(BF16)

    def core_copy(d):
        return remote(gate_made.at[d], gate_held.at[d], core_s, core_r, d, sibling)

    order = [d for k in range(line // 2) for d in (line - 1 - k, k)]
    gates = LineSums(
        line, z, core, q, gate_acc, gate_up, gate_down, (up_s, up_r, down_s, down_r), span // 8
    )
    for some in (order[:2], order[2:]):
        for d in some:
            dweight(2 * d + 1 - core, gate_made.at[d])
            core_copy(d).start()
        for d in some:
            dweight(2 * d + core, gate_acc.at[d])
            core_copy(d).wait()
            add_blocks(gate_acc.at[d], gate_acc.at[d], gate_held.at[d], span // 4, 4)
        if some[0] == order[0]:
            gates.step(0)
    dstate[...] = jnp.zeros_like(dstate)
    dcbuf[CHUNK : CHUNK + 8, :] = jnp.zeros((8, cc), F32)
    dtaps[...] = jnp.zeros_like(dtaps)
    dheads[...] = jnp.zeros_like(dheads)
    dskip[...] = jnp.zeros_like(dskip)
    loads[6].wait()
    loads[0].wait()

    def scan_rows(i, carry):
        for t in range(1, line - 1):

            @pl.when(i == min(3 * t - 2, chunks - 1))
            def _(t=t):
                gates.step(t)

        @pl.when(i == 3)
        def _():
            plane.turn(32)

        at = chunks - 1 - i
        here = pl.ds(pl.multiple_of(at * CHUNK, CHUNK), CHUNK)

        @pl.when(at > 0)
        def _():
            fetch(at).wait()

        @pl.when(at == 0)
        def _():
            fetch(0, True).wait()

        @pl.when(at > 1)
        def _():
            fetch(at - 1).start()

        @pl.when(at == 1)
        def _():
            fetch(0, True).start()

        rows = px.at[lax.rem(at, 2)]
        scan_backward_step(
            cw, at == 0, rows.at[pl.ds(8, CHUNK)], rows.at[pl.ds(0, 8)], taps, heads, skip, spread, gather,
            dy.at[here], y.at[here], states.at[at], dpx.at[here], dtaps, dheads, dskip,
            xbuf, dstate, dcbuf, slope, xact, xd_s, dxd_s, acc_s,
        )
        return carry

    lax.fori_loop(0, chunks, scan_rows, 0)
    dpx_out = pltpu.make_async_copy(dpx, dpx_h, store.at[1])
    dpx_out.start()
    small[...] = jnp.zeros_like(small)
    wide_rows, own_rows = cc // LANES, cw // LANES
    for tap in range(TAPS + 1):
        for b in range(wide_rows):
            to = tap * wide_rows + b
            small[to : to + 1, :] = dtaps[tap : tap + 1, b * LANES : (b + 1) * LANES]
    to = (TAPS + 1) * wide_rows
    for b in range(own_rows):
        small[to + b : to + b + 1, :] = dgain[0:1, b * LANES : (b + 1) * LANES]
    hq = cw // P_SIZE
    skips = spread_heads(dskip[...], gather[...])
    small[to + own_rows : to + own_rows + 1, :] = (
        dheads[0:1, :]
        + pltpu.roll(dheads[...], hq, 1)[1:2, :]
        + pltpu.roll(skips, 2 * hq, 1)[0:1, :]
    )
    plane.finish(wide_sum, 32)
    gates.finish(gate_sum)
    gates.sent()
    dz_out.wait()
    dpx_out.wait()


def backward(
    collective_id, back, coefs, normed, px, y, z, states, wide, gain, taps, heads, skip, spread, gather
):
    parts, line = wide.shape[:2]
    length, width = px.shape
    cw = skip.shape[1]
    cc = cw + 2 * N
    span = D // (2 * line)
    sem = pltpu.SemaphoreType.DMA
    vmem = pl.BlockSpec(memory_space=pltpu.VMEM)
    hbm = pl.BlockSpec(memory_space=pltpu.HBM)
    small_rows = (TAPS + 1) * (cc // LANES) + cw // LANES + 1
    small_rows = -(-small_rows // 8) * 8
    return pl.pallas_call(
        functools.partial(backward_kernel, 2 * line, parts, cw),
        in_specs=[*([hbm] * 8), *([vmem] * 6)],
        out_specs=[hbm, hbm, vmem, vmem, vmem],
        out_shape=[
            jax.ShapeDtypeStruct((length, cw), BF16),
            jax.ShapeDtypeStruct((length, width), BF16),
            jax.ShapeDtypeStruct((small_rows, LANES), F32),
            jax.ShapeDtypeStruct(wide.shape[1:], BF16),
            jax.ShapeDtypeStruct((span, cw), BF16),
        ],
        scratch_shapes=[
            *[pltpu.VMEM(a.shape, a.dtype) for a in (back, coefs, normed)],
            pltpu.VMEM((2, CHUNK + 8, width), F32),
            *[pltpu.VMEM(a.shape, a.dtype) for a in (y, z, states, wide)],
            pltpu.VMEM((length, width), BF16),
            pltpu.VMEM((8, cc), F32),
            pltpu.VMEM((8, LANES), F32),
            pltpu.VMEM((8, cw), F32),
            pltpu.VMEM((8, cw), F32),
            pltpu.VMEM((CHUNK + 8, cc), F32),
            pltpu.VMEM((N, cw), F32),
            pltpu.VMEM((CHUNK + 8, cc), F32),
            pltpu.VMEM((CHUNK, cc), F32),
            pltpu.VMEM((CHUNK, cc), F32),
            pltpu.VMEM((CHUNK, cw), BF16),
            pltpu.VMEM((CHUNK, cw), F32),
            pltpu.VMEM((CHUNK, CHUNK), F32),
            *PlaneSum.scratch(parts, wide.shape[1:], BF16),
            *([pltpu.VMEM((line, span, cw), BF16)] * 5),
            sem((line,)), sem((line,)), *([sem((2, line))] * 4),
            sem((9,)), sem((2,)),
        ],
        compiler_params=pltpu.CompilerParams(
            collective_id=collective_id, has_side_effects=True, vmem_limit_bytes=63 * 2**20
        ),
        name="backward",
    )(back, coefs, normed, px, y, z, states, wide, gain, taps, heads, skip, spread, gather)


def owners_kernel(
    groups, parts, rows, cw,
    normed, left, right, gate, small, dz, dpx, wz, wx,
    part, rest_out, left_out, right_out, gate_out, back_out, small_all,
    made, held, acc, up, down, final, left_up, left_down, right_acc, right_up, right_down,
    rest_made, rest_held, rest, rest_acc, rest_up, rest_down,
    normed_v, dz_v, dpx_v, wz_v, wx_v, back, back_sum,
    right_1, right_2, right_s, right_r, back_1, back_2, back_s, back_r,
    rest_1, rest_2, rest_s, rest_r,
    core_s, core_r, up_s, up_r, down_s, down_r, lup_s, lup_r, ldown_s, ldown_r,
    rup_s, rup_r, rdown_s, rdown_r, tup_s, tup_r, tdown_s, tdown_r, rcore_s, rcore_r,
    part_s, part_r, gate_s, gate_r, small_s, small_r, load, local,
):
    line = groups // 2
    span = parts * rows
    group, q = lax.axis_index("dp"), lax.axis_index("seq")
    z, core = group // 2, lax.rem(group, 2)
    sibling = (2 * z + 1 - core, q)
    peers, others = seq_peers(parts), dp_peers(groups)
    tokens = back.shape[1]
    loads = [
        pltpu.make_async_copy(source, target, load.at[k])
        for k, (source, target) in enumerate(
            [(normed, normed_v), (dpx, dpx_v), (dz, dz_v), (wz, wz_v), (wx, wx_v)]
        )
    ]
    for copy in loads[:2]:
        copy.start()
    greet(peers + others)
    half_rows = left.shape[1] // 2
    lefts = LineSum(
        line, z, core, q, left, left_up, left_down, lup_s, lup_r, ldown_s, ldown_r, half_rows, 2
    )
    rights = LineSum(
        line, z, core, q, right_acc, right_up, right_down, rup_s, rup_r, rdown_s, rdown_r,
        half_rows, 2,
    )
    wholes = LineSum(
        line, z, core, q, acc, up, down, up_s, up_r, down_s, down_r, rows, parts
    )
    lefts.step(0)
    right_plane = PlaneSum(parts, group, q, right, right_1, right_2, right_s, right_r)
    rest_plane = PlaneSum(parts, group, q, rest, rest_1, rest_2, rest_s, rest_r)
    rests = LineSum(
        line, z, core, q, rest_acc, rest_up, rest_down, tup_s, tup_r, tdown_s, tdown_r, rows, 1
    )
    back_plane = PlaneSum(parts, group, q, back, back_1, back_2, back_s, back_r)
    right_plane.start(0)
    right_plane.start(1)
    waiting = []
    for k, peer in enumerate(peers):
        copy = remote(gate.at[peer[1]], gate_out.at[q], gate_s, gate_r, k, peer)
        copy.start()
        waiting.append(copy)
    for k, peer in enumerate(others):
        copy = remote(small, small_all.at[group], small_s, small_r, k, peer)
        copy.start()
        waiting.append(copy)
    own = [
        pltpu.make_async_copy(gate.at[q], gate_out.at[q], local.at[0]),
        pltpu.make_async_copy(small, small_all.at[group], local.at[1]),
    ]
    for copy in own:
        copy.start()
    loads[0].wait()
    loads[1].wait()
    for copy in loads[2:]:
        copy.start()
    tile = 512

    def dweight(of):
        at = pl.ds(pl.multiple_of(of * span, span), span)
        return dot(normed_v[:, at], dpx_v[...], TN)

    cores = {}
    order = [d for k in range(line // 2) for d in (line - 1 - k, k)]

    def share_core(d):
        total = dweight(2 * d + 1 - core)
        made[d] = total[:, :cw].astype(BF16)
        rest_made[d] = total[:, cw:].astype(BF16)
        cores[d] = [
            remote(made.at[d], held.at[d], core_s, core_r, d, sibling),
            remote(rest_made.at[d], rest_held.at[d], rcore_s, rcore_r, d, sibling),
        ]
        for copy in cores[d]:
            copy.start()

    def sum_core(d):
        total = dweight(2 * d + core)
        for copy in cores[d]:
            copy.wait()
        acc[d] = (total[:, :cw] + held[d].astype(F32)).astype(BF16)
        others = (total[:, cw:] + rest_held[d].astype(F32)).astype(BF16)
        for k in range(parts):
            rest[k, d] = others[k * rows : (k + 1) * rows]

    def dnormed(of):
        at = pl.ds(pl.multiple_of(of * tokens, tokens), tokens)

        def step(j, carry):
            cols = pl.ds(pl.multiple_of(j * tile, tile), tile)
            back[of, :, cols] = (
                dot(dz_v[at, :], wz_v[cols, :], NT) + dot(dpx_v[at, :], wx_v[cols, :], NT)
            ).astype(BF16)
            return carry

        lax.fori_loop(0, D // tile, step, 0)

    share_core(order[0])
    lefts.sent(0)
    lefts.step(1)
    share_core(order[1])
    sum_core(order[0])
    sum_core(order[1])
    wholes.step(0)
    for t in range(2, line - 1):
        lefts.sent(t - 1)
        lefts.step(t)
    for copy in loads[2:]:
        copy.wait()
    if parts == 4:
        dnormed(back_plane.far)
        back_plane.start_far()
    for d in order[2:]:
        share_core(d)
    for d in order[2:]:
        sum_core(d)
    right_plane.turn(32)
    if parts == 4:
        dnormed(back_plane.near[0])
        back_plane.start_near(0)
    wholes.sent(0)
    wholes.step(1)
    if parts == 4:
        dnormed(back_plane.near[1])
        back_plane.start_near(1)
    else:
        for peer in peers:
            dnormed(peer[1])
        back_plane.start(1)
    rest_plane.start(0)
    rest_plane.start(1)
    dnormed(q)
    right_plane.finish(right_acc, 32)
    for t in range(2, line - 1):
        wholes.sent(t - 1)
        wholes.step(t)
    rights.step(0)
    rest_plane.turn(rows)
    rest_plane.finish(rest_acc, rows)
    rests.step(0)
    back_plane.turn(32)
    lefts.finish(left_out)
    lefts.sent(line - 2)
    rests.sent(0)
    rests.step(1)
    rights.sent(0)
    rights.step(1)
    wholes.sent(line - 2)
    wholes.finish(final)
    for k, peer in enumerate(peers):
        block = final.at[pl.ds(pl.multiple_of(peer[1] * rows, rows), rows)]
        copy = remote(block, part.at[q], part_s, part_r, k, peer)
        copy.start()
        waiting.append(copy)
    copy = pltpu.make_async_copy(
        final.at[pl.ds(pl.multiple_of(q * rows, rows), rows)], part.at[q], local.at[2]
    )
    copy.start()
    own.append(copy)
    for t in range(2, line - 1):
        rights.sent(t - 1)
        rights.step(t)
    for t in range(2, line - 1):
        rests.sent(t - 1)
        rests.step(t)
    back_plane.finish(back_sum, 32)
    copy = pltpu.make_async_copy(back_sum, back_out, local.at[3])
    copy.start()
    own.append(copy)
    rests.finish(rest_out)
    rests.sent(line - 2)
    rights.finish(right_out)
    rights.sent(line - 2)
    for copy in own + waiting:
        copy.wait()


def sum_to_owners(collective_id, normed, left, right, gate, small, dz, dpx, wz, wx):
    parts, line, out_rows, slim = right.shape
    groups = 2 * line
    rows, cw = gate.shape[1:]
    span = rows * parts
    extra = dpx.shape[1] - cw
    tokens = dz.shape[0] // parts
    sem = pltpu.SemaphoreType.DMA
    vmem = pl.BlockSpec(memory_space=pltpu.VMEM)
    hbm = pl.BlockSpec(memory_space=pltpu.HBM)
    right_sum = (line, out_rows, slim)
    rest = (parts, line, rows, extra)
    return pl.pallas_call(
        functools.partial(owners_kernel, groups, parts, rows, cw),
        in_specs=[hbm, vmem, vmem, hbm, vmem, hbm, hbm, hbm, hbm],
        out_specs=[hbm, vmem, vmem, vmem, hbm, hbm, vmem],
        out_shape=[
            jax.ShapeDtypeStruct((parts, rows, cw), BF16),
            jax.ShapeDtypeStruct((rows, extra), F32),
            jax.ShapeDtypeStruct((out_rows, left.shape[-1]), F32),
            jax.ShapeDtypeStruct((out_rows, slim), F32),
            jax.ShapeDtypeStruct(gate.shape, BF16),
            jax.ShapeDtypeStruct((tokens, D), F32),
            jax.ShapeDtypeStruct((groups,) + small.shape, F32),
        ],
        scratch_shapes=[
            *([pltpu.VMEM((line, span, cw), BF16)] * 5),
            pltpu.VMEM((span, cw), BF16),
            *([pltpu.VMEM(left.shape, BF16)] * 2),
            *([pltpu.VMEM(right_sum, BF16)] * 3),
            *([pltpu.VMEM((line, span, extra), BF16)] * 2),
            pltpu.VMEM(rest, BF16),
            *([pltpu.VMEM(rest[1:], BF16)] * 3),
            *[pltpu.VMEM(a.shape, BF16) for a in (normed, dz, dpx, wz, wx)],
            pltpu.VMEM((parts, tokens, D), BF16),
            pltpu.VMEM((tokens, D), F32),
            *PlaneSum.scratch(parts, right.shape[1:], BF16),
            *PlaneSum.scratch(parts, (tokens, D), BF16),
            *PlaneSum.scratch(parts, rest[1:], BF16),
            *([sem((line,))] * 20),
            *([sem((parts - 1,))] * 4),
            *([sem((groups - 1,))] * 2),
            sem((5,)),
            sem((4,)),
        ],
        compiler_params=pltpu.CompilerParams(
            collective_id=collective_id, has_side_effects=True, vmem_limit_bytes=63 * 2**20
        ),
        name="sum_to_owners",
    )(normed, left, right, gate, small, dz, dpx, wz, wx)


def on_device(
    hidden_in, out_grads, w_in, w_in_m, w_in_v, w_out, w_out_m, w_out_v,
    chan_params, chan_m, chan_v, head_params, head_m, head_v,
):
    parts = lax.axis_size("seq")
    groups = lax.axis_size("dp")
    q = lax.axis_index("seq")
    rows = hidden_in.shape[1]
    length = rows * parts
    cw = INNER // parts
    hq = H // parts
    cc = cw + 2 * N
    in_rows = w_in.shape[0]
    out_rows = w_out.shape[0]

    chan_len = chan_params.shape[0]
    line = groups // 2
    group = lax.axis_index("dp")
    owner = group * parts + q
    chan_block = lax.dynamic_update_slice(
        jnp.zeros((8 * LANES,), F32),
        lax.reduce_precision(chan_params, 8, 7),
        (lax.rem(owner * chan_len, LANES),),
    ).reshape(8, LANES)
    head_block = jnp.pad(head_params, ((0, 5), (0, LANES - H)))
    hidden, wx, gate, wo, gain_in, own_gain, taps, heads, skip, spread, gather = collect(
        0, hidden_in[0], w_in, w_out, chan_block, head_block, chan_len, groups, parts
    )

    normed, px, y, states, z, u, stats, wz, wo = forward(
        1, hidden.reshape(length, D), wx.reshape(D, cc + LANES), gate, wo, gain_in, own_gain,
        taps, heads, skip, spread,
    )
    wx, wz = wx.reshape(D, cc + LANES), wz.reshape(D, cw)
    cotangent = out_grads[:, 0]
    back_own, coefs, block_out, dwo_left, dwo_right = middle(
        2, u, stats, wo, cotangent, hidden_in[0]
    )

    dz, dpx, small, dwo_left, dwz = backward(
        5, back_own.reshape(length, cw), coefs.reshape(length, LANES), normed, px, y, z, states,
        dwo_left, own_gain, taps, heads, skip, spread, gather,
    )
    x_part, rest, left_part, right_part, z_part, dnormed, small = sum_to_owners(
        4, normed, dwo_left, dwo_right, dwz.reshape(parts, in_rows, cw), small, dz, dpx, wz, wx
    )
    hidden_grad, chan_total, head_total, norm = gradient_norm(
        6, x_part, rest, z_part, left_part, right_part, dnormed, small, hidden_in[0],
        gain_in, cotangent, groups,
    )
    (
        hidden_grad, block_out, w_in_new, w_in_m_new, w_in_v_new, w_in_copy,
        w_out_new, w_out_m_new, w_out_v_new, w_out_copy,
    ) = update_weights(
        norm, x_part, rest, z_part, left_part, right_part, hidden_grad, block_out,
        (w_in, w_in_m, w_in_v, w_out, w_out_m, w_out_v),
    )
    hidden_grad, block_out = hidden_grad[None], block_out[:, None]
    grad_norm, clip_factor = norm[0, 0], norm[1, 0]
    chan_part = lax.dynamic_slice(chan_total.reshape(-1), (owner * chan_len,), (chan_len,))
    head_total = head_total[:parts, : 3 * hq].reshape(parts, 3, hq)
    head_total = head_total.transpose(1, 0, 2).reshape(3, H)
    chan_new, chan_m_new, chan_v_new = adam_tile(
        chan_params, clip_factor * chan_part, chan_m, chan_v, 0.2, 0.0
    )
    head_new, head_m_new, head_v_new = adam_tile(
        head_params, clip_factor * head_total, head_m, head_v, 1.0, 0.0
    )
    return (
        block_out, hidden_grad, grad_norm,
        w_in_new, w_in_m_new, w_in_v_new, w_in_copy,
        w_out_new, w_out_m_new, w_out_v_new, w_out_copy,
        chan_new, chan_m_new, chan_v_new, head_new, head_m_new, head_v_new,
    )


def solution(mesh):
    rows = P(("dp", "seq"), None)
    flat = P(("dp", "seq"))
    in_specs = (
        P("dp", "seq", None),
        P(None, "dp", "seq", None),
        *([rows] * 6),
        *([flat] * 3),
        *([P()] * 3),
    )
    out_specs = (
        P(None, "dp", "seq", None),
        P("dp", "seq", None),
        P(),
        *([rows] * 8),
        *([flat] * 3),
        *([P()] * 3),
    )
    return jax.shard_map(
        on_device, mesh=mesh, in_specs=in_specs, out_specs=out_specs, check_vma=False
    )
```

```python
import functools

import jax
import jax.numpy as jnp
from jax import lax
from jax.experimental import pallas as pl
from jax.experimental.pallas import tpu as pltpu
from jax.sharding import PartitionSpec as P

D = 2048
INNER = 4096
H = 64
P_SIZE = 64
N = 128
TAPS = 4
STEP = 10
E_IN = 8512
CONV_CH = 4352
LANES = 128
CHUNK = 128
LEVELS = 4

EXACT = lax.Precision.HIGHEST
EPS_IN = 1e-06
EPS_OUT = 1e-05
ADAM_EPS = 1e-08
BETA = 0.5
CLIP = 1.0
F32 = jnp.float32
BF16 = jnp.bfloat16
MASKED = -1e30


def level_width(level):
    return INNER * 2**level // 8


SEGMENTS = tuple(
    (0 if level == 0 else level_width(level - 1), level_width(level)) for level in range(LEVELS)
)


def dot(a, b, dims=((1,), (0,)), precision=None):
    return lax.dot_general(a, b, (dims, ((), ())), precision=precision, preferred_element_type=F32)


NT = ((1,), (1,))
TN = ((0,), (0,))


def softplus(v):
    return jnp.maximum(v, 0.0) + jnp.log1p(jnp.exp(-jnp.abs(v)))


def two_terms(v):
    high = v.astype(BF16)
    return high, (v - high.astype(F32)).astype(BF16)


def spread_heads(v, spread):
    high, rest = two_terms(v)
    return dot(high, spread) + dot(rest, spread)


def own_heads_first(dt_raw, hq, back=False):
    by = lax.axis_index("seq") * hq
    return pltpu.roll(dt_raw, by if back else lax.rem(LANES - by, LANES), 1)


def rates(dt_raw, heads):
    step = softplus(dt_raw + heads[0:1, :])
    return step, step * heads[1:2, :]


def triangle(size):
    row = lax.broadcasted_iota(jnp.int32, (size, size), 0)
    col = lax.broadcasted_iota(jnp.int32, (size, size), 1)
    return row, col


def conv_block(taps, xbuf, lanes):
    out = taps[TAPS : TAPS + 1, lanes]
    for tap in range(TAPS):
        out = out + taps[tap : tap + 1, lanes] * xbuf[5 + tap : 5 + tap + CHUNK, lanes]
    return out


def pair_decay(cum, cum_t, causal, head):
    gap = cum[:, head : head + 1] - cum_t[head : head + 1, :]
    return jnp.exp(jnp.where(causal, gap, MASKED))


def scan_forward_step(cw, px, taps, heads, skip, spread, y, states, xbuf, state, xdt, carried):
    cc = cw + 2 * N
    xbuf[8 : 8 + CHUNK, :] = px[:, :cc]
    step, rate = rates(own_heads_first(px[:, cc:], cw // P_SIZE), heads)
    row, col = triangle(CHUNK)
    causal = row >= col
    cum = dot(causal.astype(F32), rate, precision=EXACT)
    cum_t = cum.T
    spread_m = spread[...]
    last = cum[CHUNK - 1 : CHUNK, :]
    step_x = spread_heads(step, spread_m)
    grow_x = spread_heads(jnp.exp(cum), spread_m)
    tail_x = spread_heads(jnp.exp(last - cum), spread_m)

    def activated(lanes):
        conv = conv_block(taps, xbuf, lanes)
        return conv * jax.nn.sigmoid(conv)

    state_in = activated(slice(cw, cw + N))
    state_out = activated(slice(cw + N, cw + 2 * N))
    scores = dot(state_out, state_in, NT, EXACT)
    states[...] = state[...].astype(BF16)
    carried[...] = dot(state_out.astype(BF16), state[...].astype(BF16))
    first = lax.broadcasted_iota(jnp.int32, (1, LANES), 1) < P_SIZE
    for pair in range(cw // LANES):
        lanes = slice(pair * LANES, (pair + 1) * LANES)
        x = activated(lanes)
        xd = (x * step_x[:, lanes]).astype(BF16).astype(F32)
        xdt[:, lanes] = (xd * tail_x[:, lanes]).astype(BF16)
        stacked = jnp.concatenate([jnp.where(first, xd, 0.0), jnp.where(first, 0.0, xd)], axis=0)
        mixing = jnp.concatenate(
            [
                (pair_decay(cum, cum_t, causal, 2 * pair + k) * scores).astype(BF16)
                for k in range(2)
            ],
            axis=1,
        )
        y[:, lanes] = (
            dot(mixing, stacked.astype(BF16))
            + grow_x[:, lanes] * carried[:, lanes]
            + skip[:, lanes] * x
        )
    state[...] = grow_x[CHUNK - 1 : CHUNK, :] * state[...] + dot(
        state_in.astype(BF16), xdt[...], TN
    )
    xbuf[0:8, :] = xbuf[CHUNK : CHUNK + 8, :]


def scan_backward_step(
    cw, start, px, halo, taps, heads, skip, spread, gather, dy, y, states,
    dpx, dtaps, dheads, dskip,
    xbuf, dstate, dcbuf, slope, xact, xd_s, dxd_s, acc_s,
):
    cc = cw + 2 * N
    xbuf[0:8, :] = jnp.where(start, 0.0, halo[:, :cc])
    xbuf[8 : 8 + CHUNK, :] = px[:, :cc]
    dt_raw = own_heads_first(px[:, cc:], cw // P_SIZE)
    step, rate = rates(dt_raw, heads)
    row, col = triangle(CHUNK)
    causal = row >= col
    cum = dot(causal.astype(F32), rate, precision=EXACT)
    cum_t = cum.T
    spread_m = spread[...]
    last = cum[CHUNK - 1 : CHUNK, :]
    step_x = spread_heads(step, spread_m)
    grow_x = spread_heads(jnp.exp(cum), spread_m)
    tail_x = spread_heads(jnp.exp(last - cum), spread_m)

    for block in range(cc // LANES):
        lanes = slice(block * LANES, (block + 1) * LANES)
        conv = conv_block(taps, xbuf, lanes)
        sig = jax.nn.sigmoid(conv)
        act = conv * sig
        xact[:, lanes] = act
        slope[:, lanes] = sig + act * (1.0 - sig)
    state_in = xact[:, cw : cw + N]
    state_out = xact[:, cw + N : cc]
    scores = dot(state_out, state_in, NT, EXACT)
    in_low = state_in.astype(BF16)
    out_low = state_out.astype(BF16)
    dstate_low = dstate[...].astype(BF16)
    acc_s[...] = jnp.zeros_like(acc_s)
    dxd_s[...] = tail_x * dot(in_low, dstate_low)
    dskip[0:1, :] += jnp.sum(xact[:, :cw] * dy[...], axis=0, keepdims=True)
    first = lax.broadcasted_iota(jnp.int32, (1, LANES), 1) < P_SIZE
    xd_s[...] = (xact[:, :cw] * step_x).astype(BF16)
    total = jnp.sum(xd_s[...].astype(F32) * dxd_s[...], axis=0, keepdims=True) + grow_x[
        CHUNK - 1 : CHUNK, :
    ] * jnp.sum(dstate[...] * states[...].astype(F32), axis=0, keepdims=True)
    dscores = jnp.zeros((CHUNK, CHUNK), F32)
    for pair in range(cw // LANES):
        lanes = slice(pair * LANES, (pair + 1) * LANES)
        dyp = dy[:, lanes]
        stacked = jnp.concatenate(
            [jnp.where(first, dyp, 0.0), jnp.where(first, 0.0, dyp)], axis=0
        ).astype(BF16)
        decays = [pair_decay(cum, cum_t, causal, 2 * pair + k) for k in range(2)]
        mixing = jnp.concatenate([(decay * scores).astype(BF16) for decay in decays], axis=0)
        dxd_s[:, lanes] += dot(mixing, stacked, TN)
        dmix = dot(stacked, xd_s[:, lanes], NT)
        dscores = dscores + decays[0] * dmix[:CHUNK] + decays[1] * dmix[CHUNK:]
    dy_low = dy[...].astype(BF16)
    dy_f = dy_low.astype(F32)
    xd_f = xd_s[...].astype(F32)
    dxd = dxd_s[...]
    y_scan = y[...] - skip[...] * xact[:, :cw]
    final = lax.broadcasted_iota(jnp.int32, (CHUNK, 1), 0) == CHUNK - 1
    gather_m = gather[...]
    dcum = spread_heads(dy_f * y_scan - xd_f * dxd + jnp.where(final, total, 0.0), gather_m)
    dstep = spread_heads(xact[:, :cw] * dxd, gather_m)
    drate = dot((row <= col).astype(F32), dcum, precision=EXACT)
    dstep = dstep + drate * heads[1:2, :]
    ddt = dstep * jax.nn.sigmoid(dt_raw + heads[0:1, :])
    dheads[0:1, :] += jnp.sum(ddt, axis=0, keepdims=True)
    dheads[1:2, :] += jnp.sum(drate * rate, axis=0, keepdims=True)
    grown = (grow_x * dy_f).astype(BF16)
    dscores_low = dscores.astype(BF16)
    dout = dot(dscores_low, in_low) + dot(grown, states[...], NT)
    din = dot(dscores_low, out_low, TN) + dot((tail_x * xd_f).astype(BF16), dstate_low, NT)
    dstate[...] = grow_x[CHUNK - 1 : CHUNK, :] * dstate[...] + dot(out_low, grown, TN)
    dcbuf[:CHUNK, :cw] = (step_x * dxd + skip[...] * dy[...]) * slope[:, :cw]
    dcbuf[:CHUNK, cw : cw + N] = din * slope[:, cw : cw + N]
    dcbuf[:CHUNK, cw + N :] = dout * slope[:, cw + N :]
    for block in range(cc // LANES):
        lanes = slice(block * LANES, (block + 1) * LANES)
        dconv = dcbuf[:CHUNK, lanes]
        dtaps[TAPS : TAPS + 1, lanes] += jnp.sum(dconv, axis=0, keepdims=True)
        back = taps[TAPS - 1 : TAPS, lanes] * dconv
        for tap in range(TAPS):
            dtaps[tap : tap + 1, lanes] += jnp.sum(
                dconv * xbuf[5 + tap : 5 + tap + CHUNK, lanes], axis=0, keepdims=True
            )
            if tap < TAPS - 1:
                reach = TAPS - 1 - tap
                back = back + taps[tap : tap + 1, lanes] * dcbuf[reach : reach + CHUNK, lanes]
        dpx[:, lanes] = back.astype(BF16)
    ours = lax.broadcasted_iota(jnp.int32, (1, LANES), 1) < cw // P_SIZE
    ddt = own_heads_first(jnp.where(ours, ddt, 0.0), cw // P_SIZE, back=True)
    dpx[:, cc:] = ddt.astype(BF16)
    dcbuf[CHUNK : CHUNK + 8, :] = dcbuf[0:8, :]


WIDE = 512
LEFT = 1280
SPLIT = 256


MESH = pl.DeviceIdType.MESH


def remote(src, dst, sends, recvs, index, device):
    return pltpu.make_async_remote_copy(
        src_ref=src,
        dst_ref=dst,
        send_sem=sends.at[index],
        recv_sem=recvs.at[index],
        device_id=device,
        device_id_type=MESH,
    )


def greet(devices):
    barrier = pltpu.get_barrier_semaphore()
    for device in devices:
        pl.semaphore_signal(barrier, inc=1, device_id=device, device_id_type=MESH)
    pl.semaphore_wait(barrier, len(devices))


def seq_peers(parts):
    group, q = lax.axis_index("dp"), lax.axis_index("seq")
    return [(group, lax.rem(q + k, parts)) for k in range(1, parts)]


def dp_peers(groups):
    group, q = lax.axis_index("dp"), lax.axis_index("seq")
    return [(lax.rem(group + k, groups), q) for k in range(1, groups)]


def all_peers(groups, parts):
    devices = groups * parts
    me = lax.axis_index("dp") * parts + lax.axis_index("seq")
    peers = []
    for k in range(1, devices):
        other = lax.rem(me + k, devices)
        peers.append((other // parts, lax.rem(other, parts)))
    return peers


CHAN_ROWS = ((TAPS + 1) * CONV_CH + D + INNER) // LANES


def adam_tile(weight, gradient, moment, second, step_rate, weight_decay):
    new_moment = BETA * moment + (1.0 - BETA) * gradient
    new_second = BETA * second + (1.0 - BETA) * gradient * gradient
    correction = 1.0 - BETA**STEP
    update = new_moment / correction / (jnp.sqrt(new_second / correction) + ADAM_EPS)
    return weight - step_rate * (update + weight_decay * weight), new_moment, new_second


def total_of(value):
    return jnp.sum(jnp.sum(value, axis=1, keepdims=True), axis=0, keepdims=True)


def norm_kernel(
    groups, parts,
    part_h, rest_h, gate_h, left_h, right_h, back_h, small_h, hidden_h, gain, cotangent,
    hidden_grad, chan, head, norm,
    part, rest, gate, left, right, back, small, hidden,
    cot_v, block, near, all_block, all_near, sends, recvs, near_s, near_r, load, local,
):
    group, q = lax.axis_index("dp"), lax.axis_index("seq")
    me = group * parts + q
    cw = INNER // parts
    cc = cw + 2 * N
    everyone = all_peers(groups, parts)
    fetches = [
        pltpu.make_async_copy(source, target, load.at[k])
        for k, (source, target) in enumerate(
            [(back_h, back), (hidden_h, hidden), (part_h, part), (gate_h, gate),
             (left_h, left), (right_h, right), (small_h, small), (rest_h, rest),
             (cotangent, cot_v)]
        )
    ]
    for copy in fetches:
        copy.start()
    barrier = pltpu.get_barrier_semaphore()
    for device in everyone:
        pl.semaphore_signal(barrier, inc=1, device_id=device, device_id_type=MESH)
    for copy in fetches[:8]:
        copy.wait()
    total = small[0]
    for k in range(1, groups):
        total = total + small[k]
    near[...] = total
    rows = 32

    def summed(at):
        down = back[at, :]
        tokens = hidden[at, :].astype(F32)
        mean = jnp.sum(tokens * tokens, axis=-1, keepdims=True) / D
        return down, tokens, lax.rsqrt(mean + EPS_IN)

    def gain_rows(i, dgain):
        at = pl.ds(pl.multiple_of(i * rows, rows), rows)
        down, tokens, scale = summed(at)
        return dgain + jnp.sum(down * tokens * scale, axis=0, keepdims=True)

    dgain = lax.fori_loop(0, hidden.shape[0] // rows, gain_rows, jnp.zeros((1, D), F32))
    tail = rest[:, : 2 * N + H]
    squares = total_of(tail * tail)
    for k in range(parts):
        x = part[k].astype(F32)
        g = gate[k].astype(F32)
        squares = squares + total_of(x * x + g * g)
    squares = squares + total_of(left[...] * left[...]) + total_of(right[...] * right[...])
    for k in range(D // LANES):
        block[k : k + 1, :] = dgain[:, k * LANES : (k + 1) * LANES]
    block[D // LANES :, :] = jnp.broadcast_to(squares, (8, LANES))
    pl.semaphore_wait(barrier, len(everyone))
    copies = [
        remote(block, all_block.at[me], sends, recvs, k, peer) for k, peer in enumerate(everyone)
    ]
    copies += [
        remote(near, all_near.at[q], near_s, near_r, k, peer)
        for k, peer in enumerate(seq_peers(parts))
    ]
    copies += [
        pltpu.make_async_copy(block, all_block.at[me], local.at[0]),
        pltpu.make_async_copy(near, all_near.at[q], local.at[1]),
    ]
    for copy in copies:
        copy.start()
    fetches[8].wait()

    def grad_rows(i, carry):
        at = pl.ds(pl.multiple_of(i * rows, rows), rows)
        down, tokens, scale = summed(at)
        scaled = down * gain[...]
        inner = jnp.sum(scaled * tokens, axis=-1, keepdims=True) / D
        direct = cot_v[0, at, :].astype(F32)
        for k in range(1, LEVELS):
            direct = direct + cot_v[k, at, :].astype(F32)
        hidden_grad[at, :] = (
            scale * scaled - tokens * (scale * scale * scale * inner) + direct
        )
        return carry

    lax.fori_loop(0, hidden.shape[0] // rows, grad_rows, 0)
    for copy in copies:
        copy.wait()
    total = jnp.sum(all_block[...], axis=0)
    own, wide = cw // LANES, cc // LANES
    span = CONV_CH // LANES
    for tap in range(TAPS + 1):
        for k in range(parts):
            at = tap * span + k * own
            chan[at : at + own, :] = all_near[k, tap * wide : tap * wide + own, :]
        shared = all_near[0, tap * wide + own : (tap + 1) * wide, :]
        for k in range(1, parts):
            shared = shared + all_near[k, tap * wide + own : (tap + 1) * wide, :]
        chan[tap * span + INNER // LANES : (tap + 1) * span, :] = shared
    at = (TAPS + 1) * span
    chan[at : at + D // LANES, :] = total[: D // LANES]
    at = at + D // LANES
    for k in range(parts):
        first = (TAPS + 1) * wide
        chan[at + k * own : at + (k + 1) * own, :] = all_near[k, first : first + own, :]
        head[k : k + 1, :] = all_near[k, first + own : first + own + 1, :]
    squares = (
        total[D // LANES : D // LANES + 1, :1]
        + total_of(chan[:CHAN_ROWS, :] * chan[:CHAN_ROWS, :])
        + total_of(head[:parts, :] * head[:parts, :])
    )
    grad_norm = jnp.sqrt(squares)
    norm[0:1, :] = jnp.broadcast_to(grad_norm, (1, LANES))
    norm[1:2, :] = jnp.broadcast_to(jnp.minimum(1.0, CLIP / grad_norm), (1, LANES))


def gradient_norm(
    collective_id, part, rest, gate, left, right, back, small, hidden, gain, cotangent, groups
):
    parts = part.shape[0]
    devices = groups * parts
    sem = pltpu.SemaphoreType.DMA
    vmem = pl.BlockSpec(memory_space=pltpu.VMEM)
    hbm = pl.BlockSpec(memory_space=pltpu.HBM)
    block = (D // LANES + 8, LANES)
    chan_rows = -(-CHAN_ROWS // 8) * 8
    return pl.pallas_call(
        functools.partial(norm_kernel, groups, parts),
        in_specs=[*([hbm] * 8), vmem, hbm],
        out_specs=[vmem] * 4,
        out_shape=[
            jax.ShapeDtypeStruct(hidden.shape, F32),
            jax.ShapeDtypeStruct((chan_rows, LANES), F32),
            jax.ShapeDtypeStruct((8, LANES), F32),
            jax.ShapeDtypeStruct((8, LANES), F32),
        ],
        scratch_shapes=[
            *[
                pltpu.VMEM(a.shape, a.dtype)
                for a in (part, rest, gate, left, right, back, small, hidden)
            ],
            pltpu.VMEM(cotangent.shape, BF16),
            pltpu.VMEM(block, F32),
            pltpu.VMEM(small.shape[1:], F32),
            pltpu.VMEM((devices,) + block, F32),
            pltpu.VMEM((parts,) + small.shape[1:], F32),
            sem((devices - 1,)), sem((devices - 1,)), sem((parts - 1,)), sem((parts - 1,)),
            sem((9,)), sem((2,)),
        ],
        compiler_params=pltpu.CompilerParams(
            collective_id=collective_id, has_side_effects=True, vmem_limit_bytes=63 * 2**20
        ),
        name="gradient_norm",
    )(part, rest, gate, left, right, back, small, hidden, gain, cotangent)


BLOCKS = 4


def update_kernel(
    parts, norm, part_h, rest_h, gate_h, left_h, right_h, hidden_grad, block, *refs
):
    ins, refs = refs[:6], refs[6:]
    hidden_out, block_out, outs, refs = refs[0], refs[1], refs[2:10], refs[10:]
    held, made = refs[:6], refs[6:14]
    part, rest, gate, left, right, hidden_v, block_v, load, store, grads = refs[14:]
    clip = norm[1:2, :1]
    cw = INNER // parts
    fetches = [
        pltpu.make_async_copy(source, target, grads.at[k])
        for k, (source, target) in enumerate(
            [(part_h, part), (gate_h, gate), (left_h, left), (right_h, right), (rest_h, rest),
             (hidden_grad, hidden_v), (block, block_v)]
        )
    ]
    for copy in fetches[:5]:
        copy.start()

    def at(a, i):
        rows = ins[a].shape[0] // BLOCKS
        return pl.ds(i * rows, rows)

    loads = [
        [
            pltpu.make_async_copy(ins[a].at[at(a, i)], held[a].at[at(a, i)], load.at[a * BLOCKS + i])
            for a in range(6)
        ]
        for i in range(BLOCKS)
    ]
    for weight in (0, 3):
        for i in range(BLOCKS):
            for a in range(weight, weight + 3):
                loads[i][a].start()
    for copy in fetches[5:]:
        copy.start()
    stores = []

    def update(weight, rows, lanes, gradient, rate, decay):
        first = 0 if weight == 0 else 4
        new, moment, second = adam_tile(
            held[weight][rows, lanes], clip * gradient, held[weight + 1][rows, lanes],
            held[weight + 2][rows, lanes], rate, decay,
        )
        made[first][rows, lanes] = new
        made[first + 1][rows, lanes] = moment
        made[first + 2][rows, lanes] = second
        made[first + 3][rows, lanes] = new.astype(BF16)

    def send(first, rows, i):
        for a in range(first, first + 4):
            copy = pltpu.make_async_copy(
                made[a].at[rows], outs[a].at[rows], store.at[a * BLOCKS + i]
            )
            copy.start()
            stores.append(copy)

    for copy in fetches[:5]:
        copy.wait()
    for i in range(BLOCKS):
        rows = at(0, i)
        for a in range(3):
            loads[i][a].wait()
        for source, first in ((gate, 0), (part, INNER)):

            def step(k, carry, source=source, first=first, rows=rows):
                to = pl.ds(pl.multiple_of(first + k * cw, cw), cw)
                update(0, rows, to, source[k, rows, :cw].astype(F32), 0.02, 0.1)
                return carry

            lax.fori_loop(0, parts, step, 0)
        update(0, rows, slice(2 * INNER, E_IN), rest[rows, : 2 * N + H], 0.02, 0.1)
        send(0, rows, i)
    fetches[5].wait()
    fetches[6].wait()
    for source, target, k in ((hidden_v, hidden_out, 7), (block_v, block_out, 8)):
        copy = pltpu.make_async_copy(source, target, grads.at[k])
        copy.start()
        stores.append(copy)
    for i in range(BLOCKS):
        rows = at(3, i)
        for a in range(3, 6):
            loads[i][a].wait()
        update(3, rows, slice(0, LEFT), left[rows, :], 0.03, 0.1)
        update(3, rows, slice(LEFT, D), right[rows, :], 0.03, 0.1)
        send(4, rows, i)
    for copy in stores:
        copy.wait()


def update_weights(norm, part, rest, gate, left, right, hidden_grad, block, weights):
    parts = part.shape[0]
    w_in, w_out = weights[0], weights[3]
    sem = pltpu.SemaphoreType.DMA
    vmem = pl.BlockSpec(memory_space=pltpu.VMEM)
    hbm = pl.BlockSpec(memory_space=pltpu.HBM)
    made = [
        jax.ShapeDtypeStruct(w.shape, dtype) for w in (w_in, w_out) for dtype in (F32, F32, F32, BF16)
    ]
    return pl.pallas_call(
        functools.partial(update_kernel, parts),
        in_specs=[vmem, *([hbm] * 13)],
        out_specs=[hbm] * 10,
        out_shape=[
            jax.ShapeDtypeStruct(hidden_grad.shape, F32),
            jax.ShapeDtypeStruct(block.shape, BF16),
            *made,
        ],
        scratch_shapes=[
            *[pltpu.VMEM(w.shape, F32) for w in weights],
            *[pltpu.VMEM(m.shape, m.dtype) for m in made],
            *[
                pltpu.VMEM(a.shape, a.dtype)
                for a in (part, rest, gate, left, right, hidden_grad, block)
            ],
            sem((6 * BLOCKS,)), sem((8 * BLOCKS,)), sem((9,)),
        ],
        compiler_params=pltpu.CompilerParams(vmem_limit_bytes=63 * 2**20),
        name="update_weights",
    )(norm, part, rest, gate, left, right, hidden_grad, block, *weights)


WO_ALL, WO_REST = pl.ds(0, SPLIT), pl.ds(SPLIT, D - SPLIT)


class LineGather:
    def __init__(self, line, z, core, q, slot, own, sends, recvs):
        self.line, self.z, self.core, self.q = line, z, core, q
        self.slot, self.own, self.sends, self.recvs = slot, own, sends, recvs

    def along(self, from_z, up, first=False):
        to = self.z + 1 if up else self.z - 1
        return remote(
            self.own if first else self.slot(from_z),
            self.slot(from_z),
            self.sends.at[0 if up else 1],
            self.recvs.at[0 if up else 1],
            from_z,
            (2 * to + self.core, self.q),
        )

    def push(self, t):
        z, line = self.z, self.line

        @pl.when((z - t >= 0) & (z < line - 1))
        def _():
            self.along(z - t, True, t == 0).start()

        @pl.when((z + t <= line - 1) & (z > 0))
        def _():
            self.along(z + t, False, t == 0).start()

    def pushed(self, t):
        z, line = self.z, self.line

        @pl.when((z - t >= 0) & (z < line - 1))
        def _():
            self.along(z - t, True, t == 0).wait_send()

        @pl.when((z + t <= line - 1) & (z > 0))
        def _():
            self.along(z + t, False, t == 0).wait_send()

    def step(self, t, got=None, push=True):
        z, line = self.z, self.line

        @pl.when(z - t >= 0)
        def _():
            self.along(z - t, True).wait_recv()

            if push:

                @pl.when(z < line - 1)
                def _():
                    self.along(z - t, True).start()

            if got is not None:
                got(z - t)

        @pl.when(z + t <= line - 1)
        def _():
            self.along(z + t, False).wait_recv()

            if push:

                @pl.when(z > 0)
                def _():
                    self.along(z + t, False).start()

            if got is not None:
                got(z + t)


class LineGathers:
    def __init__(self, line, z, core, q, slot, own, sends, recvs):
        half = own.shape[0] // 2
        self.line = line
        self.halves = []
        for h in range(2):
            rows = pl.ds(h * half, half)
            self.halves.append(
                LineGather(
                    line, z, core, q, lambda from_z, rows=rows: slot(from_z).at[rows],
                    own.at[rows], sends.at[h], recvs.at[h],
                )
            )

    def push(self, t):
        for part in self.halves:
            part.push(t)

    def step(self, t, got=None, push=True):
        self.halves[0].step(t, None, push)
        self.halves[1].step(t, got, push)

    def pushed(self):
        for t in range(self.line - 1):
            for part in self.halves:
                part.pushed(t)


class PlaneGather:
    def __init__(self, parts, slot, own, sends, recvs, base=0):
        self.parts, self.slot, self.own = parts, slot, own
        self.sends, self.recvs, self.base = sends, recvs, base
        self.group, self.q = lax.axis_index("dp"), lax.axis_index("seq")
        if parts == 4:
            self.near = [self.q + 1 - 2 * lax.rem(self.q, 2), lax.rem(self.q + 2, 4)]
            self.half = own.shape[0] // 2

    def early(self):
        to = self.near if self.parts == 4 else [peer[1] for peer in seq_peers(self.parts)]
        return [
            remote(
                self.own, self.slot(self.q), self.sends, self.recvs, self.base + k, (self.group, d)
            )
            for k, d in enumerate(to)
        ]

    def late(self):
        if self.parts != 4:
            return []
        copies = []
        for h in range(2):
            block = self.slot(self.near[h]).at[pl.ds(h * self.half, self.half)]
            to = (self.group, self.near[1 - h])
            copies.append(remote(block, block, self.sends, self.recvs, self.base + 2 + h, to))
        return copies

    def start(self):
        for copy in self.early():
            copy.start()

    def turn(self):
        if self.parts == 4:
            for copy in self.early():
                copy.wait()
            for copy in self.late():
                copy.start()

    def finish(self):
        for copy in self.late() if self.parts == 4 else self.early():
            copy.wait()


def chan_rows_of(chan_len, devices):
    return -(-((devices - 1) * chan_len // LANES + 8) // 8) * 8


def unpack_chan(
    chan_len, parts, q, all_chan, full, hp, gain_in, gain_out, taps, heads, skip, spread, gather
):
    cw = INNER // parts
    hq = H // parts
    own, span, shared = cw // LANES, CONV_CH // LANES, 2 * N // LANES
    full[...] = jnp.zeros_like(full)
    for o in range(all_chan.shape[0]):
        at = o * chan_len // LANES
        full[at : at + 8, :] += all_chan[o]
    taps[...] = jnp.zeros_like(taps)
    for tap in range(TAPS + 1):
        for b in range(own):
            taps[tap : tap + 1, b * LANES : (b + 1) * LANES] = full[
                pl.ds(tap * span + q * own + b, 1), :
            ]
        for b in range(shared):
            at = tap * span + INNER // LANES + b
            taps[tap : tap + 1, cw + b * LANES : cw + (b + 1) * LANES] = full[at : at + 1, :]
    at = (TAPS + 1) * span
    for b in range(D // LANES):
        gain_in[:, b * LANES : (b + 1) * LANES] = full[at + b : at + b + 1, :]
    at = at + D // LANES
    for b in range(own):
        gain_out[:, b * LANES : (b + 1) * LANES] = full[pl.ds(at + q * own + b, 1), :]
    for out, axis in ((spread, 0), (gather, 1)):
        head = lax.broadcasted_iota(jnp.int32, out.shape, axis)
        channel = lax.broadcasted_iota(jnp.int32, out.shape, 1 - axis)
        inside = (channel >= head * P_SIZE) & (channel < (head + 1) * P_SIZE)
        out[...] = jnp.where(inside, 1.0, 0.0).astype(BF16)
    ours = own_heads_first(hp[...], hq)
    row = lax.broadcasted_iota(jnp.int32, ours.shape, 0)
    heads[...] = jnp.where(row == 0, ours, jnp.where(row == 1, -jnp.exp(ours), 0.0))
    skip[...] = spread_heads(ours, spread[...])[2:3, :]


def collect_kernel(
    groups, parts, chan_len, hidden, w_in_h, w_own_h, chan, hp,
    hid_out, w_out, gate_out, wo_out, gain_in, gain_out, taps, heads, skip, spread, gather,
    chan_out, full, w_in, w_own, blocks, gates, low, chan_s, chan_r, hid_s, hid_r, swap_s, swap_r, gate_s, gate_r,
    wo_s, wo_r, line_s, line_r, lwo_s, lwo_r, core_s, core_r, local,
):
    line = groups // 2
    cw = INNER // parts
    cc = cw + 2 * N
    group, q = lax.axis_index("dp"), lax.axis_index("seq")
    z, core = group // 2, lax.rem(group, 2)
    sibling = (2 * z + 1 - core, q)
    peers = seq_peers(parts)
    everyone = all_peers(groups, parts)
    loads = [
        pltpu.make_async_copy(w_in_h, w_in, local.at[5]),
        pltpu.make_async_copy(w_own_h, w_own, local.at[6]),
    ]
    for copy in loads:
        copy.start()
    barrier = pltpu.get_barrier_semaphore()
    for device in everyone:
        pl.semaphore_signal(barrier, inc=1, device_id=device, device_id_type=MESH)
    for copy in loads:
        copy.wait()
    shared = w_in[:, 2 * INNER :].astype(BF16)
    for part in range(parts):
        at = INNER + part * cw
        blocks[part, :, :cw] = w_in[:, at : at + cw].astype(BF16)
        blocks[part, :, cw : cc + H] = shared
        blocks[part, :, cc + H :] = jnp.zeros((w_in.shape[0], LANES - H), BF16)
    low[...] = w_own[...].astype(BF16)
    pl.semaphore_wait(barrier, len(everyone))
    swaps = []
    for k, peer in enumerate(peers):
        copy = remote(blocks.at[peer[1]], w_out.at[group, q], swap_s, swap_r, k, peer)
        copy.start()
        swaps.append(copy)
    outs = LineGather(
        line, z, core, q, lambda from_z: wo_out.at[2 * from_z + core, q, :, WO_REST],
        low.at[:, WO_REST], lwo_s, lwo_r,
    )
    outs.push(0)
    own = [
        pltpu.make_async_copy(blocks.at[q], w_out.at[group, q], local.at[0]),
        pltpu.make_async_copy(hidden, hid_out.at[q], local.at[1]),
        pltpu.make_async_copy(chan, chan_out.at[group * parts + q], local.at[2]),
        pltpu.make_async_copy(low, wo_out.at[group, q], local.at[3]),
    ]
    for copy in own:
        copy.start()
    waiting = []
    chans = [
        remote(chan, chan_out.at[group * parts + q], chan_s, chan_r, k, peer)
        for k, peer in enumerate(everyone)
    ]
    for copy in chans:
        copy.start()
    for part in range(parts):
        gates[part] = w_in[:, part * cw : (part + 1) * cw].astype(BF16)
    copy = pltpu.make_async_copy(gates.at[q], gate_out.at[q], local.at[4])
    copy.start()
    own.append(copy)
    own[0].wait()
    for copy in swaps:
        copy.wait()
    hids = PlaneGather(parts, lambda of: hid_out.at[of], hidden, hid_s, hid_r)
    lows = PlaneGather(parts, lambda of: wo_out.at[group, of], low, wo_s, wo_r)
    hids.start()

    def across(from_z):
        block = w_out.at[2 * from_z + core]
        return remote(block, block, core_s, core_r, from_z, sibling)

    ins = LineGathers(
        line, z, core, q, lambda from_z: w_out.at[2 * from_z + core], w_out.at[group],
        line_s, line_r,
    )
    across(z).start()
    ins.push(0)
    lows.start()
    for t in range(1, line):
        ins.step(t, lambda from_z: across(from_z).start(), t < line - 1)
        if t == 1:
            own[2].wait()
            for copy in chans:
                copy.wait()
            unpack_chan(
                chan_len, parts, q, chan_out, full, hp, gain_in, gain_out, taps, heads, skip,
                spread, gather,
            )
        if t == line - 2:
            outs.step(1)
            hids.turn()
            lows.turn()
            for k, peer in enumerate(peers):
                copy = remote(gates.at[peer[1]], gate_out.at[q], gate_s, gate_r, k, peer)
                copy.start()
                waiting.append(copy)
    ins.pushed()
    outs.step(2, None, False)
    outs.pushed(0)
    outs.pushed(1)
    hids.finish()
    lows.finish()
    for from_z in range(line):
        across(from_z).wait_send()
        block = w_out.at[2 * from_z + 1 - core]
        remote(block, block, core_s, core_r, from_z, sibling).wait_recv()
    for copy in own[1:2] + own[3:] + waiting:
        copy.wait()


def collect(collective_id, hidden, w_in, w_own, chan, hp, chan_len, groups, parts):
    rows = w_in.shape[0]
    line = groups // 2
    cw = INNER // parts
    width = cw + 2 * N + LANES
    sem = pltpu.SemaphoreType.DMA
    hbm = pl.BlockSpec(memory_space=pltpu.HBM)
    vmem = pl.BlockSpec(memory_space=pltpu.VMEM)
    return pl.pallas_call(
        functools.partial(collect_kernel, groups, parts, chan_len),
        in_specs=[hbm, hbm, hbm, vmem, vmem],
        out_specs=[*([hbm] * 4), *([vmem] * 7)],
        out_shape=[
            jax.ShapeDtypeStruct((parts,) + hidden.shape, hidden.dtype),
            jax.ShapeDtypeStruct((groups, parts, rows, width), BF16),
            jax.ShapeDtypeStruct((parts, rows, cw), BF16),
            jax.ShapeDtypeStruct((groups, parts) + w_own.shape, BF16),
            jax.ShapeDtypeStruct((1, D), F32),
            jax.ShapeDtypeStruct((1, cw), F32),
            jax.ShapeDtypeStruct((8, cw + 2 * N), F32),
            jax.ShapeDtypeStruct((8, LANES), F32),
            jax.ShapeDtypeStruct((1, cw), F32),
            jax.ShapeDtypeStruct((LANES, cw), BF16),
            jax.ShapeDtypeStruct((cw, LANES), BF16),
        ],
        scratch_shapes=[
            pltpu.VMEM((groups * parts,) + chan.shape, F32),
            pltpu.VMEM((chan_rows_of(chan_len, groups * parts), LANES), F32),
            pltpu.VMEM(w_in.shape, F32),
            pltpu.VMEM(w_own.shape, F32),
            pltpu.VMEM((parts, rows, width), BF16),
            pltpu.VMEM((parts, rows, cw), BF16),
            pltpu.VMEM(w_own.shape, BF16),
            *([sem((groups * parts - 1,))] * 2),
            *([sem((parts + 1,))] * 8),
            *([sem((2, 2, line))] * 2), *([sem((2, line))] * 2),
            sem((line,)), sem((line,)), sem((7,)),
        ],
        compiler_params=pltpu.CompilerParams(
            collective_id=collective_id, has_side_effects=True, vmem_limit_bytes=63 * 2**20
        ),
        name="collect",
    )(hidden, w_in, w_own, chan, hp)


def forward_kernel(
    groups, parts, cw,
    hidden_h, wx_h, gate_h, wo_in, gain_in, gain_out, taps, heads, skip, spread,
    normed_h, px_h, y_h, states_h, z_h, u_h, stat_h, wz_h, wo,
    hidden, wx, wz, normed, px, y, states, zs, us, stats, xbuf, state, xdt, carried,
    line_s, line_r, lwo_s, lwo_r, wide_s, wide_r, stat_s, stat_r, core_s, core_r, wo_s, wo_r, out_s, out_r, u_s, u_r, load, store,
):
    line = groups // 2
    cc = cw + 2 * N
    length = px.shape[0]
    chunks = length // CHUNK
    group, q = lax.axis_index("dp"), lax.axis_index("seq")
    z, core = group // 2, lax.rem(group, 2)
    sibling = (2 * z + 1 - core, q)
    peers = mirror_peers(parts)
    loads = [
        pltpu.make_async_copy(source, target, load.at[k])
        for k, (source, target) in enumerate(
            [(hidden_h, hidden), (wx_h, wx), (gate_h, wz.at[group])]
        )
    ]
    for copy in loads:
        copy.start()
    greet(peers + dp_peers(groups))

    outs = LineGather(
        line, z, core, q, lambda from_z: wo.at[2 * from_z + core, q, :, WO_REST],
        wo.at[group, q, :, WO_REST], lwo_s, lwo_r,
    )
    wides = LineGather(
        line, z, core, q, lambda from_z: wo.at[2 * from_z + core, :, :, WO_ALL],
        wo.at[group, :, :, WO_ALL], wide_s, wide_r,
    )

    def planes(t, act):
        for from_z, there in ((z - t, z - t >= 0), (z + t, z + t <= line - 1)):

            @pl.when(there)
            def _(from_z=from_z):
                block = wo.at[2 * from_z + core]
                act(
                    PlaneGather(
                        parts, lambda of: block.at[of, :, WO_REST], block.at[q, :, WO_REST],
                        out_s, out_r,
                        from_z * (parts + 1),
                    )
                )

    outs.push(2)
    planes(1, PlaneGather.start)
    planes(2, PlaneGather.start)

    def parity(from_z, of, columns):
        block = wo.at[2 * from_z + of, :, :, columns]
        at = from_z if columns is WO_REST else line + from_z
        return remote(block, block, wo_s, wo_r, at, sibling)

    def across_planes(t):
        planes(t, PlaneGather.finish)
        for from_z, there in ((z - t, z - t >= 0), (z + t, z + t <= line - 1)):

            @pl.when(there)
            def _(from_z=from_z):
                parity(from_z, core, WO_REST).start()

    def across_wide(from_z):
        parity(from_z, core, WO_ALL).start()

    across_wide(z)
    parity(z, core, WO_REST).start()

    def across(from_z):
        block = wz.at[2 * from_z + core]
        return remote(block, block, core_s, core_r, from_z, sibling)

    gates = LineGathers(
        line, z, core, q, lambda from_z: wz.at[2 * from_z + core], wz.at[group], line_s, line_r
    )
    loads[2].wait()
    across(z).start()
    gates.push(0)
    loads[0].wait()

    def norm_rows(i, carry):
        rows = pl.ds(pl.multiple_of(i * 32, 32), 32)
        tokens = hidden[rows, :].astype(F32)
        mean = jnp.sum(tokens * tokens, axis=-1, keepdims=True) / D
        normed[rows, :] = (tokens * lax.rsqrt(mean + EPS_IN) * gain_in[...]).astype(BF16)
        return carry

    lax.fori_loop(0, length // 32, norm_rows, 0)
    loads[1].wait()
    tall = 256

    def project_rows(i, carry):
        rows = pl.ds(pl.multiple_of(i * tall, tall), tall)
        px[rows, :] = dot(normed[rows, :], wx[...])
        return carry

    lax.fori_loop(0, length // tall, project_rows, 0)
    stores = [
        pltpu.make_async_copy(normed, normed_h, store.at[0]),
        pltpu.make_async_copy(px, px_h, store.at[1]),
    ]
    for copy in stores:
        copy.start()
    state[...] = jnp.zeros_like(state)
    xbuf[0:8, :] = jnp.zeros((8, cc), F32)

    def scan_rows(i, carry):
        for t in range(1, line - 1):

            @pl.when(i == min(5 * t - 4, chunks - 1))
            def _(t=t):
                gates.step(t, lambda from_z: across(from_z).start(), t < line - 1)
                if t == line - 2:
                    wides.push(0)

        for t in range(3, line):

            @pl.when(i == min(2 * t - 3, chunks - 1))
            def _(t=t):
                outs.step(t, None, t < line - 1)
                planes(t, PlaneGather.start)

        @pl.when(i == min(5, chunks - 1))
        def _():
            planes(1, PlaneGather.turn)
            planes(2, PlaneGather.turn)

        rows = pl.ds(pl.multiple_of(i * CHUNK, CHUNK), CHUNK)
        scan_forward_step(
            cw, px.at[rows], taps, heads, skip, spread, y.at[rows], states.at[i],
            xbuf, state, xdt, carried,
        )
        return carry

    lax.fori_loop(0, chunks, scan_rows, 0)
    for source, target, at in ((y, y_h, 2), (states, states_h, 3)):
        copy = pltpu.make_async_copy(source, target, store.at[at])
        copy.start()
        stores.append(copy)
    for t in range(3, line):
        planes(t, PlaneGather.turn)
    gates.step(line - 1, lambda from_z: across(from_z).start(), False)
    for from_z in range(line):
        across(from_z).wait_send()
        block = wz.at[2 * from_z + 1 - core]
        remote(block, block, core_s, core_r, from_z, sibling).wait_recv()
    gates.pushed()
    for t in range(2, line - 1):
        outs.pushed(t)
    copy = pltpu.make_async_copy(wz, wz_h, store.at[4])
    copy.start()
    stores.append(copy)
    lane = lax.broadcasted_iota(jnp.int32, (1, LANES), 1)
    wide = 512

    def gate_rows(rows):
        gate_in = dot(normed[rows, :], wz[...].reshape(D, cw))
        zs[rows, :] = gate_in
        gated = y[rows, :] * (gate_in * jax.nn.sigmoid(gate_in))
        us[rows, :] = (gated * gain_out[...]).astype(BF16)
        squares = jnp.zeros((tall, LANES), F32)
        for b in range(cw // wide):
            block = gated[:, b * wide : (b + 1) * wide]
            total = jnp.sum(block * block, axis=-1, keepdims=True)
            level = level_of(q * cw + b * wide, wide)
            squares = squares + jnp.where(lane == level, total, 0.0)
        stats[:, rows] = squares.T[:8, :]

    waiting = []
    tokens = length // parts
    for k, dest in enumerate([peer[1] for peer in peers] + [q]):

        def block_rows(i, carry, dest=dest):
            gate_rows(pl.ds(pl.multiple_of(dest * tokens + i * tall, tall), tall))
            return carry

        lax.fori_loop(0, tokens // tall, block_rows, 0)
        ours = us.at[pl.ds(pl.multiple_of(dest * tokens, tokens), tokens)]
        stat = stats.at[:, pl.ds(pl.multiple_of(dest * tokens, tokens), tokens)]
        if k < len(peers):
            some = [
                remote(ours, u_h.at[q], u_s, u_r, k, peers[k]),
                remote(stat, stat_h.at[q], stat_s, stat_r, k, peers[k]),
            ]
        else:
            some = [
                pltpu.make_async_copy(ours, u_h.at[q], store.at[6]),
                pltpu.make_async_copy(stat, stat_h.at[q], store.at[7]),
            ]
        for copy in some:
            copy.start()
        waiting += some
        if k == 0:
            wides.step(1, across_wide)
        if k == 1:
            for t in range(2, line - 1):
                wides.step(t, across_wide)
        if k in (1, 2):
            across_planes(k)
    copy = pltpu.make_async_copy(zs, z_h, store.at[5])
    copy.start()
    stores.append(copy)

    for t in range(3, line):
        across_planes(t)
    wides.step(line - 1, across_wide, False)
    for t in range(line - 1):
        wides.pushed(t)
    for copy in waiting + stores:
        copy.wait()
    for columns in (WO_REST, WO_ALL):
        for d in range(line):
            parity(d, core, columns).wait_send()
            parity(d, 1 - core, columns).wait_recv()


def forward(collective_id, hidden, wx, gate, wo, gain_in, gain_out, taps, heads, skip, spread):
    groups, parts = wo.shape[:2]
    line = groups // 2
    length = hidden.shape[0]
    rows, cw = gate.shape[1:]
    cc = cw + 2 * N
    width = cc + LANES
    chunks = length // CHUNK
    sem = pltpu.SemaphoreType.DMA
    hbm = pl.BlockSpec(memory_space=pltpu.HBM)
    vmem = pl.BlockSpec(memory_space=pltpu.VMEM)
    u = jax.ShapeDtypeStruct((parts, length // parts, cw), BF16)
    stat = jax.ShapeDtypeStruct((parts, 8, length // parts), F32)
    made = [
        jax.ShapeDtypeStruct((length, D), BF16),
        jax.ShapeDtypeStruct((length, width), F32),
        jax.ShapeDtypeStruct((length, cw), F32),
        jax.ShapeDtypeStruct((chunks, N, cw), BF16),
        jax.ShapeDtypeStruct((length, cw), F32),
        jax.ShapeDtypeStruct((length, cw), BF16),
        jax.ShapeDtypeStruct((8, length), F32),
    ]
    wz = jax.ShapeDtypeStruct((groups, parts, rows, cw), BF16)
    return pl.pallas_call(
        functools.partial(forward_kernel, groups, parts, cw),
        in_specs=[*([hbm] * 4), *([vmem] * 6)],
        out_specs=[hbm] * 9,
        out_shape=[*made[:-2], u, stat, wz, jax.ShapeDtypeStruct(wo.shape, BF16)],
        input_output_aliases={3: 8},
        scratch_shapes=[
            pltpu.VMEM(hidden.shape, BF16),
            pltpu.VMEM(wx.shape, BF16),
            pltpu.VMEM(wz.shape, BF16),
            *[pltpu.VMEM(m.shape, m.dtype) for m in made],
            pltpu.VMEM((CHUNK + 8, cc), F32),
            pltpu.VMEM((N, cw), F32),
            pltpu.VMEM((CHUNK, cw), BF16),
            pltpu.VMEM((CHUNK, cw), F32),
            *([sem((2, 2, line))] * 2), *([sem((2, line))] * 4),
            sem((parts - 1,)), sem((parts - 1,)),
            sem((line,)), sem((line,)), sem((2 * line,)), sem((2 * line,)),
            sem((line * (parts + 1),)), sem((line * (parts + 1),)),
            sem((parts - 1,)), sem((parts - 1,)),
            sem((3,)), sem((8,)),
        ],
        compiler_params=pltpu.CompilerParams(
            collective_id=collective_id, has_side_effects=True, vmem_limit_bytes=63 * 2**20
        ),
        name="forward",
    )(hidden, wx, gate, wo, gain_in, gain_out, taps, heads, skip, spread)


def add_blocks(out, a, b, rows, steps):
    def step(i, carry):
        at = pl.ds(pl.multiple_of(i * rows, rows), rows)
        out[at] = (a[at].astype(F32) + b[at].astype(F32)).astype(out.dtype)
        return carry

    lax.fori_loop(0, steps, step, 0)


def level_of(channel, width):
    return sum((channel >= level_width(k)).astype(jnp.int32) for k in range(LEVELS - 1))


def mirror_peers(parts):
    group, q = lax.axis_index("dp"), lax.axis_index("seq")
    if parts != 4:
        return seq_peers(parts)
    return [(group, 3 - q), (group, q + 1 - 2 * lax.rem(q, 2)), (group, lax.rem(q + 2, 4))]


def middle_kernel(
    groups, parts, cw,
    u_h, stat_h, wo, cot_h, tokens_h,
    back_h, coef_h, block_h, left_h, right_h,
    u, stats, cot, tokens, mixed, branch, norms, pulls, back, coefs, weights, sent, held, left, right,
    back_s, back_r, coef_s, coef_r, core_s, core_r, fetch, load, store, local,
):
    line = groups // 2
    group, q = lax.axis_index("dp"), lax.axis_index("seq")
    z, core = group // 2, lax.rem(group, 2)
    sibling = (2 * z + 1 - core, q)
    peers = mirror_peers(parts)
    loads = [
        pltpu.make_async_copy(stat_h, stats, load.at[3]),
        pltpu.make_async_copy(cot_h, cot, load.at[1]),
        pltpu.make_async_copy(u_h, u, load.at[0]),
        pltpu.make_async_copy(tokens_h, tokens, load.at[2]),
    ]
    for copy in loads:
        copy.start()
    greet(peers + [sibling])
    for copy in loads[:2]:
        copy.wait()

    terms = stats[0]
    for part in range(1, parts):
        terms = terms + stats[part]
    terms = jnp.concatenate([terms, jnp.zeros((LANES - 8, terms.shape[1]), F32)], axis=0).T
    squares = jnp.zeros((terms.shape[0], 1), F32)
    for k in range(LEVELS):
        squares = squares + terms[:, k : k + 1]
        norms[:, k : k + 1] = lax.rsqrt(squares / level_width(k) + EPS_OUT)
    rows = 32

    def mix_rows(i, carry):
        at = pl.ds(pl.multiple_of(i * rows, rows), rows)
        running = norms[at, LEVELS - 1 : LEVELS] * cot[LEVELS - 1, at, :].astype(F32)
        mixed[LEVELS - 1, at, :] = running.astype(BF16)
        for k in reversed(range(LEVELS - 1)):
            running = running + norms[at, k : k + 1] * cot[k, at, :].astype(F32)
            mixed[k, at, :] = running.astype(BF16)
        return carry

    lax.fori_loop(0, tokens.shape[0] // rows, mix_rows, 0)

    width = INNER // groups
    per = WIDE // width
    slots = weights.shape[0]
    dests = [peer[1] for peer in peers] + [q]
    firsts = [dest * cw + b * WIDE for dest in dests for b in range(cw // WIDE)]
    firsts += [b * WIDE for b in range(INNER // WIDE)]

    def get(i):
        return pltpu.make_async_copy(
            wo.at[pl.ds(firsts[i] // width, per)], weights.at[i % slots], fetch.at[i % slots]
        )

    def block_of(i):
        get(i).wait()
        return weights[i % slots].reshape(WIDE, D)

    for i in range(slots - 1):
        get(i).start()
    outgoing = []
    for i in range(len(dests) * (cw // WIDE)):
        get(i + slots - 1).start()
        at, b = divmod(i, cw // WIDE)
        lanes = slice(b * WIDE, (b + 1) * WIDE)
        level = level_of(firsts[i], WIDE)
        back[dests[at], :, lanes] = dot(mixed[level], block_of(i), NT).astype(BF16)
        if b == cw // WIDE - 1:
            if at < len(peers):
                copy = remote(back.at[dests[at]], back_h.at[q], back_s, back_r, at, peers[at])
            else:
                copy = pltpu.make_async_copy(back.at[q], back_h.at[q], local.at[0])
            copy.start()
            outgoing.append(copy)
    first = len(dests) * (cw // WIDE)
    for copy in loads[2:]:
        copy.wait()
    branch[...] = jnp.zeros_like(branch)
    for b in range(INNER // WIDE):
        if first + b + slots - 1 < len(firsts):
            get(first + b + slots - 1).start()
        part, at = divmod(b * WIDE, cw)
        branch[...] += dot(u[part, :, at : at + WIDE], block_of(first + b))
        for k in range(LEVELS):
            if level_width(k) == (b + 1) * WIDE:

                def level_rows(i, carry, k=k):
                    at = pl.ds(pl.multiple_of(i * rows, rows), rows)
                    norm = norms[at, k : k + 1]
                    total = branch[at, :]
                    inner = jnp.sum(cot[k, at, :].astype(F32) * total, axis=-1, keepdims=True)
                    pulls[at, k : k + 1] = norm * norm * norm * (inner / level_width(k))
                    cot[k, at, :] = (tokens[at, :].astype(F32) + norm * total).astype(BF16)
                    return carry

                lax.fori_loop(0, tokens.shape[0] // rows, level_rows, 0)
                copy = pltpu.make_async_copy(cot.at[k], block_h.at[k], store.at[k])
                copy.start()
                outgoing.append(copy)
    coef = jnp.zeros((tokens.shape[0], 1), F32)
    lane = lax.broadcasted_iota(jnp.int32, (1, LANES), 1)
    packed = jnp.zeros((tokens.shape[0], LANES), F32)
    for k in reversed(range(LEVELS)):
        coef = coef + pulls[:, k : k + 1]
        high, rest = two_terms(coef)
        packed = jnp.where(lane == k, high.astype(F32), packed)
        packed = jnp.where(lane == LEVELS + k, rest.astype(F32), packed)
    coefs[...] = packed.astype(BF16)
    for k, peer in enumerate(peers):
        copy = remote(coefs, coef_h.at[q], coef_s, coef_r, k, peer)
        copy.start()
        outgoing.append(copy)
    copy = pltpu.make_async_copy(coefs, coef_h.at[q], local.at[1])
    copy.start()
    outgoing.append(copy)

    share = width // parts

    def product(of, cols):
        channel = of * width
        lanes = pl.ds(pl.multiple_of(lax.rem(channel, cw), width), width)
        return dot(u[channel // cw, :, lanes], mixed[level_of(channel, width), :, cols], TN)

    cores = []
    for d in range(line):

        for cols in (slice(0, D // 2), slice(D // 2, D)):
            sent[d, :, cols] = product(2 * d + 1 - core, cols).astype(BF16)
        copy = remote(sent.at[d], held.at[d], core_s, core_r, d, sibling)
        copy.start()
        cores.append(copy)
    for d in range(line):
        cores[d].wait_recv()
        half = LEFT // 2
        for out, target, at, cuts in (
            (left, left_h, 0, ((0, half), (half, LEFT))),
            (right, right_h, 1, ((LEFT, D),)),
        ):
            for low, high in cuts:
                cols = slice(low, high)
                total = product(2 * d + core, cols) + held[d, :, cols].astype(F32)
                total = total.astype(BF16)
                to = slice(low - cuts[0][0], high - cuts[0][0])
                for part in range(parts):
                    out[part, d, :, to] = total[part * share : (part + 1) * share]
            copy = pltpu.make_async_copy(
                out.at[:, d], target.at[:, d], store.at[LEVELS + 2 * d + at]
            )
            copy.start()
            outgoing.append(copy)
    for copy in cores:
        copy.wait_send()
    for copy in outgoing:
        copy.wait()


def middle(collective_id, u, stats, wo, cotangent, tokens):
    groups, parts, share = wo.shape[:3]
    line = groups // 2
    rows, cw = u.shape[1:]
    width = share * parts
    sem = pltpu.SemaphoreType.DMA
    hbm = pl.BlockSpec(memory_space=pltpu.HBM)
    left = (parts, line, share, LEFT)
    right = (parts, line, share, D - LEFT)
    return pl.pallas_call(
        functools.partial(middle_kernel, groups, parts, cw),
        in_specs=[hbm] * 5,
        out_specs=[hbm] * 5,
        out_shape=[
            jax.ShapeDtypeStruct((parts, rows, cw), BF16),
            jax.ShapeDtypeStruct((parts, rows, LANES), BF16),
            jax.ShapeDtypeStruct(cotangent.shape, BF16),
            jax.ShapeDtypeStruct(left, BF16),
            jax.ShapeDtypeStruct(right, BF16),
        ],
        scratch_shapes=[
            pltpu.VMEM(u.shape, BF16),
            pltpu.VMEM(stats.shape, F32),
            pltpu.VMEM(cotangent.shape, BF16),
            pltpu.VMEM(tokens.shape, BF16),
            pltpu.VMEM(cotangent.shape, BF16),
            pltpu.VMEM((rows, D), F32),
            pltpu.VMEM((rows, LANES), F32),
            pltpu.VMEM((rows, LANES), F32),
            pltpu.VMEM((parts, rows, cw), BF16),
            pltpu.VMEM((rows, LANES), BF16),
            pltpu.VMEM((3, WIDE // width, parts, share, D), BF16),
            pltpu.VMEM((line, width, D), BF16),
            pltpu.VMEM((line, width, D), BF16),
            pltpu.VMEM(left, BF16),
            pltpu.VMEM(right, BF16),
            *([sem((parts - 1,))] * 4),
            sem((line,)), sem((line,)), sem((3,)), sem((4,)), sem((LEVELS + 2 * line,)), sem((2,)),
        ],
        compiler_params=pltpu.CompilerParams(
            collective_id=collective_id, has_side_effects=True, vmem_limit_bytes=63 * 2**20
        ),
        name="middle",
    )(u, stats, wo, cotangent, tokens)


def sum_blocks(out, blocks, rows):
    def step(i, carry):
        at = pl.ds(pl.multiple_of(i * rows, rows), rows)
        total = blocks[0][at].astype(F32)
        for block in blocks[1:]:
            total = total + block[at].astype(F32)
        out[at] = total.astype(out.dtype)
        return carry

    lax.fori_loop(0, out.shape[0] // rows, step, 0)


class PlaneSum:
    def __init__(self, parts, group, q, blocks, first, second, sends, recvs, source=None):
        self.parts, self.group, self.q = parts, group, q
        self.source = blocks if source is None else source
        self.blocks, self.first, self.second = blocks, first, second
        self.sends, self.recvs = sends, recvs
        self.half = blocks.shape[1] // 2
        if parts == 4:
            self.near = [q + 1 - 2 * lax.rem(q, 2), lax.rem(q + 2, 4)]
            self.far = 3 - q

    @staticmethod
    def scratch(parts, shape, dtype):
        if parts == 4:
            half = (shape[0] // 2,) + shape[1:]
            first, second, count = (2, 2) + half, (2, 2) + half, 6
        else:
            first, second, count = (parts - 1,) + shape, (1, 16, LANES), parts - 1
        sem = pltpu.SemaphoreType.DMA
        return [pltpu.VMEM(first, dtype), pltpu.VMEM(second, dtype), sem((count,)), sem((count,))]

    def piece(self, of, h, source=None):
        blocks = self.blocks if source is None else source
        return blocks.at[of, pl.ds(h * self.half, self.half)]

    def early(self, h):
        if self.parts != 4:
            return []
        near = self.near[h]
        to = (self.group, near)
        return [
            remote(
                self.piece(of, h, self.source), self.first.at[h, k],
                self.sends, self.recvs, 2 * h + k, to,
            )
            for k, of in enumerate((near, self.far))
        ]

    def late(self, h):
        to = (self.group, self.near[1 - h])
        return remote(
            self.second.at[h, 0], self.second.at[h, 1], self.sends, self.recvs, 4 + h, to
        )

    def direct(self):
        peers = seq_peers(self.parts)
        return [
            remote(self.source.at[peer[1]], self.first.at[k], self.sends, self.recvs, k, peer)
            for k, peer in enumerate(peers)
        ]

    def start_far(self):
        for h in range(2):
            for copy in self.early(h)[1:]:
                copy.start()

    def start_near(self, h):
        for copy in self.early(h)[:1]:
            copy.start()

    def start(self, h):
        for copy in self.early(h):
            copy.start()
        if self.parts != 4 and h == 1:
            for copy in self.direct():
                copy.start()

    def turn(self, rows):
        if self.parts != 4:
            return
        for h in range(2):
            for copy in self.early(h):
                copy.wait()
            beyond = self.piece(self.near[1 - h], h)
            each(self.second.at[h, 0], [beyond, self.first.at[h, 1]], rows)
            self.late(h).start()

    def finish(self, out, rows):
        if self.parts != 4:
            for copy in self.direct():
                copy.wait()
            each(
                out,
                [self.blocks.at[self.q]] + [self.first.at[k] for k in range(self.parts - 1)],
                rows,
            )
            return
        for h in range(2):
            self.late(h).wait()
            each(
                out.at[pl.ds(h * self.half, self.half)],
                [self.piece(self.q, h), self.first.at[h, 0], self.second.at[h, 1]],
                rows,
            )


def each(out, blocks, rows):
    if len(out.shape) == 2:
        sum_blocks(out, blocks, rows)
        return
    for d in range(out.shape[0]):
        sum_blocks(out.at[d], [block.at[d] for block in blocks], rows)


class LineSum:
    def __init__(self, line, z, core, q, acc, up, down, up_s, up_r, down_s, down_r, rows, steps):
        self.line, self.z, self.core, self.q = line, z, core, q
        self.acc, self.up, self.down = acc, up, down
        self.up_s, self.up_r, self.down_s, self.down_r = up_s, up_r, down_s, down_r
        self.rows, self.steps = rows, steps

    def ahead(self, d, first):
        block = self.acc.at[d] if first else self.up.at[d]
        to = (2 * (self.z + 1) + self.core, self.q)
        return remote(block, self.up.at[d], self.up_s, self.up_r, d, to)

    def behind(self, d, first):
        block = self.acc.at[d] if first else self.down.at[d]
        to = (2 * (self.z - 1) + self.core, self.q)
        return remote(block, self.down.at[d], self.down_s, self.down_r, d, to)

    def add(self, into, d):
        add_blocks(into.at[d], into.at[d], self.acc.at[d], self.rows, self.steps)

    def step(self, t):
        line, z = self.line, self.z
        far, near = line - 1 - t + z, t - (line - 1 - z)

        @pl.when(z == 0)
        def _():
            self.ahead(line - 1 - t, True).start()

        @pl.when((z > 0) & (z <= t))
        def _():
            self.ahead(far, False).wait_recv()
            self.add(self.up, far)
            self.ahead(far, False).start()

        @pl.when(z == line - 1)
        def _():
            self.behind(t, True).start()

        @pl.when((z < line - 1) & (line - 1 - z <= t))
        def _():
            self.behind(near, False).wait_recv()
            self.add(self.down, near)
            self.behind(near, False).start()

    def sent(self, t):
        line, z = self.line, self.z
        far, near = line - 1 - t + z, t - (line - 1 - z)

        @pl.when(z == 0)
        def _():
            self.ahead(line - 1 - t, True).wait_send()

        @pl.when((z > 0) & (z <= t))
        def _():
            self.ahead(far, False).wait_send()

        @pl.when(z == line - 1)
        def _():
            self.behind(t, True).wait_send()

        @pl.when((z < line - 1) & (line - 1 - z <= t))
        def _():
            self.behind(near, False).wait_send()

    def finish(self, out):
        line, z = self.line, self.z

        @pl.when(z == 0)
        def _():
            self.behind(z, False).wait_recv()
            add_blocks(out, self.acc.at[z], self.down.at[z], self.rows, self.steps)

        @pl.when(z == line - 1)
        def _():
            self.ahead(z, False).wait_recv()
            add_blocks(out, self.acc.at[z], self.up.at[z], self.rows, self.steps)

        @pl.when((z > 0) & (z < line - 1))
        def _():
            self.ahead(z, False).wait_recv()
            self.add(self.up, z)
            self.behind(z, False).wait_recv()
            add_blocks(out, self.up.at[z], self.down.at[z], self.rows, self.steps)


class LineSums:
    def __init__(self, line, z, core, q, acc, up, down, sems, rows):
        half = acc.shape[1] // 2
        self.line = line
        self.halves = [
            LineSum(
                line, z, core, q, *[a.at[:, pl.ds(h * half, half)] for a in (acc, up, down)],
                *[s.at[h] for s in sems], rows, half // rows,
            )
            for h in range(2)
        ]
        self.half = half

    def step(self, t):
        for part in self.halves:
            part.step(t)

    def finish(self, out):
        for h, part in enumerate(self.halves):
            part.finish(out.at[pl.ds(h * self.half, self.half)])

    def sent(self):
        for t in range(self.line - 1):
            for part in self.halves:
                part.sent(t)


def backward_kernel(
    groups, parts, cw,
    back_h, coefs_h, normed_h, px_h, y_h, z_h, states_h, wide_h,
    gain, taps, heads, skip, spread, gather,
    dz_h, dpx_h, small, wide_sum, gate_sum,
    dz, coefs, normed, px, y, dy, states, wide, dpx, dtaps, dheads, dskip, dgain,
    xbuf, dstate, dcbuf, slope, xact, xd_s, dxd_s, acc_s,
    first, second, wide_s, wide_r, gate_made, gate_held, gate_acc, gate_up, gate_down,
    core_s, core_r, up_s, up_r, down_s, down_r, load, store,
):
    line = groups // 2
    cc = cw + 2 * N
    length = y.shape[0]
    chunks = length // CHUNK
    group, q = lax.axis_index("dp"), lax.axis_index("seq")
    z, core = group // 2, lax.rem(group, 2)
    sibling = (2 * z + 1 - core, q)
    loads = [
        pltpu.make_async_copy(source, target, load.at[k])
        for k, (source, target) in enumerate(
            [(wide_h, wide), (back_h, dz), (coefs_h, coefs), (y_h, y), (z_h, dy),
             (normed_h, normed), (states_h, states)]
        )
    ]
    for copy in loads[1:5]:
        copy.start()

    def fetch(at, first=False):
        slot = lax.rem(at, 2)
        if first:
            return pltpu.make_async_copy(
                px_h.at[pl.ds(0, CHUNK)], px.at[0, pl.ds(8, CHUNK)], load.at[7]
            )
        rows = pl.ds(pl.multiple_of(at * CHUNK - 8, 8), CHUNK + 8)
        return pltpu.make_async_copy(px_h.at[rows], px.at[slot], load.at[7 + slot])

    greet(seq_peers(parts) + dp_peers(groups))
    plane = PlaneSum(parts, group, q, wide, first, second, wide_s, wide_r, wide_h)
    plane.start(0)
    plane.start(1)
    for copy in loads[1:5]:
        copy.wait()
    loads[5].start()
    loads[6].start()
    loads[0].start()
    fetch(chunks - 1).start()

    rows = 32
    lane = lax.broadcasted_iota(jnp.int32, (1, LANES), 1)
    dgain[...] = jnp.zeros_like(dgain)

    def gate_rows(i, carry):
        at = pl.ds(pl.multiple_of(i * rows, rows), rows)
        coef = coefs[at, :].astype(F32)
        for b in range(cw // WIDE):
            lanes = slice(b * WIDE, (b + 1) * WIDE)
            level = level_of(q * cw + b * WIDE, WIDE)
            ours = (lane == level) | (lane == level + LEVELS)
            pull = jnp.sum(jnp.where(ours, coef, 0.0), axis=-1, keepdims=True)
            gate_in = dy[at, lanes]
            sig = jax.nn.sigmoid(gate_in)
            gate = gate_in * sig
            y_at = y[at, lanes]
            gated = y_at * gate
            back = dz[at, lanes].astype(F32)
            dgated = gain[:, lanes] * back - gated * pull
            dgain[0:1, lanes] += jnp.sum(back * gated, axis=0, keepdims=True)
            dz[at, lanes] = (dgated * y_at * (sig + gate * (1.0 - sig))).astype(BF16)
            dy[at, lanes] = dgated * gate
        return carry

    lax.fori_loop(0, length // rows, gate_rows, 0)
    dz_out = pltpu.make_async_copy(dz, dz_h, store.at[0])
    dz_out.start()
    loads[5].wait()
    span = gate_acc.shape[1]

    def dweight(of, out):
        at = pl.ds(pl.multiple_of(of * span, span), span)
        out[...] = dot(normed[:, at], dz[...], TN).astype(BF16)

    def core_copy(d):
        return remote(gate_made.at[d], gate_held.at[d], core_s, core_r, d, sibling)

    order = [d for k in range(line // 2) for d in (line - 1 - k, k)]
    gates = LineSums(
        line, z, core, q, gate_acc, gate_up, gate_down, (up_s, up_r, down_s, down_r), span // 8
    )
    for some in (order[:2], order[2:]):
        for d in some:
            dweight(2 * d + 1 - core, gate_made.at[d])
            core_copy(d).start()
        for d in some:
            dweight(2 * d + core, gate_acc.at[d])
            core_copy(d).wait()
            add_blocks(gate_acc.at[d], gate_acc.at[d], gate_held.at[d], span // 4, 4)
        if some[0] == order[0]:
            gates.step(0)
    dstate[...] = jnp.zeros_like(dstate)
    dcbuf[CHUNK : CHUNK + 8, :] = jnp.zeros((8, cc), F32)
    dtaps[...] = jnp.zeros_like(dtaps)
    dheads[...] = jnp.zeros_like(dheads)
    dskip[...] = jnp.zeros_like(dskip)
    loads[6].wait()
    loads[0].wait()

    def scan_rows(i, carry):
        for t in range(1, line - 1):

            @pl.when(i == min(3 * t - 1, chunks - 1))
            def _(t=t):
                gates.step(t)

        @pl.when(i == 4)
        def _():
            plane.turn(32)

        at = chunks - 1 - i
        here = pl.ds(pl.multiple_of(at * CHUNK, CHUNK), CHUNK)

        @pl.when(at > 0)
        def _():
            fetch(at).wait()

        @pl.when(at == 0)
        def _():
            fetch(0, True).wait()

        @pl.when(at > 1)
        def _():
            fetch(at - 1).start()

        @pl.when(at == 1)
        def _():
            fetch(0, True).start()

        rows = px.at[lax.rem(at, 2)]
        scan_backward_step(
            cw, at == 0, rows.at[pl.ds(8, CHUNK)], rows.at[pl.ds(0, 8)], taps, heads, skip, spread, gather,
            dy.at[here], y.at[here], states.at[at], dpx.at[here], dtaps, dheads, dskip,
            xbuf, dstate, dcbuf, slope, xact, xd_s, dxd_s, acc_s,
        )
        return carry

    lax.fori_loop(0, chunks, scan_rows, 0)
    dpx_out = pltpu.make_async_copy(dpx, dpx_h, store.at[1])
    dpx_out.start()
    small[...] = jnp.zeros_like(small)
    wide_rows, own_rows = cc // LANES, cw // LANES
    for tap in range(TAPS + 1):
        for b in range(wide_rows):
            to = tap * wide_rows + b
            small[to : to + 1, :] = dtaps[tap : tap + 1, b * LANES : (b + 1) * LANES]
    to = (TAPS + 1) * wide_rows
    for b in range(own_rows):
        small[to + b : to + b + 1, :] = dgain[0:1, b * LANES : (b + 1) * LANES]
    hq = cw // P_SIZE
    skips = spread_heads(dskip[...], gather[...])
    small[to + own_rows : to + own_rows + 1, :] = (
        dheads[0:1, :]
        + pltpu.roll(dheads[...], hq, 1)[1:2, :]
        + pltpu.roll(skips, 2 * hq, 1)[0:1, :]
    )
    plane.finish(wide_sum, 32)
    gates.finish(gate_sum)
    gates.sent()
    dz_out.wait()
    dpx_out.wait()


def backward(
    collective_id, back, coefs, normed, px, y, z, states, wide, gain, taps, heads, skip, spread, gather
):
    parts, line = wide.shape[:2]
    length, width = px.shape
    cw = skip.shape[1]
    cc = cw + 2 * N
    span = D // (2 * line)
    sem = pltpu.SemaphoreType.DMA
    vmem = pl.BlockSpec(memory_space=pltpu.VMEM)
    hbm = pl.BlockSpec(memory_space=pltpu.HBM)
    small_rows = (TAPS + 1) * (cc // LANES) + cw // LANES + 1
    small_rows = -(-small_rows // 8) * 8
    return pl.pallas_call(
        functools.partial(backward_kernel, 2 * line, parts, cw),
        in_specs=[*([hbm] * 8), *([vmem] * 6)],
        out_specs=[hbm, hbm, vmem, vmem, vmem],
        out_shape=[
            jax.ShapeDtypeStruct((length, cw), BF16),
            jax.ShapeDtypeStruct((length, width), BF16),
            jax.ShapeDtypeStruct((small_rows, LANES), F32),
            jax.ShapeDtypeStruct(wide.shape[1:], BF16),
            jax.ShapeDtypeStruct((span, cw), BF16),
        ],
        scratch_shapes=[
            *[pltpu.VMEM(a.shape, a.dtype) for a in (back, coefs, normed)],
            pltpu.VMEM((2, CHUNK + 8, width), F32),
            *[pltpu.VMEM(a.shape, a.dtype) for a in (y, z, states, wide)],
            pltpu.VMEM((length, width), BF16),
            pltpu.VMEM((8, cc), F32),
            pltpu.VMEM((8, LANES), F32),
            pltpu.VMEM((8, cw), F32),
            pltpu.VMEM((8, cw), F32),
            pltpu.VMEM((CHUNK + 8, cc), F32),
            pltpu.VMEM((N, cw), F32),
            pltpu.VMEM((CHUNK + 8, cc), F32),
            pltpu.VMEM((CHUNK, cc), F32),
            pltpu.VMEM((CHUNK, cc), F32),
            pltpu.VMEM((CHUNK, cw), BF16),
            pltpu.VMEM((CHUNK, cw), F32),
            pltpu.VMEM((CHUNK, CHUNK), F32),
            *PlaneSum.scratch(parts, wide.shape[1:], BF16),
            *([pltpu.VMEM((line, span, cw), BF16)] * 5),
            sem((line,)), sem((line,)), *([sem((2, line))] * 4),
            sem((9,)), sem((2,)),
        ],
        compiler_params=pltpu.CompilerParams(
            collective_id=collective_id, has_side_effects=True, vmem_limit_bytes=63 * 2**20
        ),
        name="backward",
    )(back, coefs, normed, px, y, z, states, wide, gain, taps, heads, skip, spread, gather)


def owners_kernel(
    groups, parts, rows, cw,
    normed, left, right, gate, small, dz, dpx, wz, wx,
    part, rest_out, left_out, right_out, gate_out, back_out, small_all,
    made, held, acc, up, down, final, left_up, left_down, right_acc, right_up, right_down,
    rest_made, rest_held, rest, rest_acc, rest_up, rest_down,
    normed_v, dz_v, dpx_v, wz_v, wx_v, back, back_sum,
    right_1, right_2, right_s, right_r, back_1, back_2, back_s, back_r,
    rest_1, rest_2, rest_s, rest_r,
    core_s, core_r, up_s, up_r, down_s, down_r, lup_s, lup_r, ldown_s, ldown_r,
    rup_s, rup_r, rdown_s, rdown_r, tup_s, tup_r, tdown_s, tdown_r, rcore_s, rcore_r,
    part_s, part_r, gate_s, gate_r, small_s, small_r, load, local,
):
    line = groups // 2
    span = parts * rows
    group, q = lax.axis_index("dp"), lax.axis_index("seq")
    z, core = group // 2, lax.rem(group, 2)
    sibling = (2 * z + 1 - core, q)
    peers, others = seq_peers(parts), dp_peers(groups)
    tokens = back.shape[1]
    loads = [
        pltpu.make_async_copy(source, target, load.at[k])
        for k, (source, target) in enumerate(
            [(normed, normed_v), (dpx, dpx_v), (dz, dz_v), (wz, wz_v), (wx, wx_v)]
        )
    ]
    for copy in loads[:2]:
        copy.start()
    greet(peers + others)
    half_rows = left.shape[1] // 2
    lefts = LineSum(
        line, z, core, q, left, left_up, left_down, lup_s, lup_r, ldown_s, ldown_r, half_rows, 2
    )
    rights = LineSum(
        line, z, core, q, right_acc, right_up, right_down, rup_s, rup_r, rdown_s, rdown_r,
        half_rows, 2,
    )
    wholes = LineSum(
        line, z, core, q, acc, up, down, up_s, up_r, down_s, down_r, rows, parts
    )
    lefts.step(0)
    right_plane = PlaneSum(parts, group, q, right, right_1, right_2, right_s, right_r)
    rest_plane = PlaneSum(parts, group, q, rest, rest_1, rest_2, rest_s, rest_r)
    rests = LineSum(
        line, z, core, q, rest_acc, rest_up, rest_down, tup_s, tup_r, tdown_s, tdown_r, rows, 1
    )
    back_plane = PlaneSum(parts, group, q, back, back_1, back_2, back_s, back_r)
    right_plane.start(0)
    right_plane.start(1)
    waiting = []
    for k, peer in enumerate(peers):
        copy = remote(gate.at[peer[1]], gate_out.at[q], gate_s, gate_r, k, peer)
        copy.start()
        waiting.append(copy)
    for k, peer in enumerate(others):
        copy = remote(small, small_all.at[group], small_s, small_r, k, peer)
        copy.start()
        waiting.append(copy)
    own = [
        pltpu.make_async_copy(gate.at[q], gate_out.at[q], local.at[0]),
        pltpu.make_async_copy(small, small_all.at[group], local.at[1]),
    ]
    for copy in own:
        copy.start()
    loads[0].wait()
    loads[1].wait()
    for copy in loads[2:]:
        copy.start()
    tile = 512

    def dweight(of):
        at = pl.ds(pl.multiple_of(of * span, span), span)
        return dot(normed_v[:, at], dpx_v[...], TN)

    cores = {}
    order = [d for k in range(line // 2) for d in (line - 1 - k, k)]

    def share_core(d):
        total = dweight(2 * d + 1 - core)
        made[d] = total[:, :cw].astype(BF16)
        rest_made[d] = total[:, cw:].astype(BF16)
        cores[d] = [
            remote(made.at[d], held.at[d], core_s, core_r, d, sibling),
            remote(rest_made.at[d], rest_held.at[d], rcore_s, rcore_r, d, sibling),
        ]
        for copy in cores[d]:
            copy.start()

    def sum_core(d):
        total = dweight(2 * d + core)
        for copy in cores[d]:
            copy.wait()
        acc[d] = (total[:, :cw] + held[d].astype(F32)).astype(BF16)
        others = (total[:, cw:] + rest_held[d].astype(F32)).astype(BF16)
        for k in range(parts):
            rest[k, d] = others[k * rows : (k + 1) * rows]

    def dnormed(of):
        at = pl.ds(pl.multiple_of(of * tokens, tokens), tokens)

        def step(j, carry):
            cols = pl.ds(pl.multiple_of(j * tile, tile), tile)
            back[of, :, cols] = (
                dot(dz_v[at, :], wz_v[cols, :], NT) + dot(dpx_v[at, :], wx_v[cols, :], NT)
            ).astype(BF16)
            return carry

        lax.fori_loop(0, D // tile, step, 0)

    share_core(order[0])
    lefts.sent(0)
    lefts.step(1)
    share_core(order[1])
    sum_core(order[0])
    sum_core(order[1])
    wholes.step(0)
    for t in range(2, line - 1):
        lefts.sent(t - 1)
        lefts.step(t)
    for copy in loads[2:]:
        copy.wait()
    if parts == 4:
        dnormed(back_plane.far)
        back_plane.start_far()
    for d in order[2:]:
        share_core(d)
    for d in order[2:]:
        sum_core(d)
    right_plane.turn(32)
    if parts == 4:
        dnormed(back_plane.near[0])
        back_plane.start_near(0)
    wholes.sent(0)
    wholes.step(1)
    if parts == 4:
        dnormed(back_plane.near[1])
        back_plane.start_near(1)
    else:
        for peer in peers:
            dnormed(peer[1])
        back_plane.start(1)
    rest_plane.start(0)
    rest_plane.start(1)
    dnormed(q)
    right_plane.finish(right_acc, 32)
    for t in range(2, line - 1):
        wholes.sent(t - 1)
        wholes.step(t)
    rights.step(0)
    rest_plane.turn(rows)
    rest_plane.finish(rest_acc, rows)
    rests.step(0)
    back_plane.turn(32)
    lefts.finish(left_out)
    lefts.sent(line - 2)
    rests.sent(0)
    rests.step(1)
    rights.sent(0)
    rights.step(1)
    wholes.sent(line - 2)
    wholes.finish(final)
    for k, peer in enumerate(peers):
        block = final.at[pl.ds(pl.multiple_of(peer[1] * rows, rows), rows)]
        copy = remote(block, part.at[q], part_s, part_r, k, peer)
        copy.start()
        waiting.append(copy)
    copy = pltpu.make_async_copy(
        final.at[pl.ds(pl.multiple_of(q * rows, rows), rows)], part.at[q], local.at[2]
    )
    copy.start()
    own.append(copy)
    for t in range(2, line - 1):
        rights.sent(t - 1)
        rights.step(t)
    for t in range(2, line - 1):
        rests.sent(t - 1)
        rests.step(t)
    back_plane.finish(back_sum, 32)
    copy = pltpu.make_async_copy(back_sum, back_out, local.at[3])
    copy.start()
    own.append(copy)
    rests.finish(rest_out)
    rests.sent(line - 2)
    rights.finish(right_out)
    rights.sent(line - 2)
    for copy in own + waiting:
        copy.wait()


def sum_to_owners(collective_id, normed, left, right, gate, small, dz, dpx, wz, wx):
    parts, line, out_rows, slim = right.shape
    groups = 2 * line
    rows, cw = gate.shape[1:]
    span = rows * parts
    extra = dpx.shape[1] - cw
    tokens = dz.shape[0] // parts
    sem = pltpu.SemaphoreType.DMA
    vmem = pl.BlockSpec(memory_space=pltpu.VMEM)
    hbm = pl.BlockSpec(memory_space=pltpu.HBM)
    right_sum = (line, out_rows, slim)
    rest = (parts, line, rows, extra)
    return pl.pallas_call(
        functools.partial(owners_kernel, groups, parts, rows, cw),
        in_specs=[hbm, vmem, vmem, hbm, vmem, hbm, hbm, hbm, hbm],
        out_specs=[hbm, vmem, vmem, vmem, hbm, hbm, vmem],
        out_shape=[
            jax.ShapeDtypeStruct((parts, rows, cw), BF16),
            jax.ShapeDtypeStruct((rows, extra), F32),
            jax.ShapeDtypeStruct((out_rows, left.shape[-1]), F32),
            jax.ShapeDtypeStruct((out_rows, slim), F32),
            jax.ShapeDtypeStruct(gate.shape, BF16),
            jax.ShapeDtypeStruct((tokens, D), F32),
            jax.ShapeDtypeStruct((groups,) + small.shape, F32),
        ],
        scratch_shapes=[
            *([pltpu.VMEM((line, span, cw), BF16)] * 5),
            pltpu.VMEM((span, cw), BF16),
            *([pltpu.VMEM(left.shape, BF16)] * 2),
            *([pltpu.VMEM(right_sum, BF16)] * 3),
            *([pltpu.VMEM((line, span, extra), BF16)] * 2),
            pltpu.VMEM(rest, BF16),
            *([pltpu.VMEM(rest[1:], BF16)] * 3),
            *[pltpu.VMEM(a.shape, BF16) for a in (normed, dz, dpx, wz, wx)],
            pltpu.VMEM((parts, tokens, D), BF16),
            pltpu.VMEM((tokens, D), F32),
            *PlaneSum.scratch(parts, right.shape[1:], BF16),
            *PlaneSum.scratch(parts, (tokens, D), BF16),
            *PlaneSum.scratch(parts, rest[1:], BF16),
            *([sem((line,))] * 20),
            *([sem((parts - 1,))] * 4),
            *([sem((groups - 1,))] * 2),
            sem((5,)),
            sem((4,)),
        ],
        compiler_params=pltpu.CompilerParams(
            collective_id=collective_id, has_side_effects=True, vmem_limit_bytes=63 * 2**20
        ),
        name="sum_to_owners",
    )(normed, left, right, gate, small, dz, dpx, wz, wx)


def on_device(
    hidden_in, out_grads, w_in, w_in_m, w_in_v, w_out, w_out_m, w_out_v,
    chan_params, chan_m, chan_v, head_params, head_m, head_v,
):
    parts = lax.axis_size("seq")
    groups = lax.axis_size("dp")
    q = lax.axis_index("seq")
    rows = hidden_in.shape[1]
    length = rows * parts
    cw = INNER // parts
    hq = H // parts
    cc = cw + 2 * N
    in_rows = w_in.shape[0]
    out_rows = w_out.shape[0]

    chan_len = chan_params.shape[0]
    line = groups // 2
    group = lax.axis_index("dp")
    owner = group * parts + q
    chan_block = lax.dynamic_update_slice(
        jnp.zeros((8 * LANES,), F32),
        lax.reduce_precision(chan_params, 8, 7),
        (lax.rem(owner * chan_len, LANES),),
    ).reshape(8, LANES)
    head_block = jnp.pad(head_params, ((0, 5), (0, LANES - H)))
    hidden, wx, gate, wo, gain_in, own_gain, taps, heads, skip, spread, gather = collect(
        0, hidden_in[0], w_in, w_out, chan_block, head_block, chan_len, groups, parts
    )

    normed, px, y, states, z, u, stats, wz, wo = forward(
        1, hidden.reshape(length, D), wx.reshape(D, cc + LANES), gate, wo, gain_in, own_gain,
        taps, heads, skip, spread,
    )
    wx, wz = wx.reshape(D, cc + LANES), wz.reshape(D, cw)
    cotangent = out_grads[:, 0]
    back_own, coefs, block_out, dwo_left, dwo_right = middle(
        2, u, stats, wo, cotangent, hidden_in[0]
    )

    dz, dpx, small, dwo_left, dwz = backward(
        5, back_own.reshape(length, cw), coefs.reshape(length, LANES), normed, px, y, z, states,
        dwo_left, own_gain, taps, heads, skip, spread, gather,
    )
    x_part, rest, left_part, right_part, z_part, dnormed, small = sum_to_owners(
        4, normed, dwo_left, dwo_right, dwz.reshape(parts, in_rows, cw), small, dz, dpx, wz, wx
    )
    hidden_grad, chan_total, head_total, norm = gradient_norm(
        6, x_part, rest, z_part, left_part, right_part, dnormed, small, hidden_in[0],
        gain_in, cotangent, groups,
    )
    (
        hidden_grad, block_out, w_in_new, w_in_m_new, w_in_v_new, w_in_copy,
        w_out_new, w_out_m_new, w_out_v_new, w_out_copy,
    ) = update_weights(
        norm, x_part, rest, z_part, left_part, right_part, hidden_grad, block_out,
        (w_in, w_in_m, w_in_v, w_out, w_out_m, w_out_v),
    )
    hidden_grad, block_out = hidden_grad[None], block_out[:, None]
    grad_norm, clip_factor = norm[0, 0], norm[1, 0]
    chan_part = lax.dynamic_slice(chan_total.reshape(-1), (owner * chan_len,), (chan_len,))
    head_total = head_total[:parts, : 3 * hq].reshape(parts, 3, hq)
    head_total = head_total.transpose(1, 0, 2).reshape(3, H)
    chan_new, chan_m_new, chan_v_new = adam_tile(
        chan_params, clip_factor * chan_part, chan_m, chan_v, 0.2, 0.0
    )
    head_new, head_m_new, head_v_new = adam_tile(
        head_params, clip_factor * head_total, head_m, head_v, 1.0, 0.0
    )
    return (
        block_out, hidden_grad, grad_norm,
        w_in_new, w_in_m_new, w_in_v_new, w_in_copy,
        w_out_new, w_out_m_new, w_out_v_new, w_out_copy,
        chan_new, chan_m_new, chan_v_new, head_new, head_m_new, head_v_new,
    )


def solution(mesh):
    rows = P(("dp", "seq"), None)
    flat = P(("dp", "seq"))
    in_specs = (
        P("dp", "seq", None),
        P(None, "dp", "seq", None),
        *([rows] * 6),
        *([flat] * 3),
        *([P()] * 3),
    )
    out_specs = (
        P(None, "dp", "seq", None),
        P("dp", "seq", None),
        P(),
        *([rows] * 8),
        *([flat] * 3),
        *([P()] * 3),
    )
    return jax.shard_map(
        on_device, mesh=mesh, in_specs=in_specs, out_specs=out_specs, check_vma=False
    )
```

```python
import functools

import jax
import jax.numpy as jnp
from jax import lax
from jax.experimental import pallas as pl
from jax.experimental.pallas import tpu as pltpu
from jax.sharding import PartitionSpec as P

D = 2048
INNER = 4096
H = 64
P_SIZE = 64
N = 128
TAPS = 4
STEP = 10
E_IN = 8512
CONV_CH = 4352
LANES = 128
CHUNK = 128
LEVELS = 4

EXACT = lax.Precision.HIGHEST
EPS_IN = 1e-06
EPS_OUT = 1e-05
ADAM_EPS = 1e-08
BETA = 0.5
CLIP = 1.0
F32 = jnp.float32
BF16 = jnp.bfloat16
MASKED = -1e30


def level_width(level):
    return INNER * 2**level // 8


SEGMENTS = tuple(
    (0 if level == 0 else level_width(level - 1), level_width(level)) for level in range(LEVELS)
)


def dot(a, b, dims=((1,), (0,)), precision=None):
    return lax.dot_general(a, b, (dims, ((), ())), precision=precision, preferred_element_type=F32)


NT = ((1,), (1,))
TN = ((0,), (0,))


def softplus(v):
    return jnp.maximum(v, 0.0) + jnp.log1p(jnp.exp(-jnp.abs(v)))


def two_terms(v):
    high = v.astype(BF16)
    return high, (v - high.astype(F32)).astype(BF16)


def spread_heads(v, spread):
    high, rest = two_terms(v)
    return dot(high, spread) + dot(rest, spread)


def own_heads_first(dt_raw, hq, back=False):
    by = lax.axis_index("seq") * hq
    return pltpu.roll(dt_raw, by if back else lax.rem(LANES - by, LANES), 1)


def rates(dt_raw, heads):
    step = softplus(dt_raw + heads[0:1, :])
    return step, step * heads[1:2, :]


def triangle(size):
    row = lax.broadcasted_iota(jnp.int32, (size, size), 0)
    col = lax.broadcasted_iota(jnp.int32, (size, size), 1)
    return row, col


def conv_block(taps, xbuf, lanes):
    out = taps[TAPS : TAPS + 1, lanes]
    for tap in range(TAPS):
        out = out + taps[tap : tap + 1, lanes] * xbuf[5 + tap : 5 + tap + CHUNK, lanes]
    return out


def pair_decay(cum, cum_t, causal, head):
    gap = cum[:, head : head + 1] - cum_t[head : head + 1, :]
    return jnp.exp(jnp.where(causal, gap, MASKED))


def scan_forward_step(cw, px, taps, heads, skip, spread, y, states, xbuf, state, xdt, carried):
    cc = cw + 2 * N
    xbuf[8 : 8 + CHUNK, :] = px[:, :cc]
    step, rate = rates(own_heads_first(px[:, cc:], cw // P_SIZE), heads)
    row, col = triangle(CHUNK)
    causal = row >= col
    cum = dot(causal.astype(F32), rate, precision=EXACT)
    cum_t = cum.T
    spread_m = spread[...]
    last = cum[CHUNK - 1 : CHUNK, :]
    step_x = spread_heads(step, spread_m)
    grow_x = spread_heads(jnp.exp(cum), spread_m)
    tail_x = spread_heads(jnp.exp(last - cum), spread_m)

    def activated(lanes):
        conv = conv_block(taps, xbuf, lanes)
        return conv * jax.nn.sigmoid(conv)

    state_in = activated(slice(cw, cw + N))
    state_out = activated(slice(cw + N, cw + 2 * N))
    scores = dot(state_out, state_in, NT, EXACT)
    states[...] = state[...].astype(BF16)
    carried[...] = dot(state_out.astype(BF16), state[...].astype(BF16))
    first = lax.broadcasted_iota(jnp.int32, (1, LANES), 1) < P_SIZE
    for pair in range(cw // LANES):
        lanes = slice(pair * LANES, (pair + 1) * LANES)
        x = activated(lanes)
        xd = (x * step_x[:, lanes]).astype(BF16).astype(F32)
        xdt[:, lanes] = (xd * tail_x[:, lanes]).astype(BF16)
        stacked = jnp.concatenate([jnp.where(first, xd, 0.0), jnp.where(first, 0.0, xd)], axis=0)
        mixing = jnp.concatenate(
            [
                (pair_decay(cum, cum_t, causal, 2 * pair + k) * scores).astype(BF16)
                for k in range(2)
            ],
            axis=1,
        )
        y[:, lanes] = (
            dot(mixing, stacked.astype(BF16))
            + grow_x[:, lanes] * carried[:, lanes]
            + skip[:, lanes] * x
        )
    state[...] = grow_x[CHUNK - 1 : CHUNK, :] * state[...] + dot(
        state_in.astype(BF16), xdt[...], TN
    )
    xbuf[0:8, :] = xbuf[CHUNK : CHUNK + 8, :]


def scan_backward_step(
    cw, start, px, halo, taps, heads, skip, spread, gather, dy, y, states,
    dpx, dtaps, dheads, dskip,
    xbuf, dstate, dcbuf, slope, xact, xd_s, dxd_s, acc_s,
):
    cc = cw + 2 * N
    xbuf[0:8, :] = jnp.where(start, 0.0, halo[:, :cc])
    xbuf[8 : 8 + CHUNK, :] = px[:, :cc]
    dt_raw = own_heads_first(px[:, cc:], cw // P_SIZE)
    step, rate = rates(dt_raw, heads)
    row, col = triangle(CHUNK)
    causal = row >= col
    cum = dot(causal.astype(F32), rate, precision=EXACT)
    cum_t = cum.T
    spread_m = spread[...]
    last = cum[CHUNK - 1 : CHUNK, :]
    step_x = spread_heads(step, spread_m)
    grow_x = spread_heads(jnp.exp(cum), spread_m)
    tail_x = spread_heads(jnp.exp(last - cum), spread_m)

    for block in range(cc // LANES):
        lanes = slice(block * LANES, (block + 1) * LANES)
        conv = conv_block(taps, xbuf, lanes)
        sig = jax.nn.sigmoid(conv)
        act = conv * sig
        xact[:, lanes] = act
        slope[:, lanes] = sig + act * (1.0 - sig)
    state_in = xact[:, cw : cw + N]
    state_out = xact[:, cw + N : cc]
    scores = dot(state_out, state_in, NT, EXACT)
    in_low = state_in.astype(BF16)
    out_low = state_out.astype(BF16)
    dstate_low = dstate[...].astype(BF16)
    acc_s[...] = jnp.zeros_like(acc_s)
    dxd_s[...] = tail_x * dot(in_low, dstate_low)
    dskip[0:1, :] += jnp.sum(xact[:, :cw] * dy[...], axis=0, keepdims=True)
    first = lax.broadcasted_iota(jnp.int32, (1, LANES), 1) < P_SIZE
    xd_s[...] = (xact[:, :cw] * step_x).astype(BF16)
    total = jnp.sum(xd_s[...].astype(F32) * dxd_s[...], axis=0, keepdims=True) + grow_x[
        CHUNK - 1 : CHUNK, :
    ] * jnp.sum(dstate[...] * states[...].astype(F32), axis=0, keepdims=True)
    dscores = jnp.zeros((CHUNK, CHUNK), F32)
    for pair in range(cw // LANES):
        lanes = slice(pair * LANES, (pair + 1) * LANES)
        dyp = dy[:, lanes]
        stacked = jnp.concatenate(
            [jnp.where(first, dyp, 0.0), jnp.where(first, 0.0, dyp)], axis=0
        ).astype(BF16)
        decays = [pair_decay(cum, cum_t, causal, 2 * pair + k) for k in range(2)]
        mixing = jnp.concatenate([(decay * scores).astype(BF16) for decay in decays], axis=0)
        dxd_s[:, lanes] += dot(mixing, stacked, TN)
        dmix = dot(stacked, xd_s[:, lanes], NT)
        dscores = dscores + decays[0] * dmix[:CHUNK] + decays[1] * dmix[CHUNK:]
    dy_low = dy[...].astype(BF16)
    dy_f = dy_low.astype(F32)
    xd_f = xd_s[...].astype(F32)
    dxd = dxd_s[...]
    y_scan = y[...] - skip[...] * xact[:, :cw]
    final = lax.broadcasted_iota(jnp.int32, (CHUNK, 1), 0) == CHUNK - 1
    gather_m = gather[...]
    dcum = spread_heads(dy_f * y_scan - xd_f * dxd + jnp.where(final, total, 0.0), gather_m)
    dstep = spread_heads(xact[:, :cw] * dxd, gather_m)
    drate = dot((row <= col).astype(F32), dcum, precision=EXACT)
    dstep = dstep + drate * heads[1:2, :]
    ddt = dstep * jax.nn.sigmoid(dt_raw + heads[0:1, :])
    dheads[0:1, :] += jnp.sum(ddt, axis=0, keepdims=True)
    dheads[1:2, :] += jnp.sum(drate * rate, axis=0, keepdims=True)
    grown = (grow_x * dy_f).astype(BF16)
    dscores_low = dscores.astype(BF16)
    dout = dot(dscores_low, in_low) + dot(grown, states[...], NT)
    din = dot(dscores_low, out_low, TN) + dot((tail_x * xd_f).astype(BF16), dstate_low, NT)
    dstate[...] = grow_x[CHUNK - 1 : CHUNK, :] * dstate[...] + dot(out_low, grown, TN)
    dcbuf[:CHUNK, :cw] = (step_x * dxd + skip[...] * dy[...]) * slope[:, :cw]
    dcbuf[:CHUNK, cw : cw + N] = din * slope[:, cw : cw + N]
    dcbuf[:CHUNK, cw + N :] = dout * slope[:, cw + N :]
    for block in range(cc // LANES):
        lanes = slice(block * LANES, (block + 1) * LANES)
        dconv = dcbuf[:CHUNK, lanes]
        dtaps[TAPS : TAPS + 1, lanes] += jnp.sum(dconv, axis=0, keepdims=True)
        back = taps[TAPS - 1 : TAPS, lanes] * dconv
        for tap in range(TAPS):
            dtaps[tap : tap + 1, lanes] += jnp.sum(
                dconv * xbuf[5 + tap : 5 + tap + CHUNK, lanes], axis=0, keepdims=True
            )
            if tap < TAPS - 1:
                reach = TAPS - 1 - tap
                back = back + taps[tap : tap + 1, lanes] * dcbuf[reach : reach + CHUNK, lanes]
        dpx[:, lanes] = back.astype(BF16)
    ours = lax.broadcasted_iota(jnp.int32, (1, LANES), 1) < cw // P_SIZE
    ddt = own_heads_first(jnp.where(ours, ddt, 0.0), cw // P_SIZE, back=True)
    dpx[:, cc:] = ddt.astype(BF16)
    dcbuf[CHUNK : CHUNK + 8, :] = dcbuf[0:8, :]


WIDE = 512
LEFT = 1280
SPLIT = 384


MESH = pl.DeviceIdType.MESH


def remote(src, dst, sends, recvs, index, device):
    return pltpu.make_async_remote_copy(
        src_ref=src,
        dst_ref=dst,
        send_sem=sends.at[index],
        recv_sem=recvs.at[index],
        device_id=device,
        device_id_type=MESH,
    )


def greet(devices):
    barrier = pltpu.get_barrier_semaphore()
    for device in devices:
        pl.semaphore_signal(barrier, inc=1, device_id=device, device_id_type=MESH)
    pl.semaphore_wait(barrier, len(devices))


def seq_peers(parts):
    group, q = lax.axis_index("dp"), lax.axis_index("seq")
    return [(group, lax.rem(q + k, parts)) for k in range(1, parts)]


def dp_peers(groups):
    group, q = lax.axis_index("dp"), lax.axis_index("seq")
    return [(lax.rem(group + k, groups), q) for k in range(1, groups)]


def all_peers(groups, parts):
    devices = groups * parts
    me = lax.axis_index("dp") * parts + lax.axis_index("seq")
    peers = []
    for k in range(1, devices):
        other = lax.rem(me + k, devices)
        peers.append((other // parts, lax.rem(other, parts)))
    return peers


CHAN_ROWS = ((TAPS + 1) * CONV_CH + D + INNER) // LANES


def adam_tile(weight, gradient, moment, second, step_rate, weight_decay):
    new_moment = BETA * moment + (1.0 - BETA) * gradient
    new_second = BETA * second + (1.0 - BETA) * gradient * gradient
    correction = 1.0 - BETA**STEP
    update = new_moment / correction / (jnp.sqrt(new_second / correction) + ADAM_EPS)
    return weight - step_rate * (update + weight_decay * weight), new_moment, new_second


def total_of(value):
    return jnp.sum(jnp.sum(value, axis=1, keepdims=True), axis=0, keepdims=True)


def norm_kernel(
    groups, parts,
    part_h, rest_h, gate_h, left_h, right_h, back_h, small_h, hidden_h, gain, cotangent,
    hidden_grad, chan, head, norm,
    part, rest, gate, left, right, back, small, hidden,
    cot_v, block, near, all_block, all_near, sends, recvs, near_s, near_r, load, local,
):
    group, q = lax.axis_index("dp"), lax.axis_index("seq")
    me = group * parts + q
    cw = INNER // parts
    cc = cw + 2 * N
    everyone = all_peers(groups, parts)
    fetches = [
        pltpu.make_async_copy(source, target, load.at[k])
        for k, (source, target) in enumerate(
            [(back_h, back), (hidden_h, hidden), (part_h, part), (gate_h, gate),
             (left_h, left), (right_h, right), (small_h, small), (rest_h, rest),
             (cotangent, cot_v)]
        )
    ]
    for copy in fetches:
        copy.start()
    barrier = pltpu.get_barrier_semaphore()
    for device in everyone:
        pl.semaphore_signal(barrier, inc=1, device_id=device, device_id_type=MESH)
    for copy in fetches[:8]:
        copy.wait()
    total = small[0]
    for k in range(1, groups):
        total = total + small[k]
    near[...] = total
    rows = 32

    def summed(at):
        down = back[at, :]
        tokens = hidden[at, :].astype(F32)
        mean = jnp.sum(tokens * tokens, axis=-1, keepdims=True) / D
        return down, tokens, lax.rsqrt(mean + EPS_IN)

    def gain_rows(i, dgain):
        at = pl.ds(pl.multiple_of(i * rows, rows), rows)
        down, tokens, scale = summed(at)
        return dgain + jnp.sum(down * tokens * scale, axis=0, keepdims=True)

    dgain = lax.fori_loop(0, hidden.shape[0] // rows, gain_rows, jnp.zeros((1, D), F32))
    tail = rest[:, : 2 * N + H]
    squares = total_of(tail * tail)
    for k in range(parts):
        x = part[k].astype(F32)
        g = gate[k].astype(F32)
        squares = squares + total_of(x * x + g * g)
    squares = squares + total_of(left[...] * left[...]) + total_of(right[...] * right[...])
    for k in range(D // LANES):
        block[k : k + 1, :] = dgain[:, k * LANES : (k + 1) * LANES]
    block[D // LANES :, :] = jnp.broadcast_to(squares, (8, LANES))
    pl.semaphore_wait(barrier, len(everyone))
    copies = [
        remote(block, all_block.at[me], sends, recvs, k, peer) for k, peer in enumerate(everyone)
    ]
    copies += [
        remote(near, all_near.at[q], near_s, near_r, k, peer)
        for k, peer in enumerate(seq_peers(parts))
    ]
    copies += [
        pltpu.make_async_copy(block, all_block.at[me], local.at[0]),
        pltpu.make_async_copy(near, all_near.at[q], local.at[1]),
    ]
    for copy in copies:
        copy.start()
    fetches[8].wait()

    def grad_rows(i, carry):
        at = pl.ds(pl.multiple_of(i * rows, rows), rows)
        down, tokens, scale = summed(at)
        scaled = down * gain[...]
        inner = jnp.sum(scaled * tokens, axis=-1, keepdims=True) / D
        direct = cot_v[0, at, :].astype(F32)
        for k in range(1, LEVELS):
            direct = direct + cot_v[k, at, :].astype(F32)
        hidden_grad[at, :] = (
            scale * scaled - tokens * (scale * scale * scale * inner) + direct
        )
        return carry

    lax.fori_loop(0, hidden.shape[0] // rows, grad_rows, 0)
    for copy in copies:
        copy.wait()
    total = jnp.sum(all_block[...], axis=0)
    own, wide = cw // LANES, cc // LANES
    span = CONV_CH // LANES
    for tap in range(TAPS + 1):
        for k in range(parts):
            at = tap * span + k * own
            chan[at : at + own, :] = all_near[k, tap * wide : tap * wide + own, :]
        shared = all_near[0, tap * wide + own : (tap + 1) * wide, :]
        for k in range(1, parts):
            shared = shared + all_near[k, tap * wide + own : (tap + 1) * wide, :]
        chan[tap * span + INNER // LANES : (tap + 1) * span, :] = shared
    at = (TAPS + 1) * span
    chan[at : at + D // LANES, :] = total[: D // LANES]
    at = at + D // LANES
    for k in range(parts):
        first = (TAPS + 1) * wide
        chan[at + k * own : at + (k + 1) * own, :] = all_near[k, first : first + own, :]
        head[k : k + 1, :] = all_near[k, first + own : first + own + 1, :]
    squares = (
        total[D // LANES : D // LANES + 1, :1]
        + total_of(chan[:CHAN_ROWS, :] * chan[:CHAN_ROWS, :])
        + total_of(head[:parts, :] * head[:parts, :])
    )
    grad_norm = jnp.sqrt(squares)
    norm[0:1, :] = jnp.broadcast_to(grad_norm, (1, LANES))
    norm[1:2, :] = jnp.broadcast_to(jnp.minimum(1.0, CLIP / grad_norm), (1, LANES))


def gradient_norm(
    collective_id, part, rest, gate, left, right, back, small, hidden, gain, cotangent, groups
):
    parts = part.shape[0]
    devices = groups * parts
    sem = pltpu.SemaphoreType.DMA
    vmem = pl.BlockSpec(memory_space=pltpu.VMEM)
    hbm = pl.BlockSpec(memory_space=pltpu.HBM)
    block = (D // LANES + 8, LANES)
    chan_rows = -(-CHAN_ROWS // 8) * 8
    return pl.pallas_call(
        functools.partial(norm_kernel, groups, parts),
        in_specs=[*([hbm] * 8), vmem, hbm],
        out_specs=[vmem] * 4,
        out_shape=[
            jax.ShapeDtypeStruct(hidden.shape, F32),
            jax.ShapeDtypeStruct((chan_rows, LANES), F32),
            jax.ShapeDtypeStruct((8, LANES), F32),
            jax.ShapeDtypeStruct((8, LANES), F32),
        ],
        scratch_shapes=[
            *[
                pltpu.VMEM(a.shape, a.dtype)
                for a in (part, rest, gate, left, right, back, small, hidden)
            ],
            pltpu.VMEM(cotangent.shape, BF16),
            pltpu.VMEM(block, F32),
            pltpu.VMEM(small.shape[1:], F32),
            pltpu.VMEM((devices,) + block, F32),
            pltpu.VMEM((parts,) + small.shape[1:], F32),
            sem((devices - 1,)), sem((devices - 1,)), sem((parts - 1,)), sem((parts - 1,)),
            sem((9,)), sem((2,)),
        ],
        compiler_params=pltpu.CompilerParams(
            collective_id=collective_id, has_side_effects=True, vmem_limit_bytes=63 * 2**20
        ),
        name="gradient_norm",
    )(part, rest, gate, left, right, back, small, hidden, gain, cotangent)


BLOCKS = 4


def update_kernel(
    parts, norm, part_h, rest_h, gate_h, left_h, right_h, hidden_grad, block, *refs
):
    ins, refs = refs[:6], refs[6:]
    hidden_out, block_out, outs, refs = refs[0], refs[1], refs[2:10], refs[10:]
    held, made = refs[:6], refs[6:14]
    part, rest, gate, left, right, hidden_v, block_v, load, store, grads = refs[14:]
    clip = norm[1:2, :1]
    cw = INNER // parts
    fetches = [
        pltpu.make_async_copy(source, target, grads.at[k])
        for k, (source, target) in enumerate(
            [(part_h, part), (gate_h, gate), (left_h, left), (right_h, right), (rest_h, rest),
             (hidden_grad, hidden_v), (block, block_v)]
        )
    ]
    for copy in fetches[:5]:
        copy.start()

    def at(a, i):
        rows = ins[a].shape[0] // BLOCKS
        return pl.ds(i * rows, rows)

    loads = [
        [
            pltpu.make_async_copy(ins[a].at[at(a, i)], held[a].at[at(a, i)], load.at[a * BLOCKS + i])
            for a in range(6)
        ]
        for i in range(BLOCKS)
    ]
    for weight in (0, 3):
        for i in range(BLOCKS):
            for a in range(weight, weight + 3):
                loads[i][a].start()
    for copy in fetches[5:]:
        copy.start()
    stores = []

    def update(weight, rows, lanes, gradient, rate, decay):
        first = 0 if weight == 0 else 4
        new, moment, second = adam_tile(
            held[weight][rows, lanes], clip * gradient, held[weight + 1][rows, lanes],
            held[weight + 2][rows, lanes], rate, decay,
        )
        made[first][rows, lanes] = new
        made[first + 1][rows, lanes] = moment
        made[first + 2][rows, lanes] = second
        made[first + 3][rows, lanes] = new.astype(BF16)

    def send(first, rows, i):
        for a in range(first, first + 4):
            copy = pltpu.make_async_copy(
                made[a].at[rows], outs[a].at[rows], store.at[a * BLOCKS + i]
            )
            copy.start()
            stores.append(copy)

    for copy in fetches[:5]:
        copy.wait()
    for i in range(BLOCKS):
        rows = at(0, i)
        for a in range(3):
            loads[i][a].wait()
        for source, first in ((gate, 0), (part, INNER)):

            def step(k, carry, source=source, first=first, rows=rows):
                to = pl.ds(pl.multiple_of(first + k * cw, cw), cw)
                update(0, rows, to, source[k, rows, :cw].astype(F32), 0.02, 0.1)
                return carry

            lax.fori_loop(0, parts, step, 0)
        update(0, rows, slice(2 * INNER, E_IN), rest[rows, : 2 * N + H], 0.02, 0.1)
        send(0, rows, i)
    fetches[5].wait()
    fetches[6].wait()
    for source, target, k in ((hidden_v, hidden_out, 7), (block_v, block_out, 8)):
        copy = pltpu.make_async_copy(source, target, grads.at[k])
        copy.start()
        stores.append(copy)
    for i in range(BLOCKS):
        rows = at(3, i)
        for a in range(3, 6):
            loads[i][a].wait()
        update(3, rows, slice(0, LEFT), left[rows, :], 0.03, 0.1)
        update(3, rows, slice(LEFT, D), right[rows, :], 0.03, 0.1)
        send(4, rows, i)
    for copy in stores:
        copy.wait()


def update_weights(norm, part, rest, gate, left, right, hidden_grad, block, weights):
    parts = part.shape[0]
    w_in, w_out = weights[0], weights[3]
    sem = pltpu.SemaphoreType.DMA
    vmem = pl.BlockSpec(memory_space=pltpu.VMEM)
    hbm = pl.BlockSpec(memory_space=pltpu.HBM)
    made = [
        jax.ShapeDtypeStruct(w.shape, dtype) for w in (w_in, w_out) for dtype in (F32, F32, F32, BF16)
    ]
    return pl.pallas_call(
        functools.partial(update_kernel, parts),
        in_specs=[vmem, *([hbm] * 13)],
        out_specs=[hbm] * 10,
        out_shape=[
            jax.ShapeDtypeStruct(hidden_grad.shape, F32),
            jax.ShapeDtypeStruct(block.shape, BF16),
            *made,
        ],
        scratch_shapes=[
            *[pltpu.VMEM(w.shape, F32) for w in weights],
            *[pltpu.VMEM(m.shape, m.dtype) for m in made],
            *[
                pltpu.VMEM(a.shape, a.dtype)
                for a in (part, rest, gate, left, right, hidden_grad, block)
            ],
            sem((6 * BLOCKS,)), sem((8 * BLOCKS,)), sem((9,)),
        ],
        compiler_params=pltpu.CompilerParams(vmem_limit_bytes=63 * 2**20),
        name="update_weights",
    )(norm, part, rest, gate, left, right, hidden_grad, block, *weights)


WO_ALL, WO_REST = pl.ds(0, SPLIT), pl.ds(SPLIT, D - SPLIT)


class LineGather:
    def __init__(self, line, z, core, q, slot, own, sends, recvs):
        self.line, self.z, self.core, self.q = line, z, core, q
        self.slot, self.own, self.sends, self.recvs = slot, own, sends, recvs

    def along(self, from_z, up, first=False):
        to = self.z + 1 if up else self.z - 1
        return remote(
            self.own if first else self.slot(from_z),
            self.slot(from_z),
            self.sends.at[0 if up else 1],
            self.recvs.at[0 if up else 1],
            from_z,
            (2 * to + self.core, self.q),
        )

    def push(self, t):
        z, line = self.z, self.line

        @pl.when((z - t >= 0) & (z < line - 1))
        def _():
            self.along(z - t, True, t == 0).start()

        @pl.when((z + t <= line - 1) & (z > 0))
        def _():
            self.along(z + t, False, t == 0).start()

    def pushed(self, t):
        z, line = self.z, self.line

        @pl.when((z - t >= 0) & (z < line - 1))
        def _():
            self.along(z - t, True, t == 0).wait_send()

        @pl.when((z + t <= line - 1) & (z > 0))
        def _():
            self.along(z + t, False, t == 0).wait_send()

    def step(self, t, got=None, push=True):
        z, line = self.z, self.line

        @pl.when(z - t >= 0)
        def _():
            self.along(z - t, True).wait_recv()

            if push:

                @pl.when(z < line - 1)
                def _():
                    self.along(z - t, True).start()

            if got is not None:
                got(z - t)

        @pl.when(z + t <= line - 1)
        def _():
            self.along(z + t, False).wait_recv()

            if push:

                @pl.when(z > 0)
                def _():
                    self.along(z + t, False).start()

            if got is not None:
                got(z + t)


class LineGathers:
    def __init__(self, line, z, core, q, slot, own, sends, recvs):
        half = own.shape[0] // 2
        self.line = line
        self.halves = []
        for h in range(2):
            rows = pl.ds(h * half, half)
            self.halves.append(
                LineGather(
                    line, z, core, q, lambda from_z, rows=rows: slot(from_z).at[rows],
                    own.at[rows], sends.at[h], recvs.at[h],
                )
            )

    def push(self, t):
        for part in self.halves:
            part.push(t)

    def step(self, t, got=None, push=True):
        self.halves[0].step(t, None, push)
        self.halves[1].step(t, got, push)

    def pushed(self):
        for t in range(self.line - 1):
            for part in self.halves:
                part.pushed(t)


class PlaneGather:
    def __init__(self, parts, slot, own, sends, recvs, base=0):
        self.parts, self.slot, self.own = parts, slot, own
        self.sends, self.recvs, self.base = sends, recvs, base
        self.group, self.q = lax.axis_index("dp"), lax.axis_index("seq")
        if parts == 4:
            self.near = [self.q + 1 - 2 * lax.rem(self.q, 2), lax.rem(self.q + 2, 4)]
            self.half = own.shape[0] // 2

    def early(self):
        to = self.near if self.parts == 4 else [peer[1] for peer in seq_peers(self.parts)]
        return [
            remote(
                self.own, self.slot(self.q), self.sends, self.recvs, self.base + k, (self.group, d)
            )
            for k, d in enumerate(to)
        ]

    def late(self):
        if self.parts != 4:
            return []
        copies = []
        for h in range(2):
            block = self.slot(self.near[h]).at[pl.ds(h * self.half, self.half)]
            to = (self.group, self.near[1 - h])
            copies.append(remote(block, block, self.sends, self.recvs, self.base + 2 + h, to))
        return copies

    def start(self):
        for copy in self.early():
            copy.start()

    def turn(self):
        if self.parts == 4:
            for copy in self.early():
                copy.wait()
            for copy in self.late():
                copy.start()

    def finish(self):
        for copy in self.late() if self.parts == 4 else self.early():
            copy.wait()


def chan_rows_of(chan_len, devices):
    return -(-((devices - 1) * chan_len // LANES + 8) // 8) * 8


def unpack_chan(
    chan_len, parts, q, all_chan, full, hp, gain_in, gain_out, taps, heads, skip, spread, gather
):
    cw = INNER // parts
    hq = H // parts
    own, span, shared = cw // LANES, CONV_CH // LANES, 2 * N // LANES
    full[...] = jnp.zeros_like(full)
    for o in range(all_chan.shape[0]):
        at = o * chan_len // LANES
        full[at : at + 8, :] += all_chan[o]
    taps[...] = jnp.zeros_like(taps)
    for tap in range(TAPS + 1):
        for b in range(own):
            taps[tap : tap + 1, b * LANES : (b + 1) * LANES] = full[
                pl.ds(tap * span + q * own + b, 1), :
            ]
        for b in range(shared):
            at = tap * span + INNER // LANES + b
            taps[tap : tap + 1, cw + b * LANES : cw + (b + 1) * LANES] = full[at : at + 1, :]
    at = (TAPS + 1) * span
    for b in range(D // LANES):
        gain_in[:, b * LANES : (b + 1) * LANES] = full[at + b : at + b + 1, :]
    at = at + D // LANES
    for b in range(own):
        gain_out[:, b * LANES : (b + 1) * LANES] = full[pl.ds(at + q * own + b, 1), :]
    for out, axis in ((spread, 0), (gather, 1)):
        head = lax.broadcasted_iota(jnp.int32, out.shape, axis)
        channel = lax.broadcasted_iota(jnp.int32, out.shape, 1 - axis)
        inside = (channel >= head * P_SIZE) & (channel < (head + 1) * P_SIZE)
        out[...] = jnp.where(inside, 1.0, 0.0).astype(BF16)
    ours = own_heads_first(hp[...], hq)
    row = lax.broadcasted_iota(jnp.int32, ours.shape, 0)
    heads[...] = jnp.where(row == 0, ours, jnp.where(row == 1, -jnp.exp(ours), 0.0))
    skip[...] = spread_heads(ours, spread[...])[2:3, :]


def collect_kernel(
    groups, parts, chan_len, hidden, w_in_h, w_own_h, chan, hp,
    hid_out, w_out, gate_out, wo_out, gain_in, gain_out, taps, heads, skip, spread, gather,
    chan_out, full, w_in, w_own, blocks, gates, low, chan_s, chan_r, hid_s, hid_r, swap_s, swap_r, gate_s, gate_r,
    wo_s, wo_r, line_s, line_r, lwo_s, lwo_r, core_s, core_r, local,
):
    line = groups // 2
    cw = INNER // parts
    cc = cw + 2 * N
    group, q = lax.axis_index("dp"), lax.axis_index("seq")
    z, core = group // 2, lax.rem(group, 2)
    sibling = (2 * z + 1 - core, q)
    peers = seq_peers(parts)
    everyone = all_peers(groups, parts)
    loads = [
        pltpu.make_async_copy(w_in_h, w_in, local.at[5]),
        pltpu.make_async_copy(w_own_h, w_own, local.at[6]),
    ]
    for copy in loads:
        copy.start()
    barrier = pltpu.get_barrier_semaphore()
    for device in everyone:
        pl.semaphore_signal(barrier, inc=1, device_id=device, device_id_type=MESH)
    for copy in loads:
        copy.wait()
    shared = w_in[:, 2 * INNER :].astype(BF16)
    for part in range(parts):
        at = INNER + part * cw
        blocks[part, :, :cw] = w_in[:, at : at + cw].astype(BF16)
        blocks[part, :, cw : cc + H] = shared
        blocks[part, :, cc + H :] = jnp.zeros((w_in.shape[0], LANES - H), BF16)
    low[...] = w_own[...].astype(BF16)
    pl.semaphore_wait(barrier, len(everyone))
    swaps = []
    for k, peer in enumerate(peers):
        copy = remote(blocks.at[peer[1]], w_out.at[group, q], swap_s, swap_r, k, peer)
        copy.start()
        swaps.append(copy)
    outs = LineGather(
        line, z, core, q, lambda from_z: wo_out.at[2 * from_z + core, q, :, WO_REST],
        low.at[:, WO_REST], lwo_s, lwo_r,
    )
    outs.push(0)
    own = [
        pltpu.make_async_copy(blocks.at[q], w_out.at[group, q], local.at[0]),
        pltpu.make_async_copy(hidden, hid_out.at[q], local.at[1]),
        pltpu.make_async_copy(chan, chan_out.at[group * parts + q], local.at[2]),
        pltpu.make_async_copy(low, wo_out.at[group, q], local.at[3]),
    ]
    for copy in own:
        copy.start()
    waiting = []
    chans = [
        remote(chan, chan_out.at[group * parts + q], chan_s, chan_r, k, peer)
        for k, peer in enumerate(everyone)
    ]
    for copy in chans:
        copy.start()
    for part in range(parts):
        gates[part] = w_in[:, part * cw : (part + 1) * cw].astype(BF16)
    copy = pltpu.make_async_copy(gates.at[q], gate_out.at[q], local.at[4])
    copy.start()
    own.append(copy)
    own[0].wait()
    for copy in swaps:
        copy.wait()
    hids = PlaneGather(parts, lambda of: hid_out.at[of], hidden, hid_s, hid_r)
    lows = PlaneGather(parts, lambda of: wo_out.at[group, of], low, wo_s, wo_r)
    hids.start()

    def across(from_z):
        block = w_out.at[2 * from_z + core]
        return remote(block, block, core_s, core_r, from_z, sibling)

    ins = LineGathers(
        line, z, core, q, lambda from_z: w_out.at[2 * from_z + core], w_out.at[group],
        line_s, line_r,
    )
    across(z).start()
    ins.push(0)
    lows.start()
    for t in range(1, line):
        ins.step(t, lambda from_z: across(from_z).start(), t < line - 1)
        if t == 1:
            own[2].wait()
            for copy in chans:
                copy.wait()
            unpack_chan(
                chan_len, parts, q, chan_out, full, hp, gain_in, gain_out, taps, heads, skip,
                spread, gather,
            )
        if t == line - 2:
            outs.step(1)
            hids.turn()
            lows.turn()
            for k, peer in enumerate(peers):
                copy = remote(gates.at[peer[1]], gate_out.at[q], gate_s, gate_r, k, peer)
                copy.start()
                waiting.append(copy)
    ins.pushed()
    outs.step(2, None, False)
    outs.pushed(0)
    outs.pushed(1)
    hids.finish()
    lows.finish()
    for from_z in range(line):
        across(from_z).wait_send()
        block = w_out.at[2 * from_z + 1 - core]
        remote(block, block, core_s, core_r, from_z, sibling).wait_recv()
    for copy in own[1:2] + own[3:] + waiting:
        copy.wait()


def collect(collective_id, hidden, w_in, w_own, chan, hp, chan_len, groups, parts):
    rows = w_in.shape[0]
    line = groups // 2
    cw = INNER // parts
    width = cw + 2 * N + LANES
    sem = pltpu.SemaphoreType.DMA
    hbm = pl.BlockSpec(memory_space=pltpu.HBM)
    vmem = pl.BlockSpec(memory_space=pltpu.VMEM)
    return pl.pallas_call(
        functools.partial(collect_kernel, groups, parts, chan_len),
        in_specs=[hbm, hbm, hbm, vmem, vmem],
        out_specs=[*([hbm] * 4), *([vmem] * 7)],
        out_shape=[
            jax.ShapeDtypeStruct((parts,) + hidden.shape, hidden.dtype),
            jax.ShapeDtypeStruct((groups, parts, rows, width), BF16),
            jax.ShapeDtypeStruct((parts, rows, cw), BF16),
            jax.ShapeDtypeStruct((groups, parts) + w_own.shape, BF16),
            jax.ShapeDtypeStruct((1, D), F32),
            jax.ShapeDtypeStruct((1, cw), F32),
            jax.ShapeDtypeStruct((8, cw + 2 * N), F32),
            jax.ShapeDtypeStruct((8, LANES), F32),
            jax.ShapeDtypeStruct((1, cw), F32),
            jax.ShapeDtypeStruct((LANES, cw), BF16),
            jax.ShapeDtypeStruct((cw, LANES), BF16),
        ],
        scratch_shapes=[
            pltpu.VMEM((groups * parts,) + chan.shape, F32),
            pltpu.VMEM((chan_rows_of(chan_len, groups * parts), LANES), F32),
            pltpu.VMEM(w_in.shape, F32),
            pltpu.VMEM(w_own.shape, F32),
            pltpu.VMEM((parts, rows, width), BF16),
            pltpu.VMEM((parts, rows, cw), BF16),
            pltpu.VMEM(w_own.shape, BF16),
            *([sem((groups * parts - 1,))] * 2),
            *([sem((parts + 1,))] * 8),
            *([sem((2, 2, line))] * 2), *([sem((2, line))] * 2),
            sem((line,)), sem((line,)), sem((7,)),
        ],
        compiler_params=pltpu.CompilerParams(
            collective_id=collective_id, has_side_effects=True, vmem_limit_bytes=63 * 2**20
        ),
        name="collect",
    )(hidden, w_in, w_own, chan, hp)


def forward_kernel(
    groups, parts, cw,
    hidden_h, wx_h, gate_h, wo_in, gain_in, gain_out, taps, heads, skip, spread,
    normed_h, px_h, y_h, states_h, z_h, u_h, stat_h, wz_h, wo,
    hidden, wx, wz, normed, px, y, states, zs, us, stats, xbuf, state, xdt, carried,
    line_s, line_r, lwo_s, lwo_r, wide_s, wide_r, stat_s, stat_r, core_s, core_r, wo_s, wo_r, out_s, out_r, u_s, u_r, load, store,
):
    line = groups // 2
    cc = cw + 2 * N
    length = px.shape[0]
    chunks = length // CHUNK
    group, q = lax.axis_index("dp"), lax.axis_index("seq")
    z, core = group // 2, lax.rem(group, 2)
    sibling = (2 * z + 1 - core, q)
    peers = mirror_peers(parts)
    loads = [
        pltpu.make_async_copy(source, target, load.at[k])
        for k, (source, target) in enumerate(
            [(hidden_h, hidden), (wx_h, wx), (gate_h, wz.at[group])]
        )
    ]
    for copy in loads:
        copy.start()
    greet(peers + dp_peers(groups))

    outs = LineGather(
        line, z, core, q, lambda from_z: wo.at[2 * from_z + core, q, :, WO_REST],
        wo.at[group, q, :, WO_REST], lwo_s, lwo_r,
    )
    wides = LineGather(
        line, z, core, q, lambda from_z: wo.at[2 * from_z + core, :, :, WO_ALL],
        wo.at[group, :, :, WO_ALL], wide_s, wide_r,
    )

    def planes(t, act):
        for from_z, there in ((z - t, z - t >= 0), (z + t, z + t <= line - 1)):

            @pl.when(there)
            def _(from_z=from_z):
                block = wo.at[2 * from_z + core]
                act(
                    PlaneGather(
                        parts, lambda of: block.at[of, :, WO_REST], block.at[q, :, WO_REST],
                        out_s, out_r,
                        from_z * (parts + 1),
                    )
                )

    outs.push(2)
    planes(1, PlaneGather.start)
    planes(2, PlaneGather.start)

    def parity(from_z, of, columns):
        block = wo.at[2 * from_z + of, :, :, columns]
        at = from_z if columns is WO_REST else line + from_z
        return remote(block, block, wo_s, wo_r, at, sibling)

    def across_planes(t):
        planes(t, PlaneGather.finish)
        for from_z, there in ((z - t, z - t >= 0), (z + t, z + t <= line - 1)):

            @pl.when(there)
            def _(from_z=from_z):
                parity(from_z, core, WO_REST).start()

    def across_wide(from_z):
        parity(from_z, core, WO_ALL).start()

    across_wide(z)
    parity(z, core, WO_REST).start()

    def across(from_z):
        block = wz.at[2 * from_z + core]
        return remote(block, block, core_s, core_r, from_z, sibling)

    gates = LineGathers(
        line, z, core, q, lambda from_z: wz.at[2 * from_z + core], wz.at[group], line_s, line_r
    )
    loads[2].wait()
    across(z).start()
    gates.push(0)
    loads[0].wait()

    def norm_rows(i, carry):
        rows = pl.ds(pl.multiple_of(i * 32, 32), 32)
        tokens = hidden[rows, :].astype(F32)
        mean = jnp.sum(tokens * tokens, axis=-1, keepdims=True) / D
        normed[rows, :] = (tokens * lax.rsqrt(mean + EPS_IN) * gain_in[...]).astype(BF16)
        return carry

    lax.fori_loop(0, length // 32, norm_rows, 0)
    loads[1].wait()
    tall = 256

    def project_rows(i, carry):
        rows = pl.ds(pl.multiple_of(i * tall, tall), tall)
        px[rows, :] = dot(normed[rows, :], wx[...])
        return carry

    lax.fori_loop(0, length // tall, project_rows, 0)
    stores = [
        pltpu.make_async_copy(normed, normed_h, store.at[0]),
        pltpu.make_async_copy(px, px_h, store.at[1]),
    ]
    for copy in stores:
        copy.start()
    state[...] = jnp.zeros_like(state)
    xbuf[0:8, :] = jnp.zeros((8, cc), F32)

    def scan_rows(i, carry):
        for t in range(1, line - 1):

            @pl.when(i == min(5 * t - 4, chunks - 1))
            def _(t=t):
                gates.step(t, lambda from_z: across(from_z).start(), t < line - 1)
                if t == line - 2:
                    wides.push(0)

        for t in range(3, line):

            @pl.when(i == min(2 * t - 3, chunks - 1))
            def _(t=t):
                outs.step(t, None, t < line - 1)
                planes(t, PlaneGather.start)

        @pl.when(i == min(5, chunks - 1))
        def _():
            planes(1, PlaneGather.turn)
            planes(2, PlaneGather.turn)

        rows = pl.ds(pl.multiple_of(i * CHUNK, CHUNK), CHUNK)
        scan_forward_step(
            cw, px.at[rows], taps, heads, skip, spread, y.at[rows], states.at[i],
            xbuf, state, xdt, carried,
        )
        return carry

    lax.fori_loop(0, chunks, scan_rows, 0)
    for source, target, at in ((y, y_h, 2), (states, states_h, 3)):
        copy = pltpu.make_async_copy(source, target, store.at[at])
        copy.start()
        stores.append(copy)
    for t in range(3, line):
        planes(t, PlaneGather.turn)
    gates.step(line - 1, lambda from_z: across(from_z).start(), False)
    for from_z in range(line):
        across(from_z).wait_send()
        block = wz.at[2 * from_z + 1 - core]
        remote(block, block, core_s, core_r, from_z, sibling).wait_recv()
    gates.pushed()
    for t in range(2, line - 1):
        outs.pushed(t)
    copy = pltpu.make_async_copy(wz, wz_h, store.at[4])
    copy.start()
    stores.append(copy)
    lane = lax.broadcasted_iota(jnp.int32, (1, LANES), 1)
    wide = 512

    def gate_rows(rows):
        gate_in = dot(normed[rows, :], wz[...].reshape(D, cw))
        zs[rows, :] = gate_in
        gated = y[rows, :] * (gate_in * jax.nn.sigmoid(gate_in))
        us[rows, :] = (gated * gain_out[...]).astype(BF16)
        squares = jnp.zeros((tall, LANES), F32)
        for b in range(cw // wide):
            block = gated[:, b * wide : (b + 1) * wide]
            total = jnp.sum(block * block, axis=-1, keepdims=True)
            level = level_of(q * cw + b * wide, wide)
            squares = squares + jnp.where(lane == level, total, 0.0)
        stats[:, rows] = squares.T[:8, :]

    waiting = []
    tokens = length // parts
    for k, dest in enumerate([peer[1] for peer in peers] + [q]):

        def block_rows(i, carry, dest=dest):
            gate_rows(pl.ds(pl.multiple_of(dest * tokens + i * tall, tall), tall))
            return carry

        lax.fori_loop(0, tokens // tall, block_rows, 0)
        ours = us.at[pl.ds(pl.multiple_of(dest * tokens, tokens), tokens)]
        stat = stats.at[:, pl.ds(pl.multiple_of(dest * tokens, tokens), tokens)]
        if k < len(peers):
            some = [
                remote(ours, u_h.at[q], u_s, u_r, k, peers[k]),
                remote(stat, stat_h.at[q], stat_s, stat_r, k, peers[k]),
            ]
        else:
            some = [
                pltpu.make_async_copy(ours, u_h.at[q], store.at[6]),
                pltpu.make_async_copy(stat, stat_h.at[q], store.at[7]),
            ]
        for copy in some:
            copy.start()
        waiting += some
        if k == 0:
            wides.step(1, across_wide)
        if k == 1:
            for t in range(2, line - 1):
                wides.step(t, across_wide)
        if k in (1, 2):
            across_planes(k)
    copy = pltpu.make_async_copy(zs, z_h, store.at[5])
    copy.start()
    stores.append(copy)

    for t in range(3, line):
        across_planes(t)
    wides.step(line - 1, across_wide, False)
    for t in range(line - 1):
        wides.pushed(t)
    for copy in waiting + stores:
        copy.wait()
    for columns in (WO_REST, WO_ALL):
        for d in range(line):
            parity(d, core, columns).wait_send()
            parity(d, 1 - core, columns).wait_recv()


def forward(collective_id, hidden, wx, gate, wo, gain_in, gain_out, taps, heads, skip, spread):
    groups, parts = wo.shape[:2]
    line = groups // 2
    length = hidden.shape[0]
    rows, cw = gate.shape[1:]
    cc = cw + 2 * N
    width = cc + LANES
    chunks = length // CHUNK
    sem = pltpu.SemaphoreType.DMA
    hbm = pl.BlockSpec(memory_space=pltpu.HBM)
    vmem = pl.BlockSpec(memory_space=pltpu.VMEM)
    u = jax.ShapeDtypeStruct((parts, length // parts, cw), BF16)
    stat = jax.ShapeDtypeStruct((parts, 8, length // parts), F32)
    made = [
        jax.ShapeDtypeStruct((length, D), BF16),
        jax.ShapeDtypeStruct((length, width), F32),
        jax.ShapeDtypeStruct((length, cw), F32),
        jax.ShapeDtypeStruct((chunks, N, cw), BF16),
        jax.ShapeDtypeStruct((length, cw), F32),
        jax.ShapeDtypeStruct((length, cw), BF16),
        jax.ShapeDtypeStruct((8, length), F32),
    ]
    wz = jax.ShapeDtypeStruct((groups, parts, rows, cw), BF16)
    return pl.pallas_call(
        functools.partial(forward_kernel, groups, parts, cw),
        in_specs=[*([hbm] * 4), *([vmem] * 6)],
        out_specs=[hbm] * 9,
        out_shape=[*made[:-2], u, stat, wz, jax.ShapeDtypeStruct(wo.shape, BF16)],
        input_output_aliases={3: 8},
        scratch_shapes=[
            pltpu.VMEM(hidden.shape, BF16),
            pltpu.VMEM(wx.shape, BF16),
            pltpu.VMEM(wz.shape, BF16),
            *[pltpu.VMEM(m.shape, m.dtype) for m in made],
            pltpu.VMEM((CHUNK + 8, cc), F32),
            pltpu.VMEM((N, cw), F32),
            pltpu.VMEM((CHUNK, cw), BF16),
            pltpu.VMEM((CHUNK, cw), F32),
            *([sem((2, 2, line))] * 2), *([sem((2, line))] * 4),
            sem((parts - 1,)), sem((parts - 1,)),
            sem((line,)), sem((line,)), sem((2 * line,)), sem((2 * line,)),
            sem((line * (parts + 1),)), sem((line * (parts + 1),)),
            sem((parts - 1,)), sem((parts - 1,)),
            sem((3,)), sem((8,)),
        ],
        compiler_params=pltpu.CompilerParams(
            collective_id=collective_id, has_side_effects=True, vmem_limit_bytes=63 * 2**20
        ),
        name="forward",
    )(hidden, wx, gate, wo, gain_in, gain_out, taps, heads, skip, spread)


def add_blocks(out, a, b, rows, steps):
    def step(i, carry):
        at = pl.ds(pl.multiple_of(i * rows, rows), rows)
        out[at] = (a[at].astype(F32) + b[at].astype(F32)).astype(out.dtype)
        return carry

    lax.fori_loop(0, steps, step, 0)


def level_of(channel, width):
    return sum((channel >= level_width(k)).astype(jnp.int32) for k in range(LEVELS - 1))


def mirror_peers(parts):
    group, q = lax.axis_index("dp"), lax.axis_index("seq")
    if parts != 4:
        return seq_peers(parts)
    return [(group, 3 - q), (group, q + 1 - 2 * lax.rem(q, 2)), (group, lax.rem(q + 2, 4))]


def middle_kernel(
    groups, parts, cw,
    u_h, stat_h, wo, cot_h, tokens_h,
    back_h, coef_h, block_h, left_h, right_h,
    u, stats, cot, tokens, mixed, branch, norms, pulls, back, coefs, weights, sent, held, left, right,
    back_s, back_r, coef_s, coef_r, core_s, core_r, fetch, load, store, local,
):
    line = groups // 2
    group, q = lax.axis_index("dp"), lax.axis_index("seq")
    z, core = group // 2, lax.rem(group, 2)
    sibling = (2 * z + 1 - core, q)
    peers = mirror_peers(parts)
    loads = [
        pltpu.make_async_copy(stat_h, stats, load.at[3]),
        pltpu.make_async_copy(cot_h, cot, load.at[1]),
        pltpu.make_async_copy(u_h, u, load.at[0]),
        pltpu.make_async_copy(tokens_h, tokens, load.at[2]),
    ]
    for copy in loads:
        copy.start()
    greet(peers + [sibling])
    for copy in loads[:2]:
        copy.wait()

    terms = stats[0]
    for part in range(1, parts):
        terms = terms + stats[part]
    terms = jnp.concatenate([terms, jnp.zeros((LANES - 8, terms.shape[1]), F32)], axis=0).T
    squares = jnp.zeros((terms.shape[0], 1), F32)
    for k in range(LEVELS):
        squares = squares + terms[:, k : k + 1]
        norms[:, k : k + 1] = lax.rsqrt(squares / level_width(k) + EPS_OUT)
    rows = 32

    def mix_rows(i, carry):
        at = pl.ds(pl.multiple_of(i * rows, rows), rows)
        running = norms[at, LEVELS - 1 : LEVELS] * cot[LEVELS - 1, at, :].astype(F32)
        mixed[LEVELS - 1, at, :] = running.astype(BF16)
        for k in reversed(range(LEVELS - 1)):
            running = running + norms[at, k : k + 1] * cot[k, at, :].astype(F32)
            mixed[k, at, :] = running.astype(BF16)
        return carry

    lax.fori_loop(0, tokens.shape[0] // rows, mix_rows, 0)

    width = INNER // groups
    per = WIDE // width
    slots = weights.shape[0]
    dests = [peer[1] for peer in peers] + [q]
    firsts = [dest * cw + b * WIDE for dest in dests for b in range(cw // WIDE)]
    firsts += [b * WIDE for b in range(INNER // WIDE)]

    def get(i):
        return pltpu.make_async_copy(
            wo.at[pl.ds(firsts[i] // width, per)], weights.at[i % slots], fetch.at[i % slots]
        )

    def block_of(i):
        get(i).wait()
        return weights[i % slots].reshape(WIDE, D)

    for i in range(slots - 1):
        get(i).start()
    outgoing = []
    for i in range(len(dests) * (cw // WIDE)):
        get(i + slots - 1).start()
        at, b = divmod(i, cw // WIDE)
        lanes = slice(b * WIDE, (b + 1) * WIDE)
        level = level_of(firsts[i], WIDE)
        back[dests[at], :, lanes] = dot(mixed[level], block_of(i), NT).astype(BF16)
        if b == cw // WIDE - 1:
            if at < len(peers):
                copy = remote(back.at[dests[at]], back_h.at[q], back_s, back_r, at, peers[at])
            else:
                copy = pltpu.make_async_copy(back.at[q], back_h.at[q], local.at[0])
            copy.start()
            outgoing.append(copy)
    first = len(dests) * (cw // WIDE)
    for copy in loads[2:]:
        copy.wait()
    branch[...] = jnp.zeros_like(branch)
    for b in range(INNER // WIDE):
        if first + b + slots - 1 < len(firsts):
            get(first + b + slots - 1).start()
        part, at = divmod(b * WIDE, cw)
        branch[...] += dot(u[part, :, at : at + WIDE], block_of(first + b))
        for k in range(LEVELS):
            if level_width(k) == (b + 1) * WIDE:

                def level_rows(i, carry, k=k):
                    at = pl.ds(pl.multiple_of(i * rows, rows), rows)
                    norm = norms[at, k : k + 1]
                    total = branch[at, :]
                    inner = jnp.sum(cot[k, at, :].astype(F32) * total, axis=-1, keepdims=True)
                    pulls[at, k : k + 1] = norm * norm * norm * (inner / level_width(k))
                    cot[k, at, :] = (tokens[at, :].astype(F32) + norm * total).astype(BF16)
                    return carry

                lax.fori_loop(0, tokens.shape[0] // rows, level_rows, 0)
                copy = pltpu.make_async_copy(cot.at[k], block_h.at[k], store.at[k])
                copy.start()
                outgoing.append(copy)
    coef = jnp.zeros((tokens.shape[0], 1), F32)
    lane = lax.broadcasted_iota(jnp.int32, (1, LANES), 1)
    packed = jnp.zeros((tokens.shape[0], LANES), F32)
    for k in reversed(range(LEVELS)):
        coef = coef + pulls[:, k : k + 1]
        high, rest = two_terms(coef)
        packed = jnp.where(lane == k, high.astype(F32), packed)
        packed = jnp.where(lane == LEVELS + k, rest.astype(F32), packed)
    coefs[...] = packed.astype(BF16)
    for k, peer in enumerate(peers):
        copy = remote(coefs, coef_h.at[q], coef_s, coef_r, k, peer)
        copy.start()
        outgoing.append(copy)
    copy = pltpu.make_async_copy(coefs, coef_h.at[q], local.at[1])
    copy.start()
    outgoing.append(copy)

    share = width // parts

    def product(of, cols):
        channel = of * width
        lanes = pl.ds(pl.multiple_of(lax.rem(channel, cw), width), width)
        return dot(u[channel // cw, :, lanes], mixed[level_of(channel, width), :, cols], TN)

    cores = []
    for d in range(line):

        for cols in (slice(0, D // 2), slice(D // 2, D)):
            sent[d, :, cols] = product(2 * d + 1 - core, cols).astype(BF16)
        copy = remote(sent.at[d], held.at[d], core_s, core_r, d, sibling)
        copy.start()
        cores.append(copy)
    for d in range(line):
        cores[d].wait_recv()
        half = LEFT // 2
        for out, target, at, cuts in (
            (left, left_h, 0, ((0, half), (half, LEFT))),
            (right, right_h, 1, ((LEFT, D),)),
        ):
            for low, high in cuts:
                cols = slice(low, high)
                total = product(2 * d + core, cols) + held[d, :, cols].astype(F32)
                total = total.astype(BF16)
                to = slice(low - cuts[0][0], high - cuts[0][0])
                for part in range(parts):
                    out[part, d, :, to] = total[part * share : (part + 1) * share]
            copy = pltpu.make_async_copy(
                out.at[:, d], target.at[:, d], store.at[LEVELS + 2 * d + at]
            )
            copy.start()
            outgoing.append(copy)
    for copy in cores:
        copy.wait_send()
    for copy in outgoing:
        copy.wait()


def middle(collective_id, u, stats, wo, cotangent, tokens):
    groups, parts, share = wo.shape[:3]
    line = groups // 2
    rows, cw = u.shape[1:]
    width = share * parts
    sem = pltpu.SemaphoreType.DMA
    hbm = pl.BlockSpec(memory_space=pltpu.HBM)
    left = (parts, line, share, LEFT)
    right = (parts, line, share, D - LEFT)
    return pl.pallas_call(
        functools.partial(middle_kernel, groups, parts, cw),
        in_specs=[hbm] * 5,
        out_specs=[hbm] * 5,
        out_shape=[
            jax.ShapeDtypeStruct((parts, rows, cw), BF16),
            jax.ShapeDtypeStruct((parts, rows, LANES), BF16),
            jax.ShapeDtypeStruct(cotangent.shape, BF16),
            jax.ShapeDtypeStruct(left, BF16),
            jax.ShapeDtypeStruct(right, BF16),
        ],
        scratch_shapes=[
            pltpu.VMEM(u.shape, BF16),
            pltpu.VMEM(stats.shape, F32),
            pltpu.VMEM(cotangent.shape, BF16),
            pltpu.VMEM(tokens.shape, BF16),
            pltpu.VMEM(cotangent.shape, BF16),
            pltpu.VMEM((rows, D), F32),
            pltpu.VMEM((rows, LANES), F32),
            pltpu.VMEM((rows, LANES), F32),
            pltpu.VMEM((parts, rows, cw), BF16),
            pltpu.VMEM((rows, LANES), BF16),
            pltpu.VMEM((3, WIDE // width, parts, share, D), BF16),
            pltpu.VMEM((line, width, D), BF16),
            pltpu.VMEM((line, width, D), BF16),
            pltpu.VMEM(left, BF16),
            pltpu.VMEM(right, BF16),
            *([sem((parts - 1,))] * 4),
            sem((line,)), sem((line,)), sem((3,)), sem((4,)), sem((LEVELS + 2 * line,)), sem((2,)),
        ],
        compiler_params=pltpu.CompilerParams(
            collective_id=collective_id, has_side_effects=True, vmem_limit_bytes=63 * 2**20
        ),
        name="middle",
    )(u, stats, wo, cotangent, tokens)


def sum_blocks(out, blocks, rows):
    def step(i, carry):
        at = pl.ds(pl.multiple_of(i * rows, rows), rows)
        total = blocks[0][at].astype(F32)
        for block in blocks[1:]:
            total = total + block[at].astype(F32)
        out[at] = total.astype(out.dtype)
        return carry

    lax.fori_loop(0, out.shape[0] // rows, step, 0)


class PlaneSum:
    def __init__(self, parts, group, q, blocks, first, second, sends, recvs, source=None):
        self.parts, self.group, self.q = parts, group, q
        self.source = blocks if source is None else source
        self.blocks, self.first, self.second = blocks, first, second
        self.sends, self.recvs = sends, recvs
        self.half = blocks.shape[1] // 2
        if parts == 4:
            self.near = [q + 1 - 2 * lax.rem(q, 2), lax.rem(q + 2, 4)]
            self.far = 3 - q

    @staticmethod
    def scratch(parts, shape, dtype):
        if parts == 4:
            half = (shape[0] // 2,) + shape[1:]
            first, second, count = (2, 2) + half, (2, 2) + half, 6
        else:
            first, second, count = (parts - 1,) + shape, (1, 16, LANES), parts - 1
        sem = pltpu.SemaphoreType.DMA
        return [pltpu.VMEM(first, dtype), pltpu.VMEM(second, dtype), sem((count,)), sem((count,))]

    def piece(self, of, h, source=None):
        blocks = self.blocks if source is None else source
        return blocks.at[of, pl.ds(h * self.half, self.half)]

    def early(self, h):
        if self.parts != 4:
            return []
        near = self.near[h]
        to = (self.group, near)
        return [
            remote(
                self.piece(of, h, self.source), self.first.at[h, k],
                self.sends, self.recvs, 2 * h + k, to,
            )
            for k, of in enumerate((near, self.far))
        ]

    def late(self, h):
        to = (self.group, self.near[1 - h])
        return remote(
            self.second.at[h, 0], self.second.at[h, 1], self.sends, self.recvs, 4 + h, to
        )

    def direct(self):
        peers = seq_peers(self.parts)
        return [
            remote(self.source.at[peer[1]], self.first.at[k], self.sends, self.recvs, k, peer)
            for k, peer in enumerate(peers)
        ]

    def start_far(self):
        for h in range(2):
            for copy in self.early(h)[1:]:
                copy.start()

    def start_near(self, h):
        for copy in self.early(h)[:1]:
            copy.start()

    def start(self, h):
        for copy in self.early(h):
            copy.start()
        if self.parts != 4 and h == 1:
            for copy in self.direct():
                copy.start()

    def turn(self, rows):
        if self.parts != 4:
            return
        for h in range(2):
            for copy in self.early(h):
                copy.wait()
            beyond = self.piece(self.near[1 - h], h)
            each(self.second.at[h, 0], [beyond, self.first.at[h, 1]], rows)
            self.late(h).start()

    def finish(self, out, rows):
        if self.parts != 4:
            for copy in self.direct():
                copy.wait()
            each(
                out,
                [self.blocks.at[self.q]] + [self.first.at[k] for k in range(self.parts - 1)],
                rows,
            )
            return
        for h in range(2):
            self.late(h).wait()
            each(
                out.at[pl.ds(h * self.half, self.half)],
                [self.piece(self.q, h), self.first.at[h, 0], self.second.at[h, 1]],
                rows,
            )


def each(out, blocks, rows):
    if len(out.shape) == 2:
        sum_blocks(out, blocks, rows)
        return
    for d in range(out.shape[0]):
        sum_blocks(out.at[d], [block.at[d] for block in blocks], rows)


class LineSum:
    def __init__(self, line, z, core, q, acc, up, down, up_s, up_r, down_s, down_r, rows, steps):
        self.line, self.z, self.core, self.q = line, z, core, q
        self.acc, self.up, self.down = acc, up, down
        self.up_s, self.up_r, self.down_s, self.down_r = up_s, up_r, down_s, down_r
        self.rows, self.steps = rows, steps

    def ahead(self, d, first):
        block = self.acc.at[d] if first else self.up.at[d]
        to = (2 * (self.z + 1) + self.core, self.q)
        return remote(block, self.up.at[d], self.up_s, self.up_r, d, to)

    def behind(self, d, first):
        block = self.acc.at[d] if first else self.down.at[d]
        to = (2 * (self.z - 1) + self.core, self.q)
        return remote(block, self.down.at[d], self.down_s, self.down_r, d, to)

    def add(self, into, d):
        add_blocks(into.at[d], into.at[d], self.acc.at[d], self.rows, self.steps)

    def step(self, t):
        line, z = self.line, self.z
        far, near = line - 1 - t + z, t - (line - 1 - z)

        @pl.when(z == 0)
        def _():
            self.ahead(line - 1 - t, True).start()

        @pl.when((z > 0) & (z <= t))
        def _():
            self.ahead(far, False).wait_recv()
            self.add(self.up, far)
            self.ahead(far, False).start()

        @pl.when(z == line - 1)
        def _():
            self.behind(t, True).start()

        @pl.when((z < line - 1) & (line - 1 - z <= t))
        def _():
            self.behind(near, False).wait_recv()
            self.add(self.down, near)
            self.behind(near, False).start()

    def sent(self, t):
        line, z = self.line, self.z
        far, near = line - 1 - t + z, t - (line - 1 - z)

        @pl.when(z == 0)
        def _():
            self.ahead(line - 1 - t, True).wait_send()

        @pl.when((z > 0) & (z <= t))
        def _():
            self.ahead(far, False).wait_send()

        @pl.when(z == line - 1)
        def _():
            self.behind(t, True).wait_send()

        @pl.when((z < line - 1) & (line - 1 - z <= t))
        def _():
            self.behind(near, False).wait_send()

    def finish(self, out):
        line, z = self.line, self.z

        @pl.when(z == 0)
        def _():
            self.behind(z, False).wait_recv()
            add_blocks(out, self.acc.at[z], self.down.at[z], self.rows, self.steps)

        @pl.when(z == line - 1)
        def _():
            self.ahead(z, False).wait_recv()
            add_blocks(out, self.acc.at[z], self.up.at[z], self.rows, self.steps)

        @pl.when((z > 0) & (z < line - 1))
        def _():
            self.ahead(z, False).wait_recv()
            self.add(self.up, z)
            self.behind(z, False).wait_recv()
            add_blocks(out, self.up.at[z], self.down.at[z], self.rows, self.steps)


class LineSums:
    def __init__(self, line, z, core, q, acc, up, down, sems, rows):
        half = acc.shape[1] // 2
        self.line = line
        self.halves = [
            LineSum(
                line, z, core, q, *[a.at[:, pl.ds(h * half, half)] for a in (acc, up, down)],
                *[s.at[h] for s in sems], rows, half // rows,
            )
            for h in range(2)
        ]
        self.half = half

    def step(self, t):
        for part in self.halves:
            part.step(t)

    def finish(self, out):
        for h, part in enumerate(self.halves):
            part.finish(out.at[pl.ds(h * self.half, self.half)])

    def sent(self):
        for t in range(self.line - 1):
            for part in self.halves:
                part.sent(t)


def backward_kernel(
    groups, parts, cw,
    back_h, coefs_h, normed_h, px_h, y_h, z_h, states_h, wide_h,
    gain, taps, heads, skip, spread, gather,
    dz_h, dpx_h, small, wide_sum, gate_sum,
    dz, coefs, normed, px, y, dy, states, wide, dpx, dtaps, dheads, dskip, dgain,
    xbuf, dstate, dcbuf, slope, xact, xd_s, dxd_s, acc_s,
    first, second, wide_s, wide_r, gate_made, gate_held, gate_acc, gate_up, gate_down,
    core_s, core_r, up_s, up_r, down_s, down_r, load, store,
):
    line = groups // 2
    cc = cw + 2 * N
    length = y.shape[0]
    chunks = length // CHUNK
    group, q = lax.axis_index("dp"), lax.axis_index("seq")
    z, core = group // 2, lax.rem(group, 2)
    sibling = (2 * z + 1 - core, q)
    loads = [
        pltpu.make_async_copy(source, target, load.at[k])
        for k, (source, target) in enumerate(
            [(wide_h, wide), (back_h, dz), (coefs_h, coefs), (y_h, y), (z_h, dy),
             (normed_h, normed), (states_h, states)]
        )
    ]
    for copy in loads[1:5]:
        copy.start()

    def fetch(at, first=False):
        slot = lax.rem(at, 2)
        if first:
            return pltpu.make_async_copy(
                px_h.at[pl.ds(0, CHUNK)], px.at[0, pl.ds(8, CHUNK)], load.at[7]
            )
        rows = pl.ds(pl.multiple_of(at * CHUNK - 8, 8), CHUNK + 8)
        return pltpu.make_async_copy(px_h.at[rows], px.at[slot], load.at[7 + slot])

    greet(seq_peers(parts) + dp_peers(groups))
    plane = PlaneSum(parts, group, q, wide, first, second, wide_s, wide_r, wide_h)
    plane.start(0)
    plane.start(1)
    for copy in loads[1:5]:
        copy.wait()
    loads[5].start()
    loads[6].start()
    loads[0].start()
    fetch(chunks - 1).start()

    rows = 32
    lane = lax.broadcasted_iota(jnp.int32, (1, LANES), 1)
    dgain[...] = jnp.zeros_like(dgain)

    def gate_rows(i, carry):
        at = pl.ds(pl.multiple_of(i * rows, rows), rows)
        coef = coefs[at, :].astype(F32)
        for b in range(cw // WIDE):
            lanes = slice(b * WIDE, (b + 1) * WIDE)
            level = level_of(q * cw + b * WIDE, WIDE)
            ours = (lane == level) | (lane == level + LEVELS)
            pull = jnp.sum(jnp.where(ours, coef, 0.0), axis=-1, keepdims=True)
            gate_in = dy[at, lanes]
            sig = jax.nn.sigmoid(gate_in)
            gate = gate_in * sig
            y_at = y[at, lanes]
            gated = y_at * gate
            back = dz[at, lanes].astype(F32)
            dgated = gain[:, lanes] * back - gated * pull
            dgain[0:1, lanes] += jnp.sum(back * gated, axis=0, keepdims=True)
            dz[at, lanes] = (dgated * y_at * (sig + gate * (1.0 - sig))).astype(BF16)
            dy[at, lanes] = dgated * gate
        return carry

    lax.fori_loop(0, length // rows, gate_rows, 0)
    dz_out = pltpu.make_async_copy(dz, dz_h, store.at[0])
    dz_out.start()
    loads[5].wait()
    span = gate_acc.shape[1]

    def dweight(of, out):
        at = pl.ds(pl.multiple_of(of * span, span), span)
        out[...] = dot(normed[:, at], dz[...], TN).astype(BF16)

    def core_copy(d):
        return remote(gate_made.at[d], gate_held.at[d], core_s, core_r, d, sibling)

    order = [d for k in range(line // 2) for d in (line - 1 - k, k)]
    gates = LineSums(
        line, z, core, q, gate_acc, gate_up, gate_down, (up_s, up_r, down_s, down_r), span // 8
    )
    for some in (order[:2], order[2:]):
        for d in some:
            dweight(2 * d + 1 - core, gate_made.at[d])
            core_copy(d).start()
        for d in some:
            dweight(2 * d + core, gate_acc.at[d])
            core_copy(d).wait()
            add_blocks(gate_acc.at[d], gate_acc.at[d], gate_held.at[d], span // 4, 4)
        if some[0] == order[0]:
            gates.step(0)
    dstate[...] = jnp.zeros_like(dstate)
    dcbuf[CHUNK : CHUNK + 8, :] = jnp.zeros((8, cc), F32)
    dtaps[...] = jnp.zeros_like(dtaps)
    dheads[...] = jnp.zeros_like(dheads)
    dskip[...] = jnp.zeros_like(dskip)
    loads[6].wait()
    loads[0].wait()

    def scan_rows(i, carry):
        for t in range(1, line - 1):

            @pl.when(i == min(3 * t - 1, chunks - 1))
            def _(t=t):
                gates.step(t)

        @pl.when(i == 4)
        def _():
            plane.turn(32)

        at = chunks - 1 - i
        here = pl.ds(pl.multiple_of(at * CHUNK, CHUNK), CHUNK)

        @pl.when(at > 0)
        def _():
            fetch(at).wait()

        @pl.when(at == 0)
        def _():
            fetch(0, True).wait()

        @pl.when(at > 1)
        def _():
            fetch(at - 1).start()

        @pl.when(at == 1)
        def _():
            fetch(0, True).start()

        rows = px.at[lax.rem(at, 2)]
        scan_backward_step(
            cw, at == 0, rows.at[pl.ds(8, CHUNK)], rows.at[pl.ds(0, 8)], taps, heads, skip, spread, gather,
            dy.at[here], y.at[here], states.at[at], dpx.at[here], dtaps, dheads, dskip,
            xbuf, dstate, dcbuf, slope, xact, xd_s, dxd_s, acc_s,
        )
        return carry

    lax.fori_loop(0, chunks, scan_rows, 0)
    dpx_out = pltpu.make_async_copy(dpx, dpx_h, store.at[1])
    dpx_out.start()
    small[...] = jnp.zeros_like(small)
    wide_rows, own_rows = cc // LANES, cw // LANES
    for tap in range(TAPS + 1):
        for b in range(wide_rows):
            to = tap * wide_rows + b
            small[to : to + 1, :] = dtaps[tap : tap + 1, b * LANES : (b + 1) * LANES]
    to = (TAPS + 1) * wide_rows
    for b in range(own_rows):
        small[to + b : to + b + 1, :] = dgain[0:1, b * LANES : (b + 1) * LANES]
    hq = cw // P_SIZE
    skips = spread_heads(dskip[...], gather[...])
    small[to + own_rows : to + own_rows + 1, :] = (
        dheads[0:1, :]
        + pltpu.roll(dheads[...], hq, 1)[1:2, :]
        + pltpu.roll(skips, 2 * hq, 1)[0:1, :]
    )
    plane.finish(wide_sum, 32)
    gates.finish(gate_sum)
    gates.sent()
    dz_out.wait()
    dpx_out.wait()


def backward(
    collective_id, back, coefs, normed, px, y, z, states, wide, gain, taps, heads, skip, spread, gather
):
    parts, line = wide.shape[:2]
    length, width = px.shape
    cw = skip.shape[1]
    cc = cw + 2 * N
    span = D // (2 * line)
    sem = pltpu.SemaphoreType.DMA
    vmem = pl.BlockSpec(memory_space=pltpu.VMEM)
    hbm = pl.BlockSpec(memory_space=pltpu.HBM)
    small_rows = (TAPS + 1) * (cc // LANES) + cw // LANES + 1
    small_rows = -(-small_rows // 8) * 8
    return pl.pallas_call(
        functools.partial(backward_kernel, 2 * line, parts, cw),
        in_specs=[*([hbm] * 8), *([vmem] * 6)],
        out_specs=[hbm, hbm, vmem, vmem, vmem],
        out_shape=[
            jax.ShapeDtypeStruct((length, cw), BF16),
            jax.ShapeDtypeStruct((length, width), BF16),
            jax.ShapeDtypeStruct((small_rows, LANES), F32),
            jax.ShapeDtypeStruct(wide.shape[1:], BF16),
            jax.ShapeDtypeStruct((span, cw), BF16),
        ],
        scratch_shapes=[
            *[pltpu.VMEM(a.shape, a.dtype) for a in (back, coefs, normed)],
            pltpu.VMEM((2, CHUNK + 8, width), F32),
            *[pltpu.VMEM(a.shape, a.dtype) for a in (y, z, states, wide)],
            pltpu.VMEM((length, width), BF16),
            pltpu.VMEM((8, cc), F32),
            pltpu.VMEM((8, LANES), F32),
            pltpu.VMEM((8, cw), F32),
            pltpu.VMEM((8, cw), F32),
            pltpu.VMEM((CHUNK + 8, cc), F32),
            pltpu.VMEM((N, cw), F32),
            pltpu.VMEM((CHUNK + 8, cc), F32),
            pltpu.VMEM((CHUNK, cc), F32),
            pltpu.VMEM((CHUNK, cc), F32),
            pltpu.VMEM((CHUNK, cw), BF16),
            pltpu.VMEM((CHUNK, cw), F32),
            pltpu.VMEM((CHUNK, CHUNK), F32),
            *PlaneSum.scratch(parts, wide.shape[1:], BF16),
            *([pltpu.VMEM((line, span, cw), BF16)] * 5),
            sem((line,)), sem((line,)), *([sem((2, line))] * 4),
            sem((9,)), sem((2,)),
        ],
        compiler_params=pltpu.CompilerParams(
            collective_id=collective_id, has_side_effects=True, vmem_limit_bytes=63 * 2**20
        ),
        name="backward",
    )(back, coefs, normed, px, y, z, states, wide, gain, taps, heads, skip, spread, gather)


def owners_kernel(
    groups, parts, rows, cw,
    normed, left, right, gate, small, dz, dpx, wz, wx,
    part, rest_out, left_out, right_out, gate_out, back_out, small_all,
    made, held, acc, up, down, final, left_up, left_down, right_acc, right_up, right_down,
    rest_made, rest_held, rest, rest_acc, rest_up, rest_down,
    normed_v, dz_v, dpx_v, wz_v, wx_v, back, back_sum,
    right_1, right_2, right_s, right_r, back_1, back_2, back_s, back_r,
    rest_1, rest_2, rest_s, rest_r,
    core_s, core_r, up_s, up_r, down_s, down_r, lup_s, lup_r, ldown_s, ldown_r,
    rup_s, rup_r, rdown_s, rdown_r, tup_s, tup_r, tdown_s, tdown_r, rcore_s, rcore_r,
    part_s, part_r, gate_s, gate_r, small_s, small_r, load, local,
):
    line = groups // 2
    span = parts * rows
    group, q = lax.axis_index("dp"), lax.axis_index("seq")
    z, core = group // 2, lax.rem(group, 2)
    sibling = (2 * z + 1 - core, q)
    peers, others = seq_peers(parts), dp_peers(groups)
    tokens = back.shape[1]
    loads = [
        pltpu.make_async_copy(source, target, load.at[k])
        for k, (source, target) in enumerate(
            [(normed, normed_v), (dpx, dpx_v), (dz, dz_v), (wz, wz_v), (wx, wx_v)]
        )
    ]
    for copy in loads[:2]:
        copy.start()
    greet(peers + others)
    half_rows = left.shape[1] // 2
    lefts = LineSum(
        line, z, core, q, left, left_up, left_down, lup_s, lup_r, ldown_s, ldown_r, half_rows, 2
    )
    rights = LineSum(
        line, z, core, q, right_acc, right_up, right_down, rup_s, rup_r, rdown_s, rdown_r,
        half_rows, 2,
    )
    wholes = LineSum(
        line, z, core, q, acc, up, down, up_s, up_r, down_s, down_r, rows, parts
    )
    lefts.step(0)
    right_plane = PlaneSum(parts, group, q, right, right_1, right_2, right_s, right_r)
    rest_plane = PlaneSum(parts, group, q, rest, rest_1, rest_2, rest_s, rest_r)
    rests = LineSum(
        line, z, core, q, rest_acc, rest_up, rest_down, tup_s, tup_r, tdown_s, tdown_r, rows, 1
    )
    back_plane = PlaneSum(parts, group, q, back, back_1, back_2, back_s, back_r)
    right_plane.start(0)
    right_plane.start(1)
    waiting = []
    for k, peer in enumerate(peers):
        copy = remote(gate.at[peer[1]], gate_out.at[q], gate_s, gate_r, k, peer)
        copy.start()
        waiting.append(copy)
    for k, peer in enumerate(others):
        copy = remote(small, small_all.at[group], small_s, small_r, k, peer)
        copy.start()
        waiting.append(copy)
    own = [
        pltpu.make_async_copy(gate.at[q], gate_out.at[q], local.at[0]),
        pltpu.make_async_copy(small, small_all.at[group], local.at[1]),
    ]
    for copy in own:
        copy.start()
    loads[0].wait()
    loads[1].wait()
    for copy in loads[2:]:
        copy.start()
    tile = 512

    def dweight(of):
        at = pl.ds(pl.multiple_of(of * span, span), span)
        return dot(normed_v[:, at], dpx_v[...], TN)

    cores = {}
    order = [d for k in range(line // 2) for d in (line - 1 - k, k)]

    def share_core(d):
        total = dweight(2 * d + 1 - core)
        made[d] = total[:, :cw].astype(BF16)
        rest_made[d] = total[:, cw:].astype(BF16)
        cores[d] = [
            remote(made.at[d], held.at[d], core_s, core_r, d, sibling),
            remote(rest_made.at[d], rest_held.at[d], rcore_s, rcore_r, d, sibling),
        ]
        for copy in cores[d]:
            copy.start()

    def sum_core(d):
        total = dweight(2 * d + core)
        for copy in cores[d]:
            copy.wait()
        acc[d] = (total[:, :cw] + held[d].astype(F32)).astype(BF16)
        others = (total[:, cw:] + rest_held[d].astype(F32)).astype(BF16)
        for k in range(parts):
            rest[k, d] = others[k * rows : (k + 1) * rows]

    def dnormed(of):
        at = pl.ds(pl.multiple_of(of * tokens, tokens), tokens)

        def step(j, carry):
            cols = pl.ds(pl.multiple_of(j * tile, tile), tile)
            back[of, :, cols] = (
                dot(dz_v[at, :], wz_v[cols, :], NT) + dot(dpx_v[at, :], wx_v[cols, :], NT)
            ).astype(BF16)
            return carry

        lax.fori_loop(0, D // tile, step, 0)

    share_core(order[0])
    lefts.sent(0)
    lefts.step(1)
    share_core(order[1])
    sum_core(order[0])
    sum_core(order[1])
    wholes.step(0)
    for t in range(2, line - 1):
        lefts.sent(t - 1)
        lefts.step(t)
    for copy in loads[2:]:
        copy.wait()
    if parts == 4:
        dnormed(back_plane.far)
        back_plane.start_far()
    for d in order[2:]:
        share_core(d)
    for d in order[2:]:
        sum_core(d)
    right_plane.turn(32)
    if parts == 4:
        dnormed(back_plane.near[0])
        back_plane.start_near(0)
    wholes.sent(0)
    wholes.step(1)
    if parts == 4:
        dnormed(back_plane.near[1])
        back_plane.start_near(1)
    else:
        for peer in peers:
            dnormed(peer[1])
        back_plane.start(1)
    rest_plane.start(0)
    rest_plane.start(1)
    dnormed(q)
    right_plane.finish(right_acc, 32)
    for t in range(2, line - 1):
        wholes.sent(t - 1)
        wholes.step(t)
    rights.step(0)
    rest_plane.turn(rows)
    rest_plane.finish(rest_acc, rows)
    rests.step(0)
    back_plane.turn(32)
    lefts.finish(left_out)
    lefts.sent(line - 2)
    rests.sent(0)
    rests.step(1)
    rights.sent(0)
    rights.step(1)
    wholes.sent(line - 2)
    wholes.finish(final)
    for k, peer in enumerate(peers):
        block = final.at[pl.ds(pl.multiple_of(peer[1] * rows, rows), rows)]
        copy = remote(block, part.at[q], part_s, part_r, k, peer)
        copy.start()
        waiting.append(copy)
    copy = pltpu.make_async_copy(
        final.at[pl.ds(pl.multiple_of(q * rows, rows), rows)], part.at[q], local.at[2]
    )
    copy.start()
    own.append(copy)
    for t in range(2, line - 1):
        rights.sent(t - 1)
        rights.step(t)
    for t in range(2, line - 1):
        rests.sent(t - 1)
        rests.step(t)
    back_plane.finish(back_sum, 32)
    copy = pltpu.make_async_copy(back_sum, back_out, local.at[3])
    copy.start()
    own.append(copy)
    rests.finish(rest_out)
    rests.sent(line - 2)
    rights.finish(right_out)
    rights.sent(line - 2)
    for copy in own + waiting:
        copy.wait()


def sum_to_owners(collective_id, normed, left, right, gate, small, dz, dpx, wz, wx):
    parts, line, out_rows, slim = right.shape
    groups = 2 * line
    rows, cw = gate.shape[1:]
    span = rows * parts
    extra = dpx.shape[1] - cw
    tokens = dz.shape[0] // parts
    sem = pltpu.SemaphoreType.DMA
    vmem = pl.BlockSpec(memory_space=pltpu.VMEM)
    hbm = pl.BlockSpec(memory_space=pltpu.HBM)
    right_sum = (line, out_rows, slim)
    rest = (parts, line, rows, extra)
    return pl.pallas_call(
        functools.partial(owners_kernel, groups, parts, rows, cw),
        in_specs=[hbm, vmem, vmem, hbm, vmem, hbm, hbm, hbm, hbm],
        out_specs=[hbm, vmem, vmem, vmem, hbm, hbm, vmem],
        out_shape=[
            jax.ShapeDtypeStruct((parts, rows, cw), BF16),
            jax.ShapeDtypeStruct((rows, extra), F32),
            jax.ShapeDtypeStruct((out_rows, left.shape[-1]), F32),
            jax.ShapeDtypeStruct((out_rows, slim), F32),
            jax.ShapeDtypeStruct(gate.shape, BF16),
            jax.ShapeDtypeStruct((tokens, D), F32),
            jax.ShapeDtypeStruct((groups,) + small.shape, F32),
        ],
        scratch_shapes=[
            *([pltpu.VMEM((line, span, cw), BF16)] * 5),
            pltpu.VMEM((span, cw), BF16),
            *([pltpu.VMEM(left.shape, BF16)] * 2),
            *([pltpu.VMEM(right_sum, BF16)] * 3),
            *([pltpu.VMEM((line, span, extra), BF16)] * 2),
            pltpu.VMEM(rest, BF16),
            *([pltpu.VMEM(rest[1:], BF16)] * 3),
            *[pltpu.VMEM(a.shape, BF16) for a in (normed, dz, dpx, wz, wx)],
            pltpu.VMEM((parts, tokens, D), BF16),
            pltpu.VMEM((tokens, D), F32),
            *PlaneSum.scratch(parts, right.shape[1:], BF16),
            *PlaneSum.scratch(parts, (tokens, D), BF16),
            *PlaneSum.scratch(parts, rest[1:], BF16),
            *([sem((line,))] * 20),
            *([sem((parts - 1,))] * 4),
            *([sem((groups - 1,))] * 2),
            sem((5,)),
            sem((4,)),
        ],
        compiler_params=pltpu.CompilerParams(
            collective_id=collective_id, has_side_effects=True, vmem_limit_bytes=63 * 2**20
        ),
        name="sum_to_owners",
    )(normed, left, right, gate, small, dz, dpx, wz, wx)


def on_device(
    hidden_in, out_grads, w_in, w_in_m, w_in_v, w_out, w_out_m, w_out_v,
    chan_params, chan_m, chan_v, head_params, head_m, head_v,
):
    parts = lax.axis_size("seq")
    groups = lax.axis_size("dp")
    q = lax.axis_index("seq")
    rows = hidden_in.shape[1]
    length = rows * parts
    cw = INNER // parts
    hq = H // parts
    cc = cw + 2 * N
    in_rows = w_in.shape[0]
    out_rows = w_out.shape[0]

    chan_len = chan_params.shape[0]
    line = groups // 2
    group = lax.axis_index("dp")
    owner = group * parts + q
    chan_block = lax.dynamic_update_slice(
        jnp.zeros((8 * LANES,), F32),
        lax.reduce_precision(chan_params, 8, 7),
        (lax.rem(owner * chan_len, LANES),),
    ).reshape(8, LANES)
    head_block = jnp.pad(head_params, ((0, 5), (0, LANES - H)))
    hidden, wx, gate, wo, gain_in, own_gain, taps, heads, skip, spread, gather = collect(
        0, hidden_in[0], w_in, w_out, chan_block, head_block, chan_len, groups, parts
    )

    normed, px, y, states, z, u, stats, wz, wo = forward(
        1, hidden.reshape(length, D), wx.reshape(D, cc + LANES), gate, wo, gain_in, own_gain,
        taps, heads, skip, spread,
    )
    wx, wz = wx.reshape(D, cc + LANES), wz.reshape(D, cw)
    cotangent = out_grads[:, 0]
    back_own, coefs, block_out, dwo_left, dwo_right = middle(
        2, u, stats, wo, cotangent, hidden_in[0]
    )

    dz, dpx, small, dwo_left, dwz = backward(
        5, back_own.reshape(length, cw), coefs.reshape(length, LANES), normed, px, y, z, states,
        dwo_left, own_gain, taps, heads, skip, spread, gather,
    )
    x_part, rest, left_part, right_part, z_part, dnormed, small = sum_to_owners(
        4, normed, dwo_left, dwo_right, dwz.reshape(parts, in_rows, cw), small, dz, dpx, wz, wx
    )
    hidden_grad, chan_total, head_total, norm = gradient_norm(
        6, x_part, rest, z_part, left_part, right_part, dnormed, small, hidden_in[0],
        gain_in, cotangent, groups,
    )
    (
        hidden_grad, block_out, w_in_new, w_in_m_new, w_in_v_new, w_in_copy,
        w_out_new, w_out_m_new, w_out_v_new, w_out_copy,
    ) = update_weights(
        norm, x_part, rest, z_part, left_part, right_part, hidden_grad, block_out,
        (w_in, w_in_m, w_in_v, w_out, w_out_m, w_out_v),
    )
    hidden_grad, block_out = hidden_grad[None], block_out[:, None]
    grad_norm, clip_factor = norm[0, 0], norm[1, 0]
    chan_part = lax.dynamic_slice(chan_total.reshape(-1), (owner * chan_len,), (chan_len,))
    head_total = head_total[:parts, : 3 * hq].reshape(parts, 3, hq)
    head_total = head_total.transpose(1, 0, 2).reshape(3, H)
    chan_new, chan_m_new, chan_v_new = adam_tile(
        chan_params, clip_factor * chan_part, chan_m, chan_v, 0.2, 0.0
    )
    head_new, head_m_new, head_v_new = adam_tile(
        head_params, clip_factor * head_total, head_m, head_v, 1.0, 0.0
    )
    return (
        block_out, hidden_grad, grad_norm,
        w_in_new, w_in_m_new, w_in_v_new, w_in_copy,
        w_out_new, w_out_m_new, w_out_v_new, w_out_copy,
        chan_new, chan_m_new, chan_v_new, head_new, head_m_new, head_v_new,
    )


def solution(mesh):
    rows = P(("dp", "seq"), None)
    flat = P(("dp", "seq"))
    in_specs = (
        P("dp", "seq", None),
        P(None, "dp", "seq", None),
        *([rows] * 6),
        *([flat] * 3),
        *([P()] * 3),
    )
    out_specs = (
        P(None, "dp", "seq", None),
        P("dp", "seq", None),
        P(),
        *([rows] * 8),
        *([flat] * 3),
        *([P()] * 3),
    )
    return jax.shard_map(
        on_device, mesh=mesh, in_specs=in_specs, out_specs=out_specs, check_vma=False
    )
```

```python
import functools

import jax
import jax.numpy as jnp
from jax import lax
from jax.experimental import pallas as pl
from jax.experimental.pallas import tpu as pltpu
from jax.sharding import PartitionSpec as P

D = 2048
INNER = 4096
H = 64
P_SIZE = 64
N = 128
TAPS = 4
STEP = 10
E_IN = 8512
CONV_CH = 4352
LANES = 128
CHUNK = 128
LEVELS = 4

EXACT = lax.Precision.HIGHEST
EPS_IN = 1e-06
EPS_OUT = 1e-05
ADAM_EPS = 1e-08
BETA = 0.5
CLIP = 1.0
F32 = jnp.float32
BF16 = jnp.bfloat16
MASKED = -1e30


def level_width(level):
    return INNER * 2**level // 8


SEGMENTS = tuple(
    (0 if level == 0 else level_width(level - 1), level_width(level)) for level in range(LEVELS)
)


def dot(a, b, dims=((1,), (0,)), precision=None):
    return lax.dot_general(a, b, (dims, ((), ())), precision=precision, preferred_element_type=F32)


NT = ((1,), (1,))
TN = ((0,), (0,))


def softplus(v):
    return jnp.maximum(v, 0.0) + jnp.log1p(jnp.exp(-jnp.abs(v)))


def two_terms(v):
    high = v.astype(BF16)
    return high, (v - high.astype(F32)).astype(BF16)


def spread_heads(v, spread):
    high, rest = two_terms(v)
    return dot(high, spread) + dot(rest, spread)


def own_heads_first(dt_raw, hq, back=False):
    by = lax.axis_index("seq") * hq
    return pltpu.roll(dt_raw, by if back else lax.rem(LANES - by, LANES), 1)


def rates(dt_raw, heads):
    step = softplus(dt_raw + heads[0:1, :])
    return step, step * heads[1:2, :]


def triangle(size):
    row = lax.broadcasted_iota(jnp.int32, (size, size), 0)
    col = lax.broadcasted_iota(jnp.int32, (size, size), 1)
    return row, col


def conv_block(taps, xbuf, lanes):
    out = taps[TAPS : TAPS + 1, lanes]
    for tap in range(TAPS):
        out = out + taps[tap : tap + 1, lanes] * xbuf[5 + tap : 5 + tap + CHUNK, lanes]
    return out


def pair_decay(cum, cum_t, causal, head):
    gap = cum[:, head : head + 1] - cum_t[head : head + 1, :]
    return jnp.exp(jnp.where(causal, gap, MASKED))


def scan_forward_step(cw, px, taps, heads, skip, spread, y, states, xbuf, state, xdt, carried):
    cc = cw + 2 * N
    xbuf[8 : 8 + CHUNK, :] = px[:, :cc]
    step, rate = rates(own_heads_first(px[:, cc:], cw // P_SIZE), heads)
    row, col = triangle(CHUNK)
    causal = row >= col
    cum = dot(causal.astype(F32), rate, precision=EXACT)
    cum_t = cum.T
    spread_m = spread[...]
    last = cum[CHUNK - 1 : CHUNK, :]
    step_x = spread_heads(step, spread_m)
    grow_x = spread_heads(jnp.exp(cum), spread_m)
    tail_x = spread_heads(jnp.exp(last - cum), spread_m)

    def activated(lanes):
        conv = conv_block(taps, xbuf, lanes)
        return conv * jax.nn.sigmoid(conv)

    state_in = activated(slice(cw, cw + N))
    state_out = activated(slice(cw + N, cw + 2 * N))
    scores = dot(state_out, state_in, NT, EXACT)
    states[...] = state[...].astype(BF16)
    carried[...] = dot(state_out.astype(BF16), state[...].astype(BF16))
    first = lax.broadcasted_iota(jnp.int32, (1, LANES), 1) < P_SIZE
    for pair in range(cw // LANES):
        lanes = slice(pair * LANES, (pair + 1) * LANES)
        x = activated(lanes)
        xd = (x * step_x[:, lanes]).astype(BF16).astype(F32)
        xdt[:, lanes] = (xd * tail_x[:, lanes]).astype(BF16)
        stacked = jnp.concatenate([jnp.where(first, xd, 0.0), jnp.where(first, 0.0, xd)], axis=0)
        mixing = jnp.concatenate(
            [
                (pair_decay(cum, cum_t, causal, 2 * pair + k) * scores).astype(BF16)
                for k in range(2)
            ],
            axis=1,
        )
        y[:, lanes] = (
            dot(mixing, stacked.astype(BF16))
            + grow_x[:, lanes] * carried[:, lanes]
            + skip[:, lanes] * x
        )
    state[...] = grow_x[CHUNK - 1 : CHUNK, :] * state[...] + dot(
        state_in.astype(BF16), xdt[...], TN
    )
    xbuf[0:8, :] = xbuf[CHUNK : CHUNK + 8, :]


def scan_backward_step(
    cw, start, px, halo, taps, heads, skip, spread, gather, dy, y, states,
    dpx, dtaps, dheads, dskip,
    xbuf, dstate, dcbuf, slope, xact, xd_s, dxd_s, acc_s,
):
    cc = cw + 2 * N
    xbuf[0:8, :] = jnp.where(start, 0.0, halo[:, :cc])
    xbuf[8 : 8 + CHUNK, :] = px[:, :cc]
    dt_raw = own_heads_first(px[:, cc:], cw // P_SIZE)
    step, rate = rates(dt_raw, heads)
    row, col = triangle(CHUNK)
    causal = row >= col
    cum = dot(causal.astype(F32), rate, precision=EXACT)
    cum_t = cum.T
    spread_m = spread[...]
    last = cum[CHUNK - 1 : CHUNK, :]
    step_x = spread_heads(step, spread_m)
    grow_x = spread_heads(jnp.exp(cum), spread_m)
    tail_x = spread_heads(jnp.exp(last - cum), spread_m)

    for block in range(cc // LANES):
        lanes = slice(block * LANES, (block + 1) * LANES)
        conv = conv_block(taps, xbuf, lanes)
        sig = jax.nn.sigmoid(conv)
        act = conv * sig
        xact[:, lanes] = act
        slope[:, lanes] = sig + act * (1.0 - sig)
    state_in = xact[:, cw : cw + N]
    state_out = xact[:, cw + N : cc]
    scores = dot(state_out, state_in, NT, EXACT)
    in_low = state_in.astype(BF16)
    out_low = state_out.astype(BF16)
    dstate_low = dstate[...].astype(BF16)
    acc_s[...] = jnp.zeros_like(acc_s)
    dxd_s[...] = tail_x * dot(in_low, dstate_low)
    dskip[0:1, :] += jnp.sum(xact[:, :cw] * dy[...], axis=0, keepdims=True)
    first = lax.broadcasted_iota(jnp.int32, (1, LANES), 1) < P_SIZE
    xd_s[...] = (xact[:, :cw] * step_x).astype(BF16)
    total = jnp.sum(xd_s[...].astype(F32) * dxd_s[...], axis=0, keepdims=True) + grow_x[
        CHUNK - 1 : CHUNK, :
    ] * jnp.sum(dstate[...] * states[...].astype(F32), axis=0, keepdims=True)
    dscores = jnp.zeros((CHUNK, CHUNK), F32)
    for pair in range(cw // LANES):
        lanes = slice(pair * LANES, (pair + 1) * LANES)
        dyp = dy[:, lanes]
        stacked = jnp.concatenate(
            [jnp.where(first, dyp, 0.0), jnp.where(first, 0.0, dyp)], axis=0
        ).astype(BF16)
        decays = [pair_decay(cum, cum_t, causal, 2 * pair + k) for k in range(2)]
        mixing = jnp.concatenate([(decay * scores).astype(BF16) for decay in decays], axis=0)
        dxd_s[:, lanes] += dot(mixing, stacked, TN)
        dmix = dot(stacked, xd_s[:, lanes], NT)
        dscores = dscores + decays[0] * dmix[:CHUNK] + decays[1] * dmix[CHUNK:]
    dy_low = dy[...].astype(BF16)
    dy_f = dy_low.astype(F32)
    xd_f = xd_s[...].astype(F32)
    dxd = dxd_s[...]
    y_scan = y[...] - skip[...] * xact[:, :cw]
    final = lax.broadcasted_iota(jnp.int32, (CHUNK, 1), 0) == CHUNK - 1
    gather_m = gather[...]
    dcum = spread_heads(dy_f * y_scan - xd_f * dxd + jnp.where(final, total, 0.0), gather_m)
    dstep = spread_heads(xact[:, :cw] * dxd, gather_m)
    drate = dot((row <= col).astype(F32), dcum, precision=EXACT)
    dstep = dstep + drate * heads[1:2, :]
    ddt = dstep * jax.nn.sigmoid(dt_raw + heads[0:1, :])
    dheads[0:1, :] += jnp.sum(ddt, axis=0, keepdims=True)
    dheads[1:2, :] += jnp.sum(drate * rate, axis=0, keepdims=True)
    grown = (grow_x * dy_f).astype(BF16)
    dscores_low = dscores.astype(BF16)
    dout = dot(dscores_low, in_low) + dot(grown, states[...], NT)
    din = dot(dscores_low, out_low, TN) + dot((tail_x * xd_f).astype(BF16), dstate_low, NT)
    dstate[...] = grow_x[CHUNK - 1 : CHUNK, :] * dstate[...] + dot(out_low, grown, TN)
    dcbuf[:CHUNK, :cw] = (step_x * dxd + skip[...] * dy[...]) * slope[:, :cw]
    dcbuf[:CHUNK, cw : cw + N] = din * slope[:, cw : cw + N]
    dcbuf[:CHUNK, cw + N :] = dout * slope[:, cw + N :]
    for block in range(cc // LANES):
        lanes = slice(block * LANES, (block + 1) * LANES)
        dconv = dcbuf[:CHUNK, lanes]
        dtaps[TAPS : TAPS + 1, lanes] += jnp.sum(dconv, axis=0, keepdims=True)
        back = taps[TAPS - 1 : TAPS, lanes] * dconv
        for tap in range(TAPS):
            dtaps[tap : tap + 1, lanes] += jnp.sum(
                dconv * xbuf[5 + tap : 5 + tap + CHUNK, lanes], axis=0, keepdims=True
            )
            if tap < TAPS - 1:
                reach = TAPS - 1 - tap
                back = back + taps[tap : tap + 1, lanes] * dcbuf[reach : reach + CHUNK, lanes]
        dpx[:, lanes] = back.astype(BF16)
    ours = lax.broadcasted_iota(jnp.int32, (1, LANES), 1) < cw // P_SIZE
    ddt = own_heads_first(jnp.where(ours, ddt, 0.0), cw // P_SIZE, back=True)
    dpx[:, cc:] = ddt.astype(BF16)
    dcbuf[CHUNK : CHUNK + 8, :] = dcbuf[0:8, :]


WIDE = 512
LEFT = 1280
SPLIT = 384


MESH = pl.DeviceIdType.MESH


def remote(src, dst, sends, recvs, index, device):
    return pltpu.make_async_remote_copy(
        src_ref=src,
        dst_ref=dst,
        send_sem=sends.at[index],
        recv_sem=recvs.at[index],
        device_id=device,
        device_id_type=MESH,
    )


def greet(devices):
    barrier = pltpu.get_barrier_semaphore()
    for device in devices:
        pl.semaphore_signal(barrier, inc=1, device_id=device, device_id_type=MESH)
    pl.semaphore_wait(barrier, len(devices))


def seq_peers(parts):
    group, q = lax.axis_index("dp"), lax.axis_index("seq")
    return [(group, lax.rem(q + k, parts)) for k in range(1, parts)]


def dp_peers(groups):
    group, q = lax.axis_index("dp"), lax.axis_index("seq")
    return [(lax.rem(group + k, groups), q) for k in range(1, groups)]


def all_peers(groups, parts):
    devices = groups * parts
    me = lax.axis_index("dp") * parts + lax.axis_index("seq")
    peers = []
    for k in range(1, devices):
        other = lax.rem(me + k, devices)
        peers.append((other // parts, lax.rem(other, parts)))
    return peers


CHAN_ROWS = ((TAPS + 1) * CONV_CH + D + INNER) // LANES


def adam_tile(weight, gradient, moment, second, step_rate, weight_decay):
    new_moment = BETA * moment + (1.0 - BETA) * gradient
    new_second = BETA * second + (1.0 - BETA) * gradient * gradient
    correction = 1.0 - BETA**STEP
    update = new_moment / correction / (jnp.sqrt(new_second / correction) + ADAM_EPS)
    return weight - step_rate * (update + weight_decay * weight), new_moment, new_second


def total_of(value):
    return jnp.sum(jnp.sum(value, axis=1, keepdims=True), axis=0, keepdims=True)


def norm_kernel(
    groups, parts,
    part_h, rest_h, gate_h, left_h, right_h, back_h, small_h, hidden_h, gain, cotangent,
    hidden_grad, chan, head, norm,
    part, rest, gate, left, right, back, small, hidden,
    cot_v, block, near, all_block, all_near, sends, recvs, near_s, near_r, load, local,
):
    group, q = lax.axis_index("dp"), lax.axis_index("seq")
    me = group * parts + q
    cw = INNER // parts
    cc = cw + 2 * N
    everyone = all_peers(groups, parts)
    fetches = [
        pltpu.make_async_copy(source, target, load.at[k])
        for k, (source, target) in enumerate(
            [(back_h, back), (hidden_h, hidden), (part_h, part), (gate_h, gate),
             (left_h, left), (right_h, right), (small_h, small), (rest_h, rest),
             (cotangent, cot_v)]
        )
    ]
    for copy in fetches:
        copy.start()
    barrier = pltpu.get_barrier_semaphore()
    for device in everyone:
        pl.semaphore_signal(barrier, inc=1, device_id=device, device_id_type=MESH)
    for copy in fetches[:2]:
        copy.wait()
    rows = 32

    def summed(at):
        down = back[at, :]
        tokens = hidden[at, :].astype(F32)
        mean = jnp.sum(tokens * tokens, axis=-1, keepdims=True) / D
        return down, tokens, lax.rsqrt(mean + EPS_IN)

    def gain_rows(i, dgain):
        at = pl.ds(pl.multiple_of(i * rows, rows), rows)
        down, tokens, scale = summed(at)
        return dgain + jnp.sum(down * tokens * scale, axis=0, keepdims=True)

    dgain = lax.fori_loop(0, hidden.shape[0] // rows, gain_rows, jnp.zeros((1, D), F32))
    for copy in fetches[2:8]:
        copy.wait()
    total = small[0]
    for k in range(1, groups):
        total = total + small[k]
    near[...] = total
    tail = rest[:, : 2 * N + H]
    squares = total_of(tail * tail)
    for k in range(parts):
        x = part[k].astype(F32)
        g = gate[k].astype(F32)
        squares = squares + total_of(x * x + g * g)
    squares = squares + total_of(left[...] * left[...]) + total_of(right[...] * right[...])
    for k in range(D // LANES):
        block[k : k + 1, :] = dgain[:, k * LANES : (k + 1) * LANES]
    block[D // LANES :, :] = jnp.broadcast_to(squares, (8, LANES))
    pl.semaphore_wait(barrier, len(everyone))
    copies = [
        remote(block, all_block.at[me], sends, recvs, k, peer) for k, peer in enumerate(everyone)
    ]
    copies += [
        remote(near, all_near.at[q], near_s, near_r, k, peer)
        for k, peer in enumerate(seq_peers(parts))
    ]
    copies += [
        pltpu.make_async_copy(block, all_block.at[me], local.at[0]),
        pltpu.make_async_copy(near, all_near.at[q], local.at[1]),
    ]
    for copy in copies:
        copy.start()
    fetches[8].wait()

    def grad_rows(i, carry):
        at = pl.ds(pl.multiple_of(i * rows, rows), rows)
        down, tokens, scale = summed(at)
        scaled = down * gain[...]
        inner = jnp.sum(scaled * tokens, axis=-1, keepdims=True) / D
        direct = cot_v[0, at, :].astype(F32)
        for k in range(1, LEVELS):
            direct = direct + cot_v[k, at, :].astype(F32)
        hidden_grad[at, :] = (
            scale * scaled - tokens * (scale * scale * scale * inner) + direct
        )
        return carry

    lax.fori_loop(0, hidden.shape[0] // rows, grad_rows, 0)
    for copy in copies:
        copy.wait()
    total = jnp.sum(all_block[...], axis=0)
    own, wide = cw // LANES, cc // LANES
    span = CONV_CH // LANES
    for tap in range(TAPS + 1):
        for k in range(parts):
            at = tap * span + k * own
            chan[at : at + own, :] = all_near[k, tap * wide : tap * wide + own, :]
        shared = all_near[0, tap * wide + own : (tap + 1) * wide, :]
        for k in range(1, parts):
            shared = shared + all_near[k, tap * wide + own : (tap + 1) * wide, :]
        chan[tap * span + INNER // LANES : (tap + 1) * span, :] = shared
    at = (TAPS + 1) * span
    chan[at : at + D // LANES, :] = total[: D // LANES]
    at = at + D // LANES
    for k in range(parts):
        first = (TAPS + 1) * wide
        chan[at + k * own : at + (k + 1) * own, :] = all_near[k, first : first + own, :]
        head[k : k + 1, :] = all_near[k, first + own : first + own + 1, :]
    squares = (
        total[D // LANES : D // LANES + 1, :1]
        + total_of(chan[:CHAN_ROWS, :] * chan[:CHAN_ROWS, :])
        + total_of(head[:parts, :] * head[:parts, :])
    )
    grad_norm = jnp.sqrt(squares)
    norm[0:1, :] = jnp.broadcast_to(grad_norm, (1, LANES))
    norm[1:2, :] = jnp.broadcast_to(jnp.minimum(1.0, CLIP / grad_norm), (1, LANES))


def gradient_norm(
    collective_id, part, rest, gate, left, right, back, small, hidden, gain, cotangent, groups
):
    parts = part.shape[0]
    devices = groups * parts
    sem = pltpu.SemaphoreType.DMA
    vmem = pl.BlockSpec(memory_space=pltpu.VMEM)
    hbm = pl.BlockSpec(memory_space=pltpu.HBM)
    block = (D // LANES + 8, LANES)
    chan_rows = -(-CHAN_ROWS // 8) * 8
    return pl.pallas_call(
        functools.partial(norm_kernel, groups, parts),
        in_specs=[*([hbm] * 8), vmem, hbm],
        out_specs=[vmem] * 4,
        out_shape=[
            jax.ShapeDtypeStruct(hidden.shape, F32),
            jax.ShapeDtypeStruct((chan_rows, LANES), F32),
            jax.ShapeDtypeStruct((8, LANES), F32),
            jax.ShapeDtypeStruct((8, LANES), F32),
        ],
        scratch_shapes=[
            *[
                pltpu.VMEM(a.shape, a.dtype)
                for a in (part, rest, gate, left, right, back, small, hidden)
            ],
            pltpu.VMEM(cotangent.shape, BF16),
            pltpu.VMEM(block, F32),
            pltpu.VMEM(small.shape[1:], F32),
            pltpu.VMEM((devices,) + block, F32),
            pltpu.VMEM((parts,) + small.shape[1:], F32),
            sem((devices - 1,)), sem((devices - 1,)), sem((parts - 1,)), sem((parts - 1,)),
            sem((9,)), sem((2,)),
        ],
        compiler_params=pltpu.CompilerParams(
            collective_id=collective_id, has_side_effects=True, vmem_limit_bytes=63 * 2**20
        ),
        name="gradient_norm",
    )(part, rest, gate, left, right, back, small, hidden, gain, cotangent)


BLOCKS = 4


def update_kernel(
    parts, norm, part_h, rest_h, gate_h, left_h, right_h, hidden_grad, block, *refs
):
    ins, refs = refs[:6], refs[6:]
    hidden_out, block_out, outs, refs = refs[0], refs[1], refs[2:10], refs[10:]
    held, made = refs[:6], refs[6:14]
    part, rest, gate, left, right, hidden_v, block_v, load, store, grads = refs[14:]
    clip = norm[1:2, :1]
    cw = INNER // parts
    fetches = [
        pltpu.make_async_copy(source, target, grads.at[k])
        for k, (source, target) in enumerate(
            [(part_h, part), (gate_h, gate), (left_h, left), (right_h, right), (rest_h, rest),
             (hidden_grad, hidden_v), (block, block_v)]
        )
    ]
    for copy in fetches[:5]:
        copy.start()

    def at(a, i):
        rows = ins[a].shape[0] // BLOCKS
        return pl.ds(i * rows, rows)

    loads = [
        [
            pltpu.make_async_copy(ins[a].at[at(a, i)], held[a].at[at(a, i)], load.at[a * BLOCKS + i])
            for a in range(6)
        ]
        for i in range(BLOCKS)
    ]
    for weight in (0, 3):
        for i in range(BLOCKS):
            for a in range(weight, weight + 3):
                loads[i][a].start()
    for copy in fetches[5:]:
        copy.start()
    stores = []

    def update(weight, rows, lanes, gradient, rate, decay):
        first = 0 if weight == 0 else 4
        new, moment, second = adam_tile(
            held[weight][rows, lanes], clip * gradient, held[weight + 1][rows, lanes],
            held[weight + 2][rows, lanes], rate, decay,
        )
        made[first][rows, lanes] = new
        made[first + 1][rows, lanes] = moment
        made[first + 2][rows, lanes] = second
        made[first + 3][rows, lanes] = new.astype(BF16)

    def send(first, rows, i):
        for a in range(first, first + 4):
            copy = pltpu.make_async_copy(
                made[a].at[rows], outs[a].at[rows], store.at[a * BLOCKS + i]
            )
            copy.start()
            stores.append(copy)

    for copy in fetches[:5]:
        copy.wait()
    for i in range(BLOCKS):
        rows = at(0, i)
        for a in range(3):
            loads[i][a].wait()
        for source, first in ((gate, 0), (part, INNER)):

            def step(k, carry, source=source, first=first, rows=rows):
                to = pl.ds(pl.multiple_of(first + k * cw, cw), cw)
                update(0, rows, to, source[k, rows, :cw].astype(F32), 0.02, 0.1)
                return carry

            lax.fori_loop(0, parts, step, 0)
        update(0, rows, slice(2 * INNER, E_IN), rest[rows, : 2 * N + H], 0.02, 0.1)
        send(0, rows, i)
    fetches[5].wait()
    fetches[6].wait()
    for source, target, k in ((hidden_v, hidden_out, 7), (block_v, block_out, 8)):
        copy = pltpu.make_async_copy(source, target, grads.at[k])
        copy.start()
        stores.append(copy)
    for i in range(BLOCKS):
        rows = at(3, i)
        for a in range(3, 6):
            loads[i][a].wait()
        update(3, rows, slice(0, LEFT), left[rows, :], 0.03, 0.1)
        update(3, rows, slice(LEFT, D), right[rows, :], 0.03, 0.1)
        send(4, rows, i)
    for copy in stores:
        copy.wait()


def update_weights(norm, part, rest, gate, left, right, hidden_grad, block, weights):
    parts = part.shape[0]
    w_in, w_out = weights[0], weights[3]
    sem = pltpu.SemaphoreType.DMA
    vmem = pl.BlockSpec(memory_space=pltpu.VMEM)
    hbm = pl.BlockSpec(memory_space=pltpu.HBM)
    made = [
        jax.ShapeDtypeStruct(w.shape, dtype) for w in (w_in, w_out) for dtype in (F32, F32, F32, BF16)
    ]
    return pl.pallas_call(
        functools.partial(update_kernel, parts),
        in_specs=[vmem, *([hbm] * 13)],
        out_specs=[hbm] * 10,
        out_shape=[
            jax.ShapeDtypeStruct(hidden_grad.shape, F32),
            jax.ShapeDtypeStruct(block.shape, BF16),
            *made,
        ],
        scratch_shapes=[
            *[pltpu.VMEM(w.shape, F32) for w in weights],
            *[pltpu.VMEM(m.shape, m.dtype) for m in made],
            *[
                pltpu.VMEM(a.shape, a.dtype)
                for a in (part, rest, gate, left, right, hidden_grad, block)
            ],
            sem((6 * BLOCKS,)), sem((8 * BLOCKS,)), sem((9,)),
        ],
        compiler_params=pltpu.CompilerParams(vmem_limit_bytes=63 * 2**20),
        name="update_weights",
    )(norm, part, rest, gate, left, right, hidden_grad, block, *weights)


WO_ALL, WO_REST = pl.ds(0, SPLIT), pl.ds(SPLIT, D - SPLIT)


class LineGather:
    def __init__(self, line, z, core, q, slot, own, sends, recvs):
        self.line, self.z, self.core, self.q = line, z, core, q
        self.slot, self.own, self.sends, self.recvs = slot, own, sends, recvs

    def along(self, from_z, up, first=False):
        to = self.z + 1 if up else self.z - 1
        return remote(
            self.own if first else self.slot(from_z),
            self.slot(from_z),
            self.sends.at[0 if up else 1],
            self.recvs.at[0 if up else 1],
            from_z,
            (2 * to + self.core, self.q),
        )

    def push(self, t):
        z, line = self.z, self.line

        @pl.when((z - t >= 0) & (z < line - 1))
        def _():
            self.along(z - t, True, t == 0).start()

        @pl.when((z + t <= line - 1) & (z > 0))
        def _():
            self.along(z + t, False, t == 0).start()

    def pushed(self, t):
        z, line = self.z, self.line

        @pl.when((z - t >= 0) & (z < line - 1))
        def _():
            self.along(z - t, True, t == 0).wait_send()

        @pl.when((z + t <= line - 1) & (z > 0))
        def _():
            self.along(z + t, False, t == 0).wait_send()

    def step(self, t, got=None, push=True):
        z, line = self.z, self.line

        @pl.when(z - t >= 0)
        def _():
            self.along(z - t, True).wait_recv()

            if push:

                @pl.when(z < line - 1)
                def _():
                    self.along(z - t, True).start()

            if got is not None:
                got(z - t)

        @pl.when(z + t <= line - 1)
        def _():
            self.along(z + t, False).wait_recv()

            if push:

                @pl.when(z > 0)
                def _():
                    self.along(z + t, False).start()

            if got is not None:
                got(z + t)


class LineGathers:
    def __init__(self, line, z, core, q, slot, own, sends, recvs):
        half = own.shape[0] // 2
        self.line = line
        self.halves = []
        for h in range(2):
            rows = pl.ds(h * half, half)
            self.halves.append(
                LineGather(
                    line, z, core, q, lambda from_z, rows=rows: slot(from_z).at[rows],
                    own.at[rows], sends.at[h], recvs.at[h],
                )
            )

    def push(self, t):
        for part in self.halves:
            part.push(t)

    def step(self, t, got=None, push=True):
        self.halves[0].step(t, None, push)
        self.halves[1].step(t, got, push)

    def pushed(self):
        for t in range(self.line - 1):
            for part in self.halves:
                part.pushed(t)


class PlaneGather:
    def __init__(self, parts, slot, own, sends, recvs, base=0):
        self.parts, self.slot, self.own = parts, slot, own
        self.sends, self.recvs, self.base = sends, recvs, base
        self.group, self.q = lax.axis_index("dp"), lax.axis_index("seq")
        if parts == 4:
            self.near = [self.q + 1 - 2 * lax.rem(self.q, 2), lax.rem(self.q + 2, 4)]
            self.half = own.shape[0] // 2

    def early(self):
        to = self.near if self.parts == 4 else [peer[1] for peer in seq_peers(self.parts)]
        return [
            remote(
                self.own, self.slot(self.q), self.sends, self.recvs, self.base + k, (self.group, d)
            )
            for k, d in enumerate(to)
        ]

    def late(self):
        if self.parts != 4:
            return []
        copies = []
        for h in range(2):
            block = self.slot(self.near[h]).at[pl.ds(h * self.half, self.half)]
            to = (self.group, self.near[1 - h])
            copies.append(remote(block, block, self.sends, self.recvs, self.base + 2 + h, to))
        return copies

    def start(self):
        for copy in self.early():
            copy.start()

    def turn(self):
        if self.parts == 4:
            for copy in self.early():
                copy.wait()
            for copy in self.late():
                copy.start()

    def finish(self):
        for copy in self.late() if self.parts == 4 else self.early():
            copy.wait()


def chan_rows_of(chan_len, devices):
    return -(-((devices - 1) * chan_len // LANES + 8) // 8) * 8


def unpack_chan(
    chan_len, parts, q, all_chan, full, hp, gain_in, gain_out, taps, heads, skip, spread, gather
):
    cw = INNER // parts
    hq = H // parts
    own, span, shared = cw // LANES, CONV_CH // LANES, 2 * N // LANES
    full[...] = jnp.zeros_like(full)
    for o in range(all_chan.shape[0]):
        at = o * chan_len // LANES
        full[at : at + 8, :] += all_chan[o]
    taps[...] = jnp.zeros_like(taps)
    for tap in range(TAPS + 1):
        for b in range(own):
            taps[tap : tap + 1, b * LANES : (b + 1) * LANES] = full[
                pl.ds(tap * span + q * own + b, 1), :
            ]
        for b in range(shared):
            at = tap * span + INNER // LANES + b
            taps[tap : tap + 1, cw + b * LANES : cw + (b + 1) * LANES] = full[at : at + 1, :]
    at = (TAPS + 1) * span
    for b in range(D // LANES):
        gain_in[:, b * LANES : (b + 1) * LANES] = full[at + b : at + b + 1, :]
    at = at + D // LANES
    for b in range(own):
        gain_out[:, b * LANES : (b + 1) * LANES] = full[pl.ds(at + q * own + b, 1), :]
    for out, axis in ((spread, 0), (gather, 1)):
        head = lax.broadcasted_iota(jnp.int32, out.shape, axis)
        channel = lax.broadcasted_iota(jnp.int32, out.shape, 1 - axis)
        inside = (channel >= head * P_SIZE) & (channel < (head + 1) * P_SIZE)
        out[...] = jnp.where(inside, 1.0, 0.0).astype(BF16)
    ours = own_heads_first(hp[...], hq)
    row = lax.broadcasted_iota(jnp.int32, ours.shape, 0)
    heads[...] = jnp.where(row == 0, ours, jnp.where(row == 1, -jnp.exp(ours), 0.0))
    skip[...] = spread_heads(ours, spread[...])[2:3, :]


def collect_kernel(
    groups, parts, chan_len, hidden, w_in_h, w_own_h, chan, hp,
    hid_out, w_out, gate_out, wo_out, gain_in, gain_out, taps, heads, skip, spread, gather,
    chan_out, full, w_in, w_own, blocks, gates, low, chan_s, chan_r, hid_s, hid_r, swap_s, swap_r, gate_s, gate_r,
    wo_s, wo_r, line_s, line_r, lwo_s, lwo_r, core_s, core_r, local,
):
    line = groups // 2
    cw = INNER // parts
    cc = cw + 2 * N
    group, q = lax.axis_index("dp"), lax.axis_index("seq")
    z, core = group // 2, lax.rem(group, 2)
    sibling = (2 * z + 1 - core, q)
    peers = seq_peers(parts)
    everyone = all_peers(groups, parts)
    loads = [
        pltpu.make_async_copy(w_in_h, w_in, local.at[5]),
        pltpu.make_async_copy(w_own_h, w_own, local.at[6]),
    ]
    for copy in loads:
        copy.start()
    barrier = pltpu.get_barrier_semaphore()
    for device in everyone:
        pl.semaphore_signal(barrier, inc=1, device_id=device, device_id_type=MESH)
    for copy in loads:
        copy.wait()
    shared = w_in[:, 2 * INNER :].astype(BF16)
    for part in range(parts):
        at = INNER + part * cw
        blocks[part, :, :cw] = w_in[:, at : at + cw].astype(BF16)
        blocks[part, :, cw : cc + H] = shared
        blocks[part, :, cc + H :] = jnp.zeros((w_in.shape[0], LANES - H), BF16)
    low[...] = w_own[...].astype(BF16)
    pl.semaphore_wait(barrier, len(everyone))
    swaps = []
    for k, peer in enumerate(peers):
        copy = remote(blocks.at[peer[1]], w_out.at[group, q], swap_s, swap_r, k, peer)
        copy.start()
        swaps.append(copy)
    outs = LineGather(
        line, z, core, q, lambda from_z: wo_out.at[2 * from_z + core, q, :, WO_REST],
        low.at[:, WO_REST], lwo_s, lwo_r,
    )
    outs.push(0)
    own = [
        pltpu.make_async_copy(blocks.at[q], w_out.at[group, q], local.at[0]),
        pltpu.make_async_copy(hidden, hid_out.at[q], local.at[1]),
        pltpu.make_async_copy(chan, chan_out.at[group * parts + q], local.at[2]),
        pltpu.make_async_copy(low, wo_out.at[group, q], local.at[3]),
    ]
    for copy in own:
        copy.start()
    waiting = []
    chans = [
        remote(chan, chan_out.at[group * parts + q], chan_s, chan_r, k, peer)
        for k, peer in enumerate(everyone)
    ]
    for copy in chans:
        copy.start()
    for part in range(parts):
        gates[part] = w_in[:, part * cw : (part + 1) * cw].astype(BF16)
    copy = pltpu.make_async_copy(gates.at[q], gate_out.at[q], local.at[4])
    copy.start()
    own.append(copy)
    own[0].wait()
    for copy in swaps:
        copy.wait()
    hids = PlaneGather(parts, lambda of: hid_out.at[of], hidden, hid_s, hid_r)
    lows = PlaneGather(parts, lambda of: wo_out.at[group, of], low, wo_s, wo_r)
    hids.start()

    def across(from_z):
        block = w_out.at[2 * from_z + core]
        return remote(block, block, core_s, core_r, from_z, sibling)

    ins = LineGathers(
        line, z, core, q, lambda from_z: w_out.at[2 * from_z + core], w_out.at[group],
        line_s, line_r,
    )
    across(z).start()
    ins.push(0)
    lows.start()
    for t in range(1, line):
        ins.step(t, lambda from_z: across(from_z).start(), t < line - 1)
        if t == 1:
            own[2].wait()
            for copy in chans:
                copy.wait()
            unpack_chan(
                chan_len, parts, q, chan_out, full, hp, gain_in, gain_out, taps, heads, skip,
                spread, gather,
            )
        if t == line - 2:
            outs.step(1)
            hids.turn()
            lows.turn()
            for k, peer in enumerate(peers):
                copy = remote(gates.at[peer[1]], gate_out.at[q], gate_s, gate_r, k, peer)
                copy.start()
                waiting.append(copy)
    ins.pushed()
    outs.step(2, None, False)
    outs.pushed(0)
    outs.pushed(1)
    hids.finish()
    lows.finish()
    for from_z in range(line):
        across(from_z).wait_send()
        block = w_out.at[2 * from_z + 1 - core]
        remote(block, block, core_s, core_r, from_z, sibling).wait_recv()
    for copy in own[1:2] + own[3:] + waiting:
        copy.wait()


def collect(collective_id, hidden, w_in, w_own, chan, hp, chan_len, groups, parts):
    rows = w_in.shape[0]
    line = groups // 2
    cw = INNER // parts
    width = cw + 2 * N + LANES
    sem = pltpu.SemaphoreType.DMA
    hbm = pl.BlockSpec(memory_space=pltpu.HBM)
    vmem = pl.BlockSpec(memory_space=pltpu.VMEM)
    return pl.pallas_call(
        functools.partial(collect_kernel, groups, parts, chan_len),
        in_specs=[hbm, hbm, hbm, vmem, vmem],
        out_specs=[*([hbm] * 4), *([vmem] * 7)],
        out_shape=[
            jax.ShapeDtypeStruct((parts,) + hidden.shape, hidden.dtype),
            jax.ShapeDtypeStruct((groups, parts, rows, width), BF16),
            jax.ShapeDtypeStruct((parts, rows, cw), BF16),
            jax.ShapeDtypeStruct((groups, parts) + w_own.shape, BF16),
            jax.ShapeDtypeStruct((1, D), F32),
            jax.ShapeDtypeStruct((1, cw), F32),
            jax.ShapeDtypeStruct((8, cw + 2 * N), F32),
            jax.ShapeDtypeStruct((8, LANES), F32),
            jax.ShapeDtypeStruct((1, cw), F32),
            jax.ShapeDtypeStruct((LANES, cw), BF16),
            jax.ShapeDtypeStruct((cw, LANES), BF16),
        ],
        scratch_shapes=[
            pltpu.VMEM((groups * parts,) + chan.shape, F32),
            pltpu.VMEM((chan_rows_of(chan_len, groups * parts), LANES), F32),
            pltpu.VMEM(w_in.shape, F32),
            pltpu.VMEM(w_own.shape, F32),
            pltpu.VMEM((parts, rows, width), BF16),
            pltpu.VMEM((parts, rows, cw), BF16),
            pltpu.VMEM(w_own.shape, BF16),
            *([sem((groups * parts - 1,))] * 2),
            *([sem((parts + 1,))] * 8),
            *([sem((2, 2, line))] * 2), *([sem((2, line))] * 2),
            sem((line,)), sem((line,)), sem((7,)),
        ],
        compiler_params=pltpu.CompilerParams(
            collective_id=collective_id, has_side_effects=True, vmem_limit_bytes=63 * 2**20
        ),
        name="collect",
    )(hidden, w_in, w_own, chan, hp)


def forward_kernel(
    groups, parts, cw,
    hidden_h, wx_h, gate_h, wo_in, gain_in, gain_out, taps, heads, skip, spread,
    normed_h, px_h, y_h, states_h, z_h, u_h, stat_h, wz_h, wo,
    hidden, wx, wz, normed, px, y, states, zs, us, stats, xbuf, state, xdt, carried,
    line_s, line_r, lwo_s, lwo_r, wide_s, wide_r, stat_s, stat_r, core_s, core_r, wo_s, wo_r, out_s, out_r, u_s, u_r, load, store,
):
    line = groups // 2
    cc = cw + 2 * N
    length = px.shape[0]
    chunks = length // CHUNK
    group, q = lax.axis_index("dp"), lax.axis_index("seq")
    z, core = group // 2, lax.rem(group, 2)
    sibling = (2 * z + 1 - core, q)
    peers = mirror_peers(parts)
    loads = [
        pltpu.make_async_copy(source, target, load.at[k])
        for k, (source, target) in enumerate(
            [(hidden_h, hidden), (wx_h, wx), (gate_h, wz.at[group])]
        )
    ]
    for copy in loads:
        copy.start()
    greet(peers + dp_peers(groups))

    outs = LineGather(
        line, z, core, q, lambda from_z: wo.at[2 * from_z + core, q, :, WO_REST],
        wo.at[group, q, :, WO_REST], lwo_s, lwo_r,
    )
    wides = LineGather(
        line, z, core, q, lambda from_z: wo.at[2 * from_z + core, :, :, WO_ALL],
        wo.at[group, :, :, WO_ALL], wide_s, wide_r,
    )

    def planes(t, act):
        for from_z, there in ((z - t, z - t >= 0), (z + t, z + t <= line - 1)):

            @pl.when(there)
            def _(from_z=from_z):
                block = wo.at[2 * from_z + core]
                act(
                    PlaneGather(
                        parts, lambda of: block.at[of, :, WO_REST], block.at[q, :, WO_REST],
                        out_s, out_r,
                        from_z * (parts + 1),
                    )
                )

    outs.push(2)
    planes(1, PlaneGather.start)
    planes(2, PlaneGather.start)

    def parity(from_z, of, columns):
        block = wo.at[2 * from_z + of, :, :, columns]
        at = from_z if columns is WO_REST else line + from_z
        return remote(block, block, wo_s, wo_r, at, sibling)

    def across_planes(t):
        planes(t, PlaneGather.finish)
        for from_z, there in ((z - t, z - t >= 0), (z + t, z + t <= line - 1)):

            @pl.when(there)
            def _(from_z=from_z):
                parity(from_z, core, WO_REST).start()

    def across_wide(from_z):
        parity(from_z, core, WO_ALL).start()

    across_wide(z)
    parity(z, core, WO_REST).start()

    def across(from_z):
        block = wz.at[2 * from_z + core]
        return remote(block, block, core_s, core_r, from_z, sibling)

    gates = LineGathers(
        line, z, core, q, lambda from_z: wz.at[2 * from_z + core], wz.at[group], line_s, line_r
    )
    loads[2].wait()
    across(z).start()
    gates.push(0)
    loads[0].wait()

    def norm_rows(i, carry):
        rows = pl.ds(pl.multiple_of(i * 32, 32), 32)
        tokens = hidden[rows, :].astype(F32)
        mean = jnp.sum(tokens * tokens, axis=-1, keepdims=True) / D
        normed[rows, :] = (tokens * lax.rsqrt(mean + EPS_IN) * gain_in[...]).astype(BF16)
        return carry

    lax.fori_loop(0, length // 32, norm_rows, 0)
    loads[1].wait()
    tall = 256

    def project_rows(i, carry):
        rows = pl.ds(pl.multiple_of(i * tall, tall), tall)
        px[rows, :] = dot(normed[rows, :], wx[...])
        return carry

    lax.fori_loop(0, length // tall, project_rows, 0)
    stores = [
        pltpu.make_async_copy(normed, normed_h, store.at[0]),
        pltpu.make_async_copy(px, px_h, store.at[1]),
    ]
    for copy in stores:
        copy.start()
    state[...] = jnp.zeros_like(state)
    xbuf[0:8, :] = jnp.zeros((8, cc), F32)

    def scan_rows(i, carry):
        for t in range(1, line - 1):

            @pl.when(i == min(5 * t - 4, chunks - 1))
            def _(t=t):
                gates.step(t, lambda from_z: across(from_z).start(), t < line - 1)
                if t == line - 2:
                    wides.push(0)

        for t in range(3, line):

            @pl.when(i == min(2 * t - 3, chunks - 1))
            def _(t=t):
                outs.step(t, None, t < line - 1)
                planes(t, PlaneGather.start)

        @pl.when(i == min(5, chunks - 1))
        def _():
            planes(1, PlaneGather.turn)
            planes(2, PlaneGather.turn)

        rows = pl.ds(pl.multiple_of(i * CHUNK, CHUNK), CHUNK)
        scan_forward_step(
            cw, px.at[rows], taps, heads, skip, spread, y.at[rows], states.at[i],
            xbuf, state, xdt, carried,
        )
        return carry

    lax.fori_loop(0, chunks, scan_rows, 0)
    for source, target, at in ((y, y_h, 2), (states, states_h, 3)):
        copy = pltpu.make_async_copy(source, target, store.at[at])
        copy.start()
        stores.append(copy)
    for t in range(3, line):
        planes(t, PlaneGather.turn)
    gates.step(line - 1, lambda from_z: across(from_z).start(), False)
    for from_z in range(line):
        across(from_z).wait_send()
        block = wz.at[2 * from_z + 1 - core]
        remote(block, block, core_s, core_r, from_z, sibling).wait_recv()
    gates.pushed()
    for t in range(2, line - 1):
        outs.pushed(t)
    copy = pltpu.make_async_copy(wz, wz_h, store.at[4])
    copy.start()
    stores.append(copy)
    lane = lax.broadcasted_iota(jnp.int32, (1, LANES), 1)
    wide = 512

    def gate_rows(rows):
        gate_in = dot(normed[rows, :], wz[...].reshape(D, cw))
        zs[rows, :] = gate_in
        gated = y[rows, :] * (gate_in * jax.nn.sigmoid(gate_in))
        us[rows, :] = (gated * gain_out[...]).astype(BF16)
        squares = jnp.zeros((tall, LANES), F32)
        for b in range(cw // wide):
            block = gated[:, b * wide : (b + 1) * wide]
            total = jnp.sum(block * block, axis=-1, keepdims=True)
            level = level_of(q * cw + b * wide, wide)
            squares = squares + jnp.where(lane == level, total, 0.0)
        stats[:, rows] = squares.T[:8, :]

    waiting = []
    tokens = length // parts
    for k, dest in enumerate([peer[1] for peer in peers] + [q]):

        def block_rows(i, carry, dest=dest):
            gate_rows(pl.ds(pl.multiple_of(dest * tokens + i * tall, tall), tall))
            return carry

        lax.fori_loop(0, tokens // tall, block_rows, 0)
        ours = us.at[pl.ds(pl.multiple_of(dest * tokens, tokens), tokens)]
        stat = stats.at[:, pl.ds(pl.multiple_of(dest * tokens, tokens), tokens)]
        if k < len(peers):
            some = [
                remote(ours, u_h.at[q], u_s, u_r, k, peers[k]),
                remote(stat, stat_h.at[q], stat_s, stat_r, k, peers[k]),
            ]
        else:
            some = [
                pltpu.make_async_copy(ours, u_h.at[q], store.at[6]),
                pltpu.make_async_copy(stat, stat_h.at[q], store.at[7]),
            ]
        for copy in some:
            copy.start()
        waiting += some
        if k == 0:
            wides.step(1, across_wide)
        if k == 1:
            for t in range(2, line - 1):
                wides.step(t, across_wide)
        if k in (1, 2):
            across_planes(k)
    copy = pltpu.make_async_copy(zs, z_h, store.at[5])
    copy.start()
    stores.append(copy)

    for t in range(3, line):
        across_planes(t)
    wides.step(line - 1, across_wide, False)
    for t in range(line - 1):
        wides.pushed(t)
    for copy in waiting + stores:
        copy.wait()
    for columns in (WO_REST, WO_ALL):
        for d in range(line):
            parity(d, core, columns).wait_send()
            parity(d, 1 - core, columns).wait_recv()


def forward(collective_id, hidden, wx, gate, wo, gain_in, gain_out, taps, heads, skip, spread):
    groups, parts = wo.shape[:2]
    line = groups // 2
    length = hidden.shape[0]
    rows, cw = gate.shape[1:]
    cc = cw + 2 * N
    width = cc + LANES
    chunks = length // CHUNK
    sem = pltpu.SemaphoreType.DMA
    hbm = pl.BlockSpec(memory_space=pltpu.HBM)
    vmem = pl.BlockSpec(memory_space=pltpu.VMEM)
    u = jax.ShapeDtypeStruct((parts, length // parts, cw), BF16)
    stat = jax.ShapeDtypeStruct((parts, 8, length // parts), F32)
    made = [
        jax.ShapeDtypeStruct((length, D), BF16),
        jax.ShapeDtypeStruct((length, width), F32),
        jax.ShapeDtypeStruct((length, cw), F32),
        jax.ShapeDtypeStruct((chunks, N, cw), BF16),
        jax.ShapeDtypeStruct((length, cw), F32),
        jax.ShapeDtypeStruct((length, cw), BF16),
        jax.ShapeDtypeStruct((8, length), F32),
    ]
    wz = jax.ShapeDtypeStruct((groups, parts, rows, cw), BF16)
    return pl.pallas_call(
        functools.partial(forward_kernel, groups, parts, cw),
        in_specs=[*([hbm] * 4), *([vmem] * 6)],
        out_specs=[hbm] * 9,
        out_shape=[*made[:-2], u, stat, wz, jax.ShapeDtypeStruct(wo.shape, BF16)],
        input_output_aliases={3: 8},
        scratch_shapes=[
            pltpu.VMEM(hidden.shape, BF16),
            pltpu.VMEM(wx.shape, BF16),
            pltpu.VMEM(wz.shape, BF16),
            *[pltpu.VMEM(m.shape, m.dtype) for m in made],
            pltpu.VMEM((CHUNK + 8, cc), F32),
            pltpu.VMEM((N, cw), F32),
            pltpu.VMEM((CHUNK, cw), BF16),
            pltpu.VMEM((CHUNK, cw), F32),
            *([sem((2, 2, line))] * 2), *([sem((2, line))] * 4),
            sem((parts - 1,)), sem((parts - 1,)),
            sem((line,)), sem((line,)), sem((2 * line,)), sem((2 * line,)),
            sem((line * (parts + 1),)), sem((line * (parts + 1),)),
            sem((parts - 1,)), sem((parts - 1,)),
            sem((3,)), sem((8,)),
        ],
        compiler_params=pltpu.CompilerParams(
            collective_id=collective_id, has_side_effects=True, vmem_limit_bytes=63 * 2**20
        ),
        name="forward",
    )(hidden, wx, gate, wo, gain_in, gain_out, taps, heads, skip, spread)


def add_blocks(out, a, b, rows, steps):
    def step(i, carry):
        at = pl.ds(pl.multiple_of(i * rows, rows), rows)
        out[at] = (a[at].astype(F32) + b[at].astype(F32)).astype(out.dtype)
        return carry

    lax.fori_loop(0, steps, step, 0)


def level_of(channel, width):
    return sum((channel >= level_width(k)).astype(jnp.int32) for k in range(LEVELS - 1))


def mirror_peers(parts):
    group, q = lax.axis_index("dp"), lax.axis_index("seq")
    if parts != 4:
        return seq_peers(parts)
    return [(group, 3 - q), (group, q + 1 - 2 * lax.rem(q, 2)), (group, lax.rem(q + 2, 4))]


def middle_kernel(
    groups, parts, cw,
    u_h, stat_h, wo, cot_h, tokens_h,
    back_h, coef_h, block_h, left_h, right_h,
    u, stats, cot, tokens, mixed, branch, norms, pulls, back, coefs, weights, sent, held, left, right,
    back_s, back_r, coef_s, coef_r, core_s, core_r, fetch, load, store, local,
):
    line = groups // 2
    group, q = lax.axis_index("dp"), lax.axis_index("seq")
    z, core = group // 2, lax.rem(group, 2)
    sibling = (2 * z + 1 - core, q)
    peers = mirror_peers(parts)
    loads = [
        pltpu.make_async_copy(stat_h, stats, load.at[3]),
        pltpu.make_async_copy(cot_h, cot, load.at[1]),
        pltpu.make_async_copy(u_h, u, load.at[0]),
        pltpu.make_async_copy(tokens_h, tokens, load.at[2]),
    ]
    for copy in loads:
        copy.start()
    greet(peers + [sibling])
    for copy in loads[:2]:
        copy.wait()

    terms = stats[0]
    for part in range(1, parts):
        terms = terms + stats[part]
    terms = jnp.concatenate([terms, jnp.zeros((LANES - 8, terms.shape[1]), F32)], axis=0).T
    squares = jnp.zeros((terms.shape[0], 1), F32)
    for k in range(LEVELS):
        squares = squares + terms[:, k : k + 1]
        norms[:, k : k + 1] = lax.rsqrt(squares / level_width(k) + EPS_OUT)
    rows = 32

    def mix_rows(i, carry):
        at = pl.ds(pl.multiple_of(i * rows, rows), rows)
        running = norms[at, LEVELS - 1 : LEVELS] * cot[LEVELS - 1, at, :].astype(F32)
        mixed[LEVELS - 1, at, :] = running.astype(BF16)
        for k in reversed(range(LEVELS - 1)):
            running = running + norms[at, k : k + 1] * cot[k, at, :].astype(F32)
            mixed[k, at, :] = running.astype(BF16)
        return carry

    lax.fori_loop(0, tokens.shape[0] // rows, mix_rows, 0)

    width = INNER // groups
    per = WIDE // width
    slots = weights.shape[0]
    dests = [peer[1] for peer in peers] + [q]
    firsts = [dest * cw + b * WIDE for dest in dests for b in range(cw // WIDE)]
    firsts += [b * WIDE for b in range(INNER // WIDE)]

    def get(i):
        return pltpu.make_async_copy(
            wo.at[pl.ds(firsts[i] // width, per)], weights.at[i % slots], fetch.at[i % slots]
        )

    def block_of(i):
        get(i).wait()
        return weights[i % slots].reshape(WIDE, D)

    for i in range(slots - 1):
        get(i).start()
    outgoing = []
    for i in range(len(dests) * (cw // WIDE)):
        get(i + slots - 1).start()
        at, b = divmod(i, cw // WIDE)
        lanes = slice(b * WIDE, (b + 1) * WIDE)
        level = level_of(firsts[i], WIDE)
        back[dests[at], :, lanes] = dot(mixed[level], block_of(i), NT).astype(BF16)
        if b == cw // WIDE - 1:
            if at < len(peers):
                copy = remote(back.at[dests[at]], back_h.at[q], back_s, back_r, at, peers[at])
            else:
                copy = pltpu.make_async_copy(back.at[q], back_h.at[q], local.at[0])
            copy.start()
            outgoing.append(copy)
    first = len(dests) * (cw // WIDE)
    for copy in loads[2:]:
        copy.wait()
    branch[...] = jnp.zeros_like(branch)
    for b in range(INNER // WIDE):
        if first + b + slots - 1 < len(firsts):
            get(first + b + slots - 1).start()
        part, at = divmod(b * WIDE, cw)
        branch[...] += dot(u[part, :, at : at + WIDE], block_of(first + b))
        for k in range(LEVELS):
            if level_width(k) == (b + 1) * WIDE:

                def level_rows(i, carry, k=k):
                    at = pl.ds(pl.multiple_of(i * rows, rows), rows)
                    norm = norms[at, k : k + 1]
                    total = branch[at, :]
                    inner = jnp.sum(cot[k, at, :].astype(F32) * total, axis=-1, keepdims=True)
                    pulls[at, k : k + 1] = norm * norm * norm * (inner / level_width(k))
                    cot[k, at, :] = (tokens[at, :].astype(F32) + norm * total).astype(BF16)
                    return carry

                lax.fori_loop(0, tokens.shape[0] // rows, level_rows, 0)
                copy = pltpu.make_async_copy(cot.at[k], block_h.at[k], store.at[k])
                copy.start()
                outgoing.append(copy)
    coef = jnp.zeros((tokens.shape[0], 1), F32)
    lane = lax.broadcasted_iota(jnp.int32, (1, LANES), 1)
    packed = jnp.zeros((tokens.shape[0], LANES), F32)
    for k in reversed(range(LEVELS)):
        coef = coef + pulls[:, k : k + 1]
        high, rest = two_terms(coef)
        packed = jnp.where(lane == k, high.astype(F32), packed)
        packed = jnp.where(lane == LEVELS + k, rest.astype(F32), packed)
    coefs[...] = packed.astype(BF16)
    for k, peer in enumerate(peers):
        copy = remote(coefs, coef_h.at[q], coef_s, coef_r, k, peer)
        copy.start()
        outgoing.append(copy)
    copy = pltpu.make_async_copy(coefs, coef_h.at[q], local.at[1])
    copy.start()
    outgoing.append(copy)

    share = width // parts

    def product(of, cols):
        channel = of * width
        lanes = pl.ds(pl.multiple_of(lax.rem(channel, cw), width), width)
        return dot(u[channel // cw, :, lanes], mixed[level_of(channel, width), :, cols], TN)

    cores = []
    for d in range(line):

        for cols in (slice(0, D // 2), slice(D // 2, D)):
            sent[d, :, cols] = product(2 * d + 1 - core, cols).astype(BF16)
        copy = remote(sent.at[d], held.at[d], core_s, core_r, d, sibling)
        copy.start()
        cores.append(copy)
    for d in range(line):
        cores[d].wait_recv()
        half = LEFT // 2
        for out, target, at, cuts in (
            (left, left_h, 0, ((0, half), (half, LEFT))),
            (right, right_h, 1, ((LEFT, D),)),
        ):
            for low, high in cuts:
                cols = slice(low, high)
                total = product(2 * d + core, cols) + held[d, :, cols].astype(F32)
                total = total.astype(BF16)
                to = slice(low - cuts[0][0], high - cuts[0][0])
                for part in range(parts):
                    out[part, d, :, to] = total[part * share : (part + 1) * share]
            copy = pltpu.make_async_copy(
                out.at[:, d], target.at[:, d], store.at[LEVELS + 2 * d + at]
            )
            copy.start()
            outgoing.append(copy)
    for copy in cores:
        copy.wait_send()
    for copy in outgoing:
        copy.wait()


def middle(collective_id, u, stats, wo, cotangent, tokens):
    groups, parts, share = wo.shape[:3]
    line = groups // 2
    rows, cw = u.shape[1:]
    width = share * parts
    sem = pltpu.SemaphoreType.DMA
    hbm = pl.BlockSpec(memory_space=pltpu.HBM)
    left = (parts, line, share, LEFT)
    right = (parts, line, share, D - LEFT)
    return pl.pallas_call(
        functools.partial(middle_kernel, groups, parts, cw),
        in_specs=[hbm] * 5,
        out_specs=[hbm] * 5,
        out_shape=[
            jax.ShapeDtypeStruct((parts, rows, cw), BF16),
            jax.ShapeDtypeStruct((parts, rows, LANES), BF16),
            jax.ShapeDtypeStruct(cotangent.shape, BF16),
            jax.ShapeDtypeStruct(left, BF16),
            jax.ShapeDtypeStruct(right, BF16),
        ],
        scratch_shapes=[
            pltpu.VMEM(u.shape, BF16),
            pltpu.VMEM(stats.shape, F32),
            pltpu.VMEM(cotangent.shape, BF16),
            pltpu.VMEM(tokens.shape, BF16),
            pltpu.VMEM(cotangent.shape, BF16),
            pltpu.VMEM((rows, D), F32),
            pltpu.VMEM((rows, LANES), F32),
            pltpu.VMEM((rows, LANES), F32),
            pltpu.VMEM((parts, rows, cw), BF16),
            pltpu.VMEM((rows, LANES), BF16),
            pltpu.VMEM((3, WIDE // width, parts, share, D), BF16),
            pltpu.VMEM((line, width, D), BF16),
            pltpu.VMEM((line, width, D), BF16),
            pltpu.VMEM(left, BF16),
            pltpu.VMEM(right, BF16),
            *([sem((parts - 1,))] * 4),
            sem((line,)), sem((line,)), sem((3,)), sem((4,)), sem((LEVELS + 2 * line,)), sem((2,)),
        ],
        compiler_params=pltpu.CompilerParams(
            collective_id=collective_id, has_side_effects=True, vmem_limit_bytes=63 * 2**20
        ),
        name="middle",
    )(u, stats, wo, cotangent, tokens)


def sum_blocks(out, blocks, rows):
    def step(i, carry):
        at = pl.ds(pl.multiple_of(i * rows, rows), rows)
        total = blocks[0][at].astype(F32)
        for block in blocks[1:]:
            total = total + block[at].astype(F32)
        out[at] = total.astype(out.dtype)
        return carry

    lax.fori_loop(0, out.shape[0] // rows, step, 0)


class PlaneSum:
    def __init__(self, parts, group, q, blocks, first, second, sends, recvs, source=None):
        self.parts, self.group, self.q = parts, group, q
        self.source = blocks if source is None else source
        self.blocks, self.first, self.second = blocks, first, second
        self.sends, self.recvs = sends, recvs
        self.half = blocks.shape[1] // 2
        if parts == 4:
            self.near = [q + 1 - 2 * lax.rem(q, 2), lax.rem(q + 2, 4)]
            self.far = 3 - q

    @staticmethod
    def scratch(parts, shape, dtype):
        if parts == 4:
            half = (shape[0] // 2,) + shape[1:]
            first, second, count = (2, 2) + half, (2, 2) + half, 6
        else:
            first, second, count = (parts - 1,) + shape, (1, 16, LANES), parts - 1
        sem = pltpu.SemaphoreType.DMA
        return [pltpu.VMEM(first, dtype), pltpu.VMEM(second, dtype), sem((count,)), sem((count,))]

    def piece(self, of, h, source=None):
        blocks = self.blocks if source is None else source
        return blocks.at[of, pl.ds(h * self.half, self.half)]

    def early(self, h):
        if self.parts != 4:
            return []
        near = self.near[h]
        to = (self.group, near)
        return [
            remote(
                self.piece(of, h, self.source), self.first.at[h, k],
                self.sends, self.recvs, 2 * h + k, to,
            )
            for k, of in enumerate((near, self.far))
        ]

    def late(self, h):
        to = (self.group, self.near[1 - h])
        return remote(
            self.second.at[h, 0], self.second.at[h, 1], self.sends, self.recvs, 4 + h, to
        )

    def direct(self):
        peers = seq_peers(self.parts)
        return [
            remote(self.source.at[peer[1]], self.first.at[k], self.sends, self.recvs, k, peer)
            for k, peer in enumerate(peers)
        ]

    def start_far(self):
        for h in range(2):
            for copy in self.early(h)[1:]:
                copy.start()

    def start_near(self, h):
        for copy in self.early(h)[:1]:
            copy.start()

    def start(self, h):
        for copy in self.early(h):
            copy.start()
        if self.parts != 4 and h == 1:
            for copy in self.direct():
                copy.start()

    def turn(self, rows):
        if self.parts != 4:
            return
        for h in range(2):
            for copy in self.early(h):
                copy.wait()
            beyond = self.piece(self.near[1 - h], h)
            each(self.second.at[h, 0], [beyond, self.first.at[h, 1]], rows)
            self.late(h).start()

    def finish(self, out, rows):
        if self.parts != 4:
            for copy in self.direct():
                copy.wait()
            each(
                out,
                [self.blocks.at[self.q]] + [self.first.at[k] for k in range(self.parts - 1)],
                rows,
            )
            return
        for h in range(2):
            self.late(h).wait()
            each(
                out.at[pl.ds(h * self.half, self.half)],
                [self.piece(self.q, h), self.first.at[h, 0], self.second.at[h, 1]],
                rows,
            )


def each(out, blocks, rows):
    if len(out.shape) == 2:
        sum_blocks(out, blocks, rows)
        return
    for d in range(out.shape[0]):
        sum_blocks(out.at[d], [block.at[d] for block in blocks], rows)


class LineSum:
    def __init__(self, line, z, core, q, acc, up, down, up_s, up_r, down_s, down_r, rows, steps):
        self.line, self.z, self.core, self.q = line, z, core, q
        self.acc, self.up, self.down = acc, up, down
        self.up_s, self.up_r, self.down_s, self.down_r = up_s, up_r, down_s, down_r
        self.rows, self.steps = rows, steps

    def ahead(self, d, first):
        block = self.acc.at[d] if first else self.up.at[d]
        to = (2 * (self.z + 1) + self.core, self.q)
        return remote(block, self.up.at[d], self.up_s, self.up_r, d, to)

    def behind(self, d, first):
        block = self.acc.at[d] if first else self.down.at[d]
        to = (2 * (self.z - 1) + self.core, self.q)
        return remote(block, self.down.at[d], self.down_s, self.down_r, d, to)

    def add(self, into, d):
        add_blocks(into.at[d], into.at[d], self.acc.at[d], self.rows, self.steps)

    def step(self, t):
        line, z = self.line, self.z
        far, near = line - 1 - t + z, t - (line - 1 - z)

        @pl.when(z == 0)
        def _():
            self.ahead(line - 1 - t, True).start()

        @pl.when((z > 0) & (z <= t))
        def _():
            self.ahead(far, False).wait_recv()
            self.add(self.up, far)
            self.ahead(far, False).start()

        @pl.when(z == line - 1)
        def _():
            self.behind(t, True).start()

        @pl.when((z < line - 1) & (line - 1 - z <= t))
        def _():
            self.behind(near, False).wait_recv()
            self.add(self.down, near)
            self.behind(near, False).start()

    def sent(self, t):
        line, z = self.line, self.z
        far, near = line - 1 - t + z, t - (line - 1 - z)

        @pl.when(z == 0)
        def _():
            self.ahead(line - 1 - t, True).wait_send()

        @pl.when((z > 0) & (z <= t))
        def _():
            self.ahead(far, False).wait_send()

        @pl.when(z == line - 1)
        def _():
            self.behind(t, True).wait_send()

        @pl.when((z < line - 1) & (line - 1 - z <= t))
        def _():
            self.behind(near, False).wait_send()

    def finish(self, out):
        line, z = self.line, self.z

        @pl.when(z == 0)
        def _():
            self.behind(z, False).wait_recv()
            add_blocks(out, self.acc.at[z], self.down.at[z], self.rows, self.steps)

        @pl.when(z == line - 1)
        def _():
            self.ahead(z, False).wait_recv()
            add_blocks(out, self.acc.at[z], self.up.at[z], self.rows, self.steps)

        @pl.when((z > 0) & (z < line - 1))
        def _():
            self.ahead(z, False).wait_recv()
            self.add(self.up, z)
            self.behind(z, False).wait_recv()
            add_blocks(out, self.up.at[z], self.down.at[z], self.rows, self.steps)


class LineSums:
    def __init__(self, line, z, core, q, acc, up, down, sems, rows):
        half = acc.shape[1] // 2
        self.line = line
        self.halves = [
            LineSum(
                line, z, core, q, *[a.at[:, pl.ds(h * half, half)] for a in (acc, up, down)],
                *[s.at[h] for s in sems], rows, half // rows,
            )
            for h in range(2)
        ]
        self.half = half

    def step(self, t):
        for part in self.halves:
            part.step(t)

    def finish(self, out):
        for h, part in enumerate(self.halves):
            part.finish(out.at[pl.ds(h * self.half, self.half)])

    def sent(self):
        for t in range(self.line - 1):
            for part in self.halves:
                part.sent(t)


def backward_kernel(
    groups, parts, cw,
    back_h, coefs_h, normed_h, px_h, y_h, z_h, states_h, wide_h,
    gain, taps, heads, skip, spread, gather,
    dz_h, dpx_h, small, wide_sum, gate_sum,
    dz, coefs, normed, px, y, dy, states, wide, dpx, dtaps, dheads, dskip, dgain,
    xbuf, dstate, dcbuf, slope, xact, xd_s, dxd_s, acc_s,
    first, second, wide_s, wide_r, gate_made, gate_held, gate_acc, gate_up, gate_down,
    core_s, core_r, up_s, up_r, down_s, down_r, load, store,
):
    line = groups // 2
    cc = cw + 2 * N
    length = y.shape[0]
    chunks = length // CHUNK
    group, q = lax.axis_index("dp"), lax.axis_index("seq")
    z, core = group // 2, lax.rem(group, 2)
    sibling = (2 * z + 1 - core, q)
    loads = [
        pltpu.make_async_copy(source, target, load.at[k])
        for k, (source, target) in enumerate(
            [(wide_h, wide), (back_h, dz), (coefs_h, coefs), (y_h, y), (z_h, dy),
             (normed_h, normed), (states_h, states)]
        )
    ]
    for copy in loads[1:5]:
        copy.start()

    def fetch(at, first=False):
        slot = lax.rem(at, 2)
        if first:
            return pltpu.make_async_copy(
                px_h.at[pl.ds(0, CHUNK)], px.at[0, pl.ds(8, CHUNK)], load.at[7]
            )
        rows = pl.ds(pl.multiple_of(at * CHUNK - 8, 8), CHUNK + 8)
        return pltpu.make_async_copy(px_h.at[rows], px.at[slot], load.at[7 + slot])

    greet(seq_peers(parts) + dp_peers(groups))
    plane = PlaneSum(parts, group, q, wide, first, second, wide_s, wide_r, wide_h)
    plane.start(0)
    plane.start(1)
    for copy in loads[1:5]:
        copy.wait()
    loads[5].start()
    loads[6].start()
    loads[0].start()
    fetch(chunks - 1).start()

    rows = 32
    lane = lax.broadcasted_iota(jnp.int32, (1, LANES), 1)
    dgain[...] = jnp.zeros_like(dgain)

    def gate_rows(i, carry):
        at = pl.ds(pl.multiple_of(i * rows, rows), rows)
        coef = coefs[at, :].astype(F32)
        for b in range(cw // WIDE):
            lanes = slice(b * WIDE, (b + 1) * WIDE)
            level = level_of(q * cw + b * WIDE, WIDE)
            ours = (lane == level) | (lane == level + LEVELS)
            pull = jnp.sum(jnp.where(ours, coef, 0.0), axis=-1, keepdims=True)
            gate_in = dy[at, lanes]
            sig = jax.nn.sigmoid(gate_in)
            gate = gate_in * sig
            y_at = y[at, lanes]
            gated = y_at * gate
            back = dz[at, lanes].astype(F32)
            dgated = gain[:, lanes] * back - gated * pull
            dgain[0:1, lanes] += jnp.sum(back * gated, axis=0, keepdims=True)
            dz[at, lanes] = (dgated * y_at * (sig + gate * (1.0 - sig))).astype(BF16)
            dy[at, lanes] = dgated * gate
        return carry

    lax.fori_loop(0, length // rows, gate_rows, 0)
    dz_out = pltpu.make_async_copy(dz, dz_h, store.at[0])
    dz_out.start()
    loads[5].wait()
    span = gate_acc.shape[1]

    def dweight(of, out):
        at = pl.ds(pl.multiple_of(of * span, span), span)
        out[...] = dot(normed[:, at], dz[...], TN).astype(BF16)

    def core_copy(d):
        return remote(gate_made.at[d], gate_held.at[d], core_s, core_r, d, sibling)

    order = [d for k in range(line // 2) for d in (line - 1 - k, k)]
    gates = LineSums(
        line, z, core, q, gate_acc, gate_up, gate_down, (up_s, up_r, down_s, down_r), span // 8
    )
    for some in (order[:2], order[2:]):
        for d in some:
            dweight(2 * d + 1 - core, gate_made.at[d])
            core_copy(d).start()
        for d in some:
            dweight(2 * d + core, gate_acc.at[d])
            core_copy(d).wait()
            add_blocks(gate_acc.at[d], gate_acc.at[d], gate_held.at[d], span // 4, 4)
        if some[0] == order[0]:
            gates.step(0)
    dstate[...] = jnp.zeros_like(dstate)
    dcbuf[CHUNK : CHUNK + 8, :] = jnp.zeros((8, cc), F32)
    dtaps[...] = jnp.zeros_like(dtaps)
    dheads[...] = jnp.zeros_like(dheads)
    dskip[...] = jnp.zeros_like(dskip)
    loads[6].wait()
    loads[0].wait()

    def scan_rows(i, carry):
        for t in range(1, line - 1):

            @pl.when(i == min(3 * t - 1, chunks - 1))
            def _(t=t):
                gates.step(t)

        @pl.when(i == 4)
        def _():
            plane.turn(32)

        at = chunks - 1 - i
        here = pl.ds(pl.multiple_of(at * CHUNK, CHUNK), CHUNK)

        @pl.when(at > 0)
        def _():
            fetch(at).wait()

        @pl.when(at == 0)
        def _():
            fetch(0, True).wait()

        @pl.when(at > 1)
        def _():
            fetch(at - 1).start()

        @pl.when(at == 1)
        def _():
            fetch(0, True).start()

        rows = px.at[lax.rem(at, 2)]
        scan_backward_step(
            cw, at == 0, rows.at[pl.ds(8, CHUNK)], rows.at[pl.ds(0, 8)], taps, heads, skip, spread, gather,
            dy.at[here], y.at[here], states.at[at], dpx.at[here], dtaps, dheads, dskip,
            xbuf, dstate, dcbuf, slope, xact, xd_s, dxd_s, acc_s,
        )
        return carry

    lax.fori_loop(0, chunks, scan_rows, 0)
    dpx_out = pltpu.make_async_copy(dpx, dpx_h, store.at[1])
    dpx_out.start()
    small[...] = jnp.zeros_like(small)
    wide_rows, own_rows = cc // LANES, cw // LANES
    for tap in range(TAPS + 1):
        for b in range(wide_rows):
            to = tap * wide_rows + b
            small[to : to + 1, :] = dtaps[tap : tap + 1, b * LANES : (b + 1) * LANES]
    to = (TAPS + 1) * wide_rows
    for b in range(own_rows):
        small[to + b : to + b + 1, :] = dgain[0:1, b * LANES : (b + 1) * LANES]
    hq = cw // P_SIZE
    skips = spread_heads(dskip[...], gather[...])
    small[to + own_rows : to + own_rows + 1, :] = (
        dheads[0:1, :]
        + pltpu.roll(dheads[...], hq, 1)[1:2, :]
        + pltpu.roll(skips, 2 * hq, 1)[0:1, :]
    )
    plane.finish(wide_sum, 32)
    gates.finish(gate_sum)
    gates.sent()
    dz_out.wait()
    dpx_out.wait()


def backward(
    collective_id, back, coefs, normed, px, y, z, states, wide, gain, taps, heads, skip, spread, gather
):
    parts, line = wide.shape[:2]
    length, width = px.shape
    cw = skip.shape[1]
    cc = cw + 2 * N
    span = D // (2 * line)
    sem = pltpu.SemaphoreType.DMA
    vmem = pl.BlockSpec(memory_space=pltpu.VMEM)
    hbm = pl.BlockSpec(memory_space=pltpu.HBM)
    small_rows = (TAPS + 1) * (cc // LANES) + cw // LANES + 1
    small_rows = -(-small_rows // 8) * 8
    return pl.pallas_call(
        functools.partial(backward_kernel, 2 * line, parts, cw),
        in_specs=[*([hbm] * 8), *([vmem] * 6)],
        out_specs=[hbm, hbm, vmem, vmem, vmem],
        out_shape=[
            jax.ShapeDtypeStruct((length, cw), BF16),
            jax.ShapeDtypeStruct((length, width), BF16),
            jax.ShapeDtypeStruct((small_rows, LANES), F32),
            jax.ShapeDtypeStruct(wide.shape[1:], BF16),
            jax.ShapeDtypeStruct((span, cw), BF16),
        ],
        scratch_shapes=[
            *[pltpu.VMEM(a.shape, a.dtype) for a in (back, coefs, normed)],
            pltpu.VMEM((2, CHUNK + 8, width), F32),
            *[pltpu.VMEM(a.shape, a.dtype) for a in (y, z, states, wide)],
            pltpu.VMEM((length, width), BF16),
            pltpu.VMEM((8, cc), F32),
            pltpu.VMEM((8, LANES), F32),
            pltpu.VMEM((8, cw), F32),
            pltpu.VMEM((8, cw), F32),
            pltpu.VMEM((CHUNK + 8, cc), F32),
            pltpu.VMEM((N, cw), F32),
            pltpu.VMEM((CHUNK + 8, cc), F32),
            pltpu.VMEM((CHUNK, cc), F32),
            pltpu.VMEM((CHUNK, cc), F32),
            pltpu.VMEM((CHUNK, cw), BF16),
            pltpu.VMEM((CHUNK, cw), F32),
            pltpu.VMEM((CHUNK, CHUNK), F32),
            *PlaneSum.scratch(parts, wide.shape[1:], BF16),
            *([pltpu.VMEM((line, span, cw), BF16)] * 5),
            sem((line,)), sem((line,)), *([sem((2, line))] * 4),
            sem((9,)), sem((2,)),
        ],
        compiler_params=pltpu.CompilerParams(
            collective_id=collective_id, has_side_effects=True, vmem_limit_bytes=63 * 2**20
        ),
        name="backward",
    )(back, coefs, normed, px, y, z, states, wide, gain, taps, heads, skip, spread, gather)


def owners_kernel(
    groups, parts, rows, cw,
    normed, left, right, gate, small, dz, dpx, wz, wx,
    part, rest_out, left_out, right_out, gate_out, back_out, small_all,
    made, held, acc, up, down, final, left_up, left_down, right_acc, right_up, right_down,
    rest_made, rest_held, rest, rest_acc, rest_up, rest_down,
    normed_v, dz_v, dpx_v, wz_v, wx_v, back, back_sum,
    right_1, right_2, right_s, right_r, back_1, back_2, back_s, back_r,
    rest_1, rest_2, rest_s, rest_r,
    core_s, core_r, up_s, up_r, down_s, down_r, lup_s, lup_r, ldown_s, ldown_r,
    rup_s, rup_r, rdown_s, rdown_r, tup_s, tup_r, tdown_s, tdown_r, rcore_s, rcore_r,
    part_s, part_r, gate_s, gate_r, small_s, small_r, load, local,
):
    line = groups // 2
    span = parts * rows
    group, q = lax.axis_index("dp"), lax.axis_index("seq")
    z, core = group // 2, lax.rem(group, 2)
    sibling = (2 * z + 1 - core, q)
    peers, others = seq_peers(parts), dp_peers(groups)
    tokens = back.shape[1]
    loads = [
        pltpu.make_async_copy(source, target, load.at[k])
        for k, (source, target) in enumerate(
            [(normed, normed_v), (dpx, dpx_v), (dz, dz_v), (wz, wz_v), (wx, wx_v)]
        )
    ]
    for copy in loads[:2]:
        copy.start()
    greet(peers + others)
    half_rows = left.shape[1] // 2
    lefts = LineSum(
        line, z, core, q, left, left_up, left_down, lup_s, lup_r, ldown_s, ldown_r, half_rows, 2
    )
    rights = LineSum(
        line, z, core, q, right_acc, right_up, right_down, rup_s, rup_r, rdown_s, rdown_r,
        half_rows, 2,
    )
    wholes = LineSum(
        line, z, core, q, acc, up, down, up_s, up_r, down_s, down_r, rows, parts
    )
    lefts.step(0)
    right_plane = PlaneSum(parts, group, q, right, right_1, right_2, right_s, right_r)
    rest_plane = PlaneSum(parts, group, q, rest, rest_1, rest_2, rest_s, rest_r)
    rests = LineSum(
        line, z, core, q, rest_acc, rest_up, rest_down, tup_s, tup_r, tdown_s, tdown_r, rows, 1
    )
    back_plane = PlaneSum(parts, group, q, back, back_1, back_2, back_s, back_r)
    right_plane.start(0)
    right_plane.start(1)
    waiting = []
    for k, peer in enumerate(peers):
        copy = remote(gate.at[peer[1]], gate_out.at[q], gate_s, gate_r, k, peer)
        copy.start()
        waiting.append(copy)
    for k, peer in enumerate(others):
        copy = remote(small, small_all.at[group], small_s, small_r, k, peer)
        copy.start()
        waiting.append(copy)
    own = [
        pltpu.make_async_copy(gate.at[q], gate_out.at[q], local.at[0]),
        pltpu.make_async_copy(small, small_all.at[group], local.at[1]),
    ]
    for copy in own:
        copy.start()
    loads[0].wait()
    loads[1].wait()
    for copy in loads[2:]:
        copy.start()
    tile = 512

    def dweight(of):
        at = pl.ds(pl.multiple_of(of * span, span), span)
        return dot(normed_v[:, at], dpx_v[...], TN)

    cores = {}
    order = [d for k in range(line // 2) for d in (line - 1 - k, k)]

    def share_core(d):
        total = dweight(2 * d + 1 - core)
        made[d] = total[:, :cw].astype(BF16)
        rest_made[d] = total[:, cw:].astype(BF16)
        cores[d] = [
            remote(made.at[d], held.at[d], core_s, core_r, d, sibling),
            remote(rest_made.at[d], rest_held.at[d], rcore_s, rcore_r, d, sibling),
        ]
        for copy in cores[d]:
            copy.start()

    def sum_core(d):
        total = dweight(2 * d + core)
        for copy in cores[d]:
            copy.wait()
        acc[d] = (total[:, :cw] + held[d].astype(F32)).astype(BF16)
        others = (total[:, cw:] + rest_held[d].astype(F32)).astype(BF16)
        for k in range(parts):
            rest[k, d] = others[k * rows : (k + 1) * rows]

    def dnormed(of):
        at = pl.ds(pl.multiple_of(of * tokens, tokens), tokens)

        def step(j, carry):
            cols = pl.ds(pl.multiple_of(j * tile, tile), tile)
            back[of, :, cols] = (
                dot(dz_v[at, :], wz_v[cols, :], NT) + dot(dpx_v[at, :], wx_v[cols, :], NT)
            ).astype(BF16)
            return carry

        lax.fori_loop(0, D // tile, step, 0)

    share_core(order[0])
    lefts.sent(0)
    lefts.step(1)
    share_core(order[1])
    sum_core(order[0])
    sum_core(order[1])
    wholes.step(0)
    for t in range(2, line - 1):
        lefts.sent(t - 1)
        lefts.step(t)
    for copy in loads[2:]:
        copy.wait()
    if parts == 4:
        dnormed(back_plane.far)
        back_plane.start_far()
    for d in order[2:]:
        share_core(d)
    for d in order[2:]:
        sum_core(d)
    right_plane.turn(32)
    if parts == 4:
        dnormed(back_plane.near[0])
        back_plane.start_near(0)
    wholes.sent(0)
    wholes.step(1)
    if parts == 4:
        dnormed(back_plane.near[1])
        back_plane.start_near(1)
    else:
        for peer in peers:
            dnormed(peer[1])
        back_plane.start(1)
    rest_plane.start(0)
    rest_plane.start(1)
    dnormed(q)
    right_plane.finish(right_acc, 32)
    for t in range(2, line - 1):
        wholes.sent(t - 1)
        wholes.step(t)
    rights.step(0)
    rest_plane.turn(rows)
    rest_plane.finish(rest_acc, rows)
    rests.step(0)
    back_plane.turn(32)
    lefts.finish(left_out)
    lefts.sent(line - 2)
    rests.sent(0)
    rests.step(1)
    rights.sent(0)
    rights.step(1)
    wholes.sent(line - 2)
    wholes.finish(final)
    for k, peer in enumerate(peers):
        block = final.at[pl.ds(pl.multiple_of(peer[1] * rows, rows), rows)]
        copy = remote(block, part.at[q], part_s, part_r, k, peer)
        copy.start()
        waiting.append(copy)
    copy = pltpu.make_async_copy(
        final.at[pl.ds(pl.multiple_of(q * rows, rows), rows)], part.at[q], local.at[2]
    )
    copy.start()
    own.append(copy)
    for t in range(2, line - 1):
        rights.sent(t - 1)
        rights.step(t)
    for t in range(2, line - 1):
        rests.sent(t - 1)
        rests.step(t)
    back_plane.finish(back_sum, 32)
    copy = pltpu.make_async_copy(back_sum, back_out, local.at[3])
    copy.start()
    own.append(copy)
    rests.finish(rest_out)
    rests.sent(line - 2)
    rights.finish(right_out)
    rights.sent(line - 2)
    for copy in own + waiting:
        copy.wait()


def sum_to_owners(collective_id, normed, left, right, gate, small, dz, dpx, wz, wx):
    parts, line, out_rows, slim = right.shape
    groups = 2 * line
    rows, cw = gate.shape[1:]
    span = rows * parts
    extra = dpx.shape[1] - cw
    tokens = dz.shape[0] // parts
    sem = pltpu.SemaphoreType.DMA
    vmem = pl.BlockSpec(memory_space=pltpu.VMEM)
    hbm = pl.BlockSpec(memory_space=pltpu.HBM)
    right_sum = (line, out_rows, slim)
    rest = (parts, line, rows, extra)
    return pl.pallas_call(
        functools.partial(owners_kernel, groups, parts, rows, cw),
        in_specs=[hbm, vmem, vmem, hbm, vmem, hbm, hbm, hbm, hbm],
        out_specs=[hbm, vmem, vmem, vmem, hbm, hbm, vmem],
        out_shape=[
            jax.ShapeDtypeStruct((parts, rows, cw), BF16),
            jax.ShapeDtypeStruct((rows, extra), F32),
            jax.ShapeDtypeStruct((out_rows, left.shape[-1]), F32),
            jax.ShapeDtypeStruct((out_rows, slim), F32),
            jax.ShapeDtypeStruct(gate.shape, BF16),
            jax.ShapeDtypeStruct((tokens, D), F32),
            jax.ShapeDtypeStruct((groups,) + small.shape, F32),
        ],
        scratch_shapes=[
            *([pltpu.VMEM((line, span, cw), BF16)] * 5),
            pltpu.VMEM((span, cw), BF16),
            *([pltpu.VMEM(left.shape, BF16)] * 2),
            *([pltpu.VMEM(right_sum, BF16)] * 3),
            *([pltpu.VMEM((line, span, extra), BF16)] * 2),
            pltpu.VMEM(rest, BF16),
            *([pltpu.VMEM(rest[1:], BF16)] * 3),
            *[pltpu.VMEM(a.shape, BF16) for a in (normed, dz, dpx, wz, wx)],
            pltpu.VMEM((parts, tokens, D), BF16),
            pltpu.VMEM((tokens, D), F32),
            *PlaneSum.scratch(parts, right.shape[1:], BF16),
            *PlaneSum.scratch(parts, (tokens, D), BF16),
            *PlaneSum.scratch(parts, rest[1:], BF16),
            *([sem((line,))] * 20),
            *([sem((parts - 1,))] * 4),
            *([sem((groups - 1,))] * 2),
            sem((5,)),
            sem((4,)),
        ],
        compiler_params=pltpu.CompilerParams(
            collective_id=collective_id, has_side_effects=True, vmem_limit_bytes=63 * 2**20
        ),
        name="sum_to_owners",
    )(normed, left, right, gate, small, dz, dpx, wz, wx)


def on_device(
    hidden_in, out_grads, w_in, w_in_m, w_in_v, w_out, w_out_m, w_out_v,
    chan_params, chan_m, chan_v, head_params, head_m, head_v,
):
    parts = lax.axis_size("seq")
    groups = lax.axis_size("dp")
    q = lax.axis_index("seq")
    rows = hidden_in.shape[1]
    length = rows * parts
    cw = INNER // parts
    hq = H // parts
    cc = cw + 2 * N
    in_rows = w_in.shape[0]
    out_rows = w_out.shape[0]

    chan_len = chan_params.shape[0]
    line = groups // 2
    group = lax.axis_index("dp")
    owner = group * parts + q
    chan_block = lax.dynamic_update_slice(
        jnp.zeros((8 * LANES,), F32),
        lax.reduce_precision(chan_params, 8, 7),
        (lax.rem(owner * chan_len, LANES),),
    ).reshape(8, LANES)
    head_block = jnp.pad(head_params, ((0, 5), (0, LANES - H)))
    hidden, wx, gate, wo, gain_in, own_gain, taps, heads, skip, spread, gather = collect(
        0, hidden_in[0], w_in, w_out, chan_block, head_block, chan_len, groups, parts
    )

    normed, px, y, states, z, u, stats, wz, wo = forward(
        1, hidden.reshape(length, D), wx.reshape(D, cc + LANES), gate, wo, gain_in, own_gain,
        taps, heads, skip, spread,
    )
    wx, wz = wx.reshape(D, cc + LANES), wz.reshape(D, cw)
    cotangent = out_grads[:, 0]
    back_own, coefs, block_out, dwo_left, dwo_right = middle(
        2, u, stats, wo, cotangent, hidden_in[0]
    )

    dz, dpx, small, dwo_left, dwz = backward(
        5, back_own.reshape(length, cw), coefs.reshape(length, LANES), normed, px, y, z, states,
        dwo_left, own_gain, taps, heads, skip, spread, gather,
    )
    x_part, rest, left_part, right_part, z_part, dnormed, small = sum_to_owners(
        4, normed, dwo_left, dwo_right, dwz.reshape(parts, in_rows, cw), small, dz, dpx, wz, wx
    )
    hidden_grad, chan_total, head_total, norm = gradient_norm(
        6, x_part, rest, z_part, left_part, right_part, dnormed, small, hidden_in[0],
        gain_in, cotangent, groups,
    )
    (
        hidden_grad, block_out, w_in_new, w_in_m_new, w_in_v_new, w_in_copy,
        w_out_new, w_out_m_new, w_out_v_new, w_out_copy,
    ) = update_weights(
        norm, x_part, rest, z_part, left_part, right_part, hidden_grad, block_out,
        (w_in, w_in_m, w_in_v, w_out, w_out_m, w_out_v),
    )
    hidden_grad, block_out = hidden_grad[None], block_out[:, None]
    grad_norm, clip_factor = norm[0, 0], norm[1, 0]
    chan_part = lax.dynamic_slice(chan_total.reshape(-1), (owner * chan_len,), (chan_len,))
    head_total = head_total[:parts, : 3 * hq].reshape(parts, 3, hq)
    head_total = head_total.transpose(1, 0, 2).reshape(3, H)
    chan_new, chan_m_new, chan_v_new = adam_tile(
        chan_params, clip_factor * chan_part, chan_m, chan_v, 0.2, 0.0
    )
    head_new, head_m_new, head_v_new = adam_tile(
        head_params, clip_factor * head_total, head_m, head_v, 1.0, 0.0
    )
    return (
        block_out, hidden_grad, grad_norm,
        w_in_new, w_in_m_new, w_in_v_new, w_in_copy,
        w_out_new, w_out_m_new, w_out_v_new, w_out_copy,
        chan_new, chan_m_new, chan_v_new, head_new, head_m_new, head_v_new,
    )


def solution(mesh):
    rows = P(("dp", "seq"), None)
    flat = P(("dp", "seq"))
    in_specs = (
        P("dp", "seq", None),
        P(None, "dp", "seq", None),
        *([rows] * 6),
        *([flat] * 3),
        *([P()] * 3),
    )
    out_specs = (
        P(None, "dp", "seq", None),
        P("dp", "seq", None),
        P(),
        *([rows] * 8),
        *([flat] * 3),
        *([P()] * 3),
    )
    return jax.shard_map(
        on_device, mesh=mesh, in_specs=in_specs, out_specs=out_specs, check_vma=False
    )
```
